32 devices in a mesh: section: 2 (over core), dp: 8 (over z, y), mp: 2 (over x).
Axes of the slice: x: 2, y: 2, z: 4, core: 2. Of those that a mesh axis runs over, the one named last changes fastest.
Arguments:
- tokens: bfloat16 [2, 8, 256, 768], P(None, 'dp', 'mp'), may hold values from -6 to 6
- clip_lengths: int32 [2, 8], P(None, 'dp'), may hold values from 156 to 157
- clip_cells: int32 [2, 8, 256], P(None, 'dp'), may hold values from 0 to 1567, as said below
- enc_qkv: bfloat16 [768, 3, 768], P(None, None, 'mp'), may hold values from -0.21875 to 0.21875
- enc_attn_out: bfloat16 [768, 768], P('mp'), may hold values from -0.875 to 0.875
- enc_up: bfloat16 [768, 3072], P(None, 'mp'), may hold values from -0.21875 to 0.21875
- enc_down: bfloat16 [3072, 768], P('mp'), may hold values from -0.109375 to 0.109375
- enc_gain_one: float32 [768], replicated, may hold values from 0.1 to 1.9
- enc_gain_two: float32 [768], replicated, may hold values from 0.1 to 1.9
- bridge_weight: bfloat16 [768, 384], replicated, may hold values from -0.21875 to 0.21875
- mask_token: float32 [384], replicated, may hold values from -6 to 6
- position_embed: float32 [1568, 384], P('mp'), may hold values from -6 to 6
- dec_qkv: bfloat16 [384, 3, 384], P(None, None, 'mp'), may hold values from -0.3125 to 0.3125
- dec_attn_out: bfloat16 [384, 384], P('mp'), may hold values from -1.75 to 1.75
- dec_up: bfloat16 [384, 1536], P(None, 'mp'), may hold values from -0.875 to 0.875
- dec_down: bfloat16 [1536, 384], P('mp'), may hold values from -0.15625 to 0.15625
- dec_gain_one: float32 [384], replicated, may hold values from 0.1 to 1.9
- dec_gain_two: float32 [384], replicated, may hold values from 0.1 to 1.9
- cotangent: bfloat16 [2, 8, 1568, 384], P(None, 'dp', 'mp'), may hold values from -6 to 6
Outputs:
- decoded: float32 [2, 8, 1568, 384], P(None, 'dp', 'mp', 'section')
- tokens_grad: float32 [2, 8, 256, 768], P(None, 'dp', 'mp', 'section')
- enc_qkv_grad: float32 [768, 3, 768], P(('section', 'dp'), None, 'mp')
- enc_attn_out_grad: float32 [768, 768], P('mp', ('section', 'dp'))
- enc_up_grad: float32 [768, 3072], P(('section', 'dp'), 'mp')
- enc_down_grad: float32 [3072, 768], P('mp', ('section', 'dp'))
- enc_gain_one_grad: float32 [768], replicated
- enc_gain_two_grad: float32 [768], replicated
- bridge_grad: float32 [768, 384], replicated
- mask_grad: float32 [384], replicated
- position_grad: float32 [1568, 384], P('mp', ('section', 'dp'))
- dec_qkv_grad: float32 [384, 3, 384], P(('section', 'dp'), None, 'mp')
- dec_attn_out_grad: float32 [384, 384], P('mp', ('section', 'dp'))
- dec_up_grad: float32 [384, 1536], P(('section', 'dp'), 'mp')
- dec_down_grad: float32 [1536, 384], P('mp', ('section', 'dp'))
- dec_gain_one_grad: float32 [384], replicated
- dec_gain_two_grad: float32 [384], replicated
The draws below stay inside these ranges and needn't reach their ends.
Inputs may be any that keep to these rules, and one draw needn't show every extreme that they name: `clip_cells`: within each row of 256 slots the entries are distinct.
All inputs are finite; a program needn't handle non-finite values.
Results may differ from the reference program's by a relative error of at most 0.03.
Values may be sent and summed in bfloat16 or wider, within the bound.
A program may use at most 256 MiB of HBM per device.

```python
import jax
import jax.numpy as jnp
from jax import lax

DE = 768
HEAD = 64
FE = 3072
DD = 384
FD = 1536
LDEC = 1568
VIS = 156
ROW = 256
M = 2
N_DP = 8


def draw_clip_lengths(key, part):
    key = jax.random.fold_in(key, 11)
    key_base, key_pick = jax.random.split(key)
    base = VIS + jax.random.randint(key_base, (M * N_DP,), 0, 2)
    order = jax.random.permutation(key_pick, M * N_DP)
    indices = jnp.arange(M * N_DP)
    filled = jnp.where(indices == order[0], VIS + 1, base)
    filled = jnp.where(indices == order[1], VIS, filled)
    return filled.reshape(M, N_DP).astype(jnp.int32)


def draw_clip_cells(key, part):
    key = jax.random.fold_in(key, 23)
    row_keys = jax.random.split(key, M * N_DP)

    def one_row(row_key):
        key_order, key_spot = jax.random.split(row_key)
        order = jax.random.permutation(key_order, LDEC).astype(jnp.int32)
        spot = jax.random.randint(key_spot, (), 0, VIS)
        where_top = jnp.argmax(order == LDEC - 1)
        indices = jnp.arange(LDEC)
        swapped = jnp.where(indices == where_top, order[spot], order)
        swapped = jnp.where(indices == spot, LDEC - 1, swapped)
        return swapped[:ROW]
    return jax.vmap(one_row)(row_keys).reshape(M, N_DP, ROW).astype(jnp.int32)


def shard_levels(key, dims, shards, low, largest):
    factor_of, own = 1.0, jax.random.fold_in(key, 6)
    for axis_at, blocks in shards:
        draws = jnp.exp(jax.random.uniform(jax.random.fold_in(own, axis_at), (blocks,), jnp.float32, low / len(shards), largest / len(shards)))
        factor_of = factor_of * jnp.repeat(draws, dims[axis_at] // blocks).reshape([-1 if axis == axis_at else 1 for axis in range(len(dims))])
    return factor_of


def gaussian(rng, dims, scale, reach, shards=(), dtype=jnp.bfloat16):
    array = scale * jax.random.normal(rng, dims, jnp.float32)
    if shards:
        array = array * shard_levels(rng, dims, shards, -0.22, 0.18)
    return jnp.clip(array, -reach, reach).astype(dtype)


def setup_inputs(seed: int = 0) -> dict:
    seeds = jax.random.split(jax.random.key(seed), 20)
    tokens = gaussian(seeds[0], (M, N_DP, ROW, DE), 1.0, 6.0, ((1, 8), (2, 2)))
    clip_lengths = draw_clip_lengths(jax.random.fold_in(seeds[19], 71), 0)
    clip_cells = draw_clip_cells(jax.random.fold_in(seeds[19], 71), 0)
    enc_qkv = gaussian(seeds[3], (DE, 3, DE), DE ** -0.5, 0.21875, ((2, 2),))
    enc_attn_out = gaussian(seeds[4], (DE, DE), (DE // 16) ** -0.5, 0.875, ((0, 2),))
    enc_up = gaussian(seeds[5], (DE, FE), DE ** -0.5, 0.21875, ((1, 2),))
    enc_down = gaussian(seeds[6], (FE, DE), FE ** -0.5, 0.109375, ((0, 2),))
    enc_gain_one = jnp.clip(1.0 + 0.18 * jax.random.normal(seeds[7], (DE,), jnp.float32), 0.1, 1.9)
    enc_gain_two = jnp.clip(1.0 + 0.18 * jax.random.normal(seeds[8], (DE,), jnp.float32), 0.1, 1.9)
    bridge_weight = gaussian(seeds[9], (DE, DD), DE ** -0.5, 0.21875)
    mask_token = gaussian(seeds[10], (DD,), 1.0, 6.0, (), jnp.float32)
    position_embed = gaussian(seeds[11], (LDEC, DD), 1.0, 6.0, ((0, 2),), jnp.float32)
    dec_qkv = gaussian(seeds[12], (DD, 3, DD), DD ** -0.5, 0.3125, ((2, 2),))
    dec_attn_out = gaussian(seeds[13], (DD, DD), (DD // 32) ** -0.5, 1.75, ((0, 2),))
    dec_up = gaussian(seeds[14], (DD, FD), (DD // 8) ** -0.5, 0.875, ((1, 2),))
    dec_down = gaussian(seeds[15], (FD, DD), FD ** -0.5, 0.15625, ((0, 2),))
    dec_gain_one = jnp.clip(1.0 + 0.18 * jax.random.normal(seeds[16], (DD,), jnp.float32), 0.1, 1.9)
    dec_gain_two = jnp.clip(1.0 + 0.18 * jax.random.normal(seeds[17], (DD,), jnp.float32), 0.1, 1.9)
    cotangent = gaussian(seeds[18], (M, N_DP, LDEC, DD), 1.0, 6.0, ((1, 8), (2, 2)))
    return {"tokens": tokens, "clip_lengths": clip_lengths, "clip_cells": clip_cells, "enc_qkv": enc_qkv, "enc_attn_out": enc_attn_out, "enc_up": enc_up, "enc_down": enc_down, "enc_gain_one": enc_gain_one, "enc_gain_two": enc_gain_two, "bridge_weight": bridge_weight, "mask_token": mask_token, "position_embed": position_embed, "dec_qkv": dec_qkv, "dec_attn_out": dec_attn_out, "dec_up": dec_up, "dec_down": dec_down, "dec_gain_one": dec_gain_one, "dec_gain_two": dec_gain_two, "cotangent": cotangent}


EPS = 1e-06
NEG = -1e+30
HIGH = lax.Precision.HIGHEST

@jax.custom_vjp
def low(v):
    return lax.optimization_barrier(v.astype(jnp.bfloat16)).astype(jnp.float32)

@jax.custom_vjp
def low_back(v):
    return v

def low_keep(v):
    return (low(v), None)

def low_pass(kept, grad):
    return (grad,)

def back_keep(v):
    return (v, None)

def back_low(kept, grad):
    return (low(grad),)
low.defvjp(low_keep, low_pass)
low_back.defvjp(back_keep, back_low)

def matmul(operand, second):
    return jnp.dot(operand, second, precision=HIGH, preferred_element_type=jnp.float32)

def layer_norm(stream, norm_gain):
    centre = stream - lax.optimization_barrier(jnp.mean(stream, -1, keepdims=True))
    spread = lax.optimization_barrier(jnp.mean(centre * centre, -1, keepdims=True))
    return centre * lax.rsqrt(spread + EPS) * norm_gain

def attention(queries, keys_all, values, usable):
    seq_len = queries.shape[0]
    head_count = queries.shape[1]
    blocks = 2 if seq_len >= 1024 and seq_len % 2 == 0 else 1
    score_scale = HEAD ** (-0.5)

    def one_block(query_block):
        scores = jnp.einsum('qhd,khd->hqk', query_block, keys_all, precision=HIGH) * score_scale
        scores = low_back(jnp.where(usable[None, None, :], scores, NEG))
        weights = jax.nn.softmax(scores, axis=-1)
        return jnp.einsum('hqk,khd->qhd', low(weights), values, precision=HIGH)
    outputs = lax.map(jax.checkpoint(one_block), queries.reshape(blocks, seq_len // blocks, head_count, HEAD))
    return outputs.reshape(seq_len, head_count * HEAD)

def block(stream, params, usable):
    qkv_weight, out_weight, up_weight, down_weight, gain_one, gain_two = params
    seq_len, feature_dim = stream.shape
    head_count = feature_dim // HEAD
    normed = low(layer_norm(stream, gain_one))
    triple = low(low_back(matmul(normed, qkv_weight.reshape(feature_dim, 3 * feature_dim))))
    triple = triple.reshape(seq_len, 3, head_count, HEAD)
    blended = low(low_back(attention(triple[:, 0], triple[:, 1], triple[:, 2], usable)))
    middle = stream + low_back(matmul(blended, out_weight))
    normed_two = low(layer_norm(middle, gain_two))
    before = low_back(matmul(normed_two, up_weight))
    hidden = low(jax.nn.gelu(before, approximate=False))
    return middle + low_back(matmul(hidden, down_weight))

def fill(visible, length_one, cells_one, mask_vec, position_table):
    place = (cells_one[None, :] == jnp.arange(LDEC)[:, None]) & (jnp.arange(ROW)[None, :] < length_one)
    place = place.astype(jnp.float32)
    seen_count = lax.optimization_barrier(jnp.sum(place, 1, keepdims=True))
    return matmul(place, visible) + (1.0 - seen_count) * mask_vec + position_table

def reference(tokens, clip_lengths, clip_cells, enc_qkv, enc_attn_out, enc_up, enc_down, enc_gain_one, enc_gain_two, bridge_weight, mask_token, position_embed, dec_qkv, dec_attn_out, dec_up, dec_down, dec_gain_one, dec_gain_two, cotangent):
    lengths_flat = clip_lengths.reshape(-1)
    cells_flat = clip_cells.reshape(-1, ROW)

    def forward(inputs, enc_params, bridge, mask_vec, position_table, dec_params):
        rows_in = inputs.reshape(M * N_DP, ROW, DE)

        def one_row(row_tokens, length_one, cells_one):
            usable = jnp.arange(ROW) < length_one
            encoded = block(row_tokens, enc_params, usable)
            visible = low(low_back(matmul(low(encoded), bridge)))
            filled = fill(visible, length_one, cells_one, mask_vec, position_table)
            return block(filled, dec_params, jnp.ones((LDEC,), bool))
        checked = jax.checkpoint(one_row)

        def scan_step(carry, items):
            return (carry, checked(items[0], items[1], items[2]))
        carry_end, outputs = lax.scan(scan_step, jnp.zeros((), jnp.float32), (rows_in, lengths_flat, cells_flat))
        return outputs.reshape(M, N_DP, LDEC, DD)
    to_float = lambda item: item.astype(jnp.float32)
    enc_params = (to_float(enc_qkv), to_float(enc_attn_out), to_float(enc_up), to_float(enc_down), to_float(enc_gain_one), to_float(enc_gain_two))
    dec_params = (to_float(dec_qkv), to_float(dec_attn_out), to_float(dec_up), to_float(dec_down), to_float(dec_gain_one), to_float(dec_gain_two))
    decoded, pull = jax.vjp(forward, to_float(tokens), enc_params, to_float(bridge_weight), to_float(mask_token), to_float(position_embed), dec_params)
    token_grad, enc_grads, bridge_grad, mask_grad, position_grad, dec_grads = pull(to_float(cotangent))
    return (decoded, token_grad, enc_grads[0], enc_grads[1], enc_grads[2], enc_grads[3], enc_grads[4], enc_grads[5], bridge_grad, mask_grad, position_grad, dec_grads[0], dec_grads[1], dec_grads[2], dec_grads[3], dec_grads[4], dec_grads[5])
```

```python
import functools

import jax
import jax.numpy as jnp
from jax import lax
from jax.experimental import pallas as pl
from jax.experimental.pallas import tpu as pltpu
from jax.sharding import PartitionSpec as P

HEAD = 64
LONGEST = 157
EPS = 1e-06
NEG = -1e30
F32 = jnp.float32
B16 = jnp.bfloat16
MESH = pl.DeviceIdType.MESH
VMEM = pltpu.VMEM
LIMIT = 56 * 1024 * 1024


def place_of():
    return lax.axis_index("section"), lax.axis_index("dp"), lax.axis_index("mp")


def greet(partners):
    barrier = pltpu.get_barrier_semaphore()
    for partner in partners:
        pl.semaphore_signal(barrier, inc=1, device_id=partner, device_id_type=MESH)
    pl.semaphore_wait(barrier, len(partners))


def send(src, dst, send_sem, recv_sem, partner):
    return pltpu.make_async_remote_copy(
        src_ref=src,
        dst_ref=dst,
        send_sem=send_sem,
        recv_sem=recv_sem,
        device_id=partner,
        device_id_type=MESH,
    )


def remote_params(ident):
    return pltpu.CompilerParams(
        collective_id=ident, has_side_effects=True, vmem_limit_bytes=LIMIT
    )


def swap_kernel(kind, count, *refs):
    ins, outs, (send_sem, recv_sem) = refs[:count], refs[count : 2 * count], refs[2 * count :]
    s, d, m = place_of()
    partner = (1 - s, d, m) if kind == "core" else (s, d, 1 - m)
    greet([partner])
    copies = [
        send(ins[i], outs[i], send_sem.at[i], recv_sem.at[i], partner) for i in range(count)
    ]
    for copy in copies:
        copy.start()
    for copy in copies:
        copy.wait()


def swap(arrays, kind, ident):
    count = len(arrays)
    return pl.pallas_call(
        functools.partial(swap_kernel, kind, count),
        out_shape=[jax.ShapeDtypeStruct(a.shape, a.dtype) for a in arrays],
        in_specs=[pl.BlockSpec(memory_space=pl.ANY)] * count,
        out_specs=[pl.BlockSpec(memory_space=pl.ANY)] * count,
        scratch_shapes=[pltpu.SemaphoreType.DMA((count,)), pltpu.SemaphoreType.DMA((count,))],
        compiler_params=remote_params(ident),
        name=f"swap_{kind}_{ident}",
    )(*arrays)


def route_kernel(x_ref, out_ref, send_sem, recv_sem, local_sem):
    s, d, m = place_of()
    greet([(1 - s, d, m), (s, d, 1 - m), (1 - s, d, 1 - m)])
    stays = s == m

    @pl.when(stays)
    def _():
        mine = pltpu.make_async_copy(x_ref.at[s], out_ref.at[m], local_sem)
        mine.start()
        out = send(x_ref.at[1 - s], out_ref.at[m], send_sem.at[0], recv_sem.at[m], (1 - s, d, m))
        out.start()
        mine.wait()
        out.wait_send()

    @pl.when(jnp.logical_not(stays))
    def _():
        near = send(x_ref.at[s], out_ref.at[m], send_sem.at[0], recv_sem.at[m], (s, d, 1 - m))
        far = send(
            x_ref.at[1 - s], out_ref.at[m], send_sem.at[1], recv_sem.at[m], (1 - s, d, 1 - m)
        )
        near.start()
        far.start()
        near.wait_send()
        far.wait_send()

    pltpu.make_async_copy(out_ref.at[1 - m], out_ref.at[1 - m], recv_sem.at[1 - m]).wait()

    @pl.when(jnp.logical_not(stays))
    def _():
        pltpu.make_async_copy(out_ref.at[m], out_ref.at[m], recv_sem.at[m]).wait()


def route(x, ident):
    return pl.pallas_call(
        route_kernel,
        out_shape=jax.ShapeDtypeStruct(x.shape, x.dtype),
        in_specs=[pl.BlockSpec(memory_space=pl.ANY)],
        out_specs=pl.BlockSpec(memory_space=pl.ANY),
        scratch_shapes=[
            pltpu.SemaphoreType.DMA((2,)),
            pltpu.SemaphoreType.DMA((2,)),
            pltpu.SemaphoreType.DMA,
        ],
        compiler_params=remote_params(ident),
        name=f"route_{ident}",
    )(x)


def scatter_kernel(n, across, g_ref, out_ref, near, work, far, over, sems):
    near_send, near_recv, far_send, far_recv, over_send, over_recv = sems
    s, d, m = place_of()
    sibling, facing = (1 - s, d, m), (s, d, 1 - m)
    greet([sibling] + [facing] * across + [(s, lax.rem(d + k, n), m) for k in range(1, n)])
    order = [*range(1, n), 0]
    sides = 1 + across
    first = {}
    for side in reversed(range(sides)):
        for k in order:
            to = lax.rem(d + k, n)
            first[side, k] = send(
                g_ref.at[side, (1 - s) * n + to],
                near.at[side, to],
                near_send.at[side, k],
                near_recv.at[side, k],
                sibling,
            )
            first[side, k].start()

    def summed(side, k):
        to = lax.rem(d + k, n)
        first[side, k].wait()
        return to, g_ref[side, s * n + to].astype(F32) + near[side, to].astype(F32)

    second = {}
    if across:
        for k in order:
            to, part = summed(1, k)
            work[1, to] = part.astype(B16)
            second[k] = send(work.at[1, to], over.at[to], over_send.at[k], over_recv.at[k], facing)
            second[k].start()
    third = []
    for k in order:
        to, part = summed(0, k)
        if across:
            second[k].wait()
            part = part + over[to].astype(F32)
        if k:
            work[0, to] = part.astype(B16)
            copy = send(work.at[0, to], far.at[d], far_send.at[k], far_recv.at[k], (s, to, m))
            copy.start()
            third.append((k, copy))
    for k, copy in third:
        copy.wait()
        part = part + far[lax.rem(d + n - k, n)].astype(F32)
    out_ref[...] = part


def scatter(g, ident):
    sides, owners, rows, cols = g.shape
    n = owners // 2
    across = sides - 1
    kernel = functools.partial(scatter_kernel, n, across)

    def body(g_ref, out_ref, near, work, far, over, *sems):
        kernel(g_ref, out_ref, near, work, far, over, sems)

    pieces = (n, rows, cols)
    return pl.pallas_call(
        body,
        out_shape=jax.ShapeDtypeStruct((rows, cols), F32),
        in_specs=[pl.BlockSpec(memory_space=VMEM)],
        out_specs=pl.BlockSpec(memory_space=VMEM),
        scratch_shapes=[
            VMEM((sides,) + pieces, B16),
            VMEM((sides,) + pieces, B16),
            VMEM(pieces, B16),
            VMEM(pieces if across else (8, 128), B16),
            pltpu.SemaphoreType.DMA((sides, n)),
            pltpu.SemaphoreType.DMA((sides, n)),
            pltpu.SemaphoreType.DMA((n,)),
            pltpu.SemaphoreType.DMA((n,)),
            pltpu.SemaphoreType.DMA((n,)),
            pltpu.SemaphoreType.DMA((n,)),
        ],
        compiler_params=remote_params(ident),
        name=f"scatter_{ident}",
    )(g)


def gather_kernel(n, x_ref, out_ref, local_sem, send_sem, recv_sem):
    s, d, m = place_of()
    steps = [(a, k, b) for k in range(n) for a in range(2) for b in range(2) if a or k or b]

    def partner(step):
        a, k, b = step
        return (lax.rem(s + a, 2), lax.rem(d + k, n), lax.rem(m + b, 2))

    greet([partner(step) for step in steps])
    slot = (s * n + d) * 2 + m
    mine = pltpu.make_async_copy(x_ref, out_ref.at[slot], local_sem)
    mine.start()
    copies = [
        send(x_ref, out_ref.at[slot], send_sem.at[i], recv_sem.at[i], partner(step))
        for i, step in enumerate(steps)
    ]
    for copy in copies:
        copy.start()
    mine.wait()
    for copy in copies:
        copy.wait()


def gather(x, n, ident):
    count = 4 * n
    return pl.pallas_call(
        functools.partial(gather_kernel, n),
        out_shape=jax.ShapeDtypeStruct((count,) + x.shape, x.dtype),
        in_specs=[pl.BlockSpec(memory_space=VMEM)],
        out_specs=pl.BlockSpec(memory_space=VMEM),
        scratch_shapes=[
            pltpu.SemaphoreType.DMA,
            pltpu.SemaphoreType.DMA((count - 1,)),
            pltpu.SemaphoreType.DMA((count - 1,)),
        ],
        compiler_params=remote_params(ident),
        name=f"gather_{ident}",
    )(x)


def dot_nt(a, b):
    return lax.dot_general(a, b, (((1,), (1,)), ((), ())), preferred_element_type=F32)


def dot_nn(a, b):
    return lax.dot_general(a, b, (((1,), (0,)), ((), ())), preferred_element_type=F32)


def dot_tn(a, b):
    return lax.dot_general(a, b, (((0,), (0,)), ((), ())), preferred_element_type=F32)


def chunks_of(length, most=256):
    units = length // 16
    count = -(-length // most)
    cuts = [16 * (units * i // count) for i in range(count)] + [length]
    return [(a, b - a) for a, b in zip(cuts, cuts[1:])]


def head_masks():
    lanes = lax.broadcasted_iota(jnp.int32, (1, 2 * HEAD), 1)
    return (lanes < HEAD, lanes >= HEAD)


def attend_kernel(q_ref, k_ref, v_ref, o_ref, p_ref):
    masks = head_masks()
    k = k_ref[...]
    v = v_ref[...]
    for start, size in chunks_of(q_ref.shape[0], 128):
        rows = pl.ds(start, size)
        q = q_ref[rows] * jnp.asarray(HEAD**-0.5, B16)
        halves = []
        for head in range(2):
            scores = dot_nt(jnp.where(masks[head], q, 0), k)
            top = jnp.max(scores, -1, keepdims=True)
            raised = jnp.exp(scores - top)
            whole = jnp.sum(raised, -1, keepdims=True)
            p = (raised * (1.0 / whole)).astype(B16)
            p_ref[head, rows] = p
            halves.append(dot_nn(p, v))
        o_ref[rows] = jnp.where(masks[0], halves[0], halves[1]).astype(B16)


def attend(q, k, v):
    length, width = q.shape
    keys = k.shape[0]
    pairs = width // (2 * HEAD)
    return pl.pallas_call(
        attend_kernel,
        grid=(pairs,),
        out_shape=[
            jax.ShapeDtypeStruct((length, width), B16),
            jax.ShapeDtypeStruct((2 * pairs, length, keys), B16),
        ],
        in_specs=[
            pl.BlockSpec((length, 2 * HEAD), lambda i: (0, i)),
            pl.BlockSpec((keys, 2 * HEAD), lambda i: (0, i)),
            pl.BlockSpec((keys, 2 * HEAD), lambda i: (0, i)),
        ],
        out_specs=[
            pl.BlockSpec((length, 2 * HEAD), lambda i: (0, i)),
            pl.BlockSpec((2, length, keys), lambda i: (i, 0, 0)),
        ],
        compiler_params=pltpu.CompilerParams(vmem_limit_bytes=LIMIT),
        name="attend",
    )(q, k, v)


def attend_back_kernel(q_ref, k_ref, v_ref, o_ref, do_ref, p_ref, dq_ref, dk_ref, dv_ref, dk_t, dv_t):
    masks = head_masks()
    k = k_ref[...]
    v = v_ref[...]
    scale = HEAD**-0.5
    for index, (start, size) in enumerate(chunks_of(q_ref.shape[0], 256)):
        rows = pl.ds(start, size)
        q = q_ref[rows]
        do = do_ref[rows]
        both = do.astype(F32) * o_ref[rows].astype(F32)
        dq = []
        for head in range(2):
            do_head = jnp.where(masks[head], do, 0)
            delta = jnp.sum(jnp.where(masks[head], both, 0.0), -1, keepdims=True)
            p = p_ref[head, rows]
            dp = dot_nt(do_head, v)
            ds = (p.astype(F32) * (dp - delta)).astype(B16)
            dq.append(dot_nn(ds, k))
            feats = pl.ds(head * HEAD, HEAD)
            dv_part = dot_tn(do[:, head * HEAD : (head + 1) * HEAD], p)
            dk_part = dot_tn(q[:, head * HEAD : (head + 1) * HEAD], ds)
            if index:
                dv_part = dv_part + dv_t[feats]
                dk_part = dk_part + dk_t[feats]
            dv_t[feats] = dv_part
            dk_t[feats] = dk_part
        dq_ref[rows] = (jnp.where(masks[0], dq[0], dq[1]) * scale).astype(B16)
    dk_ref[...] = (jnp.transpose(dk_t[...]) * scale).astype(dk_ref.dtype)
    dv_ref[...] = jnp.transpose(dv_t[...]).astype(dv_ref.dtype)


def attend_back(q, k, v, o, do, p):
    length, width = q.shape
    keys = k.shape[0]
    pairs = width // (2 * HEAD)
    short = pl.BlockSpec((length, 2 * HEAD), lambda i: (0, i))
    long = pl.BlockSpec((keys, 2 * HEAD), lambda i: (0, i))
    return pl.pallas_call(
        attend_back_kernel,
        grid=(pairs,),
        out_shape=[
            jax.ShapeDtypeStruct((length, width), B16),
            jax.ShapeDtypeStruct((keys, width), F32),
            jax.ShapeDtypeStruct((keys, width), F32),
        ],
        in_specs=[
            short,
            long,
            long,
            short,
            short,
            pl.BlockSpec((2, length, keys), lambda i: (i, 0, 0)),
        ],
        out_specs=[short, long, long],
        scratch_shapes=[VMEM((2 * HEAD, keys), F32), VMEM((2 * HEAD, keys), F32)],
        compiler_params=pltpu.CompilerParams(vmem_limit_bytes=LIMIT),
        name="attend_back",
    )(q, k, v, o, do, p)


def normed(z, gain):
    centre = z - jnp.mean(z, -1, keepdims=True)
    inverse = lax.rsqrt(jnp.mean(centre * centre, -1, keepdims=True) + EPS)
    unit = centre * inverse
    return unit, inverse, (unit * gain).astype(B16)


def norm_back(grad, unit, inverse, gain):
    scaled = grad * gain
    return inverse * (
        scaled
        - jnp.mean(scaled, -1, keepdims=True)
        - unit * jnp.mean(scaled * unit, -1, keepdims=True)
    )


def gelu(u):
    return 0.5 * u * (1.0 + lax.erf(u * 0.5**0.5))


def gelu_slope(u):
    return 0.5 * (1.0 + lax.erf(u * 0.5**0.5)) + u * jnp.exp(-0.5 * u * u) * (
        0.5 / jnp.pi
    ) ** 0.5


def small_attend(triple, length):
    rows = triple.shape[0]
    q, k, v = (triple[:, i] for i in range(3))
    scores = jnp.einsum("qhd,khd->hqk", q, k, preferred_element_type=F32) * HEAD**-0.5
    scores = jnp.where(jnp.arange(rows)[None, None, :] < length, scores, NEG)
    p = jax.nn.softmax(scores, axis=-1)
    o = jnp.einsum("hqk,khd->qhd", p.astype(B16), v, preferred_element_type=F32)
    return p, o.reshape(rows, -1).astype(B16)


def small_attend_back(triple, p, do):
    q, k, v = (triple[:, i] for i in range(3))
    do = do.reshape(q.shape)
    dp = jnp.einsum("qhd,khd->hqk", do, v, preferred_element_type=F32)
    ds = (p * (dp - jnp.sum(p * dp, -1, keepdims=True))).astype(B16)
    scale = HEAD**-0.5
    dq = jnp.einsum("hqk,khd->qhd", ds, k, preferred_element_type=F32) * scale
    dk = jnp.einsum("hqk,qhd->khd", ds, q, preferred_element_type=F32) * scale
    dv = jnp.einsum("hqk,qhd->khd", p.astype(B16), do, preferred_element_type=F32)
    return jnp.stack([dq, dk, dv], 1).astype(B16).reshape(q.shape[0], -1)


def pack(grad, owners):
    rows, cols = grad.shape
    own = rows // owners
    fold = 1
    while own * fold % 16:
        fold *= 2
    grad = grad.astype(B16).reshape(owners, own, fold, cols // fold)
    return jnp.swapaxes(grad, 1, 2).reshape(owners, fold * own, cols // fold)


def unpack(piece, own):
    fold = piece.shape[0] // own
    return jnp.swapaxes(piece.reshape(fold, own, -1), 0, 1).reshape(own, -1)


def pick(pair, index):
    return lax.dynamic_index_in_dim(pair, index, 0, keepdims=False)


def per_device(
    tokens,
    clip_lengths,
    clip_cells,
    enc_qkv,
    enc_attn_out,
    enc_up,
    enc_down,
    enc_gain_one,
    enc_gain_two,
    bridge_weight,
    mask_token,
    position_embed,
    dec_qkv,
    dec_attn_out,
    dec_up,
    dec_down,
    dec_gain_one,
    dec_gain_two,
    cotangent,
):
    s, d, m = place_of()
    n = lax.axis_size("dp")
    owners = 2 * n
    stays = s == m
    cells_half, dec_wide = position_embed.shape
    slots = clip_cells.shape[2]
    half_slots = tokens.shape[2]
    enc_wide = tokens.shape[3]
    used = -(-LONGEST // 32) * 32

    swapped = swap(
        [
            pick(tokens[:, 0], s),
            dec_qkv.reshape(dec_wide, -1),
            dec_attn_out,
            dec_up,
            dec_down,
            pick(cotangent[:, 0], 1 - m),
            position_embed.astype(B16),
        ],
        "x",
        1,
    )
    tok_far, dqkv_far, dout_far, dup_far, ddown_far, cot_far, pos_far = swapped
    cot = jnp.where(stays, pick(cotangent[:, 0], m), cot_far)
    pos = jnp.where(stays, position_embed, pos_far.astype(F32))
    w_qkv = jnp.concatenate(
        [dec_qkv, dqkv_far.reshape(dec_qkv.shape)], 2
    ).reshape(dec_wide, -1)
    w_out = jnp.concatenate([dec_attn_out, dout_far], 0)
    w_up = jnp.concatenate([dec_up, dup_far], 1)
    w_down = jnp.concatenate([dec_down, ddown_far], 0)

    tok_near = pick(tokens[:, 0], s)
    x = jnp.concatenate(
        [jnp.where(m == 0, tok_near, tok_far), jnp.where(m == 0, tok_far, tok_near)], 0
    )[:used].astype(F32)
    length = pick(clip_lengths[:, 0], s)
    e_qkv = enc_qkv.reshape(enc_wide, -1)
    unit1, inv1, a = normed(x, enc_gain_one)
    triple = jnp.dot(a, e_qkv, preferred_element_type=F32).astype(B16)
    triple = triple.reshape(used, 3, -1, HEAD)
    ep, eo = small_attend(triple, length)
    part = jnp.dot(eo, enc_attn_out, preferred_element_type=F32)
    z2 = x + part + swap([part.astype(B16)], "x", 2)[0].astype(F32)
    unit2, inv2, b = normed(z2, enc_gain_two)
    u = jnp.dot(b, enc_up, preferred_element_type=F32)
    h = gelu(u).astype(B16)
    part = jnp.dot(h, enc_down, preferred_element_type=F32)
    enc = (z2 + part + swap([part.astype(B16)], "x", 3)[0].astype(F32)).astype(B16)
    vis = jnp.dot(enc, bridge_weight, preferred_element_type=F32).astype(B16)
    vis_far = swap([vis], "core", 4)[0]

    vis_used = jnp.where(stays, vis, vis_far)
    cell_ids = s * cells_half + jnp.arange(cells_half, dtype=jnp.int32)
    place = (pick(clip_cells[:, 0], m)[None, :used] == cell_ids[:, None]) & (
        jnp.arange(used)[None, :] < pick(clip_lengths[:, 0], m)
    )
    place = place.astype(B16)
    unseen = 1.0 - jnp.sum(place.astype(F32), 1, keepdims=True)
    filled = jnp.dot(place, vis_used, preferred_element_type=F32) + unseen * mask_token + pos
    dunit1, dinv1, da_in = normed(filled, dec_gain_one)
    dqkv = jnp.dot(da_in, w_qkv, preferred_element_type=F32).astype(B16)
    q, kv = dqkv[:, :dec_wide], dqkv[:, dec_wide:]
    kv_all = jnp.concatenate([kv, swap([kv], "core", 5)[0]], 0)
    k_all, v_all = kv_all[:, :dec_wide], kv_all[:, dec_wide:]
    do_out, dp_saved = attend(q, k_all, v_all)
    dz2 = filled + jnp.dot(do_out, w_out, preferred_element_type=F32)
    dunit2, dinv2, db_in = normed(dz2, dec_gain_two)
    du = jnp.dot(db_in, w_up, preferred_element_type=F32)
    dh = gelu(du).astype(B16)
    dec = dz2 + jnp.dot(dh, w_down, preferred_element_type=F32)

    def cut(value):
        return jnp.stack(jnp.split(value.astype(B16), 2, axis=1))

    decoded = route(cut(dec), 6)

    dy = cot.astype(F32)
    grad_h = dot_nt(cot, w_down)
    g_down = dot_tn(cot, dh)
    grad_u = (grad_h * gelu_slope(du)).astype(B16)
    g_up = dot_tn(db_in, grad_u)
    grad_b = dot_nt(grad_u, w_up)
    g_dtwo = jnp.sum(grad_b * dunit2, 0)
    grad_z2 = dy + norm_back(grad_b, dunit2, dinv2, dec_gain_two)
    grad_a = grad_z2.astype(B16)
    g_out = dot_tn(grad_a, do_out)
    grad_o = dot_nt(grad_a, w_out).astype(B16)
    grad_q, grad_k, grad_v = attend_back(q, k_all, v_all, do_out, grad_o, dp_saved)
    half = cells_half
    far_kv = jnp.concatenate([grad_k[half:], grad_v[half:]], 1).astype(B16)
    near_kv = jnp.concatenate([grad_k[:half], grad_v[:half]], 1)
    grad_kv = (near_kv + swap([far_kv], "core", 7)[0].astype(F32)).astype(B16)
    grad_qkv = jnp.concatenate([grad_q, grad_kv], 1)
    g_qkv = dot_tn(da_in, grad_qkv)
    grad_n = dot_nt(grad_qkv, w_qkv)
    g_done = jnp.sum(grad_n * dunit1, 0)
    grad_filled = grad_z2 + norm_back(grad_n, dunit1, dinv1, dec_gain_one)
    g_mask = jnp.sum(unseen * grad_filled, 0)
    position_parts = route(cut(grad_filled), 8)

    dvis = dot_tn(place, grad_filled.astype(B16)).astype(B16)
    dvis = dvis + swap([dvis], "core", 9)[0]
    dvis = jnp.where(stays, dvis, swap([dvis], "x", 10)[0])

    g_qkv = g_qkv.reshape(dec_wide, 3, 2, -1)
    g_out = g_out.reshape(dec_wide, 2, -1)
    g_up = g_up.reshape(dec_wide, 2, -1)
    g_down = g_down.reshape(dec_wide, 2, -1)
    packed = jnp.stack(
        [
            pack(
                jnp.concatenate(
                    [
                        g_qkv[:, :, side].reshape(dec_wide, -1),
                        g_out[:, side],
                        g_up[:, side],
                        g_down[:, side],
                    ],
                    1,
                ),
                owners,
            )
            for side in range(2)
        ]
    )
    own = dec_wide // owners
    dec_final = unpack(scatter(packed, 11), own)
    pos_sum = (position_parts[0].astype(F32) + position_parts[1].astype(F32))
    pos_t = jnp.transpose(pos_sum)

    grad_out = dot_nt(dvis, bridge_weight)
    dm = grad_out.astype(B16)
    enc_mine = lax.dynamic_slice_in_dim(enc, m * (enc_wide // 2), enc_wide // 2, 1)
    g_bridge = dot_tn(enc_mine, dvis)
    eg_h = dot_nt(dm, enc_down)
    eg_down = dot_tn(dm, h)
    eg_u = (eg_h * gelu_slope(u)).astype(B16)
    eg_up = dot_tn(b, eg_u)
    part = dot_nt(eg_u, enc_up)
    g_etwo = jnp.sum(part * unit2, 0)
    whole = part + swap([part.astype(B16)], "x", 12)[0].astype(F32)
    eg_z2 = grad_out + norm_back(whole, unit2, inv2, enc_gain_two)
    eg_a = eg_z2.astype(B16)
    eg_out = dot_tn(eg_a, eo)
    eg_o = dot_nt(eg_a, enc_attn_out).astype(B16)
    eg_triple = small_attend_back(triple, ep, eg_o)
    eg_qkv = dot_tn(a, eg_triple)
    part = dot_nt(eg_triple, e_qkv)
    g_eone = jnp.sum(part * unit1, 0)
    whole = part + swap([part.astype(B16)], "x", 13)[0].astype(F32)
    grad_x = eg_z2 + norm_back(whole, unit1, inv1, enc_gain_one)
    grad_x = jnp.pad(grad_x, ((0, slots - used), (0, 0)))
    grad_x = lax.dynamic_slice_in_dim(grad_x, m * half_slots, half_slots, 0)
    halves = jnp.stack(jnp.split(grad_x, 2, axis=1))
    other = swap([pick(halves, 1 - s)], "core", 14)[0]
    mine = pick(halves, s)
    tokens_grad = jnp.stack([jnp.where(s == 0, mine, other), jnp.where(s == 0, other, mine)])

    packed = pack(jnp.concatenate([eg_qkv, eg_up, eg_out, eg_down], 1), owners)
    enc_own = enc_wide // owners
    enc_final = unpack(scatter(packed[None], 15), enc_own)

    pos_rows = dec_wide // 2 // n
    pos_packed = pack(pos_t, n)
    zero = jnp.zeros_like(pos_packed)
    pos_two = jnp.concatenate(
        [jnp.where(s == 0, pos_packed, zero), jnp.where(s == 1, pos_packed, zero)], 0
    )
    pos_final = unpack(scatter(pos_two[None], 16), pos_rows)

    small = jnp.concatenate([g_eone, g_etwo, g_done, g_dtwo, g_mask])
    per = -(-small.shape[0] // owners)
    small = jnp.pad(small, (0, per * owners - small.shape[0])).reshape(owners, 1, per)
    small = jnp.pad(small, ((0, 0), (0, 0), (0, dec_wide - per)))
    bridge_own = enc_wide // 2 // owners
    rows = -(-(bridge_own + 1) // 16) * 16
    rep = jnp.concatenate(
        [
            g_bridge.reshape(owners, bridge_own, dec_wide),
            small,
            jnp.zeros((owners, rows - bridge_own - 1, dec_wide), F32),
        ],
        1,
    ).astype(B16)
    rep = scatter(rep[None], 17).astype(B16)
    everyone = gather(rep, n, 18).reshape(owners, 2, rows, dec_wide)
    bridge_grad = jnp.swapaxes(everyone[:, :, :bridge_own], 0, 1).reshape(enc_wide, dec_wide)
    small = everyone[:, 0, bridge_own, :per].astype(F32) + everyone[:, 1, bridge_own, :per].astype(F32)
    small = small.reshape(-1)
    cuts = [enc_wide, 2 * enc_wide, 2 * enc_wide + dec_wide, 2 * enc_wide + 2 * dec_wide]
    one_e, two_e, one_d, two_d, mask_grad = (
        part for part in jnp.split(small[: 2 * enc_wide + 3 * dec_wide], cuts)
    )

    enc_cols = enc_qkv.shape[2]
    sizes = [3 * enc_cols, enc_up.shape[1], enc_attn_out.shape[0]]
    e1, e2, e3, e4 = jnp.split(enc_final, [sizes[0], sizes[0] + sizes[1], sum(sizes)], 1)
    dec_cols = dec_qkv.shape[2]
    sizes = [3 * dec_cols, dec_attn_out.shape[0], dec_up.shape[1]]
    d1, d3, d2, d4 = jnp.split(dec_final, [sizes[0], sizes[0] + sizes[1], sum(sizes)], 1)
    return (
        decoded.astype(F32)[:, None],
        tokens_grad[:, None],
        e1.reshape(enc_own, 3, -1),
        e3.T,
        e2,
        e4.T,
        one_e,
        two_e,
        bridge_grad.astype(F32),
        mask_grad,
        pos_final.T,
        d1.reshape(own, 3, -1),
        d3.T,
        d2,
        d4.T,
        one_d,
        two_d,
    )


def solution(mesh):
    return jax.shard_map(
        per_device,
        mesh=mesh,
        in_specs=(
            P(None, "dp", "mp", None),
            P(None, "dp"),
            P(None, "dp", None),
            P(None, None, "mp"),
            P("mp", None),
            P(None, "mp"),
            P("mp", None),
            P(),
            P(),
            P(),
            P(),
            P("mp", None),
            P(None, None, "mp"),
            P("mp", None),
            P(None, "mp"),
            P("mp", None),
            P(),
            P(),
            P(None, "dp", "mp", None),
        ),
        out_specs=(
            P(None, "dp", "mp", "section"),
            P(None, "dp", "mp", "section"),
            P(("section", "dp"), None, "mp"),
            P("mp", ("section", "dp")),
            P(("section", "dp"), "mp"),
            P("mp", ("section", "dp")),
            P(),
            P(),
            P(),
            P(),
            P("mp", ("section", "dp")),
            P(("section", "dp"), None, "mp"),
            P("mp", ("section", "dp")),
            P(("section", "dp"), "mp"),
            P("mp", ("section", "dp")),
            P(),
            P(),
        ),
        check_vma=False,
    )
```

```python
import functools

import jax
import jax.numpy as jnp
from jax import lax
from jax.experimental import pallas as pl
from jax.experimental.pallas import tpu as pltpu
from jax.sharding import PartitionSpec as P

HEAD = 64
LONGEST = 157
EPS = 1e-06
NEG = -1e30
F32 = jnp.float32
B16 = jnp.bfloat16
MESH = pl.DeviceIdType.MESH
VMEM = pltpu.VMEM
LIMIT = 56 * 1024 * 1024


def place_of():
    return lax.axis_index("section"), lax.axis_index("dp"), lax.axis_index("mp")


def greet(partners):
    barrier = pltpu.get_barrier_semaphore()
    for partner in partners:
        pl.semaphore_signal(barrier, inc=1, device_id=partner, device_id_type=MESH)
    pl.semaphore_wait(barrier, len(partners))


def send(src, dst, send_sem, recv_sem, partner):
    return pltpu.make_async_remote_copy(
        src_ref=src,
        dst_ref=dst,
        send_sem=send_sem,
        recv_sem=recv_sem,
        device_id=partner,
        device_id_type=MESH,
    )


def remote_params(ident):
    return pltpu.CompilerParams(
        collective_id=ident, has_side_effects=True, vmem_limit_bytes=LIMIT
    )


def swap_kernel(kind, count, *refs):
    ins, outs, (send_sem, recv_sem) = refs[:count], refs[count : 2 * count], refs[2 * count :]
    s, d, m = place_of()
    partner = (1 - s, d, m) if kind == "core" else (s, d, 1 - m)
    greet([partner])
    copies = [
        send(ins[i], outs[i], send_sem.at[i], recv_sem.at[i], partner) for i in range(count)
    ]
    for copy in copies:
        copy.start()
    for copy in copies:
        copy.wait()


def swap(arrays, kind, ident):
    count = len(arrays)
    return pl.pallas_call(
        functools.partial(swap_kernel, kind, count),
        out_shape=[jax.ShapeDtypeStruct(a.shape, a.dtype) for a in arrays],
        in_specs=[pl.BlockSpec(memory_space=pl.ANY)] * count,
        out_specs=[pl.BlockSpec(memory_space=pl.ANY)] * count,
        scratch_shapes=[pltpu.SemaphoreType.DMA((count,)), pltpu.SemaphoreType.DMA((count,))],
        compiler_params=remote_params(ident),
        name=f"swap_{kind}_{ident}",
    )(*arrays)


def route_kernel(x_ref, out_ref, send_sem, recv_sem, local_sem):
    s, d, m = place_of()
    greet([(1 - s, d, m), (s, d, 1 - m), (1 - s, d, 1 - m)])
    stays = s == m

    @pl.when(stays)
    def _():
        mine = pltpu.make_async_copy(x_ref.at[s], out_ref.at[m], local_sem)
        mine.start()
        out = send(x_ref.at[1 - s], out_ref.at[m], send_sem.at[0], recv_sem.at[m], (1 - s, d, m))
        out.start()
        mine.wait()
        out.wait_send()

    @pl.when(jnp.logical_not(stays))
    def _():
        near = send(x_ref.at[s], out_ref.at[m], send_sem.at[0], recv_sem.at[m], (s, d, 1 - m))
        far = send(
            x_ref.at[1 - s], out_ref.at[m], send_sem.at[1], recv_sem.at[m], (1 - s, d, 1 - m)
        )
        near.start()
        far.start()
        near.wait_send()
        far.wait_send()

    pltpu.make_async_copy(out_ref.at[1 - m], out_ref.at[1 - m], recv_sem.at[1 - m]).wait()

    @pl.when(jnp.logical_not(stays))
    def _():
        pltpu.make_async_copy(out_ref.at[m], out_ref.at[m], recv_sem.at[m]).wait()


def route(x, ident):
    return pl.pallas_call(
        route_kernel,
        out_shape=jax.ShapeDtypeStruct(x.shape, x.dtype),
        in_specs=[pl.BlockSpec(memory_space=pl.ANY)],
        out_specs=pl.BlockSpec(memory_space=pl.ANY),
        scratch_shapes=[
            pltpu.SemaphoreType.DMA((2,)),
            pltpu.SemaphoreType.DMA((2,)),
            pltpu.SemaphoreType.DMA,
        ],
        compiler_params=remote_params(ident),
        name=f"route_{ident}",
    )(x)


def scatter_kernel(n, across, g_ref, out_ref, near, work, far, over, sems):
    near_send, near_recv, far_send, far_recv, over_send, over_recv = sems
    s, d, m = place_of()
    sibling, facing = (1 - s, d, m), (s, d, 1 - m)
    greet([sibling] + [facing] * across + [(s, lax.rem(d + k, n), m) for k in range(1, n)])
    order = [*range(1, n), 0]
    sides = 1 + across
    first = {}
    for side in reversed(range(sides)):
        for k in order:
            to = lax.rem(d + k, n)
            first[side, k] = send(
                g_ref.at[side, (1 - s) * n + to],
                near.at[side, to],
                near_send.at[side, k],
                near_recv.at[side, k],
                sibling,
            )
            first[side, k].start()

    def summed(side, k):
        to = lax.rem(d + k, n)
        first[side, k].wait()
        return to, g_ref[side, s * n + to].astype(F32) + near[side, to].astype(F32)

    second = {}
    if across:
        for k in order:
            to, part = summed(1, k)
            work[1, to] = part.astype(B16)
            second[k] = send(work.at[1, to], over.at[to], over_send.at[k], over_recv.at[k], facing)
            second[k].start()
    third = []
    for k in order:
        to, part = summed(0, k)
        if across:
            second[k].wait()
            part = part + over[to].astype(F32)
        if k:
            work[0, to] = part.astype(B16)
            copy = send(work.at[0, to], far.at[d], far_send.at[k], far_recv.at[k], (s, to, m))
            copy.start()
            third.append((k, copy))
    for k, copy in third:
        copy.wait()
        part = part + far[lax.rem(d + n - k, n)].astype(F32)
    out_ref[...] = part


def scatter(g, ident):
    sides, owners, rows, cols = g.shape
    n = owners // 2
    across = sides - 1
    kernel = functools.partial(scatter_kernel, n, across)

    def body(g_ref, out_ref, near, work, far, over, *sems):
        kernel(g_ref, out_ref, near, work, far, over, sems)

    pieces = (n, rows, cols)
    return pl.pallas_call(
        body,
        out_shape=jax.ShapeDtypeStruct((rows, cols), F32),
        in_specs=[pl.BlockSpec(memory_space=VMEM)],
        out_specs=pl.BlockSpec(memory_space=VMEM),
        scratch_shapes=[
            VMEM((sides,) + pieces, B16),
            VMEM((sides,) + pieces, B16),
            VMEM(pieces, B16),
            VMEM(pieces if across else (8, 128), B16),
            pltpu.SemaphoreType.DMA((sides, n)),
            pltpu.SemaphoreType.DMA((sides, n)),
            pltpu.SemaphoreType.DMA((n,)),
            pltpu.SemaphoreType.DMA((n,)),
            pltpu.SemaphoreType.DMA((n,)),
            pltpu.SemaphoreType.DMA((n,)),
        ],
        compiler_params=remote_params(ident),
        name=f"scatter_{ident}",
    )(g)


def gather_kernel(n, x_ref, out_ref, local_sem, send_sem, recv_sem):
    s, d, m = place_of()
    steps = [(a, k, b) for k in range(n) for a in range(2) for b in range(2) if a or k or b]

    def partner(step):
        a, k, b = step
        return (lax.rem(s + a, 2), lax.rem(d + k, n), lax.rem(m + b, 2))

    greet([partner(step) for step in steps])
    slot = (s * n + d) * 2 + m
    mine = pltpu.make_async_copy(x_ref, out_ref.at[slot], local_sem)
    mine.start()
    copies = [
        send(x_ref, out_ref.at[slot], send_sem.at[i], recv_sem.at[i], partner(step))
        for i, step in enumerate(steps)
    ]
    for copy in copies:
        copy.start()
    mine.wait()
    for copy in copies:
        copy.wait()


def gather(x, n, ident):
    count = 4 * n
    return pl.pallas_call(
        functools.partial(gather_kernel, n),
        out_shape=jax.ShapeDtypeStruct((count,) + x.shape, x.dtype),
        in_specs=[pl.BlockSpec(memory_space=VMEM)],
        out_specs=pl.BlockSpec(memory_space=VMEM),
        scratch_shapes=[
            pltpu.SemaphoreType.DMA,
            pltpu.SemaphoreType.DMA((count - 1,)),
            pltpu.SemaphoreType.DMA((count - 1,)),
        ],
        compiler_params=remote_params(ident),
        name=f"gather_{ident}",
    )(x)


def dot_nt(a, b):
    return lax.dot_general(a, b, (((1,), (1,)), ((), ())), preferred_element_type=F32)


def dot_nn(a, b):
    return lax.dot_general(a, b, (((1,), (0,)), ((), ())), preferred_element_type=F32)


def dot_tn(a, b):
    return lax.dot_general(a, b, (((0,), (0,)), ((), ())), preferred_element_type=F32)


def chunks_of(length, most=256):
    units = length // 16
    count = -(-length // most)
    cuts = [16 * (units * i // count) for i in range(count)] + [length]
    return [(a, b - a) for a, b in zip(cuts, cuts[1:])]


def head_masks():
    lanes = lax.broadcasted_iota(jnp.int32, (1, 2 * HEAD), 1)
    return (lanes < HEAD, lanes >= HEAD)


def attend_kernel(q_ref, k_ref, v_ref, o_ref, p_ref):
    masks = head_masks()
    k = k_ref[...]
    v = v_ref[...]
    for start, size in chunks_of(q_ref.shape[0], 128):
        rows = pl.ds(start, size)
        q = q_ref[rows] * jnp.asarray(HEAD**-0.5, B16)
        halves = []
        for head in range(2):
            scores = dot_nt(jnp.where(masks[head], q, 0), k)
            top = jnp.max(scores, -1, keepdims=True)
            raised = jnp.exp(scores - top)
            whole = jnp.sum(raised, -1, keepdims=True)
            p = (raised * (1.0 / whole)).astype(B16)
            p_ref[head, rows] = p
            halves.append(dot_nn(p, v))
        o_ref[rows] = jnp.where(masks[0], halves[0], halves[1]).astype(B16)


def attend(q, k, v):
    length, width = q.shape
    keys = k.shape[0]
    pairs = width // (2 * HEAD)
    return pl.pallas_call(
        attend_kernel,
        grid=(pairs,),
        out_shape=[
            jax.ShapeDtypeStruct((length, width), B16),
            jax.ShapeDtypeStruct((2 * pairs, length, keys), B16),
        ],
        in_specs=[
            pl.BlockSpec((length, 2 * HEAD), lambda i: (0, i)),
            pl.BlockSpec((keys, 2 * HEAD), lambda i: (0, i)),
            pl.BlockSpec((keys, 2 * HEAD), lambda i: (0, i)),
        ],
        out_specs=[
            pl.BlockSpec((length, 2 * HEAD), lambda i: (0, i)),
            pl.BlockSpec((2, length, keys), lambda i: (i, 0, 0)),
        ],
        compiler_params=pltpu.CompilerParams(vmem_limit_bytes=LIMIT),
        name="attend",
    )(q, k, v)


def attend_back_kernel(q_ref, k_ref, v_ref, o_ref, do_ref, p_ref, dq_ref, dk_ref, dv_ref, dk_t, dv_t):
    masks = head_masks()
    k = k_ref[...]
    v = v_ref[...]
    scale = HEAD**-0.5
    for index, (start, size) in enumerate(chunks_of(q_ref.shape[0], 256)):
        rows = pl.ds(start, size)
        q = q_ref[rows]
        do = do_ref[rows]
        both = do.astype(F32) * o_ref[rows].astype(F32)
        dq = []
        for head in range(2):
            do_head = jnp.where(masks[head], do, 0)
            delta = jnp.sum(jnp.where(masks[head], both, 0.0), -1, keepdims=True)
            p = p_ref[head, rows]
            dp = dot_nt(do_head, v)
            ds = (p.astype(F32) * (dp - delta)).astype(B16)
            dq.append(dot_nn(ds, k))
            feats = pl.ds(head * HEAD, HEAD)
            dv_part = dot_tn(do[:, head * HEAD : (head + 1) * HEAD], p)
            dk_part = dot_tn(q[:, head * HEAD : (head + 1) * HEAD], ds)
            if index:
                dv_part = dv_part + dv_t[feats]
                dk_part = dk_part + dk_t[feats]
            dv_t[feats] = dv_part
            dk_t[feats] = dk_part
        dq_ref[rows] = (jnp.where(masks[0], dq[0], dq[1]) * scale).astype(B16)
    dk_ref[...] = (jnp.transpose(dk_t[...]) * scale).astype(dk_ref.dtype)
    dv_ref[...] = jnp.transpose(dv_t[...]).astype(dv_ref.dtype)


def attend_back(q, k, v, o, do, p):
    length, width = q.shape
    keys = k.shape[0]
    pairs = width // (2 * HEAD)
    short = pl.BlockSpec((length, 2 * HEAD), lambda i: (0, i))
    long = pl.BlockSpec((keys, 2 * HEAD), lambda i: (0, i))
    return pl.pallas_call(
        attend_back_kernel,
        grid=(pairs,),
        out_shape=[
            jax.ShapeDtypeStruct((length, width), B16),
            jax.ShapeDtypeStruct((keys, width), F32),
            jax.ShapeDtypeStruct((keys, width), F32),
        ],
        in_specs=[
            short,
            long,
            long,
            short,
            short,
            pl.BlockSpec((2, length, keys), lambda i: (i, 0, 0)),
        ],
        out_specs=[short, long, long],
        scratch_shapes=[VMEM((2 * HEAD, keys), F32), VMEM((2 * HEAD, keys), F32)],
        compiler_params=pltpu.CompilerParams(vmem_limit_bytes=LIMIT),
        name="attend_back",
    )(q, k, v, o, do, p)


class Wire:
    def __init__(self, send_sem, recv_sem):
        self.send_sem, self.recv_sem, self.used = send_sem, recv_sem, 0

    def copy(self, src, dst, partner):
        index = self.used
        self.used += 1
        return send(src, dst, self.send_sem.at[index], self.recv_sem.at[index], partner)


def norm_of(z):
    centre = z - jnp.mean(z, -1, keepdims=True)
    inverse = lax.rsqrt(jnp.mean(centre * centre, -1, keepdims=True) + EPS)
    return centre * inverse, inverse


def each(count, body):
    def step(i, carry):
        body(i)
        return carry

    lax.fori_loop(0, count, step, 0)


def softmax_fwd(q, k, v):
    scores = dot_nt(q, k)
    raised = jnp.exp(scores - jnp.max(scores, -1, keepdims=True))
    scale = 1.0 / jnp.sum(raised, -1, keepdims=True)
    raised = raised.astype(B16)
    return raised, scale, dot_nn(raised, v) * scale


def dec_kernel(*refs):
    (
        vis_ref, cells_row, cells_col, pos_own, pos_far, mask_ref, gain1_ref, gain2_ref,
        qkv_own, qkv_far, out_own, out_far, up_hbm, down_hbm, cot_hbm,
        dec_out, pos_out, dvis_out, grad_out, small_out,
        w_up, w_down, cot, z1, unit1, a_ref, q_ref, keys, values, probs, stats,
        o_ref, unit2, b_ref, h_ref, slope, z2, do_ref, flip, dkt, dvt, got_kv,
        dvis_mine, dvis_near, dvis_far, local_sem, send_sem, recv_sem,
    ) = refs
    s, d, m = place_of()
    sibling, facing = (1 - s, d, m), (s, d, 1 - m)
    stays = s == m
    length, wide = z1.shape
    third = wide // 2
    heads = third // HEAD
    wire = Wire(send_sem, recv_sem)
    scale = HEAD**-0.5

    greet([sibling, facing])

    loads = [
        pltpu.make_async_copy(up_hbm, w_up.at[0], local_sem.at[0]),
        pltpu.make_async_copy(down_hbm, w_down.at[0], local_sem.at[1]),
    ]
    pos_load = pltpu.make_async_copy(pos_own, z1, local_sem.at[3])
    pos_load.start()
    cot_load = pltpu.make_async_copy(cot_hbm.at[m], cot, local_sem.at[2])
    for load in loads:
        load.start()
    over, share = [], []
    for hbm, held in ((up_hbm, w_up), (down_hbm, w_down)):
        half = hbm.shape[0] // 2
        mine = pl.ds(s * half, half)
        over.append(wire.copy(hbm.at[mine], held.at[1, mine], facing))
        share.append(wire.copy(held.at[1, mine], held.at[1, mine], sibling))
        over[-1].start()
    cot_over = wire.copy(cot_hbm.at[1 - m], cot, facing)

    @pl.when(stays)
    def _():
        cot_load.start()
        cot_over.start()

    lane = lax.broadcasted_iota(jnp.int32, (1, 128), 1)

    def keep(plane, rows, column, value):
        stats[plane, rows] = jnp.where(lane == column, value, stats[plane, rows])

    def kept(plane, rows, column):
        return stats[plane, rows][:, column : column + 1]

    pos_load.wait()
    rows_at = 112
    base = s * length

    def fill(i):
        rows = pl.ds(pl.multiple_of(i * rows_at, 16), rows_at)
        ids = lax.broadcasted_iota(jnp.int32, (rows_at, 1), 0) + (base + i * rows_at)
        place = jnp.where(cells_row[...] == ids, 1.0, 0.0)
        unseen = 1.0 - jnp.sum(place, -1, keepdims=True)
        pos = jnp.where(stays, z1[rows], pos_far[rows].astype(F32))
        z = dot_nn(place.astype(B16), vis_ref[...]) + unseen * mask_ref[...] + pos
        unit, inverse = norm_of(z)
        z1[rows] = z
        unit1[rows] = unit
        keep(0, rows, heads, inverse)
        a_ref[rows] = (unit * gain1_ref[...]).astype(B16)

    each(length // rows_at, fill)

    a = a_ref[...]
    mine_rows = pl.ds(0, length)
    kv_copies = []
    for side, weight in enumerate((qkv_own, qkv_far)):
        keys[side, mine_rows] = dot_nn(a, weight[1]).astype(B16)
        values[side, mine_rows] = dot_nn(a, weight[2]).astype(B16)
        for held in (keys, values):
            copy = wire.copy(
                held.at[side, mine_rows], held.at[side, pl.ds(length, length)], sibling
            )
            copy.start()
            kv_copies.append(copy)
    for side, weight in enumerate((qkv_own, qkv_far)):
        q_ref[side] = (dot_nn(a, weight[0]).astype(B16).astype(F32) * scale).astype(B16)
    for copy in kv_copies:
        copy.wait()

    masks = head_masks()
    pair = pl.ds(0, 2 * HEAD)
    lone = pl.ds(2 * HEAD, HEAD)

    def attend_side(side):
        for start, size in chunks_of(length, 400):
            rows = pl.ds(start, size)
            halves = []
            for head in range(2):
                q = jnp.where(masks[head], q_ref[side, rows, pair], 0)
                raised, over_sum, o = softmax_fwd(q, keys[side, :, pair], values[side, :, pair])
                probs[side, head, rows] = raised
                keep(side, rows, head, over_sum)
                halves.append(o)
            o_ref[side, rows, pair] = jnp.where(masks[0], halves[0], halves[1]).astype(B16)
            raised, over_sum, o = softmax_fwd(
                q_ref[side, rows, lone], keys[side, :, lone], values[side, :, lone]
            )
            probs[side, 2, rows] = raised
            keep(side, rows, 2, over_sum)
            o_ref[side, rows, lone] = o.astype(B16)

    each(2, attend_side)

    for copy, other in zip(over, share):
        copy.wait()
        other.start()

    z2[...] = z1[...] + dot_nn(o_ref[0], out_own[...]) + dot_nn(o_ref[1], out_far[...])

    def second(i):
        rows = pl.ds(pl.multiple_of(i * rows_at, 16), rows_at)
        unit, inverse = norm_of(z2[rows])
        unit2[rows] = unit
        keep(1, rows, heads, inverse)
        b_ref[rows] = (unit * gain2_ref[...]).astype(B16)

    each(length // rows_at, second)
    for load in loads:
        load.wait()
    for copy in share:
        copy.wait()

    step = 256
    steps = w_up.shape[2] // step

    def hidden_at(i):
        return i // steps, pl.ds(pl.multiple_of((i % steps) * step, step), step)

    def up(i):
        side, cols = hidden_at(i)
        u = dot_nn(b_ref[...], w_up[side, :, cols])
        phi = 0.5 + 0.5 * lax.erf(u * 0.5**0.5)
        h_ref[side, :, cols] = (u * phi).astype(B16)
        bell = jnp.exp(u * u * -0.5) * (0.5 / jnp.pi) ** 0.5
        slope[side, :, cols] = (phi + u * bell).astype(B16)

    each(2 * steps, up)

    def cut(value, out):
        out[0] = value[:, :third].astype(B16)
        out[1] = value[:, third:].astype(B16)

    cut(z2[...] + dot_nn(h_ref[0], w_down[0]) + dot_nn(h_ref[1], w_down[1]), dec_out)

    @pl.when(stays)
    def _():
        cot_load.wait()
        cot_over.wait_send()

    @pl.when(jnp.logical_not(stays))
    def _():
        cot_over.wait_recv()

    def transposed(value):
        return jnp.transpose(value.astype(F32)).astype(B16)

    cot_flip = flip.at[0]
    b_flip = flip.at[1]
    cot_flip[...] = transposed(cot[...])
    b_flip[...] = transposed(b_ref[...])

    def down(i):
        side, cols = hidden_at(i)
        grad_out[side, 2, :, cols] = dot_nn(cot_flip[...], h_ref[side, :, cols]).astype(B16)
        grad_u = dot_nt(cot[...], w_down[side, cols, :]) * slope[side, :, cols].astype(F32)
        grad_u = grad_u.astype(B16)
        slope[side, :, cols] = grad_u
        grad_out[side, 1, :, cols] = dot_nn(b_flip[...], grad_u).astype(B16)

    each(2 * steps, down)
    z1[...] = dot_nt(slope[0], w_up[0]) + dot_nt(slope[1], w_up[1])

    def back_norm(grad, unit, inverse, gain):
        scaled = grad * gain
        mean = jnp.mean(scaled, -1, keepdims=True)
        tilt = jnp.mean(scaled * unit, -1, keepdims=True)
        return inverse * (scaled - mean - unit * tilt)

    def add_rows(total, value):
        return total + jnp.sum(value, 0, keepdims=True)

    def second_back(i, total):
        rows = pl.ds(pl.multiple_of(i * rows_at, 16), rows_at)
        grad = z1[rows]
        unit = unit2[rows]
        z = cot[rows].astype(F32) + back_norm(grad, unit, kept(1, rows, heads), gain2_ref[...])
        z2[rows] = z
        b_ref[rows] = z.astype(B16)
        return add_rows(total, grad * unit)

    zero = jnp.zeros((1, wide), F32)
    gain2_grad = lax.fori_loop(0, length // rows_at, second_back, zero)

    grad_a = b_ref[...]
    flip[0] = transposed(grad_a)
    for side, weight in enumerate((out_own, out_far)):
        grad_out[side, 0, :, pl.ds(3 * third, third)] = dot_nn(flip[0], o_ref[side]).astype(B16)
        do_ref[side] = dot_nt(grad_a, weight[...]).astype(B16)

    def attend_back_side(side):
        for index, (start, size) in enumerate(chunks_of(length, 256)):
            rows = pl.ds(start, size)
            for feats, heads in ((pair, (0, 1)), (lone, (2,))):
                q = q_ref[side, rows, feats]
                do = do_ref[side, rows, feats].astype(F32)
                both = do * o_ref[side, rows, feats].astype(F32)
                k = keys[side, :, feats]
                v = values[side, :, feats]
                dq = []
                for head in heads:
                    over_sum = kept(side, rows, head)
                    if len(heads) == 2:
                        lanes = slice(head * HEAD, (head + 1) * HEAD)
                        mine = jnp.where(masks[head], both, 0.0)
                        do_head = jnp.where(masks[head], do, 0.0)
                    else:
                        lanes = slice(0, HEAD)
                        mine, do_head = both, do
                    delta = jnp.sum(mine, -1, keepdims=True) * over_sum
                    do_head = (do_head * over_sum).astype(B16)
                    raised = probs[side, head, rows]
                    ds = (raised.astype(F32) * (dot_nt(do_head, v) - delta)).astype(B16)
                    dq.append(dot_nn(ds, k))
                    dv_part = dot_tn(do_head[:, lanes], raised)
                    dk_part = dot_tn(q[:, lanes], ds)
                    at = pl.ds(head * HEAD, HEAD)
                    if index:
                        dv_part = dv_part + dvt[at]
                        dk_part = dk_part + dkt[at]
                    dvt[at] = dv_part
                    dkt[at] = dk_part
                dq = jnp.where(masks[0], dq[0], dq[1]) if len(heads) == 2 else dq[0]
                q_ref[side, rows, feats] = (dq * scale).astype(B16)
        for held, out in ((dkt, keys), (dvt, values)):
            for feats, at in ((pair, pl.ds(0, 2 * HEAD)), (lone, pl.ds(2 * HEAD, HEAD))):
                out[side, :, feats] = jnp.transpose(held[at]).astype(B16)

    each(2, attend_back_side)
    far_rows = pl.ds(length, length)
    kv_back = [
        [
            wire.copy(held.at[side, far_rows], got_kv.at[slot, side], sibling)
            for side in range(2)
        ]
        for slot, held in enumerate((keys, values))
    ]
    for copies in kv_back:
        for copy in copies:
            copy.start()

    a_flip = flip.at[0]
    a_flip[...] = transposed(a_ref[...])
    total = None
    for slot in range(3):
        for side, weight in enumerate((qkv_own, qkv_far)):
            if slot:
                kv_back[slot - 1][side].wait()
                own = (keys, values)[slot - 1][side, mine_rows].astype(F32)
                grad = (own + got_kv[slot - 1, side].astype(F32)).astype(B16)
            else:
                grad = q_ref[side]
            grad_out[side, 0, :, pl.ds(slot * third, third)] = dot_nn(a_flip[...], grad).astype(B16)
            part = dot_nt(grad, weight[slot])
            total = part if total is None else total + part
    z1[...] = total

    def first_back(i, totals):
        rows = pl.ds(pl.multiple_of(i * rows_at, 16), rows_at)
        grad = z1[rows]
        unit = unit1[rows]
        z = z2[rows] + back_norm(grad, unit, kept(0, rows, heads), gain1_ref[...])
        b_ref[rows] = z.astype(B16)
        pos_out[0, rows] = z[:, :third].astype(B16)
        pos_out[1, rows] = z[:, third:].astype(B16)
        ids = lax.broadcasted_iota(jnp.int32, (rows_at, 1), 0) + (base + i * rows_at)
        seen = jnp.sum(jnp.where(cells_row[...] == ids, 1.0, 0.0), -1, keepdims=True)
        return add_rows(totals[0], grad * unit), add_rows(totals[1], (1.0 - seen) * z)

    gain1_grad, mask_grad = lax.fori_loop(0, length // rows_at, first_back, (zero, zero))
    small_out[0:1] = gain1_grad
    small_out[1:2] = gain2_grad
    small_out[2:3] = mask_grad

    used = vis_ref.shape[0]
    ids = lax.broadcasted_iota(jnp.int32, (used, length), 1) + base
    place = jnp.where(cells_col[...] == ids, 1.0, 0.0).astype(B16)
    dvis_mine[...] = dot_nn(place, b_ref[...]).astype(B16)
    near = wire.copy(dvis_mine, dvis_near, sibling)
    near.start()
    near.wait()
    dvis_mine[...] = (dvis_mine[...].astype(F32) + dvis_near[...].astype(F32)).astype(B16)
    beyond = wire.copy(dvis_mine, dvis_far, facing)

    @pl.when(stays)
    def _():
        beyond.start()
        dvis_out[...] = dvis_mine[...]
        beyond.wait_send()

    @pl.when(jnp.logical_not(stays))
    def _():
        beyond.wait_recv()
        dvis_out[...] = dvis_far[...]


def decoder(vis, cells, pos_own, pos_far, mask, gains, weights, cot, ident):
    qkv_own, qkv_far, out_own, out_far, up, down = weights
    length, wide = pos_own.shape
    used = vis.shape[0]
    third = wide // 2
    hidden = up.shape[1]
    keys = 2 * length
    heads = third // HEAD
    assert heads == 3 and length % 112 == 0
    whole = pl.BlockSpec(memory_space=VMEM)
    there = pl.BlockSpec(memory_space=pl.ANY)
    return pl.pallas_call(
        dec_kernel,
        out_shape=[
            jax.ShapeDtypeStruct((2, length, third), B16),
            jax.ShapeDtypeStruct((2, length, third), B16),
            jax.ShapeDtypeStruct((used, wide), B16),
            jax.ShapeDtypeStruct((2, 3, wide, hidden), B16),
            jax.ShapeDtypeStruct((8, wide), F32),
        ],
        in_specs=[whole] * 3 + [there] + [whole] * 8 + [there] * 3,
        out_specs=[whole] * 5,
        scratch_shapes=[
            VMEM((2, wide, hidden), B16),
            VMEM((2, hidden, wide), B16),
            VMEM((length, wide), B16),
            VMEM((length, wide), F32),
            VMEM((length, wide), F32),
            VMEM((length, wide), B16),
            VMEM((2, length, third), B16),
            VMEM((2, keys, third), B16),
            VMEM((2, keys, third), B16),
            VMEM((2, heads, length, keys), B16),
            VMEM((2, length, 128), F32),
            VMEM((2, length, third), B16),
            VMEM((length, wide), F32),
            VMEM((length, wide), B16),
            VMEM((2, length, hidden), B16),
            VMEM((2, length, hidden), B16),
            VMEM((length, wide), F32),
            VMEM((2, length, third), B16),
            VMEM((2, wide, length), B16),
            VMEM((third, keys), F32),
            VMEM((third, keys), F32),
            VMEM((2, 2, length, third), B16),
            VMEM((used, wide), B16),
            VMEM((used, wide), B16),
            VMEM((used, wide), B16),
            pltpu.SemaphoreType.DMA((4,)),
            pltpu.SemaphoreType.DMA((16,)),
            pltpu.SemaphoreType.DMA((16,)),
        ],
        compiler_params=pltpu.CompilerParams(
            collective_id=ident, has_side_effects=True, vmem_limit_bytes=63 * 1024 * 1024
        ),
        name="decoder",
    )(
        vis,
        cells[None, :],
        cells[:, None],
        pos_own,
        pos_far,
        mask[None, :],
        gains[0][None, :],
        gains[1][None, :],
        qkv_own,
        qkv_far,
        out_own,
        out_far,
        up,
        down,
        cot,
    )


def normed(z, gain):
    centre = z - jnp.mean(z, -1, keepdims=True)
    inverse = lax.rsqrt(jnp.mean(centre * centre, -1, keepdims=True) + EPS)
    unit = centre * inverse
    return unit, inverse, (unit * gain).astype(B16)


def norm_back(grad, unit, inverse, gain):
    scaled = grad * gain
    return inverse * (
        scaled
        - jnp.mean(scaled, -1, keepdims=True)
        - unit * jnp.mean(scaled * unit, -1, keepdims=True)
    )


def gelu(u):
    return 0.5 * u * (1.0 + lax.erf(u * 0.5**0.5))


def gelu_slope(u):
    return 0.5 * (1.0 + lax.erf(u * 0.5**0.5)) + u * jnp.exp(-0.5 * u * u) * (
        0.5 / jnp.pi
    ) ** 0.5


def small_attend(triple, length):
    rows = triple.shape[0]
    q, k, v = (triple[:, i] for i in range(3))
    scores = jnp.einsum("qhd,khd->hqk", q, k, preferred_element_type=F32) * HEAD**-0.5
    scores = jnp.where(jnp.arange(rows)[None, None, :] < length, scores, NEG)
    p = jax.nn.softmax(scores, axis=-1)
    o = jnp.einsum("hqk,khd->qhd", p.astype(B16), v, preferred_element_type=F32)
    return p, o.reshape(rows, -1).astype(B16)


def small_attend_back(triple, p, do):
    q, k, v = (triple[:, i] for i in range(3))
    do = do.reshape(q.shape)
    dp = jnp.einsum("qhd,khd->hqk", do, v, preferred_element_type=F32)
    ds = (p * (dp - jnp.sum(p * dp, -1, keepdims=True))).astype(B16)
    scale = HEAD**-0.5
    dq = jnp.einsum("hqk,khd->qhd", ds, k, preferred_element_type=F32) * scale
    dk = jnp.einsum("hqk,qhd->khd", ds, q, preferred_element_type=F32) * scale
    dv = jnp.einsum("hqk,qhd->khd", p.astype(B16), do, preferred_element_type=F32)
    return jnp.stack([dq, dk, dv], 1).astype(B16).reshape(q.shape[0], -1)


def pack(grad, owners):
    rows, cols = grad.shape
    own = rows // owners
    fold = 1
    while own * fold % 16:
        fold *= 2
    grad = grad.astype(B16).reshape(owners, own, fold, cols // fold)
    return jnp.swapaxes(grad, 1, 2).reshape(owners, fold * own, cols // fold)


def unpack(piece, own):
    fold = piece.shape[0] // own
    return jnp.swapaxes(piece.reshape(fold, own, -1), 0, 1).reshape(own, -1)


def pick(pair, index):
    return lax.dynamic_index_in_dim(pair, index, 0, keepdims=False)


def per_device(
    tokens,
    clip_lengths,
    clip_cells,
    enc_qkv,
    enc_attn_out,
    enc_up,
    enc_down,
    enc_gain_one,
    enc_gain_two,
    bridge_weight,
    mask_token,
    position_embed,
    dec_qkv,
    dec_attn_out,
    dec_up,
    dec_down,
    dec_gain_one,
    dec_gain_two,
    cotangent,
):
    s, d, m = place_of()
    n = lax.axis_size("dp")
    owners = 2 * n
    stays = s == m
    cells_half, dec_wide = position_embed.shape
    slots = clip_cells.shape[2]
    half_slots = tokens.shape[2]
    enc_wide = tokens.shape[3]
    used = -(-LONGEST // 32) * 32

    qkv_own = jnp.swapaxes(dec_qkv, 0, 1)
    swapped = swap(
        [
            pick(tokens[:, 0], s),
            qkv_own,
            dec_attn_out,
            position_embed.astype(B16),
        ],
        "x",
        1,
    )
    tok_far, qkv_far, out_far, pos_far = swapped

    tok_near = pick(tokens[:, 0], s)
    x = jnp.concatenate(
        [jnp.where(m == 0, tok_near, tok_far), jnp.where(m == 0, tok_far, tok_near)], 0
    )[:used].astype(F32)
    length = pick(clip_lengths[:, 0], s)
    e_qkv = enc_qkv.reshape(enc_wide, -1)
    unit1, inv1, a = normed(x, enc_gain_one)
    triple = jnp.dot(a, e_qkv, preferred_element_type=F32).astype(B16)
    triple = triple.reshape(used, 3, -1, HEAD)
    ep, eo = small_attend(triple, length)
    part = jnp.dot(eo, enc_attn_out, preferred_element_type=F32)
    z2 = x + part + swap([part.astype(B16)], "x", 2)[0].astype(F32)
    unit2, inv2, b = normed(z2, enc_gain_two)
    u = jnp.dot(b, enc_up, preferred_element_type=F32)
    h = gelu(u).astype(B16)
    part = jnp.dot(h, enc_down, preferred_element_type=F32)
    enc = (z2 + part + swap([part.astype(B16)], "x", 3)[0].astype(F32)).astype(B16)
    vis = jnp.dot(enc, bridge_weight, preferred_element_type=F32).astype(B16)
    vis_far = swap([vis], "core", 4)[0]

    vis_used = jnp.where(stays, vis, vis_far)
    cells = jnp.where(jnp.arange(used) < pick(clip_lengths[:, 0], m), pick(clip_cells[:, 0], m)[:used], -1)
    dec, pos_parts, dvis, dec_grads, dec_small = decoder(
        vis_used,
        cells,
        position_embed,
        pos_far,
        mask_token,
        (dec_gain_one, dec_gain_two),
        (qkv_own, qkv_far, dec_attn_out, out_far, dec_up, dec_down),
        cotangent[:, 0],
        5,
    )
    g_done, g_dtwo, g_mask = dec_small[0], dec_small[1], dec_small[2]
    decoded = route(dec, 6)
    position_parts = route(pos_parts, 8)
    packed = jnp.stack(
        [
            pack(jnp.concatenate([dec_grads[side, 0], dec_grads[side, 1], dec_grads[side, 2]], 1), owners)
            for side in range(2)
        ]
    )
    own = dec_wide // owners
    dec_final = unpack(scatter(packed, 11), own)
    pos_sum = (position_parts[0].astype(F32) + position_parts[1].astype(F32))
    pos_t = jnp.transpose(pos_sum)

    grad_out = dot_nt(dvis, bridge_weight)
    dm = grad_out.astype(B16)
    enc_mine = lax.dynamic_slice_in_dim(enc, m * (enc_wide // 2), enc_wide // 2, 1)
    g_bridge = dot_tn(enc_mine, dvis)
    eg_h = dot_nt(dm, enc_down)
    eg_down = dot_tn(dm, h)
    eg_u = (eg_h * gelu_slope(u)).astype(B16)
    eg_up = dot_tn(b, eg_u)
    part = dot_nt(eg_u, enc_up)
    g_etwo = jnp.sum(part * unit2, 0)
    whole = part + swap([part.astype(B16)], "x", 12)[0].astype(F32)
    eg_z2 = grad_out + norm_back(whole, unit2, inv2, enc_gain_two)
    eg_a = eg_z2.astype(B16)
    eg_out = dot_tn(eg_a, eo)
    eg_o = dot_nt(eg_a, enc_attn_out).astype(B16)
    eg_triple = small_attend_back(triple, ep, eg_o)
    eg_qkv = dot_tn(a, eg_triple)
    part = dot_nt(eg_triple, e_qkv)
    g_eone = jnp.sum(part * unit1, 0)
    whole = part + swap([part.astype(B16)], "x", 13)[0].astype(F32)
    grad_x = eg_z2 + norm_back(whole, unit1, inv1, enc_gain_one)
    grad_x = jnp.pad(grad_x, ((0, slots - used), (0, 0)))
    grad_x = lax.dynamic_slice_in_dim(grad_x, m * half_slots, half_slots, 0)
    halves = jnp.stack(jnp.split(grad_x, 2, axis=1))
    other = swap([pick(halves, 1 - s)], "core", 14)[0]
    mine = pick(halves, s)
    tokens_grad = jnp.stack([jnp.where(s == 0, mine, other), jnp.where(s == 0, other, mine)])

    packed = pack(jnp.concatenate([eg_qkv, eg_up, eg_out, eg_down], 1), owners)
    enc_own = enc_wide // owners
    enc_final = unpack(scatter(packed[None], 15), enc_own)

    pos_rows = dec_wide // 2 // n
    pos_packed = pack(pos_t, n)
    zero = jnp.zeros_like(pos_packed)
    pos_two = jnp.concatenate(
        [jnp.where(s == 0, pos_packed, zero), jnp.where(s == 1, pos_packed, zero)], 0
    )
    pos_final = unpack(scatter(pos_two[None], 16), pos_rows)

    small = jnp.concatenate([g_eone, g_etwo, g_done, g_dtwo, g_mask])
    per = -(-small.shape[0] // owners)
    small = jnp.pad(small, (0, per * owners - small.shape[0])).reshape(owners, 1, per)
    small = jnp.pad(small, ((0, 0), (0, 0), (0, dec_wide - per)))
    bridge_own = enc_wide // 2 // owners
    rows = -(-(bridge_own + 1) // 16) * 16
    rep = jnp.concatenate(
        [
            g_bridge.reshape(owners, bridge_own, dec_wide),
            small,
            jnp.zeros((owners, rows - bridge_own - 1, dec_wide), F32),
        ],
        1,
    ).astype(B16)
    rep = scatter(rep[None], 17).astype(B16)
    everyone = gather(rep, n, 18).reshape(owners, 2, rows, dec_wide)
    bridge_grad = jnp.swapaxes(everyone[:, :, :bridge_own], 0, 1).reshape(enc_wide, dec_wide)
    small = everyone[:, 0, bridge_own, :per].astype(F32) + everyone[:, 1, bridge_own, :per].astype(F32)
    small = small.reshape(-1)
    cuts = [enc_wide, 2 * enc_wide, 2 * enc_wide + dec_wide, 2 * enc_wide + 2 * dec_wide]
    one_e, two_e, one_d, two_d, mask_grad = (
        part for part in jnp.split(small[: 2 * enc_wide + 3 * dec_wide], cuts)
    )

    enc_cols = enc_qkv.shape[2]
    sizes = [3 * enc_cols, enc_up.shape[1], enc_attn_out.shape[0]]
    e1, e2, e3, e4 = jnp.split(enc_final, [sizes[0], sizes[0] + sizes[1], sum(sizes)], 1)
    dec_cols = dec_qkv.shape[2]
    sizes = [3 * dec_cols, dec_attn_out.shape[0], dec_up.shape[1]]
    d1, d3, d2, d4 = jnp.split(dec_final, [sizes[0], sizes[0] + sizes[1], sum(sizes)], 1)
    return (
        decoded.astype(F32)[:, None],
        tokens_grad[:, None],
        e1.reshape(enc_own, 3, -1),
        e3.T,
        e2,
        e4.T,
        one_e,
        two_e,
        bridge_grad.astype(F32),
        mask_grad,
        pos_final.T,
        d1.reshape(own, 3, -1),
        d3.T,
        d2,
        d4.T,
        one_d,
        two_d,
    )


def solution(mesh):
    return jax.shard_map(
        per_device,
        mesh=mesh,
        in_specs=(
            P(None, "dp", "mp", None),
            P(None, "dp"),
            P(None, "dp", None),
            P(None, None, "mp"),
            P("mp", None),
            P(None, "mp"),
            P("mp", None),
            P(),
            P(),
            P(),
            P(),
            P("mp", None),
            P(None, None, "mp"),
            P("mp", None),
            P(None, "mp"),
            P("mp", None),
            P(),
            P(),
            P(None, "dp", "mp", None),
        ),
        out_specs=(
            P(None, "dp", "mp", "section"),
            P(None, "dp", "mp", "section"),
            P(("section", "dp"), None, "mp"),
            P("mp", ("section", "dp")),
            P(("section", "dp"), "mp"),
            P("mp", ("section", "dp")),
            P(),
            P(),
            P(),
            P(),
            P("mp", ("section", "dp")),
            P(("section", "dp"), None, "mp"),
            P("mp", ("section", "dp")),
            P(("section", "dp"), "mp"),
            P("mp", ("section", "dp")),
            P(),
            P(),
        ),
        check_vma=False,
    )
```

```python
import functools
import itertools

import jax
import jax.numpy as jnp
from jax import lax
from jax.experimental import pallas as pl
from jax.experimental.pallas import tpu as pltpu
from jax.sharding import PartitionSpec as P

HEAD = 64
LONGEST = 157
EPS = 1e-06
NEG = -1e30
F32 = jnp.float32
B16 = jnp.bfloat16
MESH = pl.DeviceIdType.MESH
VMEM = pltpu.VMEM
LIMIT = 56 * 1024 * 1024


def place_of():
    return lax.axis_index("section"), lax.axis_index("dp"), lax.axis_index("mp")


def greet(partners):
    barrier = pltpu.get_barrier_semaphore()
    for partner in partners:
        pl.semaphore_signal(barrier, inc=1, device_id=partner, device_id_type=MESH)
    pl.semaphore_wait(barrier, len(partners))


def send(src, dst, send_sem, recv_sem, partner):
    return pltpu.make_async_remote_copy(
        src_ref=src,
        dst_ref=dst,
        send_sem=send_sem,
        recv_sem=recv_sem,
        device_id=partner,
        device_id_type=MESH,
    )


def remote_params(ident):
    return pltpu.CompilerParams(
        collective_id=ident, has_side_effects=True, vmem_limit_bytes=LIMIT
    )


def route_kernel(x_ref, out_ref, send_sem, recv_sem, local_sem):
    s, d, m = place_of()
    greet([(1 - s, d, m), (s, d, 1 - m), (1 - s, d, 1 - m)])
    stays = s == m

    @pl.when(stays)
    def _():
        mine = pltpu.make_async_copy(x_ref.at[s], out_ref.at[m], local_sem)
        mine.start()
        out = send(x_ref.at[1 - s], out_ref.at[m], send_sem.at[0], recv_sem.at[m], (1 - s, d, m))
        out.start()
        mine.wait()
        out.wait_send()

    @pl.when(jnp.logical_not(stays))
    def _():
        near = send(x_ref.at[s], out_ref.at[m], send_sem.at[0], recv_sem.at[m], (s, d, 1 - m))
        far = send(
            x_ref.at[1 - s], out_ref.at[m], send_sem.at[1], recv_sem.at[m], (1 - s, d, 1 - m)
        )
        near.start()
        far.start()
        near.wait_send()
        far.wait_send()

    pltpu.make_async_copy(out_ref.at[1 - m], out_ref.at[1 - m], recv_sem.at[1 - m]).wait()

    @pl.when(jnp.logical_not(stays))
    def _():
        pltpu.make_async_copy(out_ref.at[m], out_ref.at[m], recv_sem.at[m]).wait()


def route(x, ident):
    return pl.pallas_call(
        route_kernel,
        out_shape=jax.ShapeDtypeStruct(x.shape, x.dtype),
        in_specs=[pl.BlockSpec(memory_space=pl.ANY)],
        out_specs=pl.BlockSpec(memory_space=pl.ANY),
        scratch_shapes=[
            pltpu.SemaphoreType.DMA((2,)),
            pltpu.SemaphoreType.DMA((2,)),
            pltpu.SemaphoreType.DMA,
        ],
        compiler_params=remote_params(ident),
        name=f"route_{ident}",
    )(x)


def scatter_kernel(n, across, g_ref, out_ref, near, work, far, over, sems):
    near_send, near_recv, far_send, far_recv, over_send, over_recv = sems
    s, d, m = place_of()
    sibling, facing = (1 - s, d, m), (s, d, 1 - m)
    greet([sibling] + [facing] * across + [(s, lax.rem(d + k, n), m) for k in range(1, n)])
    order = [*range(1, n), 0]
    sides = 1 + across
    first = {}
    for side in reversed(range(sides)):
        for k in order:
            to = lax.rem(d + k, n)
            first[side, k] = send(
                g_ref.at[side, (1 - s) * n + to],
                near.at[side, to],
                near_send.at[side, k],
                near_recv.at[side, k],
                sibling,
            )
            first[side, k].start()

    def summed(side, k):
        to = lax.rem(d + k, n)
        first[side, k].wait()
        return to, g_ref[side, s * n + to].astype(F32) + near[side, to].astype(F32)

    second = {}
    if across:
        for k in order:
            to, part = summed(1, k)
            work[1, to] = part.astype(B16)
            second[k] = send(work.at[1, to], over.at[to], over_send.at[k], over_recv.at[k], facing)
            second[k].start()
    third = []
    for k in order:
        to, part = summed(0, k)
        if across:
            second[k].wait()
            part = part + over[to].astype(F32)
        if k:
            work[0, to] = part.astype(B16)
            copy = send(work.at[0, to], far.at[d], far_send.at[k], far_recv.at[k], (s, to, m))
            copy.start()
            third.append((k, copy))
    for k, copy in third:
        copy.wait()
        part = part + far[lax.rem(d + n - k, n)].astype(F32)
    out_ref[...] = part


def scatter(g, ident):
    sides, owners, rows, cols = g.shape
    n = owners // 2
    across = sides - 1
    kernel = functools.partial(scatter_kernel, n, across)

    def body(g_ref, out_ref, near, work, far, over, *sems):
        kernel(g_ref, out_ref, near, work, far, over, sems)

    pieces = (n, rows, cols)
    return pl.pallas_call(
        body,
        out_shape=jax.ShapeDtypeStruct((rows, cols), F32),
        in_specs=[pl.BlockSpec(memory_space=VMEM)],
        out_specs=pl.BlockSpec(memory_space=VMEM),
        scratch_shapes=[
            VMEM((sides,) + pieces, B16),
            VMEM((sides,) + pieces, B16),
            VMEM(pieces, B16),
            VMEM(pieces if across else (8, 128), B16),
            pltpu.SemaphoreType.DMA((sides, n)),
            pltpu.SemaphoreType.DMA((sides, n)),
            pltpu.SemaphoreType.DMA((n,)),
            pltpu.SemaphoreType.DMA((n,)),
            pltpu.SemaphoreType.DMA((n,)),
            pltpu.SemaphoreType.DMA((n,)),
        ],
        compiler_params=remote_params(ident),
        name=f"scatter_{ident}",
    )(g)


def gather_kernel(n, x_ref, out_ref, local_sem, send_sem, recv_sem):
    s, d, m = place_of()
    steps = [(a, k, b) for k in range(n) for a in range(2) for b in range(2) if a or k or b]

    def partner(step):
        a, k, b = step
        return (lax.rem(s + a, 2), lax.rem(d + k, n), lax.rem(m + b, 2))

    greet([partner(step) for step in steps])
    slot = (s * n + d) * 2 + m
    mine = pltpu.make_async_copy(x_ref, out_ref.at[slot], local_sem)
    mine.start()
    copies = [
        send(x_ref, out_ref.at[slot], send_sem.at[i], recv_sem.at[i], partner(step))
        for i, step in enumerate(steps)
    ]
    for copy in copies:
        copy.start()
    mine.wait()
    for copy in copies:
        copy.wait()


def gather(x, n, ident):
    count = 4 * n
    return pl.pallas_call(
        functools.partial(gather_kernel, n),
        out_shape=jax.ShapeDtypeStruct((count,) + x.shape, x.dtype),
        in_specs=[pl.BlockSpec(memory_space=VMEM)],
        out_specs=pl.BlockSpec(memory_space=VMEM),
        scratch_shapes=[
            pltpu.SemaphoreType.DMA,
            pltpu.SemaphoreType.DMA((count - 1,)),
            pltpu.SemaphoreType.DMA((count - 1,)),
        ],
        compiler_params=remote_params(ident),
        name=f"gather_{ident}",
    )(x)


def dot_nt(a, b):
    return lax.dot_general(a, b, (((1,), (1,)), ((), ())), preferred_element_type=F32)


def dot_nn(a, b):
    return lax.dot_general(a, b, (((1,), (0,)), ((), ())), preferred_element_type=F32)


def dot_tn(a, b):
    return lax.dot_general(a, b, (((0,), (0,)), ((), ())), preferred_element_type=F32)


def chunks_of(length, most=256):
    units = length // 16
    count = -(-length // most)
    cuts = [16 * (units * i // count) for i in range(count)] + [length]
    return [(a, b - a) for a, b in zip(cuts, cuts[1:])]


def head_masks():
    lanes = lax.broadcasted_iota(jnp.int32, (1, 2 * HEAD), 1)
    return (lanes < HEAD, lanes >= HEAD)


class Wire:
    def __init__(self, send_sem, recv_sem):
        self.send_sem, self.recv_sem, self.used = send_sem, recv_sem, 0

    def copy(self, src, dst, partner):
        index = self.used
        self.used += 1
        return send(src, dst, self.send_sem.at[index], self.recv_sem.at[index], partner)


def norm_of(z):
    centre = z - jnp.mean(z, -1, keepdims=True)
    inverse = lax.rsqrt(jnp.mean(centre * centre, -1, keepdims=True) + EPS)
    return centre * inverse, inverse


def each(count, body):
    def step(i, carry):
        body(i)
        return carry

    lax.fori_loop(0, count, step, 0)


def softmax_fwd(q, k, v):
    scores = dot_nt(q, k)
    raised = jnp.exp(scores - jnp.max(scores, -1, keepdims=True))
    scale = 1.0 / jnp.sum(raised, -1, keepdims=True)
    raised = raised.astype(B16)
    return raised, scale, dot_nn(raised, v) * scale


def dec_kernel(early, *refs):
    (
        vis_ref, cells_row, cells_col, pos_own, pos_far, mask_ref, gain1_ref, gain2_ref,
        qkv_own, qkv_far, out_own, out_far, up_hbm, down_hbm, cot_hbm,
        routed, pos_out, dvis_out, grad_out, small_out,
        dec_out, w_up, w_down, cot, z1, unit1, a_ref, q_ref, keys, values, probs, stats,
        o_ref, unit2, b_ref, h_ref, slope, z2, do_ref, flip, dkt, dvt, got_kv,
        dvis_mine, dvis_near, dvis_far, free_sem, local_sem, send_sem, recv_sem,
    ) = refs
    s, d, m = place_of()
    sibling, facing = (1 - s, d, m), (s, d, 1 - m)
    stays = s == m
    length, wide = z1.shape
    third = wide // 2
    heads = third // HEAD
    wire = Wire(send_sem, recv_sem)
    scale = HEAD**-0.5

    beyond = (1 - s, d, 1 - m)
    greet([sibling, facing, beyond])

    loads = [
        pltpu.make_async_copy(up_hbm, w_up.at[0], local_sem.at[0]),
        pltpu.make_async_copy(down_hbm, w_down.at[0], local_sem.at[1]),
    ]
    pos_load = pltpu.make_async_copy(pos_own, z1, local_sem.at[3])
    pos_load.start()
    cot_load = pltpu.make_async_copy(cot_hbm.at[m], cot, local_sem.at[2])
    for load in loads:
        load.start()
    over, share = [], []
    for hbm, held in ((up_hbm, w_up), (down_hbm, w_down)):
        half = hbm.shape[0] // 2
        mine = pl.ds(s * half, half)
        over.append(wire.copy(hbm.at[mine], held.at[1, mine], facing))
        share.append(wire.copy(held.at[1, mine], held.at[1, mine], sibling))
        over[-1].start()
    cot_over = wire.copy(cot_hbm.at[1 - m], cot, facing)

    @pl.when(stays)
    def _():
        cot_load.start()
        cot_over.start()

    lane = lax.broadcasted_iota(jnp.int32, (1, 128), 1)

    def keep(plane, rows, column, value):
        stats[plane, rows] = jnp.where(lane == column, value, stats[plane, rows])

    def kept(plane, rows, column):
        return stats[plane, rows][:, column : column + 1]

    pos_load.wait()
    rows_at = 112
    base = s * length

    def fill(i):
        rows = pl.ds(pl.multiple_of(i * rows_at, 16), rows_at)
        ids = lax.broadcasted_iota(jnp.int32, (rows_at, 1), 0) + (base + i * rows_at)
        place = jnp.where(cells_row[...] == ids, 1.0, 0.0)
        unseen = 1.0 - jnp.sum(place, -1, keepdims=True)
        pos = jnp.where(stays, z1[rows], pos_far[rows].astype(F32))
        z = dot_nn(place.astype(B16), vis_ref[...]) + unseen * mask_ref[...] + pos
        unit, inverse = norm_of(z)
        z1[rows] = z
        unit1[rows] = unit
        keep(0, rows, heads, inverse)
        a_ref[rows] = (unit * gain1_ref[...]).astype(B16)

    each(length // rows_at, fill)

    a = a_ref[...]
    mine_rows = pl.ds(0, length)
    kv_copies = []
    for side, weight in enumerate((qkv_own, qkv_far)):
        keys[side, mine_rows] = dot_nn(a, weight[1]).astype(B16)
        values[side, mine_rows] = dot_nn(a, weight[2]).astype(B16)
        for held in (keys, values):
            copy = wire.copy(
                held.at[side, mine_rows], held.at[side, pl.ds(length, length)], sibling
            )
            copy.start()
            kv_copies.append(copy)
    for side, weight in enumerate((qkv_own, qkv_far)):
        q_ref[side] = (dot_nn(a, weight[0]).astype(B16).astype(F32) * scale).astype(B16)
    for copy in kv_copies:
        copy.wait()

    masks = head_masks()
    pair = pl.ds(0, 2 * HEAD)
    lone = pl.ds(2 * HEAD, HEAD)

    def attend_side(side):
        for start, size in chunks_of(length, 400):
            rows = pl.ds(start, size)
            halves = []
            for head in range(2):
                q = jnp.where(masks[head], q_ref[side, rows, pair], 0)
                raised, over_sum, o = softmax_fwd(q, keys[side, :, pair], values[side, :, pair])
                probs[side, head, rows] = raised
                keep(side, rows, head, over_sum)
                halves.append(o)
            o_ref[side, rows, pair] = jnp.where(masks[0], halves[0], halves[1]).astype(B16)
            raised, over_sum, o = softmax_fwd(
                q_ref[side, rows, lone], keys[side, :, lone], values[side, :, lone]
            )
            probs[side, 2, rows] = raised
            keep(side, rows, 2, over_sum)
            o_ref[side, rows, lone] = o.astype(B16)

    each(2, attend_side)

    for copy, other in zip(over, share):
        copy.wait()
        other.start()

    z2[...] = z1[...] + dot_nn(o_ref[0], out_own[...]) + dot_nn(o_ref[1], out_far[...])

    def second(i):
        rows = pl.ds(pl.multiple_of(i * rows_at, 16), rows_at)
        unit, inverse = norm_of(z2[rows])
        unit2[rows] = unit
        keep(1, rows, heads, inverse)
        b_ref[rows] = (unit * gain2_ref[...]).astype(B16)

    each(length // rows_at, second)
    for load in loads:
        load.wait()
    for copy in share:
        copy.wait()

    step = 256
    steps = w_up.shape[2] // step

    def hidden_at(i):
        return i // steps, pl.ds(pl.multiple_of((i % steps) * step, step), step)

    def up(i):
        side, cols = hidden_at(i)
        u = dot_nn(b_ref[...], w_up[side, :, cols])
        phi = 0.5 + 0.5 * lax.erf(u * 0.5**0.5)
        h_ref[side, :, cols] = (u * phi).astype(B16)
        bell = jnp.exp(u * u * -0.5) * (0.5 / jnp.pi) ** 0.5
        slope[side, :, cols] = (phi + u * bell).astype(B16)

    each(2 * steps, up)

    def cut(value, out):
        out[0] = value[:, :third].astype(B16)
        out[1] = value[:, third:].astype(B16)

    cut(z2[...] + dot_nn(h_ref[0], w_down[0]) + dot_nn(h_ref[1], w_down[1]), dec_out)

    route_local = pltpu.make_async_copy(dec_out.at[s], routed.at[m], local_sem.at[4])
    route_near = wire.copy(dec_out.at[1 - s], routed.at[m], sibling)
    route_over = wire.copy(dec_out.at[s], routed.at[m], facing)
    route_far = wire.copy(dec_out.at[1 - s], routed.at[m], beyond)

    @pl.when(stays)
    def _():
        route_local.start()
        route_near.start()

    @pl.when(jnp.logical_not(stays))
    def _():
        route_over.start()
        route_far.start()

    @pl.when(stays)
    def _():
        cot_load.wait()
        cot_over.wait_send()

    @pl.when(jnp.logical_not(stays))
    def _():
        cot_over.wait_recv()

    def transposed(value):
        return jnp.transpose(value.astype(F32)).astype(B16)

    cot_flip = flip.at[0]
    b_flip = flip.at[1]
    cot_flip[...] = transposed(cot[...])
    b_flip[...] = transposed(b_ref[...])

    def down(i):
        side, cols = hidden_at(i)
        grad_out[side, 2, :, cols] = dot_nn(cot_flip[...], h_ref[side, :, cols]).astype(B16)
        grad_u = dot_nt(cot[...], w_down[side, cols, :]) * slope[side, :, cols].astype(F32)
        grad_u = grad_u.astype(B16)
        slope[side, :, cols] = grad_u
        grad_out[side, 1, :, cols] = dot_nn(b_flip[...], grad_u).astype(B16)

    each(2 * steps, down)
    if early:
        rows = wide // 2
        mine_grads = pl.ds(pl.multiple_of(s * rows, 16), rows)
        away_grads = pl.ds(pl.multiple_of((1 - s) * rows, 16), rows)
        for partner in (sibling, facing):
            pl.semaphore_signal(free_sem, inc=1, device_id=partner, device_id_type=MESH)
        pl.semaphore_wait(free_sem, 2)
        near = {}
        for side, t in ((1, 1), (1, 2), (0, 1), (0, 2)):
            held = h_ref.at[0, pl.ds((side * 2 + t - 1) * rows, rows)]
            near[side, t] = (held, wire.copy(grad_out.at[side, t, away_grads], held, sibling))
            near[side, t][1].start()
    z1[...] = dot_nt(slope[0], w_up[0]) + dot_nt(slope[1], w_up[1])

    def back_norm(grad, unit, inverse, gain):
        scaled = grad * gain
        mean = jnp.mean(scaled, -1, keepdims=True)
        tilt = jnp.mean(scaled * unit, -1, keepdims=True)
        return inverse * (scaled - mean - unit * tilt)

    def add_rows(total, value):
        return total + jnp.sum(value, 0, keepdims=True)

    def second_back(i, total):
        rows = pl.ds(pl.multiple_of(i * rows_at, 16), rows_at)
        grad = z1[rows]
        unit = unit2[rows]
        z = cot[rows].astype(F32) + back_norm(grad, unit, kept(1, rows, heads), gain2_ref[...])
        z2[rows] = z
        b_ref[rows] = z.astype(B16)
        return add_rows(total, grad * unit)

    zero = jnp.zeros((1, wide), F32)
    gain2_grad = lax.fori_loop(0, length // rows_at, second_back, zero)

    grad_a = b_ref[...]
    flip[0] = transposed(grad_a)
    for side, weight in enumerate((out_own, out_far)):
        grad_out[side, 0, :, pl.ds(3 * third, third)] = dot_nn(flip[0], o_ref[side]).astype(B16)
        do_ref[side] = dot_nt(grad_a, weight[...]).astype(B16)

    if early:
        across = {}
        for t in (1, 2):
            held, copy = near[1, t]
            copy.wait()
            held[...] = (held[...].astype(F32) + grad_out[1, t, mine_grads].astype(F32)).astype(B16)
            got = h_ref.at[1, pl.ds((t - 1) * rows, rows)]
            across[t] = (got, wire.copy(held, got, facing))
            across[t][1].start()

    def attend_back_side(side):
        for index, (start, size) in enumerate(chunks_of(length, 256)):
            rows = pl.ds(start, size)
            for feats, heads in ((pair, (0, 1)), (lone, (2,))):
                q = q_ref[side, rows, feats]
                do = do_ref[side, rows, feats].astype(F32)
                both = do * o_ref[side, rows, feats].astype(F32)
                k = keys[side, :, feats]
                v = values[side, :, feats]
                dq = []
                for head in heads:
                    over_sum = kept(side, rows, head)
                    if len(heads) == 2:
                        lanes = slice(head * HEAD, (head + 1) * HEAD)
                        mine = jnp.where(masks[head], both, 0.0)
                        do_head = jnp.where(masks[head], do, 0.0)
                    else:
                        lanes = slice(0, HEAD)
                        mine, do_head = both, do
                    delta = jnp.sum(mine, -1, keepdims=True) * over_sum
                    do_head = (do_head * over_sum).astype(B16)
                    raised = probs[side, head, rows]
                    ds = (raised.astype(F32) * (dot_nt(do_head, v) - delta)).astype(B16)
                    dq.append(dot_nn(ds, k))
                    dv_part = dot_tn(do_head[:, lanes], raised)
                    dk_part = dot_tn(q[:, lanes], ds)
                    at = pl.ds(head * HEAD, HEAD)
                    if index:
                        dv_part = dv_part + dvt[at]
                        dk_part = dk_part + dkt[at]
                    dvt[at] = dv_part
                    dkt[at] = dk_part
                dq = jnp.where(masks[0], dq[0], dq[1]) if len(heads) == 2 else dq[0]
                q_ref[side, rows, feats] = (dq * scale).astype(B16)
        for held, out in ((dkt, keys), (dvt, values)):
            for feats, at in ((pair, pl.ds(0, 2 * HEAD)), (lone, pl.ds(2 * HEAD, HEAD))):
                out[side, :, feats] = jnp.transpose(held[at]).astype(B16)

    each(2, attend_back_side)
    far_rows = pl.ds(length, length)
    kv_back = [
        [
            wire.copy(held.at[side, far_rows], got_kv.at[slot, side], sibling)
            for side in range(2)
        ]
        for slot, held in enumerate((keys, values))
    ]
    for copies in kv_back:
        for copy in copies:
            copy.start()

    if early:
        for t in (1, 2):
            held, copy = near[0, t]
            copy.wait()
            across[t][1].wait()
            grad_out[0, t, mine_grads] = (
                held[...].astype(F32)
                + grad_out[0, t, mine_grads].astype(F32)
                + across[t][0][...].astype(F32)
            ).astype(B16)

    a_flip = flip.at[0]
    a_flip[...] = transposed(a_ref[...])
    total = None
    for slot in range(3):
        for side, weight in enumerate((qkv_own, qkv_far)):
            if slot:
                kv_back[slot - 1][side].wait()
                own = (keys, values)[slot - 1][side, mine_rows].astype(F32)
                grad = (own + got_kv[slot - 1, side].astype(F32)).astype(B16)
            else:
                grad = q_ref[side]
            grad_out[side, 0, :, pl.ds(slot * third, third)] = dot_nn(a_flip[...], grad).astype(B16)
            part = dot_nt(grad, weight[slot])
            total = part if total is None else total + part
    z1[...] = total

    def first_back(i, totals):
        rows = pl.ds(pl.multiple_of(i * rows_at, 16), rows_at)
        grad = z1[rows]
        unit = unit1[rows]
        z = z2[rows] + back_norm(grad, unit, kept(0, rows, heads), gain1_ref[...])
        b_ref[rows] = z.astype(B16)
        pos_out[0, rows] = z[:, :third].astype(B16)
        pos_out[1, rows] = z[:, third:].astype(B16)
        ids = lax.broadcasted_iota(jnp.int32, (rows_at, 1), 0) + (base + i * rows_at)
        seen = jnp.sum(jnp.where(cells_row[...] == ids, 1.0, 0.0), -1, keepdims=True)
        return add_rows(totals[0], grad * unit), add_rows(totals[1], (1.0 - seen) * z)

    gain1_grad, mask_grad = lax.fori_loop(0, length // rows_at, first_back, (zero, zero))
    small_out[0:1] = gain1_grad
    small_out[1:2] = gain2_grad
    small_out[2:3] = mask_grad

    used = vis_ref.shape[0]
    ids = lax.broadcasted_iota(jnp.int32, (used, length), 1) + base
    place = jnp.where(cells_col[...] == ids, 1.0, 0.0).astype(B16)
    dvis_mine[...] = dot_nn(place, b_ref[...]).astype(B16)
    near = wire.copy(dvis_mine, dvis_near, sibling)
    near.start()
    near.wait()
    dvis_mine[...] = (dvis_mine[...].astype(F32) + dvis_near[...].astype(F32)).astype(B16)
    dvis_over = wire.copy(dvis_mine, dvis_far, facing)

    @pl.when(stays)
    def _():
        dvis_over.start()
        dvis_out[...] = dvis_mine[...]
        dvis_over.wait_send()
        route_local.wait()
        route_near.wait_send()
        route_over.wait_recv()

    @pl.when(jnp.logical_not(stays))
    def _():
        dvis_over.wait_recv()
        dvis_out[...] = dvis_far[...]
        route_over.wait_send()
        route_far.wait_send()
        route_near.wait_recv()
        route_far.wait_recv()


def decoder(early, vis, cells, pos_own, pos_far, mask, gains, weights, cot, ident):
    qkv_own, qkv_far, out_own, out_far, up, down = weights
    length, wide = pos_own.shape
    used = vis.shape[0]
    third = wide // 2
    hidden = up.shape[1]
    keys = 2 * length
    heads = third // HEAD
    assert heads == 3 and length % 112 == 0
    whole = pl.BlockSpec(memory_space=VMEM)
    there = pl.BlockSpec(memory_space=pl.ANY)
    return pl.pallas_call(
        functools.partial(dec_kernel, early),
        out_shape=[
            jax.ShapeDtypeStruct((2, length, third), B16),
            jax.ShapeDtypeStruct((2, length, third), B16),
            jax.ShapeDtypeStruct((used, wide), B16),
            jax.ShapeDtypeStruct((2, 3, wide, hidden), B16),
            jax.ShapeDtypeStruct((8, wide), F32),
        ],
        in_specs=[whole] * 3 + [there] + [whole] * 8 + [there] * 3,
        out_specs=[there] + [whole] * 4,
        scratch_shapes=[
            VMEM((2, length, third), B16),
            VMEM((2, wide, hidden), B16),
            VMEM((2, hidden, wide), B16),
            VMEM((length, wide), B16),
            VMEM((length, wide), F32),
            VMEM((length, wide), F32),
            VMEM((length, wide), B16),
            VMEM((2, length, third), B16),
            VMEM((2, keys, third), B16),
            VMEM((2, keys, third), B16),
            VMEM((2, heads, length, keys), B16),
            VMEM((2, length, 128), F32),
            VMEM((2, length, third), B16),
            VMEM((length, wide), F32),
            VMEM((length, wide), B16),
            VMEM((2, length, hidden), B16),
            VMEM((2, length, hidden), B16),
            VMEM((length, wide), F32),
            VMEM((2, length, third), B16),
            VMEM((2, wide, length), B16),
            VMEM((third, keys), F32),
            VMEM((third, keys), F32),
            VMEM((2, 2, length, third), B16),
            VMEM((used, wide), B16),
            VMEM((used, wide), B16),
            VMEM((used, wide), B16),
            pltpu.SemaphoreType.REGULAR,
            pltpu.SemaphoreType.DMA((5,)),
            pltpu.SemaphoreType.DMA((32,)),
            pltpu.SemaphoreType.DMA((32,)),
        ],
        compiler_params=pltpu.CompilerParams(
            collective_id=ident, has_side_effects=True, vmem_limit_bytes=63 * 1024 * 1024
        ),
        name="decoder",
    )(
        vis,
        cells[None, :],
        cells[:, None],
        pos_own,
        pos_far,
        mask[None, :],
        gains[0][None, :],
        gains[1][None, :],
        qkv_own,
        qkv_far,
        out_own,
        out_far,
        up,
        down,
        cot,
    )


def pack(grad, owners):
    rows, cols = grad.shape
    own = rows // owners
    fold = 1
    while own * fold % 16:
        fold *= 2
    grad = grad.astype(B16).reshape(owners, own, fold, cols // fold)
    return jnp.swapaxes(grad, 1, 2).reshape(owners, fold * own, cols // fold)


def unpack(piece, own):
    fold = piece.shape[0] // own
    return jnp.swapaxes(piece.reshape(fold, own, -1), 0, 1).reshape(own, -1)


def pick(pair, index):
    return lax.dynamic_index_in_dim(pair, index, 0, keepdims=False)


def load(src, dst, sem):
    copy = pltpu.make_async_copy(src, dst, sem)
    copy.start()
    return copy


def enc_kernel(*refs):
    (
        length_ref, tok_hbm, qkv_hbm, out_hbm, up_hbm, down_hbm, bridge_ref, gain1_ref, gain2_ref,
        pos_hbm, dqkv_hbm, dout_hbm,
        vis_out, dqkv_far, dout_far, pos_far, unit1, unit2, stats, a_ref, triple, probs, o_ref, b_ref,
        slope, h_ref, enc_half,
        x_ref, qkv, w_out, w_up, w_down, z2, part_ref, part_far, enc_ref, pos_full, pos_half,
        local_sem, send_sem, recv_sem,
    ) = refs
    s, d, m = place_of()
    sibling, facing = (1 - s, d, m), (s, d, 1 - m)
    stays = s == m
    used, wide = x_ref.shape
    half = tok_hbm.shape[1]
    rest = used - half
    wire = Wire(send_sem, recv_sem)

    greet([sibling, facing])
    first, last = pl.ds(0, half), pl.ds(half, rest)
    tok_first = wire.copy(tok_hbm.at[s], x_ref.at[first], facing)
    tok_last = wire.copy(tok_hbm.at[s, pl.ds(0, rest)], x_ref.at[last], facing)
    own_first = pltpu.make_async_copy(tok_hbm.at[s], x_ref.at[first], local_sem.at[0])
    own_last = pltpu.make_async_copy(
        tok_hbm.at[s, pl.ds(0, rest)], x_ref.at[last], local_sem.at[0]
    )

    @pl.when(m == 0)
    def _():
        tok_first.start()
        own_first.start()

    @pl.when(m == 1)
    def _():
        tok_last.start()
        own_last.start()

    loads = [
        load(hbm, held, local_sem.at[i + 1])
        for i, (hbm, held) in enumerate(
            ((qkv_hbm, qkv), (out_hbm, w_out), (up_hbm, w_up), (down_hbm, w_down))
        )
    ]
    pos_load = load(pos_hbm, pos_full, local_sem.at[5])
    over, share = [], []
    for hbm, held in ((dqkv_hbm, dqkv_far), (dout_hbm, dout_far)):
        at = (slice(None),) * (len(hbm.shape) - 2)
        size = hbm.shape[-2] // 2
        mine = at + (pl.ds(s * size, size),)
        over.append(wire.copy(hbm.at[mine], held.at[mine], facing))
        share.append(wire.copy(held.at[mine], held.at[mine], sibling))

    @pl.when(m == 0)
    def _():
        own_first.wait()
        tok_first.wait_send()
        tok_last.wait_recv()

    @pl.when(m == 1)
    def _():
        own_last.wait()
        tok_last.wait_send()
        tok_first.wait_recv()

    for copy in over:
        copy.start()

    lane = lax.broadcasted_iota(jnp.int32, (1, 128), 1)

    unit, inverse = norm_of(x_ref[...].astype(F32))
    unit1[...] = unit
    stats[...] = jnp.where(lane == 0, inverse, 0.0)
    a = (unit * gain1_ref[...]).astype(B16)
    a_ref[...] = a
    loads[0].wait()
    for slot in range(3):
        triple[slot] = dot_nn(a, qkv[slot]).astype(B16)

    valid = lax.broadcasted_iota(jnp.int32, (1, used), 1) < length_ref[s]
    masks = head_masks()
    for pair in range(triple.shape[2] // (2 * HEAD)):
        feats = pl.ds(pair * 2 * HEAD, 2 * HEAD)
        q, k, v = (triple[slot, :, feats] for slot in range(3))
        halves = []
        for head in range(2):
            scores = dot_nt(jnp.where(masks[head], q, 0), k) * HEAD**-0.5
            scores = jnp.where(valid, scores, NEG)
            raised = jnp.exp(scores - jnp.max(scores, -1, keepdims=True))
            p = (raised / jnp.sum(raised, -1, keepdims=True)).astype(B16)
            probs[2 * pair + head] = p
            halves.append(dot_nn(p, v))
        o_ref[:, feats] = jnp.where(masks[0], halves[0], halves[1]).astype(B16)

    loads[1].wait()
    part = dot_nn(o_ref[...], w_out[...])
    part_ref[0] = part.astype(B16)
    attn = wire.copy(part_ref.at[0], part_far.at[0], facing)
    attn.start()
    z2[...] = x_ref[...].astype(F32) + part

    pos_load.wait()
    pos_over = wire.copy(pos_half, pos_far, facing)

    @pl.when(stays)
    def _():
        pos_half[...] = pos_full[...].astype(B16)
        pos_over.start()

    attn.wait()
    z = z2[...] + part_far[0].astype(F32)
    z2[...] = z
    unit, inverse = norm_of(z)
    unit2[...] = unit
    stats[...] = jnp.where(lane == 1, inverse, stats[...])
    b = (unit * gain2_ref[...]).astype(B16)
    b_ref[...] = b
    loads[2].wait()
    step = 512

    def up(i):
        cols = pl.ds(pl.multiple_of(i * step, step), step)
        u = dot_nn(b_ref[...], w_up[:, cols])
        phi = 0.5 + 0.5 * lax.erf(u * 0.5**0.5)
        h_ref[:, cols] = (u * phi).astype(B16)
        bell = jnp.exp(u * u * -0.5) * (0.5 / jnp.pi) ** 0.5
        slope[:, cols] = (phi + u * bell).astype(B16)

    each(w_up.shape[1] // step, up)
    loads[3].wait()
    part = dot_nn(h_ref[...], w_down[...])
    z2[...] = z2[...] + part
    part_ref[1] = part.astype(B16)
    mlp = wire.copy(part_ref.at[1], part_far.at[1], facing)
    vis_near = wire.copy(vis_out, vis_out, sibling)
    mid = wide // 2
    enc_over = wire.copy(
        enc_ref.at[:, pl.ds(pl.multiple_of((1 - m) * mid, 128), mid)], enc_half, facing
    )

    @pl.when(stays)
    def _():
        mlp.wait_recv()
        enc = (z2[...] + part_far[1].astype(F32)).astype(B16)
        enc_ref[...] = enc
        enc_over.start()
        vis_out[...] = dot_nn(enc, bridge_ref[...]).astype(B16)
        vis_near.start()
        enc_half[...] = enc_ref[:, pl.ds(pl.multiple_of(m * mid, 128), mid)]

    @pl.when(jnp.logical_not(stays))
    def _():
        mlp.start()

    for copy, other in zip(over, share):
        copy.wait()
        other.start()

    @pl.when(stays)
    def _():
        vis_near.wait_send()
        enc_over.wait_send()
        pos_over.wait_send()

    @pl.when(jnp.logical_not(stays))
    def _():
        mlp.wait_send()
        vis_near.wait_recv()
        enc_over.wait_recv()
        pos_over.wait_recv()

    for copy in share:
        copy.wait()


def encoder(lengths, tokens, weights, bridge, gains, pos, dqkv, dout, used, ident):
    qkv, out, up, down = weights
    wide = tokens.shape[2]
    feats = qkv.shape[2]
    hidden = up.shape[1]
    whole = pl.BlockSpec(memory_space=VMEM)
    there = pl.BlockSpec(memory_space=pl.ANY)
    shape = jax.ShapeDtypeStruct
    outs = [
        (shape((used, dout.shape[1]), B16), whole),
        (shape(dqkv.shape, B16), there),
        (shape(dout.shape, B16), there),
        (shape(pos.shape, B16), there),
        (shape((used, wide), F32), whole),
        (shape((used, wide), F32), whole),
        (shape((used, 128), F32), whole),
        (shape((used, wide), B16), whole),
        (shape((3, used, feats), B16), whole),
        (shape((feats // HEAD, used, used), B16), whole),
        (shape((used, feats), B16), whole),
        (shape((used, wide), B16), whole),
        (shape((used, hidden), B16), whole),
        (shape((used, hidden), B16), whole),
        (shape((used, wide // 2), B16), whole),
    ]
    return pl.pallas_call(
        enc_kernel,
        out_shape=[item for item, _ in outs],
        in_specs=[pl.BlockSpec(memory_space=pltpu.SMEM)]
        + [there] * 5
        + [whole] * 3
        + [there] * 3,
        out_specs=[spec for _, spec in outs],
        scratch_shapes=[
            VMEM((used, wide), B16),
            VMEM(qkv.shape, B16),
            VMEM(out.shape, B16),
            VMEM(up.shape, B16),
            VMEM(down.shape, B16),
            VMEM((used, wide), F32),
            VMEM((2, used, wide), B16),
            VMEM((2, used, wide), B16),
            VMEM((used, wide), B16),
            VMEM(pos.shape, F32),
            VMEM(pos.shape, B16),
            pltpu.SemaphoreType.DMA((6,)),
            pltpu.SemaphoreType.DMA((16,)),
            pltpu.SemaphoreType.DMA((16,)),
        ],
        compiler_params=remote_params(ident),
        name="encoder",
    )(
        lengths, tokens, qkv, out, up, down, bridge, gains[0][None, :], gains[1][None, :],
        pos, dqkv, dout,
    )


class Fold:
    def __init__(self, wire, me, held, inbox, lanes, order, rows_of, device_of, last):
        self.held, self.inbox, self.lanes = held, inbox, lanes
        self.rounds = []
        slot = 0
        for k, axis in enumerate(order):
            rest = order[k + 1 :]
            other = dict(me)
            other[axis] = 1 - me[axis]
            copies = []
            for bits in itertools.product((0, 1), repeat=len(rest)):
                mine, theirs = dict(me, **dict(zip(rest, bits))), dict(other, **dict(zip(rest, bits)))
                copy = wire.copy(
                    held.at[rows_of(theirs), lanes], inbox.at[slot, :, lanes], device_of(other)
                )
                copies.append((copy, rows_of(mine), slot))
                slot += 1
            self.rounds.append(copies)
        self.mine = rows_of(me)
        if last:
            other = dict(me, y=1 - me["y"])
            copy = wire.copy(held.at[self.mine, lanes], inbox.at[slot, :, lanes], device_of(other))
            self.rounds.append([(copy, self.mine, slot)])

    def start(self, k):
        for copy, _, _ in self.rounds[k]:
            copy.start()

    def total(self, rows, slot):
        return self.held[rows, self.lanes].astype(F32) + self.inbox[slot, :, self.lanes].astype(F32)

    def step(self, k):
        for copy, rows, slot in self.rounds[k]:
            copy.wait()
            self.held[rows, self.lanes] = self.total(rows, slot).astype(B16)
        self.start(k + 1)

    def end(self):
        ((copy, rows, slot),) = self.rounds[-1]
        copy.wait()
        return self.total(rows, slot)


def back_kernel(cube, *refs):
    (
        dvis_ref, bridge_ref, gain1_ref, gain2_ref, unit1, unit2, stats, a_ref, triple, probs, o_ref,
        b_ref, slope, h_ref, enc_half, small_dec, qkv_hbm, out_hbm, up_hbm, down_hbm, *refs,
    ) = refs
    if cube:
        (
            dec_hbm, pos_hbm,
            tok_out, small_out, enc_out, dec_out, pos_out, bridge_all,
            near, inbox, dec_raw, dec_near, dec_over, dec_held, dec_box, pos_got, pos_held, pos_box,
            bridge_near, bridge_box, small_box, grads, bridge_grad, *refs,
        ) = refs
    else:
        tok_out, small_out, grads, bridge_grad, *refs = refs
    (
        qkv, w_out, w_up, w_down, gu, dy, part, part_far, dz, da_ref, do_ref, dqkv, flip, tok_part,
        local_sem, send_sem, recv_sem,
    ) = refs
    s, d, m = place_of()
    sibling, facing = (1 - s, d, m), (s, d, 1 - m)
    stays = s == m
    used, wide = unit1.shape
    feats = o_ref.shape[1]
    hidden = h_ref.shape[1]
    half = tok_part.shape[1]
    rest = used - half
    wire = Wire(send_sem, recv_sem)
    section = wide // 2

    if cube:
        z = d // 2
        me = {"y": lax.rem(d, 2), "b": z // 2, "a": lax.rem(z + z // 2, 2)}

        def z_of(c):
            return lax.rem(c["a"] + c["b"], 2) + 2 * c["b"]

        def device_of(c):
            return (s, 2 * z_of(c) + c["y"], m)

        def rows_eight(c):
            return pl.ds(pl.multiple_of((2 * z_of(c) + c["y"]) * 48, 16), 48)

        def rows_four(c):
            return pl.ds(pl.multiple_of(z_of(c) * 48, 16), 48)

        near_chips = [device_of(dict(me, **{axis: 1 - me[axis]})) for axis in "yab"]
        across = lax.rem(z_of(me) + 2, 4)
        more = [(s, 2 * across + me["y"], m)] + [
            (s, 2 * lax.rem(z + k, 4) + me["y"], 1 - m) for k in (1, 2, 3)
        ]
        greet([sibling, facing, (1 - s, d, 1 - m)] + near_chips + more)
    else:
        greet([sibling, facing])

    loads = [
        load(hbm, held, local_sem.at[i])
        for i, (hbm, held) in enumerate(
            ((down_hbm, w_down), (up_hbm, w_up), (out_hbm, w_out), (qkv_hbm, qkv))
        )
    ]

    if cube:
        route_local = pltpu.make_async_copy(pos_hbm.at[s], pos_got.at[m], local_sem.at[4])
        route_near = wire.copy(pos_hbm.at[1 - s], pos_got.at[m], sibling)
        route_over = wire.copy(pos_hbm.at[s], pos_got.at[m], facing)
        route_far = wire.copy(pos_hbm.at[1 - s], pos_got.at[m], (1 - s, d, 1 - m))

        @pl.when(stays)
        def _():
            route_local.start()
            route_near.start()

        @pl.when(jnp.logical_not(stays))
        def _():
            route_over.start()
            route_far.start()

        dec_rows = dec_raw.shape[1] // 2
        mine = pl.ds(pl.multiple_of(s * dec_rows, 16), dec_rows)
        away = pl.ds(pl.multiple_of((1 - s) * dec_rows, 16), dec_rows)
        raw_load = load(dec_hbm.at[:, 0], dec_raw, local_sem.at[5])
        span = dec_raw.shape[2]
        sum_loads = [
            load(dec_hbm.at[0, t, mine], dec_held.at[:, pl.ds(t * span, span)], local_sem.at[5 + t])
            for t in (1, 2)
        ]
        raw_load.wait()
        dec_pair = [
            wire.copy(dec_raw.at[side, away], dec_near.at[side], sibling) for side in range(2)
        ]
        for copy in reversed(dec_pair):
            copy.start()

    def transposed(value):
        return jnp.transpose(value.astype(F32)).astype(B16)

    dvis = dvis_ref[...]
    grad = dot_nt(dvis, bridge_ref[...])
    dy[...] = grad
    dm = grad.astype(B16)
    da_ref[...] = dm
    flip[0] = transposed(dm)
    flip[1] = transposed(b_ref[...])
    bridge_grad[...] = dot_tn(enc_half[...], dvis).astype(B16)
    if cube:
        bridge_rows = bridge_near.shape[0]
        bridge_pair = wire.copy(
            bridge_grad.at[pl.ds(pl.multiple_of((1 - s) * bridge_rows, 16), bridge_rows)],
            bridge_near,
            sibling,
        )
        bridge_pair.start()
        dec_pair[1].wait()
        dec_near[1] = (dec_near[1].astype(F32) + dec_raw[1, mine].astype(F32)).astype(B16)
        dec_across = wire.copy(dec_near.at[1], dec_over, facing)
        dec_across.start()

    loads[0].wait()
    step = 512
    first_up, first_down = 3 * feats + feats, 3 * feats + feats + hidden

    def down(i):
        cols = pl.ds(pl.multiple_of(i * step, step), step)
        grads[:, pl.ds(pl.multiple_of(first_down + i * step, 128), step)] = dot_nn(
            flip[0], h_ref[:, cols]
        ).astype(B16)
        grad_u = dot_nt(da_ref[...], w_down[cols, :]) * slope[:, cols].astype(F32)
        grad_u = grad_u.astype(B16)
        gu[:, cols] = grad_u
        grads[:, pl.ds(pl.multiple_of(first_up + i * step, 128), step)] = dot_nn(
            flip[1], grad_u
        ).astype(B16)

    each(hidden // step, down)

    if cube:
        attn_lanes, mlp_lanes = pl.ds(0, first_up), pl.ds(first_up, 2 * hidden)
        theirs = pl.ds(pl.multiple_of((1 - s) * section, 16), section)
        mlp_pair = wire.copy(grads.at[theirs, mlp_lanes], near.at[:, mlp_lanes], sibling)
        mlp_pair.start()

    loads[1].wait()
    grad = dot_nt(gu[...], w_up[...])
    part[...] = grad.astype(B16)
    over = wire.copy(part, part_far.at[0], facing)
    over.start()
    dz[...] = grad
    gain2_grad = jnp.sum(grad * unit2[...], 0, keepdims=True)

    if cube:
        def pair_sum(lanes):
            def body(i):
                rows = pl.ds(pl.multiple_of(i * 48, 16), 48)
                from_rows = pl.ds(pl.multiple_of(s * section + i * 48, 16), 48)
                near[rows, lanes] = (
                    near[rows, lanes].astype(F32) + grads[from_rows, lanes].astype(F32)
                ).astype(B16)

            each(section // 48, body)

        orders = (("y", "a", "b"), ("a", "b", "y"), ("b", "y", "a"))

        def folds_of(first, size):
            third = size // 3
            return [
                Fold(
                    wire, me, near, inbox, pl.ds(first + i * third, third), orders[i], rows_eight,
                    device_of, False,
                )
                for i in range(3)
            ]

        mlp_folds = folds_of(first_up, 2 * hidden)
        mlp_pair.wait()
        pair_sum(mlp_lanes)
        for fold in mlp_folds:
            fold.start(0)

        dec_pair[0].wait()
        dec_across.wait()
        dec_held[:, pl.ds(0, span)] = (
            dec_near[0].astype(F32) + dec_raw[0, mine].astype(F32) + dec_over[...].astype(F32)
        ).astype(B16)
        for copy in sum_loads:
            copy.wait()
        side_folds = [
            Fold(
                wire, me, dec_held, dec_box, pl.ds(i * (3 * span // 2), 3 * span // 2), order,
                rows_four, device_of, True,
            )
            for i, order in enumerate((("a", "b"), ("b", "a")))
        ]
        bridge_pair.wait()
        bridge_near[...] = (
            bridge_near[...].astype(F32)
            + bridge_grad[
                pl.ds(pl.multiple_of(s * bridge_rows, 16), bridge_rows)
            ].astype(F32)
        ).astype(B16)
        side_folds.append(
            Fold(
                wire, me, bridge_near, bridge_box, pl.ds(0, bridge_near.shape[1]), ("a", "b"),
                rows_four, device_of, True,
            )
        )

        @pl.when(stays)
        def _():
            route_local.wait()
            route_near.wait_send()
            route_over.wait_recv()

        @pl.when(jnp.logical_not(stays))
        def _():
            route_over.wait_send()
            route_far.wait_send()
            route_near.wait_recv()
            route_far.wait_recv()

        pos_held[...] = transposed(pos_got[0].astype(F32) + pos_got[1].astype(F32))
        side_folds.append(
            Fold(
                wire, me, pos_held, pos_box, pl.ds(0, pos_held.shape[1]), ("b", "a"), rows_four,
                device_of, True,
            )
        )
        for fold in side_folds:
            fold.start(0)

    def back_norm(grad, unit, inverse, gain):
        scaled = grad * gain
        mean = jnp.mean(scaled, -1, keepdims=True)
        tilt = jnp.mean(scaled * unit, -1, keepdims=True)
        return inverse * (scaled - mean - unit * tilt)

    over.wait()
    whole = dz[...] + part_far[0].astype(F32)
    dz2 = dy[...] + back_norm(whole, unit2[...], stats[:, 1:2], gain2_ref[...])
    dy[...] = dz2
    grad_a = dz2.astype(B16)
    da_ref[...] = grad_a
    flip[0] = transposed(grad_a)
    loads[2].wait()
    grads[:, pl.ds(3 * feats, feats)] = dot_nn(flip[0], o_ref[...]).astype(B16)
    do_ref[...] = dot_nt(grad_a, w_out[...]).astype(B16)

    if cube:
        for fold in side_folds:
            fold.step(0)

    masks = head_masks()
    scale = HEAD**-0.5
    for pair in range(feats // (2 * HEAD)):
        at = pl.ds(pair * 2 * HEAD, 2 * HEAD)
        q, k, v = (triple[slot, :, at] for slot in range(3))
        do = do_ref[:, at]
        both = do.astype(F32) * o_ref[:, at].astype(F32)
        parts = []
        for head in range(2):
            delta = jnp.sum(jnp.where(masks[head], both, 0.0), -1, keepdims=True)
            do_head = jnp.where(masks[head], do, 0)
            p = probs[2 * pair + head]
            ds = (p.astype(F32) * (dot_nt(do_head, v) - delta)).astype(B16)
            parts.append((dot_nn(ds, k) * scale, dot_tn(ds, q) * scale, dot_tn(p, do)))
        for slot in range(3):
            dqkv[slot, :, at] = jnp.where(masks[0], parts[0][slot], parts[1][slot]).astype(B16)

    flip[1] = transposed(a_ref[...])
    loads[3].wait()
    total = None
    for slot in range(3):
        grads[:, pl.ds(slot * feats, feats)] = dot_nn(flip[1], dqkv[slot]).astype(B16)
        term = dot_nt(dqkv[slot], qkv[slot])
        total = term if total is None else total + term
    part[...] = total.astype(B16)
    dz[...] = total
    gain1_grad = jnp.sum(total * unit1[...], 0, keepdims=True)
    first, last = pl.ds(0, half), pl.ds(half, rest)
    over_first = wire.copy(part.at[first], part_far.at[1, first], facing)
    over_last = wire.copy(part.at[last], part_far.at[1, last], facing)

    @pl.when(m == 0)
    def _():
        over_last.start()

    @pl.when(m == 1)
    def _():
        over_first.start()

    small_out[...] = jnp.zeros(small_out.shape, F32)
    row = 0
    for value in (
        gain1_grad, gain2_grad, small_dec[0:1], small_dec[1:2], small_dec[2:3],
    ):
        for i in range(value.shape[1] // 128):
            small_out[row : row + 1] = value[:, i * 128 : (i + 1) * 128]
            row += 1

    if cube:
        attn_pair = wire.copy(grads.at[theirs, attn_lanes], near.at[:, attn_lanes], sibling)
        attn_pair.start()

        small_steps = [sibling, facing] + near_chips
        small_copies = [
            wire.copy(small_out, small_box.at[i], partner) for i, partner in enumerate(small_steps)
        ]

        def small_step(i):
            small_copies[i].wait()
            small_out[...] = small_out[...] + small_box[i]
            if i + 1 < len(small_copies):
                small_copies[i + 1].start()

        small_copies[0].start()
        for fold in mlp_folds:
            fold.step(0)
        for fold in side_folds:
            fold.step(1)
        small_step(0)

    def finish(rows, size):
        whole = dz[rows] + part_far[1, rows].astype(F32)
        unit = unit1[rows]
        grad = dy[rows] + back_norm(whole, unit, stats[rows][:, 0:1], gain1_ref[...])
        for side in range(2):
            tok_part[side, pl.ds(0, size)] = grad[:, side * section : (side + 1) * section]

    @pl.when(m == 0)
    def _():
        over_last.wait_send()
        over_first.wait_recv()
        finish(first, half)

    @pl.when(m == 1)
    def _():
        over_first.wait_send()
        over_last.wait_recv()
        tok_part[...] = jnp.zeros(tok_part.shape, F32)
        finish(last, rest)

    tok_pair = wire.copy(tok_part.at[1 - s], tok_out.at[s], sibling)
    tok_pair.start()
    tok_out[s] = tok_part[s]

    if cube:
        attn_folds = folds_of(0, first_up)
        attn_pair.wait()
        pair_sum(attn_lanes)
        for fold in attn_folds:
            fold.start(0)
        small_step(1)

        def own_rows(value, out):
            @pl.when(me["y"] == 0)
            def _():
                out[...] = value[:24]

            @pl.when(me["y"] == 1)
            def _():
                out[...] = value[24:]

        slot = (s * 4 + z) * 2 + m
        bridge_all[slot] = side_folds[2].end().astype(B16)
        spread = [
            wire.copy(bridge_all.at[slot], bridge_all.at[slot], partner)
            for partner in [facing]
            + [
                (s, 2 * lax.rem(z + k, 4) + me["y"], lax.rem(m + side, 2))
                for k in (1, 2, 3)
                for side in range(2)
            ]
        ]
        for copy in spread:
            copy.start()
        for i in range(2):
            own = pl.ds(i * (3 * span // 2), 3 * span // 2)
            own_rows(side_folds[i].end(), dec_out.at[:, own])
        own_rows(side_folds[3].end(), pos_out)
        for fold in mlp_folds:
            fold.step(1)
        for fold in attn_folds:
            fold.step(0)
        small_step(2)
        for copy in spread:
            copy.wait()
        ours = pl.ds(s * 8, 8)
        bridge_pair_all = wire.copy(bridge_all.at[ours], bridge_all.at[ours], sibling)
        bridge_pair_all.start()
        for fold in mlp_folds:
            enc_out[:, fold.lanes] = fold.end()
        for fold in attn_folds:
            fold.step(1)
        small_step(3)
        for fold in attn_folds:
            enc_out[:, fold.lanes] = fold.end()
        small_step(4)
        bridge_pair_all.wait()

    tok_pair.wait()


def back(cube, dvis, bridge, gains, saved, small_dec, weights, dec_grads, pos_parts, half, ident):
    unit1, unit2, stats, a, triple, probs, o, b, slope, h, enc_half = saved
    qkv, out, up, down = weights
    used, wide = unit1.shape
    feats, hidden = o.shape[1], h.shape[1]
    cols = 4 * feats + 2 * hidden
    narrow = bridge.shape[1]
    whole = pl.BlockSpec(memory_space=VMEM)
    there = pl.BlockSpec(memory_space=pl.ANY)
    shape = jax.ShapeDtypeStruct
    args = [dvis, bridge, gains[0][None, :], gains[1][None, :], *saved, small_dec, qkv, out, up, down]
    in_specs = [whole] * 16 + [there] * 4
    outs = [shape((2, half, wide // 2), F32), shape((24, 128), F32)]
    assert 2 * wide + 3 * narrow <= 24 * 128
    grads, bridge_grad = (wide, cols), (wide // 2, narrow)
    scratch = []
    if cube:
        span = dec_grads.shape[3]
        cells = pos_parts.shape[1]
        args += [dec_grads, pos_parts]
        in_specs += [there] * 2
        outs += [
            shape((48, cols), F32),
            shape((24, 3 * span), F32),
            shape((24, cells), F32),
            shape((16, 48, narrow), B16),
        ]
        scratch = [
            VMEM((wide // 2, cols), B16),
            VMEM((7, 48, cols), B16),
            VMEM((2, narrow, span), B16),
            VMEM((2, narrow // 2, span), B16),
            VMEM((narrow // 2, span), B16),
            VMEM((narrow // 2, 3 * span), B16),
            VMEM((4, 48, 3 * span), B16),
            VMEM(pos_parts.shape, B16),
            VMEM((pos_parts.shape[2], cells), B16),
            VMEM((4, 48, cells), B16),
            VMEM((narrow // 2, narrow), B16),
            VMEM((4, 48, narrow), B16),
            VMEM((5, 24, 128), F32),
            VMEM(grads, B16),
            VMEM(bridge_grad, B16),
        ]
    else:
        outs += [shape(grads, B16), shape(bridge_grad, B16)]
    scratch += [
        VMEM(qkv.shape, B16),
        VMEM(out.shape, B16),
        VMEM(up.shape, B16),
        VMEM(down.shape, B16),
        VMEM((used, hidden), B16),
        VMEM((used, wide), F32),
        VMEM((used, wide), B16),
        VMEM((2, used, wide), B16),
        VMEM((used, wide), F32),
        VMEM((used, wide), B16),
        VMEM((used, feats), B16),
        VMEM((3, used, feats), B16),
        VMEM((2, wide, used), B16),
        VMEM((2, half, wide // 2), F32),
        pltpu.SemaphoreType.DMA((8,)),
        pltpu.SemaphoreType.DMA((96,)),
        pltpu.SemaphoreType.DMA((96,)),
    ]
    return pl.pallas_call(
        functools.partial(back_kernel, cube),
        out_shape=outs,
        in_specs=in_specs,
        out_specs=[whole] * len(outs),
        scratch_shapes=scratch,
        compiler_params=remote_params(ident),
        name="encoder_back",
    )(*args)


def per_device(
    tokens,
    clip_lengths,
    clip_cells,
    enc_qkv,
    enc_attn_out,
    enc_up,
    enc_down,
    enc_gain_one,
    enc_gain_two,
    bridge_weight,
    mask_token,
    position_embed,
    dec_qkv,
    dec_attn_out,
    dec_up,
    dec_down,
    dec_gain_one,
    dec_gain_two,
    cotangent,
):
    s, d, m = place_of()
    n = lax.axis_size("dp")
    owners = 2 * n
    cube = n == 8
    dec_wide = position_embed.shape[1]
    half_slots, enc_wide = tokens.shape[2:]
    used = -(-LONGEST // 32) * 32

    e_weights = (jnp.swapaxes(enc_qkv, 0, 1), enc_attn_out, enc_up, enc_down)
    d_qkv = jnp.swapaxes(dec_qkv, 0, 1)
    vis, d_qkv_far, d_out_far, pos_far, *saved = encoder(
        clip_lengths[:, 0],
        tokens[:, 0],
        e_weights,
        bridge_weight,
        (enc_gain_one, enc_gain_two),
        position_embed,
        d_qkv,
        dec_attn_out,
        used,
        1,
    )
    cells = jnp.where(
        jnp.arange(used) < pick(clip_lengths[:, 0], m), pick(clip_cells[:, 0], m)[:used], -1
    )
    decoded, pos_parts, dvis, dec_grads, dec_small = decoder(
        cube,
        vis,
        cells,
        position_embed,
        pos_far,
        mask_token,
        (dec_gain_one, dec_gain_two),
        (d_qkv, d_qkv_far, dec_attn_out, d_out_far, dec_up, dec_down),
        cotangent[:, 0],
        2,
    )
    tokens_grad, small, *rest = back(
        cube,
        dvis,
        bridge_weight,
        (enc_gain_one, enc_gain_two),
        saved,
        dec_small,
        e_weights,
        dec_grads,
        pos_parts,
        half_slots,
        3,
    )
    if cube:
        enc_final, dec_final, pos_final, bridge_all = rest
        pieces = bridge_all.reshape(8, 2, -1, dec_wide)
        bridge_grad = jnp.swapaxes(pieces, 0, 1).reshape(enc_wide, dec_wide)
    else:
        grads, bridge = rest
        enc_final = unpack(scatter(pack(grads, owners)[None], 11), enc_wide // owners)
        packed = [
            pack(jnp.concatenate([dec_grads[side, t] for t in range(3)], 1), owners)
            for side in range(2)
        ]
        dec_final = unpack(scatter(jnp.stack(packed), 12), dec_wide // owners)
        parts = route(pos_parts, 13).astype(F32)
        packed = pack(jnp.transpose(parts[0] + parts[1]), n)
        zero = jnp.zeros_like(packed)
        packed = jnp.concatenate(
            [jnp.where(s == 0, packed, zero), jnp.where(s == 1, packed, zero)], 0
        )
        pos_final = unpack(scatter(packed[None], 14), dec_wide // owners)
        bridge_own = enc_wide // 2 // owners
        per = -(-small.size // owners)
        small = jnp.pad(small.reshape(-1), (0, per * owners - small.size)).reshape(owners, 1, per)
        rows = -(-(bridge_own + 1) // 16) * 16
        rep = jnp.concatenate(
            [
                bridge.astype(F32).reshape(owners, bridge_own, dec_wide),
                jnp.pad(small, ((0, 0), (0, 0), (0, dec_wide - per))),
                jnp.zeros((owners, rows - bridge_own - 1, dec_wide), F32),
            ],
            1,
        ).astype(B16)
        rep = scatter(rep[None], 15).astype(B16)
        everyone = gather(rep, n, 16).reshape(owners, 2, rows, dec_wide)
        bridge_grad = jnp.swapaxes(everyone[:, :, :bridge_own], 0, 1).reshape(enc_wide, dec_wide)
        small = everyone[:, 0, bridge_own, :per].astype(F32) + everyone[
            :, 1, bridge_own, :per
        ].astype(F32)
    cuts = [enc_wide, 2 * enc_wide, 2 * enc_wide + dec_wide, 2 * enc_wide + 2 * dec_wide]
    small = small.reshape(-1)[: 2 * enc_wide + 3 * dec_wide]
    one_e, two_e, one_d, two_d, mask_grad = jnp.split(small, cuts)

    def split(final, qkv, out, up):
        cols = qkv.shape[2]
        first = 3 * cols + out.shape[0]
        second = first + up.shape[1]
        return (
            final[:, : 3 * cols].reshape(-1, 3, cols),
            final[:, 3 * cols : first].T,
            final[:, first:second],
            final[:, second:].T,
        )

    return (
        decoded.astype(F32)[:, None],
        tokens_grad[:, None],
        *split(enc_final, enc_qkv, enc_attn_out, enc_up),
        one_e,
        two_e,
        bridge_grad.astype(F32),
        mask_grad,
        pos_final.T,
        *split(dec_final, dec_qkv, dec_attn_out, dec_up),
        one_d,
        two_d,
    )


def solution(mesh):
    return jax.shard_map(
        per_device,
        mesh=mesh,
        in_specs=(
            P(None, "dp", "mp", None),
            P(None, "dp"),
            P(None, "dp", None),
            P(None, None, "mp"),
            P("mp", None),
            P(None, "mp"),
            P("mp", None),
            P(),
            P(),
            P(),
            P(),
            P("mp", None),
            P(None, None, "mp"),
            P("mp", None),
            P(None, "mp"),
            P("mp", None),
            P(),
            P(),
            P(None, "dp", "mp", None),
        ),
        out_specs=(
            P(None, "dp", "mp", "section"),
            P(None, "dp", "mp", "section"),
            P(("section", "dp"), None, "mp"),
            P("mp", ("section", "dp")),
            P(("section", "dp"), "mp"),
            P("mp", ("section", "dp")),
            P(),
            P(),
            P(),
            P(),
            P("mp", ("section", "dp")),
            P(("section", "dp"), None, "mp"),
            P("mp", ("section", "dp")),
            P(("section", "dp"), "mp"),
            P("mp", ("section", "dp")),
            P(),
            P(),
        ),
        check_vma=False,
    )
```

```python
import functools
import itertools

import jax
import jax.numpy as jnp
from jax import lax
from jax.experimental import pallas as pl
from jax.experimental.pallas import tpu as pltpu
from jax.sharding import PartitionSpec as P

HEAD = 64
LONGEST = 157
EPS = 1e-06
NEG = -1e30
F32 = jnp.float32
B16 = jnp.bfloat16
MESH = pl.DeviceIdType.MESH
VMEM = pltpu.VMEM
LIMIT = 56 * 1024 * 1024


def place_of():
    return lax.axis_index("section"), lax.axis_index("dp"), lax.axis_index("mp")


def greet(partners):
    barrier = pltpu.get_barrier_semaphore()
    for partner in partners:
        pl.semaphore_signal(barrier, inc=1, device_id=partner, device_id_type=MESH)
    pl.semaphore_wait(barrier, len(partners))


def send(src, dst, send_sem, recv_sem, partner):
    return pltpu.make_async_remote_copy(
        src_ref=src,
        dst_ref=dst,
        send_sem=send_sem,
        recv_sem=recv_sem,
        device_id=partner,
        device_id_type=MESH,
    )


def remote_params(ident):
    return pltpu.CompilerParams(
        collective_id=ident, has_side_effects=True, vmem_limit_bytes=LIMIT
    )


def route_kernel(x_ref, out_ref, send_sem, recv_sem, local_sem):
    s, d, m = place_of()
    greet([(1 - s, d, m), (s, d, 1 - m), (1 - s, d, 1 - m)])
    stays = s == m

    @pl.when(stays)
    def _():
        mine = pltpu.make_async_copy(x_ref.at[s], out_ref.at[m], local_sem)
        mine.start()
        out = send(x_ref.at[1 - s], out_ref.at[m], send_sem.at[0], recv_sem.at[m], (1 - s, d, m))
        out.start()
        mine.wait()
        out.wait_send()

    @pl.when(jnp.logical_not(stays))
    def _():
        near = send(x_ref.at[s], out_ref.at[m], send_sem.at[0], recv_sem.at[m], (s, d, 1 - m))
        far = send(
            x_ref.at[1 - s], out_ref.at[m], send_sem.at[1], recv_sem.at[m], (1 - s, d, 1 - m)
        )
        near.start()
        far.start()
        near.wait_send()
        far.wait_send()

    pltpu.make_async_copy(out_ref.at[1 - m], out_ref.at[1 - m], recv_sem.at[1 - m]).wait()

    @pl.when(jnp.logical_not(stays))
    def _():
        pltpu.make_async_copy(out_ref.at[m], out_ref.at[m], recv_sem.at[m]).wait()


def route(x, ident):
    return pl.pallas_call(
        route_kernel,
        out_shape=jax.ShapeDtypeStruct(x.shape, x.dtype),
        in_specs=[pl.BlockSpec(memory_space=pl.ANY)],
        out_specs=pl.BlockSpec(memory_space=pl.ANY),
        scratch_shapes=[
            pltpu.SemaphoreType.DMA((2,)),
            pltpu.SemaphoreType.DMA((2,)),
            pltpu.SemaphoreType.DMA,
        ],
        compiler_params=remote_params(ident),
        name=f"route_{ident}",
    )(x)


def scatter_kernel(n, across, g_ref, out_ref, near, work, far, over, sems):
    near_send, near_recv, far_send, far_recv, over_send, over_recv = sems
    s, d, m = place_of()
    sibling, facing = (1 - s, d, m), (s, d, 1 - m)
    greet([sibling] + [facing] * across + [(s, lax.rem(d + k, n), m) for k in range(1, n)])
    order = [*range(1, n), 0]
    sides = 1 + across
    first = {}
    for side in reversed(range(sides)):
        for k in order:
            to = lax.rem(d + k, n)
            first[side, k] = send(
                g_ref.at[side, (1 - s) * n + to],
                near.at[side, to],
                near_send.at[side, k],
                near_recv.at[side, k],
                sibling,
            )
            first[side, k].start()

    def summed(side, k):
        to = lax.rem(d + k, n)
        first[side, k].wait()
        return to, g_ref[side, s * n + to].astype(F32) + near[side, to].astype(F32)

    second = {}
    if across:
        for k in order:
            to, part = summed(1, k)
            work[1, to] = part.astype(B16)
            second[k] = send(work.at[1, to], over.at[to], over_send.at[k], over_recv.at[k], facing)
            second[k].start()
    third = []
    for k in order:
        to, part = summed(0, k)
        if across:
            second[k].wait()
            part = part + over[to].astype(F32)
        if k:
            work[0, to] = part.astype(B16)
            copy = send(work.at[0, to], far.at[d], far_send.at[k], far_recv.at[k], (s, to, m))
            copy.start()
            third.append((k, copy))
    for k, copy in third:
        copy.wait()
        part = part + far[lax.rem(d + n - k, n)].astype(F32)
    out_ref[...] = part


def scatter(g, ident):
    sides, owners, rows, cols = g.shape
    n = owners // 2
    across = sides - 1
    kernel = functools.partial(scatter_kernel, n, across)

    def body(g_ref, out_ref, near, work, far, over, *sems):
        kernel(g_ref, out_ref, near, work, far, over, sems)

    pieces = (n, rows, cols)
    return pl.pallas_call(
        body,
        out_shape=jax.ShapeDtypeStruct((rows, cols), F32),
        in_specs=[pl.BlockSpec(memory_space=VMEM)],
        out_specs=pl.BlockSpec(memory_space=VMEM),
        scratch_shapes=[
            VMEM((sides,) + pieces, B16),
            VMEM((sides,) + pieces, B16),
            VMEM(pieces, B16),
            VMEM(pieces if across else (8, 128), B16),
            pltpu.SemaphoreType.DMA((sides, n)),
            pltpu.SemaphoreType.DMA((sides, n)),
            pltpu.SemaphoreType.DMA((n,)),
            pltpu.SemaphoreType.DMA((n,)),
            pltpu.SemaphoreType.DMA((n,)),
            pltpu.SemaphoreType.DMA((n,)),
        ],
        compiler_params=remote_params(ident),
        name=f"scatter_{ident}",
    )(g)


def gather_kernel(n, x_ref, out_ref, local_sem, send_sem, recv_sem):
    s, d, m = place_of()
    steps = [(a, k, b) for k in range(n) for a in range(2) for b in range(2) if a or k or b]

    def partner(step):
        a, k, b = step
        return (lax.rem(s + a, 2), lax.rem(d + k, n), lax.rem(m + b, 2))

    greet([partner(step) for step in steps])
    slot = (s * n + d) * 2 + m
    mine = pltpu.make_async_copy(x_ref, out_ref.at[slot], local_sem)
    mine.start()
    copies = [
        send(x_ref, out_ref.at[slot], send_sem.at[i], recv_sem.at[i], partner(step))
        for i, step in enumerate(steps)
    ]
    for copy in copies:
        copy.start()
    mine.wait()
    for copy in copies:
        copy.wait()


def gather(x, n, ident):
    count = 4 * n
    return pl.pallas_call(
        functools.partial(gather_kernel, n),
        out_shape=jax.ShapeDtypeStruct((count,) + x.shape, x.dtype),
        in_specs=[pl.BlockSpec(memory_space=VMEM)],
        out_specs=pl.BlockSpec(memory_space=VMEM),
        scratch_shapes=[
            pltpu.SemaphoreType.DMA,
            pltpu.SemaphoreType.DMA((count - 1,)),
            pltpu.SemaphoreType.DMA((count - 1,)),
        ],
        compiler_params=remote_params(ident),
        name=f"gather_{ident}",
    )(x)


def dot_nt(a, b):
    return lax.dot_general(a, b, (((1,), (1,)), ((), ())), preferred_element_type=F32)


def dot_nn(a, b):
    return lax.dot_general(a, b, (((1,), (0,)), ((), ())), preferred_element_type=F32)


def dot_tn(a, b):
    return lax.dot_general(a, b, (((0,), (0,)), ((), ())), preferred_element_type=F32)


def chunks_of(length, most=256):
    units = length // 16
    count = -(-length // most)
    cuts = [16 * (units * i // count) for i in range(count)] + [length]
    return [(a, b - a) for a, b in zip(cuts, cuts[1:])]


def head_masks():
    lanes = lax.broadcasted_iota(jnp.int32, (1, 2 * HEAD), 1)
    return (lanes < HEAD, lanes >= HEAD)


def fetch(src, dst, sem):
    copy = pltpu.make_async_copy(src, dst, sem)
    copy.start()
    return copy


class Wire:
    def __init__(self, send_sem, recv_sem):
        self.send_sem, self.recv_sem, self.used = send_sem, recv_sem, 0

    def copy(self, src, dst, partner):
        index = self.used
        self.used += 1
        assert index < self.send_sem.shape[0]
        return send(src, dst, self.send_sem.at[index], self.recv_sem.at[index], partner)


class Chip:
    def __init__(self, s, d, m):
        self.s, self.m = s, m
        z = d // 2
        self.z = z
        self.me = {"y": lax.rem(d, 2), "a": lax.rem(z + z // 2, 2), "b": z // 2}
        self.near = [self.beside(axis) for axis in "yab"]

    @staticmethod
    def z_of(a, b):
        return lax.rem(a + b, 2) + 2 * b

    @staticmethod
    def place(z):
        return (z + z // 2) % 2, z // 2

    def beside(self, axis):
        at = dict(self.me, **{axis: 1 - self.me[axis]})
        return (self.s, 2 * self.z_of(at["a"], at["b"]) + at["y"], self.m)

    def own_rows(self, value, out):
        for y in range(2):

            @pl.when(self.me["y"] == y)
            def _(y=y):
                out[...] = value[24 * y : 24 * y + 24]


class Fold:
    def __init__(self, wire, chip, held, boxes, lanes, axes, order, last):
        self.rounds = []
        kept = {}
        for k, axis in enumerate(order):

            def part(value):
                chosen = dict(kept, **{axis: value})
                index = tuple(chosen.get(name, slice(None)) for name in axes)
                return held.at[index + (slice(None), lanes)]

            box = boxes[k].at[(slice(None),) * (len(axes) - k) + (lanes,)]
            copy = wire.copy(part(1 - chip.me[axis]), box, chip.beside(axis))
            self.rounds.append((copy, part(chip.me[axis]), box))
            kept[axis] = chip.me[axis]
        if last:
            mine = held.at[tuple(kept[name] for name in axes) + (slice(None), lanes)]
            box = boxes[-1].at[:, lanes]
            self.rounds.append((wire.copy(mine, box, chip.beside("y")), mine, box))

    def start(self):
        self.rounds[0][0].start()

    def step(self, k):
        copy, mine, box = self.rounds[k]
        copy.wait()
        mine[...] = mine[...] + box[...]
        self.rounds[k + 1][0].start()

    def end(self):
        copy, mine, box = self.rounds[-1]
        copy.wait()
        return mine[...].astype(F32) + box[...].astype(F32)


def norm_of(z):
    centre = z - jnp.mean(z, -1, keepdims=True)
    inverse = lax.rsqrt(jnp.mean(centre * centre, -1, keepdims=True) + EPS)
    return centre * inverse, inverse


def each(count, body):
    def step(i, carry):
        body(i)
        return carry

    lax.fori_loop(0, count, step, 0)


def softmax_fwd(q, k, v):
    scores = dot_nt(q, k)
    raised = jnp.exp(scores - jnp.max(scores, -1, keepdims=True))
    scale = 1.0 / jnp.sum(raised, -1, keepdims=True)
    raised = raised.astype(B16)
    return raised, scale, dot_nn(raised, v) * scale


def dec_kernel(early, *refs):
    (
        vis_ref, lengths, cells_ref, pos_own, pos_far, mask_ref, gain1_ref, gain2_ref,
        qkv_own, qkv_far, out_own, out_far, up_hbm, down_hbm, cot_hbm,
        routed, dvis_out, small_out, *refs,
    ) = refs
    if early:
        pos_out, attn_out, mlp_out, grad_out, *refs = refs
    else:
        pos_out, grad_out, *refs = refs
    (
        dec_out, w_up, w_down, cot, z1, unit1, a_ref, q_ref, keys, values, probs, stats,
        o_ref, unit2, b_ref, h_ref, slope, z2, do_ref, flip, dkt, dvt, got_kv,
        dvis_mine, dvis_near, dvis_far, free_sem, local_sem, send_sem, recv_sem,
    ) = refs
    s, d, m = place_of()
    sibling, facing = (1 - s, d, m), (s, d, 1 - m)
    stays = s == m
    length, wide = z1.shape
    third = wide // 2
    heads = third // HEAD
    wire = Wire(send_sem, recv_sem)
    scale = HEAD**-0.5

    beyond = (1 - s, d, 1 - m)
    greet([sibling, facing, beyond])

    loads = [
        pltpu.make_async_copy(up_hbm, w_up.at[0], local_sem.at[0]),
        pltpu.make_async_copy(down_hbm, w_down.at[0], local_sem.at[1]),
    ]
    pos_loads = [fetch(pos_own, z1, local_sem.at[3]), fetch(pos_far, b_ref, local_sem.at[5])]
    cot_load = pltpu.make_async_copy(cot_hbm.at[m], cot, local_sem.at[2])
    for load in loads:
        load.start()
    over, share = [], []
    for hbm, held in ((up_hbm, w_up), (down_hbm, w_down)):
        half = hbm.shape[0] // 2
        mine = pl.ds(s * half, half)
        over.append(wire.copy(hbm.at[mine], held.at[1, mine], facing))
        share.append(wire.copy(held.at[1, mine], held.at[1, mine], sibling))
        over[-1].start()
    cot_over = wire.copy(cot_hbm.at[1 - m], cot, facing)

    @pl.when(stays)
    def _():
        cot_load.start()
        cot_over.start()

    lane = lax.broadcasted_iota(jnp.int32, (1, 128), 1)

    def keep(plane, rows, column, value):
        stats[plane, rows] = jnp.where(lane == column, value, stats[plane, rows])

    def kept(plane, rows, column):
        return stats[plane, rows][:, column : column + 1]

    for copy in pos_loads:
        copy.wait()
    rows_at = 112
    base = s * length

    used = vis_ref.shape[0]
    slots = lax.broadcasted_iota(jnp.int32, (1, used), 1)
    cells_row = jnp.where(m == 0, cells_ref[0:1, :used], cells_ref[1:2, :used])
    cells_row = jnp.where(slots < lengths[m], cells_row, -1)

    def fill(i):
        rows = pl.ds(pl.multiple_of(i * rows_at, 16), rows_at)
        ids = lax.broadcasted_iota(jnp.int32, (rows_at, 1), 0) + (base + i * rows_at)
        place = jnp.where(cells_row == ids, 1.0, 0.0)
        unseen = 1.0 - jnp.sum(place, -1, keepdims=True)
        pos = jnp.where(stays, z1[rows], b_ref[rows].astype(F32))
        z = dot_nn(place.astype(B16), vis_ref[...]) + unseen * mask_ref[...][None, :] + pos
        unit, inverse = norm_of(z)
        z1[rows] = z
        unit1[rows] = unit.astype(B16)
        keep(0, rows, heads, inverse)
        a_ref[rows] = (unit * gain1_ref[...][None, :]).astype(B16)

    each(length // rows_at, fill)

    a = a_ref[...]
    mine_rows = pl.ds(0, length)
    kv_copies = []
    for side, weight in enumerate((qkv_own, qkv_far)):
        keys[side, mine_rows] = dot_nt(a, weight[1]).astype(B16)
        values[side, mine_rows] = dot_nt(a, weight[2]).astype(B16)
        for held in (keys, values):
            copy = wire.copy(
                held.at[side, mine_rows], held.at[side, pl.ds(length, length)], sibling
            )
            copy.start()
            kv_copies.append(copy)
    for side, weight in enumerate((qkv_own, qkv_far)):
        q_ref[side] = (dot_nt(a, weight[0]).astype(B16).astype(F32) * scale).astype(B16)
    for copy in kv_copies:
        copy.wait()

    masks = head_masks()
    pair = pl.ds(0, 2 * HEAD)
    lone = pl.ds(2 * HEAD, HEAD)

    def attend_side(side):
        for start, size in chunks_of(length, 400):
            rows = pl.ds(start, size)
            halves = []
            for head in range(2):
                q = jnp.where(masks[head], q_ref[side, rows, pair], 0)
                raised, over_sum, o = softmax_fwd(q, keys[side, :, pair], values[side, :, pair])
                probs[side, head, rows] = raised
                keep(side, rows, head, over_sum)
                halves.append(o)
            o_ref[side, rows, pair] = jnp.where(masks[0], halves[0], halves[1]).astype(B16)
            raised, over_sum, o = softmax_fwd(
                q_ref[side, rows, lone], keys[side, :, lone], values[side, :, lone]
            )
            probs[side, 2, rows] = raised
            keep(side, rows, 2, over_sum)
            o_ref[side, rows, lone] = o.astype(B16)

    each(2, attend_side)

    for copy, other in zip(over, share):
        copy.wait()
        other.start()

    z2[...] = z1[...] + dot_nn(o_ref[0], out_own[...]) + dot_nn(o_ref[1], out_far[...])

    def second(i):
        rows = pl.ds(pl.multiple_of(i * rows_at, 16), rows_at)
        unit, inverse = norm_of(z2[rows])
        unit2[rows] = unit.astype(B16)
        keep(1, rows, heads, inverse)
        b_ref[rows] = (unit * gain2_ref[...][None, :]).astype(B16)

    each(length // rows_at, second)
    for load in loads:
        load.wait()
    for copy in share:
        copy.wait()

    step = 256
    steps = w_up.shape[2] // step

    def hidden_at(i):
        return i // steps, pl.ds(pl.multiple_of((i % steps) * step, step), step)

    def up(i):
        side, cols = hidden_at(i)
        u = dot_nn(b_ref[...], w_up[side, :, cols])
        phi = 0.5 + 0.5 * lax.erf(u * 0.5**0.5)
        h_ref[side, :, cols] = (u * phi).astype(B16)
        bell = jnp.exp(u * u * -0.5) * (0.5 / jnp.pi) ** 0.5
        slope[side, :, cols] = (phi + u * bell).astype(B16)

    each(2 * steps, up)

    def cut(value, out):
        out[0] = value[:, :third].astype(B16)
        out[1] = value[:, third:].astype(B16)

    cut(z2[...] + dot_nn(h_ref[0], w_down[0]) + dot_nn(h_ref[1], w_down[1]), dec_out)

    route_local = pltpu.make_async_copy(dec_out.at[s], routed.at[m], local_sem.at[4])
    route_near = wire.copy(dec_out.at[1 - s], routed.at[m], sibling)
    route_over = wire.copy(dec_out.at[s], routed.at[m], facing)
    route_far = wire.copy(dec_out.at[1 - s], routed.at[m], beyond)

    @pl.when(stays)
    def _():
        route_local.start()
        route_near.start()

    @pl.when(jnp.logical_not(stays))
    def _():
        route_over.start()
        route_far.start()

    @pl.when(stays)
    def _():
        cot_load.wait()
        cot_over.wait_send()

    @pl.when(jnp.logical_not(stays))
    def _():
        cot_over.wait_recv()

    def transposed(value):
        return jnp.transpose(value.astype(F32)).astype(B16)

    cot_flip = flip.at[0]
    b_flip = flip.at[1]
    cot_flip[...] = transposed(cot[...])
    b_flip[...] = transposed(b_ref[...])

    def down(i):
        side, cols = hidden_at(i)
        grad_out[side, 2, :, cols] = dot_nn(cot_flip[...], h_ref[side, :, cols]).astype(B16)
        grad_u = dot_nt(cot[...], w_down[side, cols, :]) * slope[side, :, cols].astype(F32)
        grad_u = grad_u.astype(B16)
        slope[side, :, cols] = grad_u
        grad_out[side, 1, :, cols] = dot_nn(b_flip[...], grad_u).astype(B16)

    each(2 * steps, down)
    if early:
        rows = wide // 2
        mine_grads = pl.ds(pl.multiple_of(s * rows, 16), rows)
        away_grads = pl.ds(pl.multiple_of((1 - s) * rows, 16), rows)
        for partner in (sibling, facing):
            pl.semaphore_signal(free_sem, inc=1, device_id=partner, device_id_type=MESH)
        pl.semaphore_wait(free_sem, 2)
        near = {}
        for side, t in ((1, 1), (1, 2), (0, 1), (0, 2)):
            held = h_ref.at[0, pl.ds((side * 2 + t - 1) * rows, rows)]
            near[side, t] = (held, wire.copy(grad_out.at[side, t, away_grads], held, sibling))
            near[side, t][1].start()
    z1[...] = dot_nt(slope[0], w_up[0]) + dot_nt(slope[1], w_up[1])

    def back_norm(grad, unit, inverse, gain):
        scaled = grad * gain
        mean = jnp.mean(scaled, -1, keepdims=True)
        tilt = jnp.mean(scaled * unit, -1, keepdims=True)
        return inverse * (scaled - mean - unit * tilt)

    def add_rows(total, value):
        return total + jnp.sum(value, 0, keepdims=True)

    def second_back(i, total):
        rows = pl.ds(pl.multiple_of(i * rows_at, 16), rows_at)
        grad = z1[rows]
        unit = unit2[rows].astype(F32)
        z = cot[rows].astype(F32) + back_norm(grad, unit, kept(1, rows, heads), gain2_ref[...][None, :])
        z2[rows] = z
        b_ref[rows] = z.astype(B16)
        return add_rows(total, grad * unit)

    zero = jnp.zeros((1, wide), F32)
    gain2_grad = lax.fori_loop(0, length // rows_at, second_back, zero)

    grad_a = b_ref[...]
    flip[0] = transposed(grad_a)
    for side, weight in enumerate((out_own, out_far)):
        grad_out[side, 0, :, pl.ds(3 * third, third)] = dot_nn(flip[0], o_ref[side]).astype(B16)
        do_ref[side] = dot_nt(grad_a, weight[...]).astype(B16)

    if early:
        across = {}
        for t in (1, 2):
            held, copy = near[1, t]
            copy.wait()
            held[...] = (held[...].astype(F32) + grad_out[1, t, mine_grads].astype(F32)).astype(B16)
            got = h_ref.at[1, pl.ds((t - 1) * rows, rows)]
            across[t] = (got, wire.copy(held, got, facing))
            across[t][1].start()

    def attend_back_side(side):
        for index, (start, size) in enumerate(chunks_of(length, 256)):
            rows = pl.ds(start, size)
            for feats, heads in ((pair, (0, 1)), (lone, (2,))):
                q = q_ref[side, rows, feats]
                do = do_ref[side, rows, feats].astype(F32)
                both = do * o_ref[side, rows, feats].astype(F32)
                k = keys[side, :, feats]
                v = values[side, :, feats]
                dq = []
                for head in heads:
                    over_sum = kept(side, rows, head)
                    if len(heads) == 2:
                        lanes = slice(head * HEAD, (head + 1) * HEAD)
                        mine = jnp.where(masks[head], both, 0.0)
                        do_head = jnp.where(masks[head], do, 0.0)
                    else:
                        lanes = slice(0, HEAD)
                        mine, do_head = both, do
                    delta = jnp.sum(mine, -1, keepdims=True) * over_sum
                    do_head = (do_head * over_sum).astype(B16)
                    raised = probs[side, head, rows]
                    ds = (raised.astype(F32) * (dot_nt(do_head, v) - delta)).astype(B16)
                    dq.append(dot_nn(ds, k))
                    dv_part = dot_tn(do_head[:, lanes], raised)
                    dk_part = dot_tn(q[:, lanes], ds)
                    at = pl.ds(head * HEAD, HEAD)
                    if index:
                        dv_part = dv_part + dvt[at]
                        dk_part = dk_part + dkt[at]
                    dvt[at] = dv_part
                    dkt[at] = dk_part
                dq = jnp.where(masks[0], dq[0], dq[1]) if len(heads) == 2 else dq[0]
                q_ref[side, rows, feats] = (dq * scale).astype(B16)
        for held, out in ((dkt, keys), (dvt, values)):
            for feats, at in ((pair, pl.ds(0, 2 * HEAD)), (lone, pl.ds(2 * HEAD, HEAD))):
                out[side, :, feats] = jnp.transpose(held[at]).astype(B16)

    each(2, attend_back_side)
    far_rows = pl.ds(length, length)
    kv_back = [
        [
            wire.copy(held.at[side, far_rows], got_kv.at[slot, side], sibling)
            for side in range(2)
        ]
        for slot, held in enumerate((keys, values))
    ]
    for copies in kv_back:
        for copy in copies:
            copy.start()
    if early:
        def stage(slot, halves, out, sem):
            lanes = pl.ds(0, out.shape[1])
            for owner in range(8):
                a, b = Chip.place(owner // 2)
                rows = pl.ds(48 * (4 * (owner % 2) + 2 * a + b), 48)
                piece = jnp.concatenate([half[24 * owner : 24 * owner + 24] for half in halves], 0)
                piece = jnp.pad(piece, ((0, 0), (0, out.shape[1] - piece.shape[1])))
                probs[0, slot, rows, lanes] = piece.astype(B16)
            return fetch(probs.at[0, slot, pl.ds(0, wide), lanes], out, sem)

        totals = []
        for t in (1, 2):
            held, copy = near[0, t]
            copy.wait()
            across[t][1].wait()
            totals.append(
                held[...].astype(F32)
                + grad_out[0, t, mine_grads].astype(F32)
                + across[t][0][...].astype(F32)
            )
        stores = [stage(2, totals, mlp_out, local_sem.at[1])]

    a_flip = flip.at[0]
    a_flip[...] = transposed(a_ref[...])
    total = None
    for slot in range(3):
        for side, weight in enumerate((qkv_own, qkv_far)):
            if slot:
                kv_back[slot - 1][side].wait()
                own = (keys, values)[slot - 1][side, mine_rows].astype(F32)
                grad = (own + got_kv[slot - 1, side].astype(F32)).astype(B16)
            else:
                grad = q_ref[side]
            grad_out[side, 0, :, pl.ds(slot * third, third)] = dot_nn(a_flip[...], grad).astype(B16)
            part = dot_nn(grad, weight[slot])
            total = part if total is None else total + part
    z1[...] = total
    if early:
        attn_pairs = []
        for side in (1, 0):
            held = h_ref.at[1, pl.ds((2 + side) * rows, rows)]
            copy = wire.copy(grad_out.at[side, 0, away_grads], held, sibling)
            copy.start()
            attn_pairs.append((held, copy))
    @pl.when(stays)
    def _():
        route_local.wait()
        route_near.wait_send()
        route_over.wait_recv()

    @pl.when(jnp.logical_not(stays))
    def _():
        route_over.wait_send()
        route_far.wait_send()
        route_near.wait_recv()
        route_far.wait_recv()

    def first_back(i, totals):
        rows = pl.ds(pl.multiple_of(i * rows_at, 16), rows_at)
        grad = z1[rows]
        unit = unit1[rows].astype(F32)
        z = z2[rows] + back_norm(grad, unit, kept(0, rows, heads), gain1_ref[...][None, :])
        b_ref[rows] = z.astype(B16)
        dec_out[0, rows] = z[:, :third].astype(B16)
        dec_out[1, rows] = z[:, third:].astype(B16)
        ids = lax.broadcasted_iota(jnp.int32, (rows_at, 1), 0) + (base + i * rows_at)
        seen = jnp.sum(jnp.where(cells_row == ids, 1.0, 0.0), -1, keepdims=True)
        return add_rows(totals[0], grad * unit), add_rows(totals[1], (1.0 - seen) * z)

    gain1_grad, mask_grad = lax.fori_loop(0, length // rows_at, first_back, (zero, zero))
    if not early:
        stores = [fetch(dec_out, pos_out, local_sem.at[0])]
    small_out[0:1] = gain1_grad
    small_out[1:2] = gain2_grad
    small_out[2:3] = mask_grad

    ids = (lax.broadcasted_iota(jnp.int32, (used, length), 1) + base).astype(F32)
    cells_col = jnp.transpose(jnp.broadcast_to(cells_row.astype(F32), (8, used)))[:, 0:1]
    place = jnp.where(cells_col == ids, 1.0, 0.0).astype(B16)
    dvis_mine[...] = dot_nn(place, b_ref[...]).astype(B16)
    dvis_pair = wire.copy(dvis_mine, dvis_near, sibling)
    dvis_pair.start()

    if early:
        halves = [jnp.transpose(dec_out[half].astype(F32)) for half in range(2)]
        stores.append(stage(0, halves, pos_out, local_sem.at[0]))
    dvis_pair.wait()
    dvis_mine[...] = (dvis_mine[...].astype(F32) + dvis_near[...].astype(F32)).astype(B16)
    dvis_over = wire.copy(dvis_mine, dvis_far, facing)

    @pl.when(stays)
    def _():
        dvis_over.start()
        dvis_out[...] = dvis_mine[...]

    @pl.when(stays)
    def _():
        dvis_over.wait_send()

    @pl.when(jnp.logical_not(stays))
    def _():
        dvis_over.wait_recv()
        dvis_out[...] = dvis_far[...]

    if early:
        halves = []
        for side, (held, copy) in zip((1, 0), attn_pairs):
            copy.wait()
            halves.insert(0, held[...].astype(F32) + grad_out[side, 0, mine_grads].astype(F32))
        stores.append(stage(1, halves, attn_out, local_sem.at[2]))

    for copy in stores:
        copy.wait()


def decoder(early, vis, lengths, cells, pos_own, pos_far, mask, gains, weights, cot, ident):
    qkv_own, qkv_far, out_own, out_far, up, down = weights
    length, wide = pos_own.shape
    used = vis.shape[0]
    third = wide // 2
    hidden = up.shape[1]
    keys = 2 * length
    heads = third // HEAD
    assert heads == 3 and length % 112 == 0
    whole = pl.BlockSpec(memory_space=VMEM)
    there = pl.BlockSpec(memory_space=pl.ANY)
    grads = (2, 3, wide, hidden)
    outs = [
        (jax.ShapeDtypeStruct((2, length, third), B16), there),
        (jax.ShapeDtypeStruct((used, wide), B16), whole),
        (jax.ShapeDtypeStruct((8, wide), F32), whole),
    ]
    if early:
        lanes = -(-length // 128) * 128
        outs += [
            (jax.ShapeDtypeStruct((wide, lanes), B16), there),
            (jax.ShapeDtypeStruct((wide, hidden), B16), there),
            (jax.ShapeDtypeStruct((wide, hidden), B16), there),
        ]
    else:
        outs += [
            (jax.ShapeDtypeStruct((2, length, third), B16), there),
            (jax.ShapeDtypeStruct(grads, B16), whole),
        ]
    return pl.pallas_call(
        functools.partial(dec_kernel, early),
        out_shape=[item for item, _ in outs],
        in_specs=[whole, pl.BlockSpec(memory_space=pltpu.SMEM), whole]
        + [there] * 2
        + [whole] * 7
        + [there] * 3,
        out_specs=[spec for _, spec in outs],
        scratch_shapes=[VMEM(grads, B16)] * early
        + [
            VMEM((2, length, third), B16),
            VMEM((2, wide, hidden), B16),
            VMEM((2, hidden, wide), B16),
            VMEM((length, wide), B16),
            VMEM((length, wide), F32),
            VMEM((length, wide), B16),
            VMEM((length, wide), B16),
            VMEM((2, length, third), B16),
            VMEM((2, keys, third), B16),
            VMEM((2, keys, third), B16),
            VMEM((2, heads, length, keys), B16),
            VMEM((2, length, 128), F32),
            VMEM((2, length, third), B16),
            VMEM((length, wide), B16),
            VMEM((length, wide), B16),
            VMEM((2, length, hidden), B16),
            VMEM((2, length, hidden), B16),
            VMEM((length, wide), F32),
            VMEM((2, length, third), B16),
            VMEM((2, wide, length), B16),
            VMEM((third, keys), F32),
            VMEM((third, keys), F32),
            VMEM((2, 2, length, third), B16),
            VMEM((used, wide), B16),
            VMEM((used, wide), B16),
            VMEM((used, wide), B16),
            pltpu.SemaphoreType.REGULAR,
            pltpu.SemaphoreType.DMA((6,)),
            pltpu.SemaphoreType.DMA((32,)),
            pltpu.SemaphoreType.DMA((32,)),
        ],
        compiler_params=pltpu.CompilerParams(
            collective_id=ident, has_side_effects=True, vmem_limit_bytes=int(63.9 * 1024) * 1024
        ),
        name="decoder",
    )(
        vis,
        lengths,
        cells,
        pos_own,
        pos_far,
        mask,
        gains[0],
        gains[1],
        qkv_own,
        qkv_far,
        out_own,
        out_far,
        up,
        down,
        cot,
    )


def pack(grad, owners):
    rows, cols = grad.shape
    own = rows // owners
    fold = 1
    while own * fold % 16:
        fold *= 2
    grad = grad.astype(B16).reshape(owners, own, fold, cols // fold)
    return jnp.swapaxes(grad, 1, 2).reshape(owners, fold * own, cols // fold)


def unpack(piece, own):
    fold = piece.shape[0] // own
    return jnp.swapaxes(piece.reshape(fold, own, -1), 0, 1).reshape(own, -1)


def pick(pair, index):
    return lax.dynamic_index_in_dim(pair, index, 0, keepdims=False)


def enc_kernel(*refs):
    (
        length_ref, tok_hbm, qkv_hbm, out_hbm, up_hbm, down_hbm, bridge_ref, gain1_ref, gain2_ref,
        pos_hbm, dqkv_hbm, dout_hbm,
        vis_out, dqkv_far, dout_far, pos_far, unit1, unit2, stats, a_ref, triple, probs, o_ref, b_ref,
        slope, h_ref, enc_half,
        x_ref, qkv, w_out, w_up, w_down, z2, part_ref, part_far, enc_ref, pos_full, pos_half,
        local_sem, send_sem, recv_sem,
    ) = refs
    s, d, m = place_of()
    sibling, facing = (1 - s, d, m), (s, d, 1 - m)
    stays = s == m
    used, wide = x_ref.shape
    half = tok_hbm.shape[1]
    rest = used - half
    wire = Wire(send_sem, recv_sem)

    greet([sibling, facing])
    first, last = pl.ds(0, half), pl.ds(half, rest)
    tok_first = wire.copy(tok_hbm.at[s], x_ref.at[first], facing)
    tok_last = wire.copy(tok_hbm.at[s, pl.ds(0, rest)], x_ref.at[last], facing)
    own_first = pltpu.make_async_copy(tok_hbm.at[s], x_ref.at[first], local_sem.at[0])
    own_last = pltpu.make_async_copy(
        tok_hbm.at[s, pl.ds(0, rest)], x_ref.at[last], local_sem.at[0]
    )

    @pl.when(m == 0)
    def _():
        tok_first.start()
        own_first.start()

    @pl.when(m == 1)
    def _():
        tok_last.start()
        own_last.start()

    loads = [
        fetch(hbm, held, local_sem.at[i + 1])
        for i, (hbm, held) in enumerate(
            ((qkv_hbm, qkv), (out_hbm, w_out), (up_hbm, w_up), (down_hbm, w_down))
        )
    ]
    pos_load = fetch(pos_hbm, pos_full, local_sem.at[5])
    over, share = [], []
    for hbm, held in ((dqkv_hbm, dqkv_far), (dout_hbm, dout_far)):
        at = (slice(None),) * (len(hbm.shape) - 2)
        size = hbm.shape[-2] // 2
        mine = at + (pl.ds(s * size, size),)
        over.append(wire.copy(hbm.at[mine], held.at[mine], facing))
        share.append(wire.copy(held.at[mine], held.at[mine], sibling))

    @pl.when(m == 0)
    def _():
        own_first.wait()
        tok_first.wait_send()
        tok_last.wait_recv()

    @pl.when(m == 1)
    def _():
        own_last.wait()
        tok_last.wait_send()
        tok_first.wait_recv()

    for copy in over:
        copy.start()

    lane = lax.broadcasted_iota(jnp.int32, (1, 128), 1)

    unit, inverse = norm_of(x_ref[...].astype(F32))
    unit1[...] = unit
    stats[...] = jnp.where(lane == 0, inverse, 0.0)
    a = (unit * gain1_ref[...][None, :]).astype(B16)
    a_ref[...] = a
    loads[0].wait()
    for slot in range(3):
        triple[slot] = dot_nn(a, qkv[slot]).astype(B16)

    valid = lax.broadcasted_iota(jnp.int32, (1, used), 1) < length_ref[s]
    masks = head_masks()
    for pair in range(triple.shape[2] // (2 * HEAD)):
        feats = pl.ds(pair * 2 * HEAD, 2 * HEAD)
        q, k, v = (triple[slot, :, feats] for slot in range(3))
        halves = []
        for head in range(2):
            scores = dot_nt(jnp.where(masks[head], q, 0), k) * HEAD**-0.5
            scores = jnp.where(valid, scores, NEG)
            raised = jnp.exp(scores - jnp.max(scores, -1, keepdims=True))
            p = (raised / jnp.sum(raised, -1, keepdims=True)).astype(B16)
            probs[2 * pair + head] = p
            halves.append(dot_nn(p, v))
        o_ref[:, feats] = jnp.where(masks[0], halves[0], halves[1]).astype(B16)

    loads[1].wait()
    part = dot_nn(o_ref[...], w_out[...])
    part_ref[0] = part.astype(B16)
    attn = wire.copy(part_ref.at[0], part_far.at[0], facing)
    attn.start()
    z2[...] = x_ref[...].astype(F32) + part

    pos_load.wait()
    pos_over = wire.copy(pos_half, pos_far, facing)

    @pl.when(stays)
    def _():
        pos_half[...] = pos_full[...].astype(B16)
        pos_over.start()

    attn.wait()
    z = z2[...] + part_far[0].astype(F32)
    z2[...] = z
    unit, inverse = norm_of(z)
    unit2[...] = unit
    stats[...] = jnp.where(lane == 1, inverse, stats[...])
    b = (unit * gain2_ref[...][None, :]).astype(B16)
    b_ref[...] = b
    loads[2].wait()
    step = 512

    def up(i):
        cols = pl.ds(pl.multiple_of(i * step, step), step)
        u = dot_nn(b_ref[...], w_up[:, cols])
        phi = 0.5 + 0.5 * lax.erf(u * 0.5**0.5)
        h_ref[:, cols] = (u * phi).astype(B16)
        bell = jnp.exp(u * u * -0.5) * (0.5 / jnp.pi) ** 0.5
        slope[:, cols] = (phi + u * bell).astype(B16)

    each(w_up.shape[1] // step, up)
    loads[3].wait()
    part = dot_nn(h_ref[...], w_down[...])
    z2[...] = z2[...] + part
    part_ref[1] = part.astype(B16)
    mlp = wire.copy(part_ref.at[1], part_far.at[1], facing)
    vis_near = wire.copy(vis_out, vis_out, sibling)
    mid = wide // 2
    enc_over = wire.copy(
        enc_ref.at[:, pl.ds(pl.multiple_of((1 - m) * mid, 128), mid)], enc_half, facing
    )

    @pl.when(stays)
    def _():
        mlp.wait_recv()
        enc = (z2[...] + part_far[1].astype(F32)).astype(B16)
        enc_ref[...] = enc
        enc_over.start()
        vis_out[...] = dot_nn(enc, bridge_ref[...]).astype(B16)
        vis_near.start()
        enc_half[...] = enc_ref[:, pl.ds(pl.multiple_of(m * mid, 128), mid)]

    @pl.when(jnp.logical_not(stays))
    def _():
        mlp.start()

    for copy, other in zip(over, share):
        copy.wait()
        other.start()

    @pl.when(stays)
    def _():
        vis_near.wait_send()
        enc_over.wait_send()
        pos_over.wait_send()

    @pl.when(jnp.logical_not(stays))
    def _():
        mlp.wait_send()
        vis_near.wait_recv()
        enc_over.wait_recv()
        pos_over.wait_recv()

    for copy in share:
        copy.wait()


def encoder(lengths, tokens, weights, bridge, gains, pos, dqkv, dout, used, ident):
    qkv, out, up, down = weights
    wide = tokens.shape[2]
    feats = qkv.shape[2]
    hidden = up.shape[1]
    whole = pl.BlockSpec(memory_space=VMEM)
    there = pl.BlockSpec(memory_space=pl.ANY)
    shape = jax.ShapeDtypeStruct
    outs = [
        (shape((used, dout.shape[1]), B16), whole),
        (shape(dqkv.shape, B16), there),
        (shape(dout.shape, B16), there),
        (shape(pos.shape, B16), there),
        (shape((used, wide), F32), whole),
        (shape((used, wide), F32), whole),
        (shape((used, 128), F32), whole),
        (shape((used, wide), B16), whole),
        (shape((3, used, feats), B16), whole),
        (shape((feats // HEAD, used, used), B16), whole),
        (shape((used, feats), B16), whole),
        (shape((used, wide), B16), whole),
        (shape((used, hidden), B16), whole),
        (shape((used, hidden), B16), whole),
        (shape((used, wide // 2), B16), whole),
    ]
    return pl.pallas_call(
        enc_kernel,
        out_shape=[item for item, _ in outs],
        in_specs=[pl.BlockSpec(memory_space=pltpu.SMEM)]
        + [there] * 5
        + [whole] * 3
        + [there] * 3,
        out_specs=[spec for _, spec in outs],
        scratch_shapes=[
            VMEM((used, wide), B16),
            VMEM(qkv.shape, B16),
            VMEM(out.shape, B16),
            VMEM(up.shape, B16),
            VMEM(down.shape, B16),
            VMEM((used, wide), F32),
            VMEM((2, used, wide), B16),
            VMEM((2, used, wide), B16),
            VMEM((used, wide), B16),
            VMEM(pos.shape, F32),
            VMEM(pos.shape, B16),
            pltpu.SemaphoreType.DMA((6,)),
            pltpu.SemaphoreType.DMA((16,)),
            pltpu.SemaphoreType.DMA((16,)),
        ],
        compiler_params=remote_params(ident),
        name="encoder",
    )(
        lengths, tokens, qkv, out, up, down, bridge, gains[0], gains[1],
        pos, dqkv, dout,
    )


def back_kernel(cube, *refs):
    (
        dvis_ref, bridge_ref, gain1_ref, gain2_ref, unit1, unit2, stats, a_ref, triple, probs, o_ref,
        b_ref, slope, h_ref, enc_half, small_dec, qkv_hbm, out_hbm, up_hbm, down_hbm, *refs,
    ) = refs
    if cube:
        (
            pos_hbm, attn_hbm, mlp_hbm,
            tok_out, small_out, enc_out, mlp_out, attn_out, pos_out, bridge_all,
            near, held, box0, box1, box2,
            dec_held, dec_box0, dec_box1, dec_box2, side_held, side_box0, side_box1, side_box2,
            pos_sum, pos_got, attn_sum, attn_got, bridge_near, small_box, grads, bridge_grad, *refs,
        ) = refs
    else:
        tok_out, small_out, grads, bridge_grad, *refs = refs
    (
        qkv, w_out, w_up, w_down, gu, dy, part, part_far, dz, da_ref, do_ref, dqkv, flip, tok_part,
        local_sem, send_sem, recv_sem,
    ) = refs
    s, d, m = place_of()
    sibling, facing = (1 - s, d, m), (s, d, 1 - m)
    stays = s == m
    used, wide = unit1.shape
    feats = o_ref.shape[1]
    hidden = h_ref.shape[1]
    half = tok_part.shape[1]
    rest = used - half
    wire = Wire(send_sem, recv_sem)
    section = wide // 2

    if cube:
        chip = Chip(s, d, m)
        z, y = chip.z, chip.me["y"]
        others = [(s, 2 * lax.rem(z + k, 4) + y, lax.rem(m + side, 2)) for k in (1, 2, 3) for side in (0, 1)]
        greet([sibling, facing, (1 - s, d, 1 - m), chip.near[0]] + others)
    else:
        greet([sibling, facing])

    loads = [
        fetch(hbm, held, local_sem.at[i])
        for i, (hbm, held) in enumerate(
            ((down_hbm, w_down), (up_hbm, w_up), (out_hbm, w_out), (qkv_hbm, qkv))
        )
    ]

    if cube:
        cells = pos_sum.shape[2]
        pos_lanes = pos_hbm.shape[-1]
        span = attn_hbm.shape[-1]
        blank = (slice(None),) * 4
        early_loads = [
            fetch(hbm, dec_held.at[blank + (pl.ds(first, hbm.shape[-1]),)], local_sem.at[4 + i])
            for i, (hbm, first) in enumerate(
                ((pos_hbm, 0), (attn_hbm, pos_lanes), (mlp_hbm, pos_lanes + span))
            )
        ]
        for copy in early_loads:
            copy.wait()
        orders = ("yab", "ayb", "yab")
        tiles = (pos_lanes + 2 * span) // 128
        cuts = [128 * (tiles * i // 3) for i in range(4)]
        early_folds = [
            Fold(
                wire, chip, dec_held, (dec_box0, dec_box1, dec_box2), pl.ds(low, high - low), "yab",
                order, False,
            )
            for low, high, order in zip(cuts, cuts[1:], orders)
        ]
        for fold in early_folds:
            fold.start()

    def transposed(value):
        return jnp.transpose(value.astype(F32)).astype(B16)

    dvis = dvis_ref[...]
    grad = dot_nt(dvis, bridge_ref[...])
    dy[...] = grad
    dm = grad.astype(B16)
    da_ref[...] = dm
    flip[0] = transposed(dm)
    flip[1] = transposed(b_ref[...])
    bridge_grad[...] = dot_tn(enc_half[...], dvis).astype(B16)
    if cube:
        bridge_rows = bridge_near.shape[0]
        bridge_pair = wire.copy(
            bridge_grad.at[pl.ds(pl.multiple_of((1 - s) * bridge_rows, 16), bridge_rows)],
            bridge_near,
            sibling,
        )
        bridge_pair.start()

    loads[0].wait()
    step = 512
    first_mlp = 4 * feats
    steps = hidden // step
    if cube:
        away_rows = pl.ds(pl.multiple_of((1 - s) * section, 16), section)

        class Group:
            def __init__(self, first, size, order):
                self.lanes = pl.ds(first, size)
                self.pair = wire.copy(
                    grads.at[away_rows, self.lanes], near.at[:, self.lanes], sibling
                )
                self.pair.start()
                self.order = order

            def start(self):
                self.pair.wait()
                for owner in range(8):
                    rows = pl.ds(48 * owner, 48)
                    from_rows = pl.ds(pl.multiple_of(s * section + 48 * owner, 16), 48)
                    index = (owner % 2,) + Chip.place(owner // 2) + (slice(None), self.lanes)
                    held[index] = near[rows, self.lanes] + grads[from_rows, self.lanes]
                self.fold = Fold(
                    wire, chip, held, (box0, box1, box2), self.lanes, "yab", self.order, False
                )
                self.fold.start()

            def end(self):
                enc_out[:, self.lanes] = self.fold.end()

        mlp_groups = []

    for i in range(steps):
        cols = pl.ds(i * step, step)
        grads[:, pl.ds(first_mlp + 2 * i * step, step)] = dot_nn(flip[0], h_ref[:, cols]).astype(B16)
        grad_u = dot_nt(da_ref[...], w_down[cols, :]) * slope[:, cols].astype(F32)
        grad_u = grad_u.astype(B16)
        gu[:, cols] = grad_u
        grads[:, pl.ds(first_mlp + (2 * i + 1) * step, step)] = dot_nn(flip[1], grad_u).astype(B16)
        if cube:
            mlp_groups.append(Group(first_mlp + 2 * i * step, 2 * step, orders[i % 3]))
            if i:
                mlp_groups[i - 1].start()

    loads[1].wait()
    grad = dot_nt(gu[...], w_up[...])
    part[...] = grad.astype(B16)
    over = wire.copy(part, part_far.at[0], facing)
    over.start()
    dz[...] = grad
    gain2_grad = jnp.sum(grad * unit2[...], 0, keepdims=True)

    if cube:
        mlp_groups[-1].start()

    def back_norm(grad, unit, inverse, gain):
        scaled = grad * gain
        mean = jnp.mean(scaled, -1, keepdims=True)
        tilt = jnp.mean(scaled * unit, -1, keepdims=True)
        return inverse * (scaled - mean - unit * tilt)

    over.wait()
    whole = dz[...] + part_far[0].astype(F32)
    dz2 = dy[...] + back_norm(whole, unit2[...], stats[:, 1:2], gain2_ref[...][None, :])
    dy[...] = dz2
    grad_a = dz2.astype(B16)
    da_ref[...] = grad_a
    flip[0] = transposed(grad_a)
    loads[2].wait()
    grads[:, pl.ds(3 * feats, feats)] = dot_nn(flip[0], o_ref[...]).astype(B16)
    do_ref[...] = dot_nt(grad_a, w_out[...]).astype(B16)

    if cube:
        out_group = Group(3 * feats, feats, orders[0])
        bridge_pair.wait()
        narrow = bridge_near.shape[1]
        for at in range(4):
            side_held[Chip.place(at)] = (
                bridge_near[pl.ds(48 * at, 48)]
                + bridge_grad[pl.ds(pl.multiple_of(s * bridge_rows + 48 * at, 16), 48)]
            )
        bridge_fold = Fold(
            wire, chip, side_held, (side_box0, side_box1, side_box2), pl.ds(0, narrow), "ab", "ab", True
        )
        bridge_fold.start()

    masks = head_masks()
    scale = HEAD**-0.5
    for pair in range(feats // (2 * HEAD)):
        at = pl.ds(pair * 2 * HEAD, 2 * HEAD)
        q, k, v = (triple[slot, :, at] for slot in range(3))
        do = do_ref[:, at]
        both = do.astype(F32) * o_ref[:, at].astype(F32)
        parts = []
        for head in range(2):
            delta = jnp.sum(jnp.where(masks[head], both, 0.0), -1, keepdims=True)
            do_head = jnp.where(masks[head], do, 0)
            p = probs[2 * pair + head]
            ds = (p.astype(F32) * (dot_nt(do_head, v) - delta)).astype(B16)
            parts.append((dot_nn(ds, k) * scale, dot_tn(ds, q) * scale, dot_tn(p, do)))
        for slot in range(3):
            dqkv[slot, :, at] = jnp.where(masks[0], parts[0][slot], parts[1][slot]).astype(B16)

    if cube:
        out_group.start()
        for fold in early_folds:
            fold.step(0)
        bridge_fold.step(0)

    flip[1] = transposed(a_ref[...])
    loads[3].wait()
    total = None
    for slot in range(3):
        grads[:, pl.ds(slot * feats, feats)] = dot_nn(flip[1], dqkv[slot]).astype(B16)
        term = dot_nt(dqkv[slot], qkv[slot])
        total = term if total is None else total + term
    part[...] = total.astype(B16)
    dz[...] = total
    gain1_grad = jnp.sum(total * unit1[...], 0, keepdims=True)
    first, last = pl.ds(0, half), pl.ds(half, rest)
    over_first = wire.copy(part.at[first], part_far.at[1, first], facing)
    over_last = wire.copy(part.at[last], part_far.at[1, last], facing)

    @pl.when(m == 0)
    def _():
        over_last.start()

    @pl.when(m == 1)
    def _():
        over_first.start()

    small_out[...] = jnp.zeros(small_out.shape, F32)
    row = 0
    for value in (
        gain1_grad, gain2_grad, small_dec[0:1], small_dec[1:2], small_dec[2:3],
    ):
        for i in range(value.shape[1] // 128):
            small_out[row : row + 1] = value[:, i * 128 : (i + 1) * 128]
            row += 1

    if cube:
        attn_groups = [
            Group(i * feats, feats, order) for i, order in enumerate(orders)
        ]
        small_copies = [
            wire.copy(small_out, small_box.at[i], partner)
            for i, partner in enumerate([sibling, facing] + chip.near)
        ]

        def small_step(i):
            small_copies[i].wait()
            small_out[...] = small_out[...] + small_box[i]
            if i + 1 < len(small_copies):
                small_copies[i + 1].start()

        small_copies[0].start()
        for group in attn_groups:
            group.start()
        bridge_fold.step(1)
        small_step(0)

    def finish(rows, size):
        whole = dz[rows] + part_far[1, rows].astype(F32)
        unit = unit1[rows]
        grad = dy[rows] + back_norm(whole, unit, stats[rows][:, 0:1], gain1_ref[...][None, :])
        for side in range(2):
            tok_part[side, pl.ds(0, size)] = grad[:, side * section : (side + 1) * section]

    @pl.when(m == 0)
    def _():
        over_last.wait_send()
        over_first.wait_recv()
        finish(first, half)

    @pl.when(m == 1)
    def _():
        over_first.wait_send()
        over_last.wait_recv()
        tok_part[...] = jnp.zeros(tok_part.shape, F32)
        finish(last, rest)

    tok_pair = wire.copy(tok_part.at[1 - s], tok_out.at[s], sibling)
    tok_pair.start()
    tok_out[s] = tok_part[s]

    if cube:
        for group in mlp_groups:
            group.fold.step(0)
        for fold in early_folds:
            fold.step(1)
        small_step(1)

        slot = (s * 4 + z) * 2 + m
        bridge_all[slot] = bridge_fold.end().astype(B16)
        spread = [
            wire.copy(bridge_all.at[slot], bridge_all.at[slot], partner)
            for partner in [facing] + others
        ]
        for copy in spread:
            copy.start()

        out_group.fold.step(0)
        for group in attn_groups:
            group.fold.step(0)
        small_step(2)
        for group in mlp_groups:
            group.fold.step(1)

        wholes = jnp.concatenate([fold.end() for fold in early_folds], 1)
        for half_at in range(2):
            piece = wholes[24 * half_at : 24 * half_at + 24]
            pos_sum[half_at] = piece[:, :cells]
            attn_sum[half_at] = piece[:, pos_lanes : pos_lanes + span]
            mlp_out[:, pl.ds(half_at * span, span)] = piece[:, pos_lanes + span :]
        attn_over = wire.copy(attn_sum.at[1], attn_got, facing)
        attn_over.start()
        route_near = wire.copy(pos_sum.at[1 - s], pos_got.at[m], sibling)
        route_over = wire.copy(pos_sum.at[s], pos_got.at[m], facing)
        route_far = wire.copy(pos_sum.at[1 - s], pos_got.at[m], (1 - s, d, 1 - m))

        @pl.when(stays)
        def _():
            route_near.start()
            pos_got[m] = pos_sum[s]

        @pl.when(jnp.logical_not(stays))
        def _():
            route_over.start()
            route_far.start()


        out_group.fold.step(1)
        for copy in spread:
            copy.wait()
        ours = pl.ds(s * 8, 8)
        bridge_pair_all = wire.copy(bridge_all.at[ours], bridge_all.at[ours], sibling)
        bridge_pair_all.start()
        for group in attn_groups:
            group.fold.step(1)
        small_step(3)
        for group in mlp_groups:
            group.end()
        attn_over.wait()
        attn_out[...] = attn_sum[0] + attn_got[...]

        @pl.when(stays)
        def _():
            route_near.wait_send()
            route_over.wait_recv()

        @pl.when(jnp.logical_not(stays))
        def _():
            route_over.wait_send()
            route_far.wait_send()
            route_near.wait_recv()
            route_far.wait_recv()

        pos_out[...] = pos_got[0] + pos_got[1]
        out_group.end()
        small_step(4)
        for group in attn_groups:
            group.end()
        bridge_pair_all.wait()

    tok_pair.wait()


def back(cube, dvis, bridge, gains, saved, small_dec, weights, dec_grads, cells, half, ident):
    unit1, unit2, stats, a, triple, probs, o, b, slope, h, enc_half = saved
    qkv, out, up, down = weights
    used, wide = unit1.shape
    feats, hidden = o.shape[1], h.shape[1]
    cols = 4 * feats + 2 * hidden
    narrow = bridge.shape[1]
    whole = pl.BlockSpec(memory_space=VMEM)
    there = pl.BlockSpec(memory_space=pl.ANY)
    shape = jax.ShapeDtypeStruct
    args = [dvis, bridge, gains[0], gains[1], *saved, small_dec, qkv, out, up, down]
    in_specs = [whole] * 16 + [there] * 4
    outs = [shape((2, half, wide // 2), F32), shape((24, 128), F32)]
    assert 2 * wide + 3 * narrow <= 24 * 128
    grads, bridge_grad = (wide, cols), (wide // 2, narrow)
    scratch = []
    if cube:
        pos, attn, mlp = dec_grads
        span = attn.shape[1]
        args += [
            pos.reshape(2, 2, 2, 48, -1), attn.reshape(2, 2, 2, 48, -1), mlp.reshape(2, 2, 2, 48, -1)
        ]
        in_specs += [there] * 3
        outs += [
            shape((48, cols), F32),
            shape((24, 2 * span), F32),
            shape((24, span), F32),
            shape((24, cells), F32),
            shape((16, 48, narrow), B16),
        ]

        def folded(axes, size):
            return [VMEM((2,) * (axes - k) + (48, size), B16) for k in range(axes + 1)]

        scratch = [
            VMEM((wide // 2, cols), B16),
            *folded(3, cols),
            *folded(3, pos.shape[1] + 2 * span),
            *folded(2, narrow),
            VMEM((48, narrow), B16),
            VMEM((2, 24, cells), F32),
            VMEM((2, 24, cells), F32),
            VMEM((2, 24, span), F32),
            VMEM((24, span), F32),
            VMEM((narrow // 2, narrow), B16),
            VMEM((5, 24, 128), F32),
            VMEM(grads, B16),
            VMEM(bridge_grad, B16),
        ]
    else:
        outs += [shape(grads, B16), shape(bridge_grad, B16)]
    scratch += [
        VMEM(qkv.shape, B16),
        VMEM(out.shape, B16),
        VMEM(up.shape, B16),
        VMEM(down.shape, B16),
        VMEM((used, hidden), B16),
        VMEM((used, wide), F32),
        VMEM((used, wide), B16),
        VMEM((2, used, wide), B16),
        VMEM((used, wide), F32),
        VMEM((used, wide), B16),
        VMEM((used, feats), B16),
        VMEM((3, used, feats), B16),
        VMEM((2, wide, used), B16),
        VMEM((2, half, wide // 2), F32),
        pltpu.SemaphoreType.DMA((14,)),
        pltpu.SemaphoreType.DMA((80,)),
        pltpu.SemaphoreType.DMA((80,)),
    ]
    return pl.pallas_call(
        functools.partial(back_kernel, cube),
        out_shape=outs,
        in_specs=in_specs,
        out_specs=[whole] * len(outs),
        scratch_shapes=scratch,
        compiler_params=remote_params(ident),
        name="encoder_back",
    )(*args)


def finish_kernel(step, *refs):
    decoded, tokens, small, enc, mlp, attn, pos, bridge = refs[:8]
    (
        decoded_out, tokens_out, e_qkv, e_out, e_up, e_down, one_e, two_e, bridge_out, mask_out,
        pos_out, d_qkv, d_out, d_up, d_down, one_d, two_d,
    ) = refs[8:]
    for i in range(2):
        decoded_out[i] = jnp.transpose(decoded[i].astype(F32))
    tokens_out[...] = tokens[...]
    for source, qkv, out in ((enc, e_qkv, e_out), (attn, d_qkv, d_out)):
        cols = qkv.shape[2]
        for slot in range(3):
            qkv[slot] = source[:, pl.ds(slot * cols, cols)]
        out[...] = source[:, pl.ds(3 * cols, cols)]
    first = 4 * e_qkv.shape[2]
    for i in range(e_up.shape[1] // step):
        at = pl.ds(i * step, step)
        e_down[:, at] = enc[:, pl.ds(first + 2 * i * step, step)]
        e_up[:, at] = enc[:, pl.ds(first + (2 * i + 1) * step, step)]
    hidden = d_up.shape[1]
    d_up[...] = mlp[:, :hidden]
    d_down[...] = mlp[:, hidden:]
    pos_out[...] = pos[...]
    pieces = bridge.shape[0] // 2
    for side in range(2):
        for piece in range(pieces):
            rows = pl.ds((side * pieces + piece) * bridge.shape[1], bridge.shape[1])
            bridge_out[rows] = bridge[2 * piece + side].astype(F32)
    row = 0
    for out in (one_e, two_e, one_d, two_d, mask_out):
        for i in range(out.shape[0] // 128):
            out[pl.ds(i * 128, 128)] = small[row]
            row += 1


def finish(shapes, parts, step):
    whole = pl.BlockSpec(memory_space=VMEM)
    return pl.pallas_call(
        functools.partial(finish_kernel, step),
        out_shape=[jax.ShapeDtypeStruct(shape, F32) for shape in shapes],
        in_specs=[whole] * len(parts),
        out_specs=[whole] * len(shapes),
        compiler_params=pltpu.CompilerParams(vmem_limit_bytes=LIMIT),
        name="finish",
    )(*parts)


def per_device(
    tokens,
    clip_lengths,
    clip_cells,
    enc_qkv,
    enc_attn_out,
    enc_up,
    enc_down,
    enc_gain_one,
    enc_gain_two,
    bridge_weight,
    mask_token,
    position_embed,
    dec_qkv,
    dec_attn_out,
    dec_up,
    dec_down,
    dec_gain_one,
    dec_gain_two,
    cotangent,
):
    s, d, m = place_of()
    n = lax.axis_size("dp")
    owners = 2 * n
    cube = n == 8
    dec_wide = position_embed.shape[1]
    half_slots, enc_wide = tokens.shape[2:]
    used = -(-LONGEST // 32) * 32

    e_weights = (jnp.swapaxes(enc_qkv, 0, 1), enc_attn_out, enc_up, enc_down)
    d_qkv = jnp.transpose(dec_qkv, (1, 2, 0))
    vis, d_qkv_far, d_out_far, pos_far, *saved = encoder(
        clip_lengths[:, 0],
        tokens[:, 0],
        e_weights,
        bridge_weight,
        (enc_gain_one, enc_gain_two),
        position_embed,
        d_qkv,
        dec_attn_out,
        used,
        1,
    )
    decoded, dvis, dec_small, *dec_grads = decoder(
        cube,
        vis,
        clip_lengths[:, 0],
        clip_cells[:, 0],
        position_embed,
        pos_far,
        mask_token,
        (dec_gain_one, dec_gain_two),
        (d_qkv, d_qkv_far, dec_attn_out, d_out_far, dec_up, dec_down),
        cotangent[:, 0],
        2,
    )
    tokens_grad, small, *rest = back(
        cube,
        dvis,
        bridge_weight,
        (enc_gain_one, enc_gain_two),
        saved,
        dec_small,
        e_weights,
        dec_grads,
        position_embed.shape[0],
        half_slots,
        3,
    )
    if cube:
        e_own, d_own = enc_wide // owners, dec_wide // owners
        shapes = [
            (2, decoded.shape[2], decoded.shape[1]),
            tokens_grad.shape,
            (3, e_own, enc_qkv.shape[2]),
            (e_own, enc_attn_out.shape[0]),
            (e_own, enc_up.shape[1]),
            (e_own, enc_down.shape[0]),
            (enc_wide,),
            (enc_wide,),
            (enc_wide, dec_wide),
            (dec_wide,),
            (d_own, position_embed.shape[0]),
            (3, d_own, dec_qkv.shape[2]),
            (d_own, dec_attn_out.shape[0]),
            (d_own, dec_up.shape[1]),
            (d_own, dec_down.shape[0]),
            (dec_wide,),
            (dec_wide,),
        ]
        outs = list(finish(shapes, (decoded, tokens_grad, small, *rest), 512))
        outs[0] = jnp.swapaxes(outs[0], 1, 2)[:, None]
        outs[1] = outs[1][:, None]
        for i in (2, 11):
            outs[i] = jnp.swapaxes(outs[i], 0, 1)
        for i in (3, 5, 10, 12, 14):
            outs[i] = outs[i].T
        return tuple(outs)
    else:
        grads, bridge = rest
        pos_parts, dec_grads = dec_grads
        enc_final = unpack(scatter(pack(grads, owners)[None], 11), enc_wide // owners)
        packed = [
            pack(jnp.concatenate([dec_grads[side, t] for t in range(3)], 1), owners)
            for side in range(2)
        ]
        dec_final = unpack(scatter(jnp.stack(packed), 12), dec_wide // owners)
        parts = route(pos_parts, 13).astype(F32)
        packed = pack(jnp.transpose(parts[0] + parts[1]), n)
        zero = jnp.zeros_like(packed)
        packed = jnp.concatenate(
            [jnp.where(s == 0, packed, zero), jnp.where(s == 1, packed, zero)], 0
        )
        pos_final = unpack(scatter(packed[None], 14), dec_wide // owners)
        bridge_own = enc_wide // 2 // owners
        per = -(-small.size // owners)
        small = jnp.pad(small.reshape(-1), (0, per * owners - small.size)).reshape(owners, 1, per)
        rows = -(-(bridge_own + 1) // 16) * 16
        rep = jnp.concatenate(
            [
                bridge.astype(F32).reshape(owners, bridge_own, dec_wide),
                jnp.pad(small, ((0, 0), (0, 0), (0, dec_wide - per))),
                jnp.zeros((owners, rows - bridge_own - 1, dec_wide), F32),
            ],
            1,
        ).astype(B16)
        rep = scatter(rep[None], 15).astype(B16)
        everyone = gather(rep, n, 16).reshape(owners, 2, rows, dec_wide)
        bridge_grad = jnp.swapaxes(everyone[:, :, :bridge_own], 0, 1).reshape(enc_wide, dec_wide)
        small = everyone[:, 0, bridge_own, :per].astype(F32) + everyone[
            :, 1, bridge_own, :per
        ].astype(F32)
    cuts = [enc_wide, 2 * enc_wide, 2 * enc_wide + dec_wide, 2 * enc_wide + 2 * dec_wide]
    small = small.reshape(-1)[: 2 * enc_wide + 3 * dec_wide]
    one_e, two_e, one_d, two_d, mask_grad = jnp.split(small, cuts)

    def split(final, qkv, out, up, step):
        cols = qkv.shape[2]
        first = 3 * cols + out.shape[0]
        second = first + up.shape[1]
        if step:
            mlp = final[:, first:].reshape(final.shape[0], -1, 2, step)
            downs, ups = (mlp[:, :, i].reshape(final.shape[0], -1) for i in range(2))
        else:
            downs, ups = final[:, second:], final[:, first:second]
        return (
            final[:, : 3 * cols].reshape(-1, 3, cols), final[:, 3 * cols : first].T, ups, downs.T
        )

    return (
        decoded.astype(F32)[:, None],
        tokens_grad[:, None],
        *split(enc_final, enc_qkv, enc_attn_out, enc_up, 512),
        one_e,
        two_e,
        bridge_grad.astype(F32),
        mask_grad,
        pos_final.T,
        *split(dec_final, dec_qkv, dec_attn_out, dec_up, 0),
        one_d,
        two_d,
    )


def solution(mesh):
    return jax.shard_map(
        per_device,
        mesh=mesh,
        in_specs=(
            P(None, "dp", "mp", None),
            P(None, "dp"),
            P(None, "dp", None),
            P(None, None, "mp"),
            P("mp", None),
            P(None, "mp"),
            P("mp", None),
            P(),
            P(),
            P(),
            P(),
            P("mp", None),
            P(None, None, "mp"),
            P("mp", None),
            P(None, "mp"),
            P("mp", None),
            P(),
            P(),
            P(None, "dp", "mp", None),
        ),
        out_specs=(
            P(None, "dp", "mp", "section"),
            P(None, "dp", "mp", "section"),
            P(("section", "dp"), None, "mp"),
            P("mp", ("section", "dp")),
            P(("section", "dp"), "mp"),
            P("mp", ("section", "dp")),
            P(),
            P(),
            P(),
            P(),
            P("mp", ("section", "dp")),
            P(("section", "dp"), None, "mp"),
            P("mp", ("section", "dp")),
            P(("section", "dp"), "mp"),
            P("mp", ("section", "dp")),
            P(),
            P(),
        ),
        check_vma=False,
    )
```

```python
import functools
import itertools

import jax
import jax.numpy as jnp
from jax import lax
from jax.experimental import pallas as pl
from jax.experimental.pallas import tpu as pltpu
from jax.sharding import PartitionSpec as P

HEAD = 64
LONGEST = 157
EPS = 1e-06
NEG = -1e30
F32 = jnp.float32
B16 = jnp.bfloat16
MESH = pl.DeviceIdType.MESH
VMEM = pltpu.VMEM
LIMIT = 56 * 1024 * 1024


def place_of():
    return lax.axis_index("section"), lax.axis_index("dp"), lax.axis_index("mp")


def greet(partners):
    barrier = pltpu.get_barrier_semaphore()
    for partner in partners:
        pl.semaphore_signal(barrier, inc=1, device_id=partner, device_id_type=MESH)
    pl.semaphore_wait(barrier, len(partners))


def send(src, dst, send_sem, recv_sem, partner):
    return pltpu.make_async_remote_copy(
        src_ref=src,
        dst_ref=dst,
        send_sem=send_sem,
        recv_sem=recv_sem,
        device_id=partner,
        device_id_type=MESH,
    )


def remote_params(ident):
    return pltpu.CompilerParams(
        collective_id=ident, has_side_effects=True, vmem_limit_bytes=LIMIT
    )


def route_kernel(x_ref, out_ref, send_sem, recv_sem, local_sem):
    s, d, m = place_of()
    greet([(1 - s, d, m), (s, d, 1 - m), (1 - s, d, 1 - m)])
    stays = s == m

    @pl.when(stays)
    def _():
        mine = pltpu.make_async_copy(x_ref.at[s], out_ref.at[m], local_sem)
        mine.start()
        out = send(x_ref.at[1 - s], out_ref.at[m], send_sem.at[0], recv_sem.at[m], (1 - s, d, m))
        out.start()
        mine.wait()
        out.wait_send()

    @pl.when(jnp.logical_not(stays))
    def _():
        near = send(x_ref.at[s], out_ref.at[m], send_sem.at[0], recv_sem.at[m], (s, d, 1 - m))
        far = send(
            x_ref.at[1 - s], out_ref.at[m], send_sem.at[1], recv_sem.at[m], (1 - s, d, 1 - m)
        )
        near.start()
        far.start()
        near.wait_send()
        far.wait_send()

    pltpu.make_async_copy(out_ref.at[1 - m], out_ref.at[1 - m], recv_sem.at[1 - m]).wait()

    @pl.when(jnp.logical_not(stays))
    def _():
        pltpu.make_async_copy(out_ref.at[m], out_ref.at[m], recv_sem.at[m]).wait()


def route(x, ident):
    return pl.pallas_call(
        route_kernel,
        out_shape=jax.ShapeDtypeStruct(x.shape, x.dtype),
        in_specs=[pl.BlockSpec(memory_space=pl.ANY)],
        out_specs=pl.BlockSpec(memory_space=pl.ANY),
        scratch_shapes=[
            pltpu.SemaphoreType.DMA((2,)),
            pltpu.SemaphoreType.DMA((2,)),
            pltpu.SemaphoreType.DMA,
        ],
        compiler_params=remote_params(ident),
        name=f"route_{ident}",
    )(x)


def scatter_kernel(n, across, g_ref, out_ref, near, work, far, over, sems):
    near_send, near_recv, far_send, far_recv, over_send, over_recv = sems
    s, d, m = place_of()
    sibling, facing = (1 - s, d, m), (s, d, 1 - m)
    greet([sibling] + [facing] * across + [(s, lax.rem(d + k, n), m) for k in range(1, n)])
    order = [*range(1, n), 0]
    sides = 1 + across
    first = {}
    for side in reversed(range(sides)):
        for k in order:
            to = lax.rem(d + k, n)
            first[side, k] = send(
                g_ref.at[side, (1 - s) * n + to],
                near.at[side, to],
                near_send.at[side, k],
                near_recv.at[side, k],
                sibling,
            )
            first[side, k].start()

    def summed(side, k):
        to = lax.rem(d + k, n)
        first[side, k].wait()
        return to, g_ref[side, s * n + to].astype(F32) + near[side, to].astype(F32)

    second = {}
    if across:
        for k in order:
            to, part = summed(1, k)
            work[1, to] = part.astype(B16)
            second[k] = send(work.at[1, to], over.at[to], over_send.at[k], over_recv.at[k], facing)
            second[k].start()
    third = []
    for k in order:
        to, part = summed(0, k)
        if across:
            second[k].wait()
            part = part + over[to].astype(F32)
        if k:
            work[0, to] = part.astype(B16)
            copy = send(work.at[0, to], far.at[d], far_send.at[k], far_recv.at[k], (s, to, m))
            copy.start()
            third.append((k, copy))
    for k, copy in third:
        copy.wait()
        part = part + far[lax.rem(d + n - k, n)].astype(F32)
    out_ref[...] = part


def scatter(g, ident):
    sides, owners, rows, cols = g.shape
    n = owners // 2
    across = sides - 1
    kernel = functools.partial(scatter_kernel, n, across)

    def body(g_ref, out_ref, near, work, far, over, *sems):
        kernel(g_ref, out_ref, near, work, far, over, sems)

    pieces = (n, rows, cols)
    return pl.pallas_call(
        body,
        out_shape=jax.ShapeDtypeStruct((rows, cols), F32),
        in_specs=[pl.BlockSpec(memory_space=VMEM)],
        out_specs=pl.BlockSpec(memory_space=VMEM),
        scratch_shapes=[
            VMEM((sides,) + pieces, B16),
            VMEM((sides,) + pieces, B16),
            VMEM(pieces, B16),
            VMEM(pieces if across else (8, 128), B16),
            pltpu.SemaphoreType.DMA((sides, n)),
            pltpu.SemaphoreType.DMA((sides, n)),
            pltpu.SemaphoreType.DMA((n,)),
            pltpu.SemaphoreType.DMA((n,)),
            pltpu.SemaphoreType.DMA((n,)),
            pltpu.SemaphoreType.DMA((n,)),
        ],
        compiler_params=remote_params(ident),
        name=f"scatter_{ident}",
    )(g)


def gather_kernel(n, x_ref, out_ref, local_sem, send_sem, recv_sem):
    s, d, m = place_of()
    steps = [(a, k, b) for k in range(n) for a in range(2) for b in range(2) if a or k or b]

    def partner(step):
        a, k, b = step
        return (lax.rem(s + a, 2), lax.rem(d + k, n), lax.rem(m + b, 2))

    greet([partner(step) for step in steps])
    slot = (s * n + d) * 2 + m
    mine = pltpu.make_async_copy(x_ref, out_ref.at[slot], local_sem)
    mine.start()
    copies = [
        send(x_ref, out_ref.at[slot], send_sem.at[i], recv_sem.at[i], partner(step))
        for i, step in enumerate(steps)
    ]
    for copy in copies:
        copy.start()
    mine.wait()
    for copy in copies:
        copy.wait()


def gather(x, n, ident):
    count = 4 * n
    return pl.pallas_call(
        functools.partial(gather_kernel, n),
        out_shape=jax.ShapeDtypeStruct((count,) + x.shape, x.dtype),
        in_specs=[pl.BlockSpec(memory_space=VMEM)],
        out_specs=pl.BlockSpec(memory_space=VMEM),
        scratch_shapes=[
            pltpu.SemaphoreType.DMA,
            pltpu.SemaphoreType.DMA((count - 1,)),
            pltpu.SemaphoreType.DMA((count - 1,)),
        ],
        compiler_params=remote_params(ident),
        name=f"gather_{ident}",
    )(x)


def dot_nt(a, b):
    return lax.dot_general(a, b, (((1,), (1,)), ((), ())), preferred_element_type=F32)


def dot_nn(a, b):
    return lax.dot_general(a, b, (((1,), (0,)), ((), ())), preferred_element_type=F32)


def dot_tn(a, b):
    return lax.dot_general(a, b, (((0,), (0,)), ((), ())), preferred_element_type=F32)


def chunks_of(length, most=256):
    units = length // 16
    count = -(-length // most)
    cuts = [16 * (units * i // count) for i in range(count)] + [length]
    return [(a, b - a) for a, b in zip(cuts, cuts[1:])]


def head_masks():
    lanes = lax.broadcasted_iota(jnp.int32, (1, 2 * HEAD), 1)
    return (lanes < HEAD, lanes >= HEAD)


def fetch(src, dst, sem):
    copy = pltpu.make_async_copy(src, dst, sem)
    copy.start()
    return copy


class Wire:
    def __init__(self, send_sem, recv_sem):
        self.send_sem, self.recv_sem, self.used = send_sem, recv_sem, 0

    def copy(self, src, dst, partner):
        index = self.used
        self.used += 1
        assert index < self.send_sem.shape[0]
        return send(src, dst, self.send_sem.at[index], self.recv_sem.at[index], partner)


class Chip:
    def __init__(self, s, d, m):
        self.s, self.m = s, m
        z = d // 2
        self.z = z
        self.me = {"y": lax.rem(d, 2), "a": lax.rem(z + z // 2, 2), "b": z // 2}
        self.near = [self.beside(axis) for axis in "yab"]

    @staticmethod
    def z_of(a, b):
        return lax.rem(a + b, 2) + 2 * b

    @staticmethod
    def place(z):
        return (z + z // 2) % 2, z // 2

    def beside(self, axis):
        at = dict(self.me, **{axis: 1 - self.me[axis]})
        return (self.s, 2 * self.z_of(at["a"], at["b"]) + at["y"], self.m)

    def own_rows(self, value, out):
        for y in range(2):

            @pl.when(self.me["y"] == y)
            def _(y=y):
                out[...] = value[24 * y : 24 * y + 24]


class Fold:
    def __init__(self, wire, chip, held, boxes, lanes, axes, order, last):
        self.rounds = []
        kept = {}
        for k, axis in enumerate(order):

            def part(value):
                chosen = dict(kept, **{axis: value})
                index = tuple(chosen.get(name, slice(None)) for name in axes)
                return held.at[index + (slice(None), lanes)]

            box = boxes[k].at[(slice(None),) * (len(axes) - k) + (lanes,)]
            copy = wire.copy(part(1 - chip.me[axis]), box, chip.beside(axis))
            self.rounds.append((copy, part(chip.me[axis]), box))
            kept[axis] = chip.me[axis]
        if last:
            mine = held.at[tuple(kept[name] for name in axes) + (slice(None), lanes)]
            box = boxes[-1].at[:, lanes]
            self.rounds.append((wire.copy(mine, box, chip.beside("y")), mine, box))

    def start(self):
        self.rounds[0][0].start()

    def step(self, k):
        copy, mine, box = self.rounds[k]
        copy.wait()
        mine[...] = mine[...] + box[...]
        self.rounds[k + 1][0].start()

    def end(self):
        copy, mine, box = self.rounds[-1]
        copy.wait()
        return mine[...].astype(F32) + box[...].astype(F32)


def norm_of(z):
    centre = z - jnp.mean(z, -1, keepdims=True)
    inverse = lax.rsqrt(jnp.mean(centre * centre, -1, keepdims=True) + EPS)
    return centre * inverse, inverse


def each(count, body):
    def step(i, carry):
        body(i)
        return carry

    lax.fori_loop(0, count, step, 0)


def softmax_fwd(q, k, v):
    scores = dot_nt(q, k)
    raised = jnp.exp(scores - jnp.max(scores, -1, keepdims=True))
    scale = 1.0 / jnp.sum(raised, -1, keepdims=True)
    raised = raised.astype(B16)
    return raised, scale, dot_nn(raised, v) * scale


def dec_kernel(early, *refs):
    (
        vis_ref, lengths, cells_ref, pos_own, pos_far, mask_ref, gain1_ref, gain2_ref,
        qkv_own, qkv_far, out_own, up_hbm, down_hbm, cot_hbm, enc_hbm,
        routed, dvis_out, small_out, enc_half, *refs,
    ) = refs
    if early:
        pos_out, attn_out, mlp_out, grad_out, *refs = refs
    else:
        pos_out, grad_out, *refs = refs
    (
        dec_out, out_far, w_up, w_down, cot, z1, unit1, a_ref, q_ref, keys, values, probs, stats,
        o_ref, unit2, b_ref, h_ref, slope, z2, do_ref, flip, dkt, dvt, got_kv,
        dvis_mine, dvis_near, dvis_far, free_sem, local_sem, send_sem, recv_sem,
    ) = refs
    s, d, m = place_of()
    sibling, facing = (1 - s, d, m), (s, d, 1 - m)
    stays = s == m
    length, wide = z1.shape
    third = wide // 2
    heads = third // HEAD
    wire = Wire(send_sem, recv_sem)
    scale = HEAD**-0.5

    beyond = (1 - s, d, 1 - m)
    greet([sibling, facing, beyond])

    loads = [
        pltpu.make_async_copy(up_hbm, w_up.at[0], local_sem.at[0]),
        pltpu.make_async_copy(down_hbm, w_down.at[0], local_sem.at[1]),
    ]
    pos_loads = [fetch(pos_own, z1, local_sem.at[3]), fetch(pos_far, b_ref, local_sem.at[5])]
    cot_load = pltpu.make_async_copy(cot_hbm.at[m], cot, local_sem.at[2])
    for load in loads:
        load.start()
    over, share = [], []
    for own, held in ((out_own, out_far), (up_hbm, w_up.at[1]), (down_hbm, w_down.at[1])):
        half = own.shape[0] // 2
        mine = pl.ds(s * half, half)
        over.append(wire.copy(own.at[mine], held.at[mine], facing))
        share.append(wire.copy(held.at[mine], held.at[mine], sibling))
        over[-1].start()
    cot_over = wire.copy(cot_hbm.at[1 - m], cot, facing)
    mid = enc_hbm.shape[1] // 2
    enc_parts = [enc_hbm.at[:, pl.ds(pl.multiple_of(k * mid, 128), mid)] for k in (m, 1 - m)]
    enc_load = pltpu.make_async_copy(enc_parts[0], enc_half, local_sem.at[6])
    enc_over = wire.copy(enc_parts[1], enc_half, facing)

    @pl.when(stays)
    def _():
        cot_load.start()
        cot_over.start()
        enc_load.start()
        enc_over.start()

    lane = lax.broadcasted_iota(jnp.int32, (1, 128), 1)

    def keep(plane, rows, column, value):
        stats[plane, rows] = jnp.where(lane == column, value, stats[plane, rows])

    def kept(plane, rows, column):
        return stats[plane, rows][:, column : column + 1]

    for copy in pos_loads:
        copy.wait()
    rows_at = 112
    base = s * length

    used = vis_ref.shape[0]
    slots = lax.broadcasted_iota(jnp.int32, (1, used), 1)
    cells_row = jnp.where(m == 0, cells_ref[0:1, :used], cells_ref[1:2, :used])
    cells_row = jnp.where(slots < lengths[m], cells_row, -1)

    def fill(i):
        rows = pl.ds(pl.multiple_of(i * rows_at, 16), rows_at)
        ids = lax.broadcasted_iota(jnp.int32, (rows_at, 1), 0) + (base + i * rows_at)
        place = jnp.where(cells_row == ids, 1.0, 0.0)
        unseen = 1.0 - jnp.sum(place, -1, keepdims=True)
        pos = jnp.where(stays, z1[rows], b_ref[rows].astype(F32))
        z = dot_nn(place.astype(B16), vis_ref[...]) + unseen * mask_ref[...][None, :] + pos
        unit, inverse = norm_of(z)
        z1[rows] = z
        unit1[rows] = unit.astype(B16)
        keep(0, rows, heads, inverse)
        a_ref[rows] = (unit * gain1_ref[...][None, :]).astype(B16)

    each(length // rows_at, fill)

    a = a_ref[...]
    mine_rows = pl.ds(0, length)
    kv_copies = []
    for side, weight in enumerate((qkv_own, qkv_far)):
        keys[side, mine_rows] = dot_nt(a, weight[1]).astype(B16)
        values[side, mine_rows] = dot_nt(a, weight[2]).astype(B16)
        for held in (keys, values):
            copy = wire.copy(
                held.at[side, mine_rows], held.at[side, pl.ds(length, length)], sibling
            )
            copy.start()
            kv_copies.append(copy)
    for side, weight in enumerate((qkv_own, qkv_far)):
        q_ref[side] = (dot_nt(a, weight[0]).astype(B16).astype(F32) * scale).astype(B16)
    for copy in kv_copies:
        copy.wait()

    masks = head_masks()
    pair = pl.ds(0, 2 * HEAD)
    lone = pl.ds(2 * HEAD, HEAD)

    def attend_side(side):
        for start, size in chunks_of(length, 400):
            rows = pl.ds(start, size)
            halves = []
            for head in range(2):
                q = jnp.where(masks[head], q_ref[side, rows, pair], 0)
                raised, over_sum, o = softmax_fwd(q, keys[side, :, pair], values[side, :, pair])
                probs[side, head, rows] = raised
                keep(side, rows, head, over_sum)
                halves.append(o)
            o_ref[side, rows, pair] = jnp.where(masks[0], halves[0], halves[1]).astype(B16)
            raised, over_sum, o = softmax_fwd(
                q_ref[side, rows, lone], keys[side, :, lone], values[side, :, lone]
            )
            probs[side, 2, rows] = raised
            keep(side, rows, 2, over_sum)
            o_ref[side, rows, lone] = o.astype(B16)

    each(2, attend_side)

    for copy, other in zip(over, share):
        copy.wait()
        other.start()
    share[0].wait()

    z2[...] = z1[...] + dot_nn(o_ref[0], out_own[...]) + dot_nn(o_ref[1], out_far[...])

    def second(i):
        rows = pl.ds(pl.multiple_of(i * rows_at, 16), rows_at)
        unit, inverse = norm_of(z2[rows])
        unit2[rows] = unit.astype(B16)
        keep(1, rows, heads, inverse)
        b_ref[rows] = (unit * gain2_ref[...][None, :]).astype(B16)

    each(length // rows_at, second)
    for load in loads:
        load.wait()
    for copy in share[1:]:
        copy.wait()

    step = 256
    steps = w_up.shape[2] // step

    def hidden_at(i):
        return i // steps, pl.ds(pl.multiple_of((i % steps) * step, step), step)

    def up(i):
        side, cols = hidden_at(i)
        u = dot_nn(b_ref[...], w_up[side, :, cols])
        phi = 0.5 + 0.5 * lax.erf(u * 0.5**0.5)
        h_ref[side, :, cols] = (u * phi).astype(B16)
        bell = jnp.exp(u * u * -0.5) * (0.5 / jnp.pi) ** 0.5
        slope[side, :, cols] = (phi + u * bell).astype(B16)

    each(2 * steps, up)

    def cut(value, out):
        out[0] = value[:, :third].astype(B16)
        out[1] = value[:, third:].astype(B16)

    cut(z2[...] + dot_nn(h_ref[0], w_down[0]) + dot_nn(h_ref[1], w_down[1]), dec_out)

    route_local = pltpu.make_async_copy(dec_out.at[s], routed.at[m], local_sem.at[4])
    route_near = wire.copy(dec_out.at[1 - s], routed.at[m], sibling)
    route_over = wire.copy(dec_out.at[s], routed.at[m], facing)
    route_far = wire.copy(dec_out.at[1 - s], routed.at[m], beyond)

    @pl.when(stays)
    def _():
        route_local.start()
        route_near.start()

    @pl.when(jnp.logical_not(stays))
    def _():
        route_over.start()
        route_far.start()

    @pl.when(stays)
    def _():
        cot_load.wait()
        cot_over.wait_send()
        enc_load.wait()
        enc_over.wait_send()

    @pl.when(jnp.logical_not(stays))
    def _():
        cot_over.wait_recv()
        enc_over.wait_recv()

    def transposed(value):
        return jnp.transpose(value.astype(F32)).astype(B16)

    cot_flip = flip.at[0]
    b_flip = flip.at[1]
    cot_flip[...] = transposed(cot[...])
    b_flip[...] = transposed(b_ref[...])

    def down(i):
        side, cols = hidden_at(i)
        grad_out[side, 2, :, cols] = dot_nn(cot_flip[...], h_ref[side, :, cols]).astype(B16)
        grad_u = dot_nt(cot[...], w_down[side, cols, :]) * slope[side, :, cols].astype(F32)
        grad_u = grad_u.astype(B16)
        slope[side, :, cols] = grad_u
        grad_out[side, 1, :, cols] = dot_nn(b_flip[...], grad_u).astype(B16)

    each(2 * steps, down)
    if early:
        rows = wide // 2
        mine_grads = pl.ds(pl.multiple_of(s * rows, 16), rows)
        away_grads = pl.ds(pl.multiple_of((1 - s) * rows, 16), rows)
        for partner in (sibling, facing):
            pl.semaphore_signal(free_sem, inc=1, device_id=partner, device_id_type=MESH)
        pl.semaphore_wait(free_sem, 2)
        near = {}
        for side, t in ((1, 1), (1, 2), (0, 1), (0, 2)):
            held = h_ref.at[0, pl.ds((side * 2 + t - 1) * rows, rows)]
            near[side, t] = (held, wire.copy(grad_out.at[side, t, away_grads], held, sibling))
            near[side, t][1].start()
    z1[...] = dot_nt(slope[0], w_up[0]) + dot_nt(slope[1], w_up[1])

    def back_norm(grad, unit, inverse, gain):
        scaled = grad * gain
        mean = jnp.mean(scaled, -1, keepdims=True)
        tilt = jnp.mean(scaled * unit, -1, keepdims=True)
        return inverse * (scaled - mean - unit * tilt)

    def add_rows(total, value):
        return total + jnp.sum(value, 0, keepdims=True)

    def second_back(i, total):
        rows = pl.ds(pl.multiple_of(i * rows_at, 16), rows_at)
        grad = z1[rows]
        unit = unit2[rows].astype(F32)
        z = cot[rows].astype(F32) + back_norm(grad, unit, kept(1, rows, heads), gain2_ref[...][None, :])
        z2[rows] = z
        b_ref[rows] = z.astype(B16)
        return add_rows(total, grad * unit)

    zero = jnp.zeros((1, wide), F32)
    gain2_grad = lax.fori_loop(0, length // rows_at, second_back, zero)

    grad_a = b_ref[...]
    flip[0] = transposed(grad_a)
    for side, weight in enumerate((out_own, out_far)):
        grad_out[side, 0, :, pl.ds(3 * third, third)] = dot_nn(flip[0], o_ref[side]).astype(B16)
        do_ref[side] = dot_nt(grad_a, weight[...]).astype(B16)

    if early:
        across = {}
        for t in (1, 2):
            held, copy = near[1, t]
            copy.wait()
            held[...] = (held[...].astype(F32) + grad_out[1, t, mine_grads].astype(F32)).astype(B16)
            got = h_ref.at[1, pl.ds((t - 1) * rows, rows)]
            across[t] = (got, wire.copy(held, got, facing))
            across[t][1].start()

    def attend_back_side(side):
        for index, (start, size) in enumerate(chunks_of(length, 256)):
            rows = pl.ds(start, size)
            for feats, heads in ((pair, (0, 1)), (lone, (2,))):
                q = q_ref[side, rows, feats]
                do = do_ref[side, rows, feats].astype(F32)
                both = do * o_ref[side, rows, feats].astype(F32)
                k = keys[side, :, feats]
                v = values[side, :, feats]
                dq = []
                for head in heads:
                    over_sum = kept(side, rows, head)
                    if len(heads) == 2:
                        lanes = slice(head * HEAD, (head + 1) * HEAD)
                        mine = jnp.where(masks[head], both, 0.0)
                        do_head = jnp.where(masks[head], do, 0.0)
                    else:
                        lanes = slice(0, HEAD)
                        mine, do_head = both, do
                    delta = jnp.sum(mine, -1, keepdims=True) * over_sum
                    do_head = (do_head * over_sum).astype(B16)
                    raised = probs[side, head, rows]
                    ds = (raised.astype(F32) * (dot_nt(do_head, v) - delta)).astype(B16)
                    dq.append(dot_nn(ds, k))
                    dv_part = dot_tn(do_head[:, lanes], raised)
                    dk_part = dot_tn(q[:, lanes], ds)
                    at = pl.ds(head * HEAD, HEAD)
                    if index:
                        dv_part = dv_part + dvt[at]
                        dk_part = dk_part + dkt[at]
                    dvt[at] = dv_part
                    dkt[at] = dk_part
                dq = jnp.where(masks[0], dq[0], dq[1]) if len(heads) == 2 else dq[0]
                q_ref[side, rows, feats] = (dq * scale).astype(B16)
        for held, out in ((dkt, keys), (dvt, values)):
            for feats, at in ((pair, pl.ds(0, 2 * HEAD)), (lone, pl.ds(2 * HEAD, HEAD))):
                out[side, :, feats] = jnp.transpose(held[at]).astype(B16)

    each(2, attend_back_side)
    far_rows = pl.ds(length, length)
    kv_back = [
        [
            wire.copy(held.at[side, far_rows], got_kv.at[slot, side], sibling)
            for side in range(2)
        ]
        for slot, held in enumerate((keys, values))
    ]
    for copies in kv_back:
        for copy in copies:
            copy.start()
    if early:
        def stage(slot, halves, out, sem):
            lanes = pl.ds(0, out.shape[1])
            for owner in range(8):
                a, b = Chip.place(owner // 2)
                rows = pl.ds(48 * (4 * (owner % 2) + 2 * a + b), 48)
                piece = jnp.concatenate([half[24 * owner : 24 * owner + 24] for half in halves], 0)
                piece = jnp.pad(piece, ((0, 0), (0, out.shape[1] - piece.shape[1])))
                probs[0, slot, rows, lanes] = piece.astype(B16)
            return fetch(probs.at[0, slot, pl.ds(0, wide), lanes], out, sem)

        totals = []
        for t in (1, 2):
            held, copy = near[0, t]
            copy.wait()
            across[t][1].wait()
            totals.append(
                held[...].astype(F32)
                + grad_out[0, t, mine_grads].astype(F32)
                + across[t][0][...].astype(F32)
            )
        stores = [stage(2, totals, mlp_out, local_sem.at[1])]

    a_flip = flip.at[0]
    a_flip[...] = transposed(a_ref[...])
    total = None
    for slot in range(3):
        for side, weight in enumerate((qkv_own, qkv_far)):
            if slot:
                kv_back[slot - 1][side].wait()
                own = (keys, values)[slot - 1][side, mine_rows].astype(F32)
                grad = (own + got_kv[slot - 1, side].astype(F32)).astype(B16)
            else:
                grad = q_ref[side]
            grad_out[side, 0, :, pl.ds(slot * third, third)] = dot_nn(a_flip[...], grad).astype(B16)
            part = dot_nn(grad, weight[slot])
            total = part if total is None else total + part
    z1[...] = total
    if early:
        attn_pairs = []
        for side in (1, 0):
            held = h_ref.at[1, pl.ds((2 + side) * rows, rows)]
            copy = wire.copy(grad_out.at[side, 0, away_grads], held, sibling)
            copy.start()
            attn_pairs.append((held, copy))
    @pl.when(stays)
    def _():
        route_local.wait()
        route_near.wait_send()
        route_over.wait_recv()

    @pl.when(jnp.logical_not(stays))
    def _():
        route_over.wait_send()
        route_far.wait_send()
        route_near.wait_recv()
        route_far.wait_recv()

    def first_back(i, totals):
        rows = pl.ds(pl.multiple_of(i * rows_at, 16), rows_at)
        grad = z1[rows]
        unit = unit1[rows].astype(F32)
        z = z2[rows] + back_norm(grad, unit, kept(0, rows, heads), gain1_ref[...][None, :])
        b_ref[rows] = z.astype(B16)
        dec_out[0, rows] = z[:, :third].astype(B16)
        dec_out[1, rows] = z[:, third:].astype(B16)
        ids = lax.broadcasted_iota(jnp.int32, (rows_at, 1), 0) + (base + i * rows_at)
        seen = jnp.sum(jnp.where(cells_row == ids, 1.0, 0.0), -1, keepdims=True)
        return add_rows(totals[0], grad * unit), add_rows(totals[1], (1.0 - seen) * z)

    gain1_grad, mask_grad = lax.fori_loop(0, length // rows_at, first_back, (zero, zero))
    if not early:
        stores = [fetch(dec_out, pos_out, local_sem.at[0])]
    small_out[0:1] = gain1_grad
    small_out[1:2] = gain2_grad
    small_out[2:3] = mask_grad

    ids = (lax.broadcasted_iota(jnp.int32, (used, length), 1) + base).astype(F32)
    cells_col = jnp.transpose(jnp.broadcast_to(cells_row.astype(F32), (8, used)))[:, 0:1]
    place = jnp.where(cells_col == ids, 1.0, 0.0).astype(B16)
    dvis_mine[...] = dot_nn(place, b_ref[...]).astype(B16)
    dvis_pair = wire.copy(dvis_mine, dvis_near, sibling)
    dvis_over = wire.copy(dvis_mine, dvis_far, facing)
    dvis_cross = wire.copy(dvis_mine, dvis_near, beyond)

    @pl.when(stays)
    def _():
        dvis_over.start()

    @pl.when(jnp.logical_not(stays))
    def _():
        dvis_pair.start()
        dvis_cross.start()

    if early:
        halves = [jnp.transpose(dec_out[half].astype(F32)) for half in range(2)]
        stores.append(stage(0, halves, pos_out, local_sem.at[0]))
        halves = []
        for side, (held, copy) in zip((1, 0), attn_pairs):
            copy.wait()
            halves.insert(0, held[...].astype(F32) + grad_out[side, 0, mine_grads].astype(F32))
        stores.append(stage(1, halves, attn_out, local_sem.at[2]))

    def dvis_sum(first, second):
        dvis_out[...] = (first[...].astype(F32) + second[...].astype(F32)).astype(B16)

    @pl.when(stays)
    def _():
        dvis_pair.wait_recv()
        dvis_sum(dvis_mine, dvis_near)
        dvis_over.wait_send()

    @pl.when(jnp.logical_not(stays))
    def _():
        dvis_over.wait_recv()
        dvis_cross.wait_recv()
        dvis_sum(dvis_far, dvis_near)
        dvis_pair.wait_send()
        dvis_cross.wait_send()

    for copy in stores:
        copy.wait()


def decoder(early, vis, lengths, cells, pos_own, pos_far, mask, gains, weights, cot, enc, ident):
    qkv_own, qkv_far, out_own, up, down = weights
    length, wide = pos_own.shape
    used = vis.shape[0]
    third = wide // 2
    hidden = up.shape[1]
    keys = 2 * length
    heads = third // HEAD
    assert heads == 3 and length % 112 == 0
    whole = pl.BlockSpec(memory_space=VMEM)
    there = pl.BlockSpec(memory_space=pl.ANY)
    grads = (2, 3, wide, hidden)
    outs = [
        (jax.ShapeDtypeStruct((2, length, third), B16), there),
        (jax.ShapeDtypeStruct((used, wide), B16), whole),
        (jax.ShapeDtypeStruct((8, wide), F32), whole),
        (jax.ShapeDtypeStruct((used, enc.shape[1] // 2), B16), there),
    ]
    if early:
        lanes = -(-length // 128) * 128
        outs += [
            (jax.ShapeDtypeStruct((wide, lanes), B16), there),
            (jax.ShapeDtypeStruct((wide, hidden), B16), there),
            (jax.ShapeDtypeStruct((wide, hidden), B16), there),
        ]
    else:
        outs += [
            (jax.ShapeDtypeStruct((2, length, third), B16), there),
            (jax.ShapeDtypeStruct(grads, B16), whole),
        ]
    return pl.pallas_call(
        functools.partial(dec_kernel, early),
        out_shape=[item for item, _ in outs],
        in_specs=[whole, pl.BlockSpec(memory_space=pltpu.SMEM), whole]
        + [there] * 2
        + [whole] * 6
        + [there] * 4,
        out_specs=[spec for _, spec in outs],
        scratch_shapes=[VMEM(grads, B16)] * early
        + [
            VMEM((2, length, third), B16),
            VMEM(out_own.shape, B16),
            VMEM((2, wide, hidden), B16),
            VMEM((2, hidden, wide), B16),
            VMEM((length, wide), B16),
            VMEM((length, wide), F32),
            VMEM((length, wide), B16),
            VMEM((length, wide), B16),
            VMEM((2, length, third), B16),
            VMEM((2, keys, third), B16),
            VMEM((2, keys, third), B16),
            VMEM((2, heads, length, keys), B16),
            VMEM((2, length, 128), F32),
            VMEM((2, length, third), B16),
            VMEM((length, wide), B16),
            VMEM((length, wide), B16),
            VMEM((2, length, hidden), B16),
            VMEM((2, length, hidden), B16),
            VMEM((length, wide), F32),
            VMEM((2, length, third), B16),
            VMEM((2, wide, length), B16),
            VMEM((third, keys), F32),
            VMEM((third, keys), F32),
            VMEM((2, 2, length, third), B16),
            VMEM((used, wide), B16),
            VMEM((used, wide), B16),
            VMEM((used, wide), B16),
            pltpu.SemaphoreType.REGULAR,
            pltpu.SemaphoreType.DMA((7,)),
            pltpu.SemaphoreType.DMA((40,)),
            pltpu.SemaphoreType.DMA((40,)),
        ],
        compiler_params=pltpu.CompilerParams(
            collective_id=ident, has_side_effects=True, vmem_limit_bytes=int(63.9 * 1024) * 1024
        ),
        name="decoder",
    )(
        vis,
        lengths,
        cells,
        pos_own,
        pos_far,
        mask,
        gains[0],
        gains[1],
        qkv_own,
        qkv_far,
        out_own,
        up,
        down,
        cot,
        enc,
    )


def pack(grad, owners):
    rows, cols = grad.shape
    own = rows // owners
    fold = 1
    while own * fold % 16:
        fold *= 2
    grad = grad.astype(B16).reshape(owners, own, fold, cols // fold)
    return jnp.swapaxes(grad, 1, 2).reshape(owners, fold * own, cols // fold)


def unpack(piece, own):
    fold = piece.shape[0] // own
    return jnp.swapaxes(piece.reshape(fold, own, -1), 0, 1).reshape(own, -1)


def pick(pair, index):
    return lax.dynamic_index_in_dim(pair, index, 0, keepdims=False)


def enc_kernel(*refs):
    (
        length_ref, tok_hbm, qkv_hbm, out_hbm, up_hbm, down_hbm, bridge_ref, gain1_ref, gain2_ref,
        pos_hbm, dqkv_hbm,
        vis_out, dqkv_far, pos_far, enc_ref, unit1, unit2, stats, a_ref, triple, probs, o_ref, b_ref,
        slope, h_ref,
        x_ref, qkv, w_out, w_up, w_down, z2, part_ref, part_far, pos_full, pos_half,
        local_sem, send_sem, recv_sem,
    ) = refs
    s, d, m = place_of()
    sibling, facing = (1 - s, d, m), (s, d, 1 - m)
    stays = s == m
    used, wide = x_ref.shape
    half = tok_hbm.shape[1]
    rest = used - half
    wire = Wire(send_sem, recv_sem)

    y = lax.rem(d, 2)
    beside = (s, d + 1 - 2 * y, m)

    greet([sibling, facing, beside])
    first, last = pl.ds(0, half), pl.ds(half, rest)
    tok_first = wire.copy(tok_hbm.at[s], x_ref.at[first], facing)
    tok_last = wire.copy(tok_hbm.at[s, pl.ds(0, rest)], x_ref.at[last], facing)
    own_first = pltpu.make_async_copy(tok_hbm.at[s], x_ref.at[first], local_sem.at[0])
    own_last = pltpu.make_async_copy(
        tok_hbm.at[s, pl.ds(0, rest)], x_ref.at[last], local_sem.at[0]
    )

    @pl.when(m == 0)
    def _():
        tok_first.start()
        own_first.start()

    @pl.when(m == 1)
    def _():
        tok_last.start()
        own_last.start()

    loads = [
        fetch(hbm, held, local_sem.at[i + 1])
        for i, (hbm, held) in enumerate(
            ((qkv_hbm, qkv), (out_hbm, w_out), (up_hbm, w_up), (down_hbm, w_down))
        )
    ]
    pos_load = fetch(pos_hbm, pos_full, local_sem.at[5])
    size = dqkv_hbm.shape[1] // 2
    mine = (slice(None), pl.ds(s * size, size))
    over = wire.copy(dqkv_hbm.at[mine], dqkv_far.at[mine], facing)
    share = wire.copy(dqkv_far.at[mine], dqkv_far.at[mine], sibling)

    low = pos_hbm.shape[0] // 32 * 16
    pos_parts = [pl.ds(0, low), pl.ds(low, pos_hbm.shape[0] - low)]
    pos_over = [wire.copy(pos_half.at[part], pos_far.at[part], facing) for part in pos_parts]
    pos_trade = [wire.copy(pos_far.at[part], pos_far.at[part], beside) for part in pos_parts]

    def by_place(on_stays, act):
        for part in range(2):

            @pl.when(jnp.logical_and(stays if on_stays else jnp.logical_not(stays), y == part))
            def _(part=part):
                act(part)

    @pl.when(m == 0)
    def _():
        own_first.wait()
        tok_first.wait_send()
        tok_last.wait_recv()

    @pl.when(m == 1)
    def _():
        own_last.wait()
        tok_last.wait_send()
        tok_first.wait_recv()

    over.start()
    pos_load.wait()

    def send_positions(part):
        pos_half[pos_parts[part]] = pos_full[pos_parts[part]].astype(B16)
        pos_over[part].start()

    by_place(True, send_positions)

    lane = lax.broadcasted_iota(jnp.int32, (1, 128), 1)

    unit, inverse = norm_of(x_ref[...].astype(F32))
    unit1[...] = unit
    stats[...] = jnp.where(lane == 0, inverse, 0.0)
    a = (unit * gain1_ref[...][None, :]).astype(B16)
    a_ref[...] = a
    loads[0].wait()
    for slot in range(3):
        triple[slot] = dot_nn(a, qkv[slot]).astype(B16)

    valid = lax.broadcasted_iota(jnp.int32, (1, used), 1) < length_ref[s]
    masks = head_masks()
    for pair in range(triple.shape[2] // (2 * HEAD)):
        feats = pl.ds(pair * 2 * HEAD, 2 * HEAD)
        q, k, v = (triple[slot, :, feats] for slot in range(3))
        halves = []
        for head in range(2):
            scores = dot_nt(jnp.where(masks[head], q, 0), k) * HEAD**-0.5
            scores = jnp.where(valid, scores, NEG)
            raised = jnp.exp(scores - jnp.max(scores, -1, keepdims=True))
            p = (raised / jnp.sum(raised, -1, keepdims=True)).astype(B16)
            probs[2 * pair + head] = p
            halves.append(dot_nn(p, v))
        o_ref[:, feats] = jnp.where(masks[0], halves[0], halves[1]).astype(B16)

    loads[1].wait()
    part = dot_nn(o_ref[...], w_out[...])
    part_ref[0] = part.astype(B16)
    attn = wire.copy(part_ref.at[0], part_far.at[0], facing)
    attn.start()
    z2[...] = x_ref[...].astype(F32) + part

    attn.wait()
    z = z2[...] + part_far[0].astype(F32)
    z2[...] = z
    unit, inverse = norm_of(z)
    unit2[...] = unit
    stats[...] = jnp.where(lane == 1, inverse, stats[...])
    b = (unit * gain2_ref[...][None, :]).astype(B16)
    b_ref[...] = b
    loads[2].wait()
    step = 512

    def up(i):
        cols = pl.ds(pl.multiple_of(i * step, step), step)
        u = dot_nn(b_ref[...], w_up[:, cols])
        phi = 0.5 + 0.5 * lax.erf(u * 0.5**0.5)
        h_ref[:, cols] = (u * phi).astype(B16)
        bell = jnp.exp(u * u * -0.5) * (0.5 / jnp.pi) ** 0.5
        slope[:, cols] = (phi + u * bell).astype(B16)

    each(w_up.shape[1] // step, up)

    over.wait()
    share.start()

    def trade_positions(part):
        pos_over[part].wait_recv()
        pos_trade[part].start()

    by_place(False, trade_positions)
    loads[3].wait()
    part = dot_nn(h_ref[...], w_down[...])
    z2[...] = z2[...] + part
    part_ref[1] = part.astype(B16)
    mlp = wire.copy(part_ref.at[1], part_far.at[1], facing)
    vis_near = wire.copy(vis_out, vis_out, sibling)

    @pl.when(stays)
    def _():
        mlp.wait_recv()
        enc = (z2[...] + part_far[1].astype(F32)).astype(B16)
        enc_ref[...] = enc
        vis_out[...] = dot_nn(enc, bridge_ref[...]).astype(B16)
        vis_near.start()

    @pl.when(jnp.logical_not(stays))
    def _():
        mlp.start()
        enc_ref[...] = jnp.zeros(enc_ref.shape, B16)

    @pl.when(stays)
    def _():
        vis_near.wait_send()

    @pl.when(jnp.logical_not(stays))
    def _():
        mlp.wait_send()
        vis_near.wait_recv()

    def finish_positions(part):
        pos_trade[part].wait_send()
        pos_trade[1 - part].wait_recv()

    by_place(True, lambda part: pos_over[part].wait_send())
    by_place(False, finish_positions)
    share.wait()


def encoder(lengths, tokens, weights, bridge, gains, pos, dqkv, used, ident):
    qkv, out, up, down = weights
    wide = tokens.shape[2]
    feats = qkv.shape[2]
    hidden = up.shape[1]
    whole = pl.BlockSpec(memory_space=VMEM)
    there = pl.BlockSpec(memory_space=pl.ANY)
    shape = jax.ShapeDtypeStruct
    outs = [
        (shape((used, pos.shape[1]), B16), whole),
        (shape(dqkv.shape, B16), there),
        (shape(pos.shape, B16), there),
        (shape((used, wide), B16), whole),
        (shape((used, wide), F32), whole),
        (shape((used, wide), F32), whole),
        (shape((used, 128), F32), whole),
        (shape((used, wide), B16), whole),
        (shape((3, used, feats), B16), whole),
        (shape((feats // HEAD, used, used), B16), whole),
        (shape((used, feats), B16), whole),
        (shape((used, wide), B16), whole),
        (shape((used, hidden), B16), whole),
        (shape((used, hidden), B16), whole),
    ]
    return pl.pallas_call(
        enc_kernel,
        out_shape=[item for item, _ in outs],
        in_specs=[pl.BlockSpec(memory_space=pltpu.SMEM)]
        + [there] * 5
        + [whole] * 3
        + [there] * 2,
        out_specs=[spec for _, spec in outs],
        scratch_shapes=[
            VMEM((used, wide), B16),
            VMEM(qkv.shape, B16),
            VMEM(out.shape, B16),
            VMEM(up.shape, B16),
            VMEM(down.shape, B16),
            VMEM((used, wide), F32),
            VMEM((2, used, wide), B16),
            VMEM((2, used, wide), B16),
            VMEM(pos.shape, F32),
            VMEM(pos.shape, B16),
            pltpu.SemaphoreType.DMA((6,)),
            pltpu.SemaphoreType.DMA((16,)),
            pltpu.SemaphoreType.DMA((16,)),
        ],
        compiler_params=remote_params(ident),
        name="encoder",
    )(
        lengths, tokens, qkv, out, up, down, bridge, gains[0], gains[1],
        pos, dqkv,
    )


def back_kernel(cube, *refs):
    (
        dvis_ref, bridge_ref, gain1_ref, gain2_ref, unit1, unit2, stats, a_ref, triple, probs, o_ref,
        b_ref, slope, h_ref, enc_half, small_dec, qkv_hbm, out_hbm, up_hbm, down_hbm, *refs,
    ) = refs
    if cube:
        (
            pos_hbm, attn_hbm, mlp_hbm,
            tok_out, small_out, enc_out, mlp_out, attn_out, pos_out, bridge_all,
            near, held, box0, box1, box2,
            dec_held, dec_box0, dec_box1, dec_box2, side_held, side_box0, side_box1, side_box2,
            pos_sum, pos_got, attn_sum, attn_got, bridge_near, small_box, grads, bridge_grad, *refs,
        ) = refs
    else:
        tok_out, small_out, grads, bridge_grad, *refs = refs
    (
        qkv, w_out, w_up, w_down, gu, dy, part, part_far, dz, da_ref, do_ref, dqkv, flip, tok_part,
        local_sem, send_sem, recv_sem,
    ) = refs
    s, d, m = place_of()
    sibling, facing = (1 - s, d, m), (s, d, 1 - m)
    stays = s == m
    used, wide = unit1.shape
    feats = o_ref.shape[1]
    hidden = h_ref.shape[1]
    half = tok_part.shape[1]
    rest = used - half
    wire = Wire(send_sem, recv_sem)
    section = wide // 2

    if cube:
        chip = Chip(s, d, m)
        z, y = chip.z, chip.me["y"]
        others = [(s, 2 * lax.rem(z + k, 4) + y, lax.rem(m + side, 2)) for k in (1, 2, 3) for side in (0, 1)]
        greet([sibling, facing, (1 - s, d, 1 - m), chip.near[0]] + others)
    else:
        greet([sibling, facing])

    loads = [
        fetch(hbm, held, local_sem.at[i])
        for i, (hbm, held) in enumerate(
            ((down_hbm, w_down), (up_hbm, w_up), (out_hbm, w_out), (qkv_hbm, qkv))
        )
    ]

    if cube:
        cells = pos_sum.shape[2]
        pos_lanes = pos_hbm.shape[-1]
        span = attn_hbm.shape[-1]
        blank = (slice(None),) * 4
        early_loads = [
            fetch(hbm, dec_held.at[blank + (pl.ds(first, hbm.shape[-1]),)], local_sem.at[4 + i])
            for i, (hbm, first) in enumerate(
                ((pos_hbm, 0), (attn_hbm, pos_lanes), (mlp_hbm, pos_lanes + span))
            )
        ]
        for copy in early_loads:
            copy.wait()
        orders = ("yab", "ayb", "yab", "yab")
        mlp_orders = (("yab", "ayb"), ("yab", "ayb"), ("ayb", "yab"))
        attn_orders = ("yab", "yab", "ayb", "ayb")
        tiles = (pos_lanes + 2 * span) // 128
        cuts = [128 * (tiles * i // 4) for i in range(5)]
        early_folds = [
            Fold(
                wire, chip, dec_held, (dec_box0, dec_box1, dec_box2), pl.ds(low, high - low), "yab",
                order, False,
            )
            for low, high, order in zip(cuts, cuts[1:], orders)
        ]
        for fold in early_folds:
            fold.start()

    def transposed(value):
        return jnp.transpose(value.astype(F32)).astype(B16)

    dvis = dvis_ref[...]
    grad = dot_nt(dvis, bridge_ref[...])
    dy[...] = grad
    dm = grad.astype(B16)
    da_ref[...] = dm
    flip[0] = transposed(dm)
    flip[1] = transposed(b_ref[...])
    bridge_grad[...] = dot_tn(enc_half[...], dvis).astype(B16)
    if cube:
        bridge_rows = bridge_near.shape[0]
        bridge_pair = wire.copy(
            bridge_grad.at[pl.ds(pl.multiple_of((1 - s) * bridge_rows, 16), bridge_rows)],
            bridge_near,
            sibling,
        )
        bridge_pair.start()

    loads[0].wait()
    step = 512
    first_mlp = 4 * feats
    steps = hidden // step
    if cube:
        away_rows = pl.ds(pl.multiple_of((1 - s) * section, 16), section)

        class Group:
            def __init__(self, first, size, orders):
                self.lanes, self.orders = pl.ds(first, size), orders
                self.pair = wire.copy(
                    grads.at[away_rows, self.lanes], near.at[:, self.lanes], sibling
                )
                self.pair.start()

            def start(self):
                self.pair.wait()
                for owner in range(8):
                    rows = pl.ds(48 * owner, 48)
                    from_rows = pl.ds(pl.multiple_of(s * section + 48 * owner, 16), 48)
                    index = (owner % 2,) + Chip.place(owner // 2) + (slice(None), self.lanes)
                    held[index] = near[rows, self.lanes] + grads[from_rows, self.lanes]
                part = self.lanes.size // len(self.orders)
                self.folds = [
                    Fold(
                        wire, chip, held, (box0, box1, box2), pl.ds(self.lanes.start + i * part, part),
                        "yab", order, False,
                    )
                    for i, order in enumerate(self.orders)
                ]
                for fold in self.folds:
                    fold.start()

            def step(self, k):
                for fold in self.folds:
                    fold.step(k)

            def end(self):
                part = self.lanes.size // len(self.folds)
                for i, fold in enumerate(self.folds):
                    enc_out[:, pl.ds(self.lanes.start + i * part, part)] = fold.end()

        mlp_groups = []

    for i in range(steps):
        cols = pl.ds(i * step, step)
        grads[:, pl.ds(first_mlp + 2 * i * step, step)] = dot_nn(flip[0], h_ref[:, cols]).astype(B16)
        grad_u = dot_nt(da_ref[...], w_down[cols, :]) * slope[:, cols].astype(F32)
        grad_u = grad_u.astype(B16)
        gu[:, cols] = grad_u
        grads[:, pl.ds(first_mlp + (2 * i + 1) * step, step)] = dot_nn(flip[1], grad_u).astype(B16)
        if cube:
            mlp_groups.append(Group(first_mlp + 2 * i * step, 2 * step, mlp_orders[i % 3]))
            if i:
                mlp_groups[i - 1].start()

    loads[1].wait()
    grad = dot_nt(gu[...], w_up[...])
    part[...] = grad.astype(B16)
    over = wire.copy(part, part_far.at[0], facing)
    over.start()
    dz[...] = grad
    gain2_grad = jnp.sum(grad * unit2[...], 0, keepdims=True)

    if cube:
        mlp_groups[-1].start()

    def back_norm(grad, unit, inverse, gain):
        scaled = grad * gain
        mean = jnp.mean(scaled, -1, keepdims=True)
        tilt = jnp.mean(scaled * unit, -1, keepdims=True)
        return inverse * (scaled - mean - unit * tilt)

    over.wait()
    whole = dz[...] + part_far[0].astype(F32)
    dz2 = dy[...] + back_norm(whole, unit2[...], stats[:, 1:2], gain2_ref[...][None, :])
    dy[...] = dz2
    grad_a = dz2.astype(B16)
    da_ref[...] = grad_a
    flip[0] = transposed(grad_a)
    loads[2].wait()
    grads[:, pl.ds(3 * feats, feats)] = dot_nn(flip[0], o_ref[...]).astype(B16)
    do_ref[...] = dot_nt(grad_a, w_out[...]).astype(B16)

    if cube:
        out_group = Group(3 * feats, feats, attn_orders[3:])
        bridge_pair.wait()
        narrow = bridge_near.shape[1]
        for at in range(4):
            side_held[Chip.place(at)] = (
                bridge_near[pl.ds(48 * at, 48)]
                + bridge_grad[pl.ds(pl.multiple_of(s * bridge_rows + 48 * at, 16), 48)]
            )
        bridge_fold = Fold(
            wire, chip, side_held, (side_box0, side_box1, side_box2), pl.ds(0, narrow), "ab", "ab", True
        )
        bridge_fold.start()

    masks = head_masks()
    scale = HEAD**-0.5
    for pair in range(feats // (2 * HEAD)):
        at = pl.ds(pair * 2 * HEAD, 2 * HEAD)
        q, k, v = (triple[slot, :, at] for slot in range(3))
        do = do_ref[:, at]
        both = do.astype(F32) * o_ref[:, at].astype(F32)
        parts = []
        for head in range(2):
            delta = jnp.sum(jnp.where(masks[head], both, 0.0), -1, keepdims=True)
            do_head = jnp.where(masks[head], do, 0)
            p = probs[2 * pair + head]
            ds = (p.astype(F32) * (dot_nt(do_head, v) - delta)).astype(B16)
            parts.append((dot_nn(ds, k) * scale, dot_tn(ds, q) * scale, dot_tn(p, do)))
        for slot in range(3):
            dqkv[slot, :, at] = jnp.where(masks[0], parts[0][slot], parts[1][slot]).astype(B16)

    if cube:
        out_group.start()
        for fold in early_folds:
            fold.step(0)
        bridge_fold.step(0)

    flip[1] = transposed(a_ref[...])
    loads[3].wait()
    total = None
    for slot in range(3):
        grads[:, pl.ds(slot * feats, feats)] = dot_nn(flip[1], dqkv[slot]).astype(B16)
        term = dot_nt(dqkv[slot], qkv[slot])
        total = term if total is None else total + term
    part[...] = total.astype(B16)
    dz[...] = total
    gain1_grad = jnp.sum(total * unit1[...], 0, keepdims=True)
    first, last = pl.ds(0, half), pl.ds(half, rest)
    over_first = wire.copy(part.at[first], part_far.at[1, first], facing)
    over_last = wire.copy(part.at[last], part_far.at[1, last], facing)

    @pl.when(m == 0)
    def _():
        over_last.start()

    @pl.when(m == 1)
    def _():
        over_first.start()

    small_out[...] = jnp.zeros(small_out.shape, F32)
    row = 0
    for value in (
        gain1_grad, gain2_grad, small_dec[0:1], small_dec[1:2], small_dec[2:3],
    ):
        for i in range(value.shape[1] // 128):
            small_out[row : row + 1] = value[:, i * 128 : (i + 1) * 128]
            row += 1

    if cube:
        attn_groups = [
            Group(i * feats, feats, (order,)) for i, order in enumerate(attn_orders[:3])
        ]
        small_copies = [
            wire.copy(small_out, small_box.at[i], partner)
            for i, partner in enumerate([sibling, facing] + chip.near)
        ]

        def small_step(i):
            small_copies[i].wait()
            small_out[...] = small_out[...] + small_box[i]
            if i + 1 < len(small_copies):
                small_copies[i + 1].start()

        small_copies[0].start()
        for group in attn_groups:
            group.start()
        bridge_fold.step(1)
        small_step(0)

    def finish(rows, size):
        whole = dz[rows] + part_far[1, rows].astype(F32)
        unit = unit1[rows]
        grad = dy[rows] + back_norm(whole, unit, stats[rows][:, 0:1], gain1_ref[...][None, :])
        for side in range(2):
            tok_part[side, pl.ds(0, size)] = grad[:, side * section : (side + 1) * section]

    @pl.when(m == 0)
    def _():
        over_last.wait_send()
        over_first.wait_recv()
        finish(first, half)

    @pl.when(m == 1)
    def _():
        over_first.wait_send()
        over_last.wait_recv()
        tok_part[...] = jnp.zeros(tok_part.shape, F32)
        finish(last, rest)

    tok_pair = wire.copy(tok_part.at[1 - s], tok_out.at[s], sibling)
    tok_pair.start()
    tok_out[s] = tok_part[s]

    if cube:
        for fold in early_folds:
            fold.step(1)
        for group in mlp_groups:
            group.step(0)
        small_step(1)

        slot = (s * 4 + z) * 2 + m
        bridge_all[slot] = bridge_fold.end().astype(B16)
        spread = [
            wire.copy(bridge_all.at[slot], bridge_all.at[slot], partner)
            for partner in [facing] + others
        ]
        for copy in spread:
            copy.start()

        out_group.step(0)
        for group in attn_groups:
            group.step(0)
        small_step(2)
        for group in mlp_groups:
            group.step(1)

        wholes = jnp.concatenate([fold.end() for fold in early_folds], 1)
        for half_at in range(2):
            piece = wholes[24 * half_at : 24 * half_at + 24]
            pos_sum[half_at] = piece[:, :cells]
            attn_sum[half_at] = piece[:, pos_lanes : pos_lanes + span]
            mlp_out[:, pl.ds(half_at * span, span)] = piece[:, pos_lanes + span :]
        attn_over = wire.copy(attn_sum.at[1], attn_got, facing)
        attn_over.start()
        route_near = wire.copy(pos_sum.at[1 - s], pos_got.at[m], sibling)
        route_over = wire.copy(pos_sum.at[s], pos_got.at[m], facing)
        route_far = wire.copy(pos_sum.at[1 - s], pos_got.at[m], (1 - s, d, 1 - m))

        @pl.when(stays)
        def _():
            route_near.start()
            pos_got[m] = pos_sum[s]

        @pl.when(jnp.logical_not(stays))
        def _():
            route_over.start()
            route_far.start()


        out_group.step(1)
        for copy in spread:
            copy.wait()
        ours = pl.ds(s * 8, 8)
        bridge_pair_all = wire.copy(bridge_all.at[ours], bridge_all.at[ours], sibling)
        bridge_pair_all.start()
        for group in attn_groups:
            group.step(1)
        small_step(3)
        for group in mlp_groups:
            group.end()
        attn_over.wait()
        attn_out[...] = attn_sum[0] + attn_got[...]

        @pl.when(stays)
        def _():
            route_near.wait_send()
            route_over.wait_recv()

        @pl.when(jnp.logical_not(stays))
        def _():
            route_over.wait_send()
            route_far.wait_send()
            route_near.wait_recv()
            route_far.wait_recv()

        pos_out[...] = pos_got[0] + pos_got[1]
        out_group.end()
        small_step(4)
        for group in attn_groups:
            group.end()
        bridge_pair_all.wait()

    tok_pair.wait()


def back(cube, dvis, bridge, gains, saved, small_dec, weights, dec_grads, cells, half, ident):
    unit1, unit2, stats, a, triple, probs, o, b, slope, h, enc_half = saved
    qkv, out, up, down = weights
    used, wide = unit1.shape
    feats, hidden = o.shape[1], h.shape[1]
    cols = 4 * feats + 2 * hidden
    narrow = bridge.shape[1]
    whole = pl.BlockSpec(memory_space=VMEM)
    there = pl.BlockSpec(memory_space=pl.ANY)
    shape = jax.ShapeDtypeStruct
    args = [dvis, bridge, gains[0], gains[1], *saved, small_dec, qkv, out, up, down]
    in_specs = [whole] * 16 + [there] * 4
    outs = [shape((2, half, wide // 2), F32), shape((24, 128), F32)]
    assert 2 * wide + 3 * narrow <= 24 * 128
    grads, bridge_grad = (wide, cols), (wide // 2, narrow)
    scratch = []
    if cube:
        pos, attn, mlp = dec_grads
        span = attn.shape[1]
        args += [
            pos.reshape(2, 2, 2, 48, -1), attn.reshape(2, 2, 2, 48, -1), mlp.reshape(2, 2, 2, 48, -1)
        ]
        in_specs += [there] * 3
        outs += [
            shape((48, cols), F32),
            shape((24, 2 * span), F32),
            shape((24, span), F32),
            shape((24, cells), F32),
            shape((16, 48, narrow), B16),
        ]

        def folded(axes, size):
            return [VMEM((2,) * (axes - k) + (48, size), B16) for k in range(axes + 1)]

        scratch = [
            VMEM((wide // 2, cols), B16),
            *folded(3, cols),
            *folded(3, pos.shape[1] + 2 * span),
            *folded(2, narrow),
            VMEM((48, narrow), B16),
            VMEM((2, 24, cells), F32),
            VMEM((2, 24, cells), F32),
            VMEM((2, 24, span), F32),
            VMEM((24, span), F32),
            VMEM((narrow // 2, narrow), B16),
            VMEM((5, 24, 128), F32),
            VMEM(grads, B16),
            VMEM(bridge_grad, B16),
        ]
    else:
        outs += [shape(grads, B16), shape(bridge_grad, B16)]
    scratch += [
        VMEM(qkv.shape, B16),
        VMEM(out.shape, B16),
        VMEM(up.shape, B16),
        VMEM(down.shape, B16),
        VMEM((used, hidden), B16),
        VMEM((used, wide), F32),
        VMEM((used, wide), B16),
        VMEM((2, used, wide), B16),
        VMEM((used, wide), F32),
        VMEM((used, wide), B16),
        VMEM((used, feats), B16),
        VMEM((3, used, feats), B16),
        VMEM((2, wide, used), B16),
        VMEM((2, half, wide // 2), F32),
        pltpu.SemaphoreType.DMA((14,)),
        pltpu.SemaphoreType.DMA((96,)),
        pltpu.SemaphoreType.DMA((96,)),
    ]
    return pl.pallas_call(
        functools.partial(back_kernel, cube),
        out_shape=outs,
        in_specs=in_specs,
        out_specs=[whole] * len(outs),
        scratch_shapes=scratch,
        compiler_params=remote_params(ident),
        name="encoder_back",
    )(*args)


def finish_kernel(step, *refs):
    decoded, tokens, small, enc, mlp, attn, pos, bridge = refs[:8]
    (
        decoded_out, tokens_out, e_qkv, e_out, e_up, e_down, one_e, two_e, bridge_out, mask_out,
        pos_out, d_qkv, d_out, d_up, d_down, one_d, two_d,
    ) = refs[8:]
    for i in range(2):
        decoded_out[i] = jnp.transpose(decoded[i].astype(F32))
    tokens_out[...] = tokens[...]
    for source, qkv, out in ((enc, e_qkv, e_out), (attn, d_qkv, d_out)):
        cols = qkv.shape[2]
        for slot in range(3):
            qkv[slot] = source[:, pl.ds(slot * cols, cols)]
        out[...] = source[:, pl.ds(3 * cols, cols)]
    first = 4 * e_qkv.shape[2]
    for i in range(e_up.shape[1] // step):
        at = pl.ds(i * step, step)
        e_down[:, at] = enc[:, pl.ds(first + 2 * i * step, step)]
        e_up[:, at] = enc[:, pl.ds(first + (2 * i + 1) * step, step)]
    hidden = d_up.shape[1]
    d_up[...] = mlp[:, :hidden]
    d_down[...] = mlp[:, hidden:]
    pos_out[...] = pos[...]
    pieces = bridge.shape[0] // 2
    for side in range(2):
        for piece in range(pieces):
            rows = pl.ds((side * pieces + piece) * bridge.shape[1], bridge.shape[1])
            bridge_out[rows] = bridge[2 * piece + side].astype(F32)
    row = 0
    for out in (one_e, two_e, one_d, two_d, mask_out):
        for i in range(out.shape[0] // 128):
            out[pl.ds(i * 128, 128)] = small[row]
            row += 1


def finish(shapes, parts, step):
    whole = pl.BlockSpec(memory_space=VMEM)
    return pl.pallas_call(
        functools.partial(finish_kernel, step),
        out_shape=[jax.ShapeDtypeStruct(shape, F32) for shape in shapes],
        in_specs=[whole] * len(parts),
        out_specs=[whole] * len(shapes),
        compiler_params=pltpu.CompilerParams(vmem_limit_bytes=LIMIT),
        name="finish",
    )(*parts)


def per_device(
    tokens,
    clip_lengths,
    clip_cells,
    enc_qkv,
    enc_attn_out,
    enc_up,
    enc_down,
    enc_gain_one,
    enc_gain_two,
    bridge_weight,
    mask_token,
    position_embed,
    dec_qkv,
    dec_attn_out,
    dec_up,
    dec_down,
    dec_gain_one,
    dec_gain_two,
    cotangent,
):
    s, d, m = place_of()
    n = lax.axis_size("dp")
    owners = 2 * n
    cube = n == 8
    dec_wide = position_embed.shape[1]
    half_slots, enc_wide = tokens.shape[2:]
    used = -(-LONGEST // 32) * 32

    e_weights = (jnp.swapaxes(enc_qkv, 0, 1), enc_attn_out, enc_up, enc_down)
    d_qkv = jnp.transpose(dec_qkv, (1, 2, 0))
    vis, d_qkv_far, pos_far, enc, *saved = encoder(
        clip_lengths[:, 0],
        tokens[:, 0],
        e_weights,
        bridge_weight,
        (enc_gain_one, enc_gain_two),
        position_embed,
        d_qkv,
        used,
        1,
    )
    decoded, dvis, dec_small, enc_half, *dec_grads = decoder(
        cube,
        vis,
        clip_lengths[:, 0],
        clip_cells[:, 0],
        position_embed,
        pos_far,
        mask_token,
        (dec_gain_one, dec_gain_two),
        (d_qkv, d_qkv_far, dec_attn_out, dec_up, dec_down),
        cotangent[:, 0],
        enc,
        2,
    )
    tokens_grad, small, *rest = back(
        cube,
        dvis,
        bridge_weight,
        (enc_gain_one, enc_gain_two),
        (*saved, enc_half),
        dec_small,
        e_weights,
        dec_grads,
        position_embed.shape[0],
        half_slots,
        3,
    )
    if cube:
        e_own, d_own = enc_wide // owners, dec_wide // owners
        shapes = [
            (2, decoded.shape[2], decoded.shape[1]),
            tokens_grad.shape,
            (3, e_own, enc_qkv.shape[2]),
            (e_own, enc_attn_out.shape[0]),
            (e_own, enc_up.shape[1]),
            (e_own, enc_down.shape[0]),
            (enc_wide,),
            (enc_wide,),
            (enc_wide, dec_wide),
            (dec_wide,),
            (d_own, position_embed.shape[0]),
            (3, d_own, dec_qkv.shape[2]),
            (d_own, dec_attn_out.shape[0]),
            (d_own, dec_up.shape[1]),
            (d_own, dec_down.shape[0]),
            (dec_wide,),
            (dec_wide,),
        ]
        outs = list(finish(shapes, (decoded, tokens_grad, small, *rest), 512))
        outs[0] = jnp.swapaxes(outs[0], 1, 2)[:, None]
        outs[1] = outs[1][:, None]
        for i in (2, 11):
            outs[i] = jnp.swapaxes(outs[i], 0, 1)
        for i in (3, 5, 10, 12, 14):
            outs[i] = outs[i].T
        return tuple(outs)
    else:
        grads, bridge = rest
        pos_parts, dec_grads = dec_grads
        enc_final = unpack(scatter(pack(grads, owners)[None], 11), enc_wide // owners)
        packed = [
            pack(jnp.concatenate([dec_grads[side, t] for t in range(3)], 1), owners)
            for side in range(2)
        ]
        dec_final = unpack(scatter(jnp.stack(packed), 12), dec_wide // owners)
        parts = route(pos_parts, 13).astype(F32)
        packed = pack(jnp.transpose(parts[0] + parts[1]), n)
        zero = jnp.zeros_like(packed)
        packed = jnp.concatenate(
            [jnp.where(s == 0, packed, zero), jnp.where(s == 1, packed, zero)], 0
        )
        pos_final = unpack(scatter(packed[None], 14), dec_wide // owners)
        bridge_own = enc_wide // 2 // owners
        per = -(-small.size // owners)
        small = jnp.pad(small.reshape(-1), (0, per * owners - small.size)).reshape(owners, 1, per)
        rows = -(-(bridge_own + 1) // 16) * 16
        rep = jnp.concatenate(
            [
                bridge.astype(F32).reshape(owners, bridge_own, dec_wide),
                jnp.pad(small, ((0, 0), (0, 0), (0, dec_wide - per))),
                jnp.zeros((owners, rows - bridge_own - 1, dec_wide), F32),
            ],
            1,
        ).astype(B16)
        rep = scatter(rep[None], 15).astype(B16)
        everyone = gather(rep, n, 16).reshape(owners, 2, rows, dec_wide)
        bridge_grad = jnp.swapaxes(everyone[:, :, :bridge_own], 0, 1).reshape(enc_wide, dec_wide)
        small = everyone[:, 0, bridge_own, :per].astype(F32) + everyone[
            :, 1, bridge_own, :per
        ].astype(F32)
    cuts = [enc_wide, 2 * enc_wide, 2 * enc_wide + dec_wide, 2 * enc_wide + 2 * dec_wide]
    small = small.reshape(-1)[: 2 * enc_wide + 3 * dec_wide]
    one_e, two_e, one_d, two_d, mask_grad = jnp.split(small, cuts)

    def split(final, qkv, out, up, step):
        cols = qkv.shape[2]
        first = 3 * cols + out.shape[0]
        second = first + up.shape[1]
        if step:
            mlp = final[:, first:].reshape(final.shape[0], -1, 2, step)
            downs, ups = (mlp[:, :, i].reshape(final.shape[0], -1) for i in range(2))
        else:
            downs, ups = final[:, second:], final[:, first:second]
        return (
            final[:, : 3 * cols].reshape(-1, 3, cols), final[:, 3 * cols : first].T, ups, downs.T
        )

    return (
        decoded.astype(F32)[:, None],
        tokens_grad[:, None],
        *split(enc_final, enc_qkv, enc_attn_out, enc_up, 512),
        one_e,
        two_e,
        bridge_grad.astype(F32),
        mask_grad,
        pos_final.T,
        *split(dec_final, dec_qkv, dec_attn_out, dec_up, 0),
        one_d,
        two_d,
    )


def solution(mesh):
    return jax.shard_map(
        per_device,
        mesh=mesh,
        in_specs=(
            P(None, "dp", "mp", None),
            P(None, "dp"),
            P(None, "dp", None),
            P(None, None, "mp"),
            P("mp", None),
            P(None, "mp"),
            P("mp", None),
            P(),
            P(),
            P(),
            P(),
            P("mp", None),
            P(None, None, "mp"),
            P("mp", None),
            P(None, "mp"),
            P("mp", None),
            P(),
            P(),
            P(None, "dp", "mp", None),
        ),
        out_specs=(
            P(None, "dp", "mp", "section"),
            P(None, "dp", "mp", "section"),
            P(("section", "dp"), None, "mp"),
            P("mp", ("section", "dp")),
            P(("section", "dp"), "mp"),
            P("mp", ("section", "dp")),
            P(),
            P(),
            P(),
            P(),
            P("mp", ("section", "dp")),
            P(("section", "dp"), None, "mp"),
            P("mp", ("section", "dp")),
            P(("section", "dp"), "mp"),
            P("mp", ("section", "dp")),
            P(),
            P(),
        ),
        check_vma=False,
    )
```

```python
import functools
import itertools

import jax
import jax.numpy as jnp
from jax import lax
from jax.experimental import pallas as pl
from jax.experimental.pallas import tpu as pltpu
from jax.sharding import PartitionSpec as P

HEAD = 64
LONGEST = 157
EPS = 1e-06
NEG = -1e30
F32 = jnp.float32
B16 = jnp.bfloat16
MESH = pl.DeviceIdType.MESH
VMEM = pltpu.VMEM
LIMIT = 56 * 1024 * 1024


def place_of():
    return lax.axis_index("section"), lax.axis_index("dp"), lax.axis_index("mp")


def greet(partners):
    barrier = pltpu.get_barrier_semaphore()
    for partner in partners:
        pl.semaphore_signal(barrier, inc=1, device_id=partner, device_id_type=MESH)
    pl.semaphore_wait(barrier, len(partners))


def send(src, dst, send_sem, recv_sem, partner):
    return pltpu.make_async_remote_copy(
        src_ref=src,
        dst_ref=dst,
        send_sem=send_sem,
        recv_sem=recv_sem,
        device_id=partner,
        device_id_type=MESH,
    )


def remote_params(ident):
    return pltpu.CompilerParams(
        collective_id=ident, has_side_effects=True, vmem_limit_bytes=LIMIT
    )


def route_kernel(x_ref, out_ref, send_sem, recv_sem, local_sem):
    s, d, m = place_of()
    greet([(1 - s, d, m), (s, d, 1 - m), (1 - s, d, 1 - m)])
    stays = s == m

    @pl.when(stays)
    def _():
        mine = pltpu.make_async_copy(x_ref.at[s], out_ref.at[m], local_sem)
        mine.start()
        out = send(x_ref.at[1 - s], out_ref.at[m], send_sem.at[0], recv_sem.at[m], (1 - s, d, m))
        out.start()
        mine.wait()
        out.wait_send()

    @pl.when(jnp.logical_not(stays))
    def _():
        near = send(x_ref.at[s], out_ref.at[m], send_sem.at[0], recv_sem.at[m], (s, d, 1 - m))
        far = send(
            x_ref.at[1 - s], out_ref.at[m], send_sem.at[1], recv_sem.at[m], (1 - s, d, 1 - m)
        )
        near.start()
        far.start()
        near.wait_send()
        far.wait_send()

    pltpu.make_async_copy(out_ref.at[1 - m], out_ref.at[1 - m], recv_sem.at[1 - m]).wait()

    @pl.when(jnp.logical_not(stays))
    def _():
        pltpu.make_async_copy(out_ref.at[m], out_ref.at[m], recv_sem.at[m]).wait()


def route(x, ident):
    return pl.pallas_call(
        route_kernel,
        out_shape=jax.ShapeDtypeStruct(x.shape, x.dtype),
        in_specs=[pl.BlockSpec(memory_space=pl.ANY)],
        out_specs=pl.BlockSpec(memory_space=pl.ANY),
        scratch_shapes=[
            pltpu.SemaphoreType.DMA((2,)),
            pltpu.SemaphoreType.DMA((2,)),
            pltpu.SemaphoreType.DMA,
        ],
        compiler_params=remote_params(ident),
        name=f"route_{ident}",
    )(x)


def scatter_kernel(n, across, g_ref, out_ref, near, work, far, over, sems):
    near_send, near_recv, far_send, far_recv, over_send, over_recv = sems
    s, d, m = place_of()
    sibling, facing = (1 - s, d, m), (s, d, 1 - m)
    greet([sibling] + [facing] * across + [(s, lax.rem(d + k, n), m) for k in range(1, n)])
    order = [*range(1, n), 0]
    sides = 1 + across
    first = {}
    for side in reversed(range(sides)):
        for k in order:
            to = lax.rem(d + k, n)
            first[side, k] = send(
                g_ref.at[side, (1 - s) * n + to],
                near.at[side, to],
                near_send.at[side, k],
                near_recv.at[side, k],
                sibling,
            )
            first[side, k].start()

    def summed(side, k):
        to = lax.rem(d + k, n)
        first[side, k].wait()
        return to, g_ref[side, s * n + to].astype(F32) + near[side, to].astype(F32)

    second = {}
    if across:
        for k in order:
            to, part = summed(1, k)
            work[1, to] = part.astype(B16)
            second[k] = send(work.at[1, to], over.at[to], over_send.at[k], over_recv.at[k], facing)
            second[k].start()
    third = []
    for k in order:
        to, part = summed(0, k)
        if across:
            second[k].wait()
            part = part + over[to].astype(F32)
        if k:
            work[0, to] = part.astype(B16)
            copy = send(work.at[0, to], far.at[d], far_send.at[k], far_recv.at[k], (s, to, m))
            copy.start()
            third.append((k, copy))
    for k, copy in third:
        copy.wait()
        part = part + far[lax.rem(d + n - k, n)].astype(F32)
    out_ref[...] = part


def scatter(g, ident):
    sides, owners, rows, cols = g.shape
    n = owners // 2
    across = sides - 1
    kernel = functools.partial(scatter_kernel, n, across)

    def body(g_ref, out_ref, near, work, far, over, *sems):
        kernel(g_ref, out_ref, near, work, far, over, sems)

    pieces = (n, rows, cols)
    return pl.pallas_call(
        body,
        out_shape=jax.ShapeDtypeStruct((rows, cols), F32),
        in_specs=[pl.BlockSpec(memory_space=VMEM)],
        out_specs=pl.BlockSpec(memory_space=VMEM),
        scratch_shapes=[
            VMEM((sides,) + pieces, B16),
            VMEM((sides,) + pieces, B16),
            VMEM(pieces, B16),
            VMEM(pieces if across else (8, 128), B16),
            pltpu.SemaphoreType.DMA((sides, n)),
            pltpu.SemaphoreType.DMA((sides, n)),
            pltpu.SemaphoreType.DMA((n,)),
            pltpu.SemaphoreType.DMA((n,)),
            pltpu.SemaphoreType.DMA((n,)),
            pltpu.SemaphoreType.DMA((n,)),
        ],
        compiler_params=remote_params(ident),
        name=f"scatter_{ident}",
    )(g)


def gather_kernel(n, x_ref, out_ref, local_sem, send_sem, recv_sem):
    s, d, m = place_of()
    steps = [(a, k, b) for k in range(n) for a in range(2) for b in range(2) if a or k or b]

    def partner(step):
        a, k, b = step
        return (lax.rem(s + a, 2), lax.rem(d + k, n), lax.rem(m + b, 2))

    greet([partner(step) for step in steps])
    slot = (s * n + d) * 2 + m
    mine = pltpu.make_async_copy(x_ref, out_ref.at[slot], local_sem)
    mine.start()
    copies = [
        send(x_ref, out_ref.at[slot], send_sem.at[i], recv_sem.at[i], partner(step))
        for i, step in enumerate(steps)
    ]
    for copy in copies:
        copy.start()
    mine.wait()
    for copy in copies:
        copy.wait()


def gather(x, n, ident):
    count = 4 * n
    return pl.pallas_call(
        functools.partial(gather_kernel, n),
        out_shape=jax.ShapeDtypeStruct((count,) + x.shape, x.dtype),
        in_specs=[pl.BlockSpec(memory_space=VMEM)],
        out_specs=pl.BlockSpec(memory_space=VMEM),
        scratch_shapes=[
            pltpu.SemaphoreType.DMA,
            pltpu.SemaphoreType.DMA((count - 1,)),
            pltpu.SemaphoreType.DMA((count - 1,)),
        ],
        compiler_params=remote_params(ident),
        name=f"gather_{ident}",
    )(x)


def dot_nt(a, b):
    return lax.dot_general(a, b, (((1,), (1,)), ((), ())), preferred_element_type=F32)


def dot_nn(a, b):
    return lax.dot_general(a, b, (((1,), (0,)), ((), ())), preferred_element_type=F32)


def dot_tn(a, b):
    return lax.dot_general(a, b, (((0,), (0,)), ((), ())), preferred_element_type=F32)


def chunks_of(length, most=256):
    units = length // 16
    count = -(-length // most)
    cuts = [16 * (units * i // count) for i in range(count)] + [length]
    return [(a, b - a) for a, b in zip(cuts, cuts[1:])]


def head_masks():
    lanes = lax.broadcasted_iota(jnp.int32, (1, 2 * HEAD), 1)
    return (lanes < HEAD, lanes >= HEAD)


def fetch(src, dst, sem):
    copy = pltpu.make_async_copy(src, dst, sem)
    copy.start()
    return copy


class Wire:
    def __init__(self, send_sem, recv_sem):
        self.send_sem, self.recv_sem, self.used = send_sem, recv_sem, 0

    def copy(self, src, dst, partner):
        index = self.used
        self.used += 1
        assert index < self.send_sem.shape[0]
        return send(src, dst, self.send_sem.at[index], self.recv_sem.at[index], partner)


class Chip:
    def __init__(self, s, d, m):
        self.s, self.m = s, m
        z = d // 2
        self.z = z
        self.me = {"y": lax.rem(d, 2), "a": lax.rem(z + z // 2, 2), "b": z // 2}
        self.near = [self.beside(axis) for axis in "yab"]

    @staticmethod
    def z_of(a, b):
        return lax.rem(a + b, 2) + 2 * b

    @staticmethod
    def place(z):
        return (z + z // 2) % 2, z // 2

    def beside(self, axis):
        at = dict(self.me, **{axis: 1 - self.me[axis]})
        return (self.s, 2 * self.z_of(at["a"], at["b"]) + at["y"], self.m)

    def own_rows(self, value, out):
        for y in range(2):

            @pl.when(self.me["y"] == y)
            def _(y=y):
                out[...] = value[24 * y : 24 * y + 24]


class Fold:
    def __init__(self, wire, chip, held, boxes, lanes, axes, order, last):
        self.rounds = []
        kept = {}
        for k, axis in enumerate(order):

            def part(value):
                chosen = dict(kept, **{axis: value})
                index = tuple(chosen.get(name, slice(None)) for name in axes)
                return held.at[index + (slice(None), lanes)]

            box = boxes[k].at[(slice(None),) * (len(axes) - k) + (lanes,)]
            copy = wire.copy(part(1 - chip.me[axis]), box, chip.beside(axis))
            self.rounds.append((copy, part(chip.me[axis]), box))
            kept[axis] = chip.me[axis]
        if last:
            mine = held.at[tuple(kept[name] for name in axes) + (slice(None), lanes)]
            box = boxes[-1].at[:, lanes]
            self.rounds.append((wire.copy(mine, box, chip.beside("y")), mine, box))

    def start(self):
        self.rounds[0][0].start()

    def step(self, k):
        copy, mine, box = self.rounds[k]
        copy.wait()
        mine[...] = mine[...] + box[...]
        self.rounds[k + 1][0].start()

    def end(self):
        copy, mine, box = self.rounds[-1]
        copy.wait()
        return mine[...].astype(F32) + box[...].astype(F32)


def norm_of(z):
    centre = z - jnp.mean(z, -1, keepdims=True)
    inverse = lax.rsqrt(jnp.mean(centre * centre, -1, keepdims=True) + EPS)
    return centre * inverse, inverse


def each(count, body):
    def step(i, carry):
        body(i)
        return carry

    lax.fori_loop(0, count, step, 0)


def softmax_fwd(q, k, v):
    scores = dot_nt(q, k)
    raised = jnp.exp(scores - jnp.max(scores, -1, keepdims=True))
    scale = 1.0 / jnp.sum(raised, -1, keepdims=True)
    raised = raised.astype(B16)
    return raised, scale, dot_nn(raised, v) * scale


def dec_kernel(early, *refs):
    (
        vis_ref, lengths, cells_ref, pos_own, pos_far, mask_ref, gain1_ref, gain2_ref,
        qkv_own, qkv_far, out_own, up_hbm, down_hbm, cot_hbm, enc_hbm,
        routed, dvis_out, small_out, enc_half, *refs,
    ) = refs
    if early:
        pos_out, attn_out, mlp_out, grad_out, *refs = refs
    else:
        pos_out, grad_out, *refs = refs
    (
        dec_out, out_far, w_up, w_down, cot, z1, unit1, a_ref, q_ref, keys, values, probs, stats,
        o_ref, unit2, b_ref, h_ref, slope, z2, do_ref, flip, dkt, dvt, got_kv,
        dvis_mine, dvis_near, dvis_far, free_sem, local_sem, send_sem, recv_sem,
    ) = refs
    s, d, m = place_of()
    sibling, facing = (1 - s, d, m), (s, d, 1 - m)
    stays = s == m
    length, wide = z1.shape
    third = wide // 2
    heads = third // HEAD
    wire = Wire(send_sem, recv_sem)
    scale = HEAD**-0.5

    beyond = (1 - s, d, 1 - m)
    greet([sibling, facing, beyond])

    loads = [
        pltpu.make_async_copy(up_hbm, w_up.at[0], local_sem.at[0]),
        pltpu.make_async_copy(down_hbm, w_down.at[0], local_sem.at[1]),
    ]
    pos_loads = [fetch(pos_own, z1, local_sem.at[3]), fetch(pos_far, b_ref, local_sem.at[5])]
    cot_load = pltpu.make_async_copy(cot_hbm.at[m], cot, local_sem.at[2])
    for load in loads:
        load.start()
    over, share = [], []
    for own, held in ((out_own, out_far), (up_hbm, w_up.at[1]), (down_hbm, w_down.at[1])):
        half = own.shape[0] // 2
        mine = pl.ds(s * half, half)
        over.append(wire.copy(own.at[mine], held.at[mine], facing))
        share.append(wire.copy(held.at[mine], held.at[mine], sibling))
        over[-1].start()
    cot_over = wire.copy(cot_hbm.at[1 - m], cot, facing)
    mid = enc_hbm.shape[1] // 2
    enc_parts = [enc_hbm.at[:, pl.ds(pl.multiple_of(k * mid, 128), mid)] for k in (m, 1 - m)]
    enc_load = pltpu.make_async_copy(enc_parts[0], enc_half, local_sem.at[6])
    enc_over = wire.copy(enc_parts[1], enc_half, facing)

    @pl.when(stays)
    def _():
        cot_load.start()
        cot_over.start()
        enc_load.start()
        enc_over.start()

    lane = lax.broadcasted_iota(jnp.int32, (1, 128), 1)

    def keep(plane, rows, column, value):
        stats[plane, rows] = jnp.where(lane == column, value, stats[plane, rows])

    def kept(plane, rows, column):
        return stats[plane, rows][:, column : column + 1]

    for copy in pos_loads:
        copy.wait()
    rows_at = 112
    base = s * length

    used = vis_ref.shape[0]
    slots = lax.broadcasted_iota(jnp.int32, (1, used), 1)
    cells_row = jnp.where(m == 0, cells_ref[0:1, :used], cells_ref[1:2, :used])
    cells_row = jnp.where(slots < lengths[m], cells_row, -1)

    def fill(i):
        rows = pl.ds(pl.multiple_of(i * rows_at, 16), rows_at)
        ids = lax.broadcasted_iota(jnp.int32, (rows_at, 1), 0) + (base + i * rows_at)
        place = jnp.where(cells_row == ids, 1.0, 0.0)
        unseen = 1.0 - jnp.sum(place, -1, keepdims=True)
        pos = jnp.where(stays, z1[rows], b_ref[rows].astype(F32))
        z = dot_nn(place.astype(B16), vis_ref[...]) + unseen * mask_ref[...][None, :] + pos
        unit, inverse = norm_of(z)
        z1[rows] = z
        unit1[rows] = unit.astype(B16)
        keep(0, rows, heads, inverse)
        a_ref[rows] = (unit * gain1_ref[...][None, :]).astype(B16)

    each(length // rows_at, fill)

    a = a_ref[...]
    mine_rows = pl.ds(0, length)
    kv_copies = []
    for side, weight in enumerate((qkv_own, qkv_far)):
        keys[side, mine_rows] = dot_nt(a, weight[1]).astype(B16)
        values[side, mine_rows] = dot_nt(a, weight[2]).astype(B16)
        for held in (keys, values):
            copy = wire.copy(
                held.at[side, mine_rows], held.at[side, pl.ds(length, length)], sibling
            )
            copy.start()
            kv_copies.append(copy)
    for side, weight in enumerate((qkv_own, qkv_far)):
        q_ref[side] = (dot_nt(a, weight[0]).astype(B16).astype(F32) * scale).astype(B16)
    for copy in kv_copies:
        copy.wait()

    masks = head_masks()
    pair = pl.ds(0, 2 * HEAD)
    lone = pl.ds(2 * HEAD, HEAD)

    def attend_side(side):
        for start, size in chunks_of(length, 400):
            rows = pl.ds(start, size)
            halves = []
            for head in range(2):
                q = jnp.where(masks[head], q_ref[side, rows, pair], 0)
                raised, over_sum, o = softmax_fwd(q, keys[side, :, pair], values[side, :, pair])
                probs[side, head, rows] = raised
                keep(side, rows, head, over_sum)
                halves.append(o)
            o_ref[side, rows, pair] = jnp.where(masks[0], halves[0], halves[1]).astype(B16)
            raised, over_sum, o = softmax_fwd(
                q_ref[side, rows, lone], keys[side, :, lone], values[side, :, lone]
            )
            probs[side, 2, rows] = raised
            keep(side, rows, 2, over_sum)
            o_ref[side, rows, lone] = o.astype(B16)

    each(2, attend_side)

    for copy, other in zip(over, share):
        copy.wait()
        other.start()
    share[0].wait()

    z2[...] = z1[...] + dot_nn(o_ref[0], out_own[...]) + dot_nn(o_ref[1], out_far[...])

    def second(i):
        rows = pl.ds(pl.multiple_of(i * rows_at, 16), rows_at)
        unit, inverse = norm_of(z2[rows])
        unit2[rows] = unit.astype(B16)
        keep(1, rows, heads, inverse)
        b_ref[rows] = (unit * gain2_ref[...][None, :]).astype(B16)

    each(length // rows_at, second)
    for load in loads:
        load.wait()
    for copy in share[1:]:
        copy.wait()

    step = 256
    steps = w_up.shape[2] // step

    def hidden_at(i):
        return i // steps, pl.ds(pl.multiple_of((i % steps) * step, step), step)

    def up(i):
        side, cols = hidden_at(i)
        u = dot_nn(b_ref[...], w_up[side, :, cols])
        phi = 0.5 + 0.5 * lax.erf(u * 0.5**0.5)
        h_ref[side, :, cols] = (u * phi).astype(B16)
        bell = jnp.exp(u * u * -0.5) * (0.5 / jnp.pi) ** 0.5
        slope[side, :, cols] = (phi + u * bell).astype(B16)

    each(2 * steps, up)

    def cut(value, out):
        out[0] = value[:, :third].astype(B16)
        out[1] = value[:, third:].astype(B16)

    cut(z2[...] + dot_nn(h_ref[0], w_down[0]) + dot_nn(h_ref[1], w_down[1]), dec_out)

    route_local = pltpu.make_async_copy(dec_out.at[s], routed.at[m], local_sem.at[4])
    route_near = wire.copy(dec_out.at[1 - s], routed.at[m], sibling)
    route_over = wire.copy(dec_out.at[s], routed.at[m], facing)
    route_far = wire.copy(dec_out.at[1 - s], routed.at[m], beyond)

    @pl.when(stays)
    def _():
        route_local.start()
        route_near.start()

    @pl.when(jnp.logical_not(stays))
    def _():
        route_over.start()
        route_far.start()

    @pl.when(stays)
    def _():
        cot_load.wait()
        cot_over.wait_send()
        enc_load.wait()
        enc_over.wait_send()

    @pl.when(jnp.logical_not(stays))
    def _():
        cot_over.wait_recv()
        enc_over.wait_recv()

    def transposed(value):
        return jnp.transpose(value.astype(F32)).astype(B16)

    cot_flip = flip.at[0]
    b_flip = flip.at[1]
    cot_flip[...] = transposed(cot[...])
    b_flip[...] = transposed(b_ref[...])

    def down(i):
        side, cols = hidden_at(i)
        grad_out[side, 2, :, cols] = dot_nn(cot_flip[...], h_ref[side, :, cols]).astype(B16)
        grad_u = dot_nt(cot[...], w_down[side, cols, :]) * slope[side, :, cols].astype(F32)
        grad_u = grad_u.astype(B16)
        slope[side, :, cols] = grad_u
        grad_out[side, 1, :, cols] = dot_nn(b_flip[...], grad_u).astype(B16)

    each(2 * steps, down)
    if early:
        rows = wide // 2
        mine_grads = pl.ds(pl.multiple_of(s * rows, 16), rows)
        away_grads = pl.ds(pl.multiple_of((1 - s) * rows, 16), rows)
        for partner in (sibling, facing):
            pl.semaphore_signal(free_sem, inc=1, device_id=partner, device_id_type=MESH)
        pl.semaphore_wait(free_sem, 2)
        near = {}
        for side, t in ((1, 1), (1, 2), (0, 1), (0, 2)):
            held = h_ref.at[0, pl.ds((side * 2 + t - 1) * rows, rows)]
            near[side, t] = (held, wire.copy(grad_out.at[side, t, away_grads], held, sibling))
            near[side, t][1].start()
    z1[...] = dot_nt(slope[0], w_up[0]) + dot_nt(slope[1], w_up[1])

    def back_norm(grad, unit, inverse, gain):
        scaled = grad * gain
        mean = jnp.mean(scaled, -1, keepdims=True)
        tilt = jnp.mean(scaled * unit, -1, keepdims=True)
        return inverse * (scaled - mean - unit * tilt)

    def add_rows(total, value):
        return total + jnp.sum(value, 0, keepdims=True)

    def second_back(i, total):
        rows = pl.ds(pl.multiple_of(i * rows_at, 16), rows_at)
        grad = z1[rows]
        unit = unit2[rows].astype(F32)
        z = cot[rows].astype(F32) + back_norm(grad, unit, kept(1, rows, heads), gain2_ref[...][None, :])
        z2[rows] = z
        b_ref[rows] = z.astype(B16)
        return add_rows(total, grad * unit)

    zero = jnp.zeros((1, wide), F32)
    gain2_grad = lax.fori_loop(0, length // rows_at, second_back, zero)

    grad_a = b_ref[...]
    flip[0] = transposed(grad_a)
    for side, weight in enumerate((out_own, out_far)):
        grad_out[side, 0, :, pl.ds(3 * third, third)] = dot_nn(flip[0], o_ref[side]).astype(B16)
        do_ref[side] = dot_nt(grad_a, weight[...]).astype(B16)

    if early:
        across = {}
        for t in (1, 2):
            held, copy = near[1, t]
            copy.wait()
            held[...] = (held[...].astype(F32) + grad_out[1, t, mine_grads].astype(F32)).astype(B16)
            got = h_ref.at[1, pl.ds((t - 1) * rows, rows)]
            across[t] = (got, wire.copy(held, got, facing))
            across[t][1].start()

    def attend_back_side(side):
        for index, (start, size) in enumerate(chunks_of(length, 256)):
            rows = pl.ds(start, size)
            for feats, heads in ((pair, (0, 1)), (lone, (2,))):
                q = q_ref[side, rows, feats]
                do = do_ref[side, rows, feats].astype(F32)
                both = do * o_ref[side, rows, feats].astype(F32)
                k = keys[side, :, feats]
                v = values[side, :, feats]
                dq = []
                for head in heads:
                    over_sum = kept(side, rows, head)
                    if len(heads) == 2:
                        lanes = slice(head * HEAD, (head + 1) * HEAD)
                        mine = jnp.where(masks[head], both, 0.0)
                        do_head = jnp.where(masks[head], do, 0.0)
                    else:
                        lanes = slice(0, HEAD)
                        mine, do_head = both, do
                    delta = jnp.sum(mine, -1, keepdims=True) * over_sum
                    do_head = (do_head * over_sum).astype(B16)
                    raised = probs[side, head, rows]
                    ds = (raised.astype(F32) * (dot_nt(do_head, v) - delta)).astype(B16)
                    dq.append(dot_nn(ds, k))
                    dv_part = dot_tn(do_head[:, lanes], raised)
                    dk_part = dot_tn(q[:, lanes], ds)
                    at = pl.ds(head * HEAD, HEAD)
                    if index:
                        dv_part = dv_part + dvt[at]
                        dk_part = dk_part + dkt[at]
                    dvt[at] = dv_part
                    dkt[at] = dk_part
                dq = jnp.where(masks[0], dq[0], dq[1]) if len(heads) == 2 else dq[0]
                q_ref[side, rows, feats] = (dq * scale).astype(B16)
        for held, out in ((dkt, keys), (dvt, values)):
            for feats, at in ((pair, pl.ds(0, 2 * HEAD)), (lone, pl.ds(2 * HEAD, HEAD))):
                out[side, :, feats] = jnp.transpose(held[at]).astype(B16)

    each(2, attend_back_side)
    far_rows = pl.ds(length, length)
    kv_back = [
        [
            wire.copy(held.at[side, far_rows], got_kv.at[slot, side], sibling)
            for side in range(2)
        ]
        for slot, held in enumerate((keys, values))
    ]
    for copies in kv_back:
        for copy in copies:
            copy.start()
    if early:
        def stage(slot, halves, out, sem):
            lanes = pl.ds(0, out.shape[1])
            for owner in range(8):
                a, b = Chip.place(owner // 2)
                rows = pl.ds(48 * (4 * (owner % 2) + 2 * a + b), 48)
                piece = jnp.concatenate([half[24 * owner : 24 * owner + 24] for half in halves], 0)
                piece = jnp.pad(piece, ((0, 0), (0, out.shape[1] - piece.shape[1])))
                probs[0, slot, rows, lanes] = piece.astype(B16)
            return fetch(probs.at[0, slot, pl.ds(0, wide), lanes], out, sem)

        totals = []
        for t in (1, 2):
            held, copy = near[0, t]
            copy.wait()
            across[t][1].wait()
            totals.append(
                held[...].astype(F32)
                + grad_out[0, t, mine_grads].astype(F32)
                + across[t][0][...].astype(F32)
            )
        stores = [stage(2, totals, mlp_out, local_sem.at[1])]

    a_flip = flip.at[0]
    a_flip[...] = transposed(a_ref[...])
    total = None
    for slot in range(3):
        for side, weight in enumerate((qkv_own, qkv_far)):
            if slot:
                kv_back[slot - 1][side].wait()
                own = (keys, values)[slot - 1][side, mine_rows].astype(F32)
                grad = (own + got_kv[slot - 1, side].astype(F32)).astype(B16)
            else:
                grad = q_ref[side]
            grad_out[side, 0, :, pl.ds(slot * third, third)] = dot_nn(a_flip[...], grad).astype(B16)
            part = dot_nn(grad, weight[slot])
            total = part if total is None else total + part
    z1[...] = total
    if early:
        attn_pairs = []
        for side in (1, 0):
            held = h_ref.at[1, pl.ds((2 + side) * rows, rows)]
            copy = wire.copy(grad_out.at[side, 0, away_grads], held, sibling)
            copy.start()
            attn_pairs.append((held, copy))
    @pl.when(stays)
    def _():
        route_local.wait()
        route_near.wait_send()
        route_over.wait_recv()

    @pl.when(jnp.logical_not(stays))
    def _():
        route_over.wait_send()
        route_far.wait_send()
        route_near.wait_recv()
        route_far.wait_recv()

    def first_back(i, totals):
        rows = pl.ds(pl.multiple_of(i * rows_at, 16), rows_at)
        grad = z1[rows]
        unit = unit1[rows].astype(F32)
        z = z2[rows] + back_norm(grad, unit, kept(0, rows, heads), gain1_ref[...][None, :])
        b_ref[rows] = z.astype(B16)
        dec_out[0, rows] = z[:, :third].astype(B16)
        dec_out[1, rows] = z[:, third:].astype(B16)
        ids = lax.broadcasted_iota(jnp.int32, (rows_at, 1), 0) + (base + i * rows_at)
        seen = jnp.sum(jnp.where(cells_row == ids, 1.0, 0.0), -1, keepdims=True)
        return add_rows(totals[0], grad * unit), add_rows(totals[1], (1.0 - seen) * z)

    gain1_grad, mask_grad = lax.fori_loop(0, length // rows_at, first_back, (zero, zero))
    if not early:
        stores = [fetch(dec_out, pos_out, local_sem.at[0])]
    small_out[0:1] = gain1_grad
    small_out[1:2] = gain2_grad
    small_out[2:3] = mask_grad

    ids = (lax.broadcasted_iota(jnp.int32, (used, length), 1) + base).astype(F32)
    cells_col = jnp.transpose(jnp.broadcast_to(cells_row.astype(F32), (8, used)))[:, 0:1]
    place = jnp.where(cells_col == ids, 1.0, 0.0).astype(B16)
    dvis_mine[...] = dot_nn(place, b_ref[...]).astype(B16)
    dvis_pair = wire.copy(dvis_mine, dvis_near, sibling)
    dvis_over = wire.copy(dvis_mine, dvis_far, facing)
    dvis_cross = wire.copy(dvis_mine, dvis_near, beyond)

    @pl.when(stays)
    def _():
        dvis_over.start()

    @pl.when(jnp.logical_not(stays))
    def _():
        dvis_pair.start()
        dvis_cross.start()

    if early:
        halves = [jnp.transpose(dec_out[half].astype(F32)) for half in range(2)]
        stores.append(stage(0, halves, pos_out, local_sem.at[0]))
        halves = []
        for side, (held, copy) in zip((1, 0), attn_pairs):
            copy.wait()
            halves.insert(0, held[...].astype(F32) + grad_out[side, 0, mine_grads].astype(F32))
        stores.append(stage(1, halves, attn_out, local_sem.at[2]))

    def dvis_sum(first, second):
        dvis_out[...] = (first[...].astype(F32) + second[...].astype(F32)).astype(B16)

    @pl.when(stays)
    def _():
        dvis_pair.wait_recv()
        dvis_sum(dvis_mine, dvis_near)
        dvis_over.wait_send()

    @pl.when(jnp.logical_not(stays))
    def _():
        dvis_over.wait_recv()
        dvis_cross.wait_recv()
        dvis_sum(dvis_far, dvis_near)
        dvis_pair.wait_send()
        dvis_cross.wait_send()

    for copy in stores:
        copy.wait()


def decoder(early, vis, lengths, cells, pos_own, pos_far, mask, gains, weights, cot, enc, ident):
    qkv_own, qkv_far, out_own, up, down = weights
    length, wide = pos_own.shape
    used = vis.shape[0]
    third = wide // 2
    hidden = up.shape[1]
    keys = 2 * length
    heads = third // HEAD
    assert heads == 3 and length % 112 == 0
    whole = pl.BlockSpec(memory_space=VMEM)
    there = pl.BlockSpec(memory_space=pl.ANY)
    grads = (2, 3, wide, hidden)
    outs = [
        (jax.ShapeDtypeStruct((2, length, third), B16), there),
        (jax.ShapeDtypeStruct((used, wide), B16), whole),
        (jax.ShapeDtypeStruct((8, wide), F32), whole),
        (jax.ShapeDtypeStruct((used, enc.shape[1] // 2), B16), there),
    ]
    if early:
        lanes = -(-length // 128) * 128
        outs += [
            (jax.ShapeDtypeStruct((wide, lanes), B16), there),
            (jax.ShapeDtypeStruct((wide, hidden), B16), there),
            (jax.ShapeDtypeStruct((wide, hidden), B16), there),
        ]
    else:
        outs += [
            (jax.ShapeDtypeStruct((2, length, third), B16), there),
            (jax.ShapeDtypeStruct(grads, B16), whole),
        ]
    return pl.pallas_call(
        functools.partial(dec_kernel, early),
        out_shape=[item for item, _ in outs],
        in_specs=[whole, pl.BlockSpec(memory_space=pltpu.SMEM), whole]
        + [there] * 2
        + [whole] * 6
        + [there] * 4,
        out_specs=[spec for _, spec in outs],
        scratch_shapes=[VMEM(grads, B16)] * early
        + [
            VMEM((2, length, third), B16),
            VMEM(out_own.shape, B16),
            VMEM((2, wide, hidden), B16),
            VMEM((2, hidden, wide), B16),
            VMEM((length, wide), B16),
            VMEM((length, wide), F32),
            VMEM((length, wide), B16),
            VMEM((length, wide), B16),
            VMEM((2, length, third), B16),
            VMEM((2, keys, third), B16),
            VMEM((2, keys, third), B16),
            VMEM((2, heads, length, keys), B16),
            VMEM((2, length, 128), F32),
            VMEM((2, length, third), B16),
            VMEM((length, wide), B16),
            VMEM((length, wide), B16),
            VMEM((2, length, hidden), B16),
            VMEM((2, length, hidden), B16),
            VMEM((length, wide), F32),
            VMEM((2, length, third), B16),
            VMEM((2, wide, length), B16),
            VMEM((third, keys), F32),
            VMEM((third, keys), F32),
            VMEM((2, 2, length, third), B16),
            VMEM((used, wide), B16),
            VMEM((used, wide), B16),
            VMEM((used, wide), B16),
            pltpu.SemaphoreType.REGULAR,
            pltpu.SemaphoreType.DMA((7,)),
            pltpu.SemaphoreType.DMA((40,)),
            pltpu.SemaphoreType.DMA((40,)),
        ],
        compiler_params=pltpu.CompilerParams(
            collective_id=ident, has_side_effects=True, vmem_limit_bytes=int(63.9 * 1024) * 1024
        ),
        name="decoder",
    )(
        vis,
        lengths,
        cells,
        pos_own,
        pos_far,
        mask,
        gains[0],
        gains[1],
        qkv_own,
        qkv_far,
        out_own,
        up,
        down,
        cot,
        enc,
    )


def pack(grad, owners):
    rows, cols = grad.shape
    own = rows // owners
    fold = 1
    while own * fold % 16:
        fold *= 2
    grad = grad.astype(B16).reshape(owners, own, fold, cols // fold)
    return jnp.swapaxes(grad, 1, 2).reshape(owners, fold * own, cols // fold)


def unpack(piece, own):
    fold = piece.shape[0] // own
    return jnp.swapaxes(piece.reshape(fold, own, -1), 0, 1).reshape(own, -1)


def pick(pair, index):
    return lax.dynamic_index_in_dim(pair, index, 0, keepdims=False)


def enc_kernel(*refs):
    (
        length_ref, tok_hbm, qkv_hbm, out_hbm, up_hbm, down_hbm, bridge_ref, gain1_ref, gain2_ref,
        pos_hbm, dqkv_hbm,
        vis_out, dqkv_far, pos_far, enc_ref, unit1, unit2, stats, a_ref, triple, probs, o_ref, b_ref,
        slope, h_ref,
        x_ref, qkv, w_out, w_up, w_down, z2, part_ref, part_far, pos_full, pos_half,
        local_sem, send_sem, recv_sem,
    ) = refs
    s, d, m = place_of()
    sibling, facing = (1 - s, d, m), (s, d, 1 - m)
    stays = s == m
    used, wide = x_ref.shape
    half = tok_hbm.shape[1]
    rest = used - half
    wire = Wire(send_sem, recv_sem)

    y = lax.rem(d, 2)
    beside = (s, d + 1 - 2 * y, m)

    greet([sibling, facing, beside])
    first, last = pl.ds(0, half), pl.ds(half, rest)
    tok_first = wire.copy(tok_hbm.at[s], x_ref.at[first], facing)
    tok_last = wire.copy(tok_hbm.at[s, pl.ds(0, rest)], x_ref.at[last], facing)
    own_first = pltpu.make_async_copy(tok_hbm.at[s], x_ref.at[first], local_sem.at[0])
    own_last = pltpu.make_async_copy(
        tok_hbm.at[s, pl.ds(0, rest)], x_ref.at[last], local_sem.at[0]
    )

    @pl.when(m == 0)
    def _():
        tok_first.start()
        own_first.start()

    @pl.when(m == 1)
    def _():
        tok_last.start()
        own_last.start()

    loads = [
        fetch(hbm, held, local_sem.at[i + 1])
        for i, (hbm, held) in enumerate(
            ((qkv_hbm, qkv), (out_hbm, w_out), (up_hbm, w_up), (down_hbm, w_down))
        )
    ]
    pos_load = fetch(pos_hbm, pos_full, local_sem.at[5])
    size = dqkv_hbm.shape[1] // 2
    mine = (slice(None), pl.ds(s * size, size))
    over = wire.copy(dqkv_hbm.at[mine], dqkv_far.at[mine], facing)
    share = wire.copy(dqkv_far.at[mine], dqkv_far.at[mine], sibling)

    low = pos_hbm.shape[0] // 32 * 16
    pos_parts = [pl.ds(0, low), pl.ds(low, pos_hbm.shape[0] - low)]
    pos_over = [wire.copy(pos_half.at[part], pos_far.at[part], facing) for part in pos_parts]
    pos_trade = [wire.copy(pos_far.at[part], pos_far.at[part], beside) for part in pos_parts]

    def by_place(on_stays, act):
        for part in range(2):

            @pl.when(jnp.logical_and(stays if on_stays else jnp.logical_not(stays), y == part))
            def _(part=part):
                act(part)

    @pl.when(m == 0)
    def _():
        own_first.wait()
        tok_first.wait_send()
        tok_last.wait_recv()

    @pl.when(m == 1)
    def _():
        own_last.wait()
        tok_last.wait_send()
        tok_first.wait_recv()

    over.start()
    pos_load.wait()

    def send_positions(part):
        pos_half[pos_parts[part]] = pos_full[pos_parts[part]].astype(B16)
        pos_over[part].start()

    by_place(True, send_positions)

    lane = lax.broadcasted_iota(jnp.int32, (1, 128), 1)

    unit, inverse = norm_of(x_ref[...].astype(F32))
    unit1[...] = unit
    stats[...] = jnp.where(lane == 0, inverse, 0.0)
    a = (unit * gain1_ref[...][None, :]).astype(B16)
    a_ref[...] = a
    loads[0].wait()
    for slot in range(3):
        triple[slot] = dot_nn(a, qkv[slot]).astype(B16)

    valid = lax.broadcasted_iota(jnp.int32, (1, used), 1) < length_ref[s]
    masks = head_masks()
    for pair in range(triple.shape[2] // (2 * HEAD)):
        feats = pl.ds(pair * 2 * HEAD, 2 * HEAD)
        q, k, v = (triple[slot, :, feats] for slot in range(3))
        halves = []
        for head in range(2):
            scores = dot_nt(jnp.where(masks[head], q, 0), k) * HEAD**-0.5
            scores = jnp.where(valid, scores, NEG)
            raised = jnp.exp(scores - jnp.max(scores, -1, keepdims=True))
            p = (raised / jnp.sum(raised, -1, keepdims=True)).astype(B16)
            probs[2 * pair + head] = p
            halves.append(dot_nn(p, v))
        o_ref[:, feats] = jnp.where(masks[0], halves[0], halves[1]).astype(B16)

    loads[1].wait()
    part = dot_nn(o_ref[...], w_out[...])
    part_ref[0] = part.astype(B16)
    attn = wire.copy(part_ref.at[0], part_far.at[0], facing)
    attn.start()
    z2[...] = x_ref[...].astype(F32) + part

    attn.wait()
    z = z2[...] + part_far[0].astype(F32)
    z2[...] = z
    unit, inverse = norm_of(z)
    unit2[...] = unit
    stats[...] = jnp.where(lane == 1, inverse, stats[...])
    b = (unit * gain2_ref[...][None, :]).astype(B16)
    b_ref[...] = b
    loads[2].wait()
    step = 512

    def up(i):
        cols = pl.ds(pl.multiple_of(i * step, step), step)
        u = dot_nn(b_ref[...], w_up[:, cols])
        phi = 0.5 + 0.5 * lax.erf(u * 0.5**0.5)
        h_ref[:, cols] = (u * phi).astype(B16)
        bell = jnp.exp(u * u * -0.5) * (0.5 / jnp.pi) ** 0.5
        slope[:, cols] = (phi + u * bell).astype(B16)

    each(w_up.shape[1] // step, up)

    over.wait()
    share.start()

    def trade_positions(part):
        pos_over[part].wait_recv()
        pos_trade[part].start()

    by_place(False, trade_positions)
    loads[3].wait()
    part = dot_nn(h_ref[...], w_down[...])
    z2[...] = z2[...] + part
    part_ref[1] = part.astype(B16)
    mlp = wire.copy(part_ref.at[1], part_far.at[1], facing)
    vis_near = wire.copy(vis_out, vis_out, sibling)

    @pl.when(stays)
    def _():
        mlp.wait_recv()
        enc = (z2[...] + part_far[1].astype(F32)).astype(B16)
        enc_ref[...] = enc
        vis_out[...] = dot_nn(enc, bridge_ref[...]).astype(B16)
        vis_near.start()

    @pl.when(jnp.logical_not(stays))
    def _():
        mlp.start()
        enc_ref[...] = jnp.zeros(enc_ref.shape, B16)

    @pl.when(stays)
    def _():
        vis_near.wait_send()

    @pl.when(jnp.logical_not(stays))
    def _():
        mlp.wait_send()
        vis_near.wait_recv()

    def finish_positions(part):
        pos_trade[part].wait_send()
        pos_trade[1 - part].wait_recv()

    by_place(True, lambda part: pos_over[part].wait_send())
    by_place(False, finish_positions)
    share.wait()


def encoder(lengths, tokens, weights, bridge, gains, pos, dqkv, used, ident):
    qkv, out, up, down = weights
    wide = tokens.shape[2]
    feats = qkv.shape[2]
    hidden = up.shape[1]
    whole = pl.BlockSpec(memory_space=VMEM)
    there = pl.BlockSpec(memory_space=pl.ANY)
    shape = jax.ShapeDtypeStruct
    outs = [
        (shape((used, pos.shape[1]), B16), whole),
        (shape(dqkv.shape, B16), there),
        (shape(pos.shape, B16), there),
        (shape((used, wide), B16), whole),
        (shape((used, wide), F32), whole),
        (shape((used, wide), F32), whole),
        (shape((used, 128), F32), whole),
        (shape((used, wide), B16), whole),
        (shape((3, used, feats), B16), whole),
        (shape((feats // HEAD, used, used), B16), whole),
        (shape((used, feats), B16), whole),
        (shape((used, wide), B16), whole),
        (shape((used, hidden), B16), whole),
        (shape((used, hidden), B16), whole),
    ]
    return pl.pallas_call(
        enc_kernel,
        out_shape=[item for item, _ in outs],
        in_specs=[pl.BlockSpec(memory_space=pltpu.SMEM)]
        + [there] * 5
        + [whole] * 3
        + [there] * 2,
        out_specs=[spec for _, spec in outs],
        scratch_shapes=[
            VMEM((used, wide), B16),
            VMEM(qkv.shape, B16),
            VMEM(out.shape, B16),
            VMEM(up.shape, B16),
            VMEM(down.shape, B16),
            VMEM((used, wide), F32),
            VMEM((2, used, wide), B16),
            VMEM((2, used, wide), B16),
            VMEM(pos.shape, F32),
            VMEM(pos.shape, B16),
            pltpu.SemaphoreType.DMA((6,)),
            pltpu.SemaphoreType.DMA((16,)),
            pltpu.SemaphoreType.DMA((16,)),
        ],
        compiler_params=remote_params(ident),
        name="encoder",
    )(
        lengths, tokens, qkv, out, up, down, bridge, gains[0], gains[1],
        pos, dqkv,
    )


def back_kernel(cube, *refs):
    (
        dvis_ref, bridge_ref, gain1_ref, gain2_ref, unit1, unit2, stats, a_ref, triple, probs, o_ref,
        b_ref, slope, h_ref, enc_half, small_dec, qkv_hbm, out_hbm, up_hbm, down_hbm, *refs,
    ) = refs
    if cube:
        (
            pos_hbm, attn_hbm, mlp_hbm,
            tok_out, small_out, enc_out, mlp_out, attn_out, pos_out, bridge_all,
            near, held, box0, box1, box2,
            dec_held, dec_box0, dec_box1, dec_box2, side_held, side_box0, side_box1, side_box2,
            pos_sum, pos_got, attn_sum, attn_got, bridge_near, small_box, grads, bridge_grad, *refs,
        ) = refs
    else:
        tok_out, small_out, grads, bridge_grad, *refs = refs
    (
        qkv, w_out, w_up, w_down, gu, dy, part, part_far, dz, da_ref, do_ref, dqkv, flip, tok_part,
        local_sem, send_sem, recv_sem,
    ) = refs
    s, d, m = place_of()
    sibling, facing = (1 - s, d, m), (s, d, 1 - m)
    stays = s == m
    used, wide = unit1.shape
    feats = o_ref.shape[1]
    hidden = h_ref.shape[1]
    half = tok_part.shape[1]
    rest = used - half
    wire = Wire(send_sem, recv_sem)
    section = wide // 2

    if cube:
        chip = Chip(s, d, m)
        z, y = chip.z, chip.me["y"]
        others = [(s, 2 * lax.rem(z + k, 4) + y, m) for k in (1, 2, 3)]
        greet([sibling, facing, (1 - s, d, 1 - m), chip.near[0]] + others)
    else:
        greet([sibling, facing])

    if cube:
        cells = pos_sum.shape[2]
        pos_lanes = pos_hbm.shape[-1]
        span = attn_hbm.shape[-1]
        blank = (slice(None),) * 4
        early_loads = [
            fetch(hbm, dec_held.at[blank + (pl.ds(first, hbm.shape[-1]),)], local_sem.at[4 + i])
            for i, (hbm, first) in enumerate(
                ((pos_hbm, 0), (attn_hbm, pos_lanes), (mlp_hbm, pos_lanes + span))
            )
        ]
        for copy in early_loads:
            copy.wait()
        orders = ("yab", "ayb", "yab", "yab")
        mlp_orders = (("yab", "ayb"), ("yab", "ayb"), ("ayb", "yab"))
        attn_orders = ("yab", "yab", "ayb", "ayb")
        tiles = (pos_lanes + 2 * span) // 128
        cuts = [128 * (tiles * i // 4) for i in range(5)]
        early_folds = [
            Fold(
                wire, chip, dec_held, (dec_box0, dec_box1, dec_box2), pl.ds(low, high - low), "yab",
                order, False,
            )
            for low, high, order in zip(cuts, cuts[1:], orders)
        ]
        for fold in early_folds:
            fold.start()

    loads = [
        fetch(hbm, held, local_sem.at[i])
        for i, (hbm, held) in enumerate(
            ((down_hbm, w_down), (up_hbm, w_up), (out_hbm, w_out), (qkv_hbm, qkv))
        )
    ]

    def transposed(value):
        return jnp.transpose(value.astype(F32)).astype(B16)

    dvis = dvis_ref[...]
    grad = dot_nt(dvis, bridge_ref[...])
    dy[...] = grad
    dm = grad.astype(B16)
    da_ref[...] = dm
    flip[0] = transposed(dm)
    flip[1] = transposed(b_ref[...])
    bridge_grad[...] = dot_tn(enc_half[...], dvis).astype(B16)
    if cube:
        bridge_rows = bridge_near.shape[0]
        bridge_pair = wire.copy(
            bridge_grad.at[pl.ds(pl.multiple_of((1 - s) * bridge_rows, 16), bridge_rows)],
            bridge_near,
            sibling,
        )
        bridge_pair.start()

    loads[0].wait()
    step = 512
    first_mlp = 4 * feats
    steps = hidden // step
    if cube:
        away_rows = pl.ds(pl.multiple_of((1 - s) * section, 16), section)

        class Group:
            def __init__(self, first, size, orders):
                self.lanes, self.orders = pl.ds(first, size), orders
                self.pair = wire.copy(
                    grads.at[away_rows, self.lanes], near.at[:, self.lanes], sibling
                )
                self.pair.start()

            def start(self):
                self.pair.wait()
                for owner in range(8):
                    rows = pl.ds(48 * owner, 48)
                    from_rows = pl.ds(pl.multiple_of(s * section + 48 * owner, 16), 48)
                    index = (owner % 2,) + Chip.place(owner // 2) + (slice(None), self.lanes)
                    held[index] = near[rows, self.lanes] + grads[from_rows, self.lanes]
                part = self.lanes.size // len(self.orders)
                self.folds = [
                    Fold(
                        wire, chip, held, (box0, box1, box2), pl.ds(self.lanes.start + i * part, part),
                        "yab", order, False,
                    )
                    for i, order in enumerate(self.orders)
                ]
                for fold in self.folds:
                    fold.start()

            def step(self, k):
                for fold in self.folds:
                    fold.step(k)

            def end(self):
                part = self.lanes.size // len(self.folds)
                for i, fold in enumerate(self.folds):
                    enc_out[:, pl.ds(self.lanes.start + i * part, part)] = fold.end()

        mlp_groups = []

    for i in range(steps):
        cols = pl.ds(i * step, step)
        grads[:, pl.ds(first_mlp + 2 * i * step, step)] = dot_nn(flip[0], h_ref[:, cols]).astype(B16)
        grad_u = dot_nt(da_ref[...], w_down[cols, :]) * slope[:, cols].astype(F32)
        grad_u = grad_u.astype(B16)
        gu[:, cols] = grad_u
        grads[:, pl.ds(first_mlp + (2 * i + 1) * step, step)] = dot_nn(flip[1], grad_u).astype(B16)
        if cube:
            mlp_groups.append(Group(first_mlp + 2 * i * step, 2 * step, mlp_orders[i % 3]))
            if i:
                mlp_groups[i - 1].start()

    loads[1].wait()
    grad = dot_nt(gu[...], w_up[...])
    part[...] = grad.astype(B16)
    over = wire.copy(part, part_far.at[0], facing)
    over.start()
    dz[...] = grad
    gain2_grad = jnp.sum(grad * unit2[...], 0, keepdims=True)

    if cube:
        mlp_groups[-1].start()

    def back_norm(grad, unit, inverse, gain):
        scaled = grad * gain
        mean = jnp.mean(scaled, -1, keepdims=True)
        tilt = jnp.mean(scaled * unit, -1, keepdims=True)
        return inverse * (scaled - mean - unit * tilt)

    over.wait()
    whole = dz[...] + part_far[0].astype(F32)
    dz2 = dy[...] + back_norm(whole, unit2[...], stats[:, 1:2], gain2_ref[...][None, :])
    dy[...] = dz2
    grad_a = dz2.astype(B16)
    da_ref[...] = grad_a
    flip[0] = transposed(grad_a)
    loads[2].wait()
    grads[:, pl.ds(3 * feats, feats)] = dot_nn(flip[0], o_ref[...]).astype(B16)
    do_ref[...] = dot_nt(grad_a, w_out[...]).astype(B16)

    if cube:
        out_group = Group(3 * feats, feats, attn_orders[3:])
        bridge_pair.wait()
        narrow = bridge_near.shape[1]
        for at in range(4):
            side_held[Chip.place(at)] = (
                bridge_near[pl.ds(48 * at, 48)]
                + bridge_grad[pl.ds(pl.multiple_of(s * bridge_rows + 48 * at, 16), 48)]
            )
        bridge_fold = Fold(
            wire, chip, side_held, (side_box0, side_box1, side_box2), pl.ds(0, narrow), "ab", "ab", True
        )
        bridge_fold.start()

    masks = head_masks()
    scale = HEAD**-0.5
    for pair in range(feats // (2 * HEAD)):
        at = pl.ds(pair * 2 * HEAD, 2 * HEAD)
        q, k, v = (triple[slot, :, at] for slot in range(3))
        do = do_ref[:, at]
        both = do.astype(F32) * o_ref[:, at].astype(F32)
        parts = []
        for head in range(2):
            delta = jnp.sum(jnp.where(masks[head], both, 0.0), -1, keepdims=True)
            do_head = jnp.where(masks[head], do, 0)
            p = probs[2 * pair + head]
            ds = (p.astype(F32) * (dot_nt(do_head, v) - delta)).astype(B16)
            parts.append((dot_nn(ds, k) * scale, dot_tn(ds, q) * scale, dot_tn(p, do)))
        for slot in range(3):
            dqkv[slot, :, at] = jnp.where(masks[0], parts[0][slot], parts[1][slot]).astype(B16)

    if cube:
        out_group.start()
        for fold in early_folds:
            fold.step(0)
        bridge_fold.step(0)

    flip[1] = transposed(a_ref[...])
    loads[3].wait()
    total = None
    for slot in range(3):
        grads[:, pl.ds(slot * feats, feats)] = dot_nn(flip[1], dqkv[slot]).astype(B16)
        term = dot_nt(dqkv[slot], qkv[slot])
        total = term if total is None else total + term
    part[...] = total.astype(B16)
    dz[...] = total
    gain1_grad = jnp.sum(total * unit1[...], 0, keepdims=True)
    first, last = pl.ds(0, half), pl.ds(half, rest)
    over_first = wire.copy(part.at[first], part_far.at[1, first], facing)
    over_last = wire.copy(part.at[last], part_far.at[1, last], facing)

    @pl.when(m == 0)
    def _():
        over_last.start()

    @pl.when(m == 1)
    def _():
        over_first.start()

    small_out[...] = jnp.zeros(small_out.shape, F32)
    row = 0
    for value in (
        gain1_grad, gain2_grad, small_dec[0:1], small_dec[1:2], small_dec[2:3],
    ):
        for i in range(value.shape[1] // 128):
            small_out[row : row + 1] = value[:, i * 128 : (i + 1) * 128]
            row += 1

    if cube:
        attn_groups = [
            Group(i * feats, feats, (order,)) for i, order in enumerate(attn_orders[:3])
        ]
        small_copies = [
            wire.copy(small_out, small_box.at[i], partner)
            for i, partner in enumerate([sibling, facing] + chip.near)
        ]

        def small_step(i):
            small_copies[i].wait()
            small_out[...] = small_out[...] + small_box[i]
            if i + 1 < len(small_copies):
                small_copies[i + 1].start()

        small_copies[0].start()
        for group in attn_groups:
            group.start()
        bridge_fold.step(1)
        small_step(0)

    def finish(rows, size):
        whole = dz[rows] + part_far[1, rows].astype(F32)
        unit = unit1[rows]
        grad = dy[rows] + back_norm(whole, unit, stats[rows][:, 0:1], gain1_ref[...][None, :])
        for side in range(2):
            tok_part[side, pl.ds(0, size)] = grad[:, side * section : (side + 1) * section]

    @pl.when(m == 0)
    def _():
        over_last.wait_send()
        over_first.wait_recv()
        finish(first, half)

    @pl.when(m == 1)
    def _():
        over_first.wait_send()
        over_last.wait_recv()
        tok_part[...] = jnp.zeros(tok_part.shape, F32)
        finish(last, rest)

    tok_pair = wire.copy(tok_part.at[1 - s], tok_out.at[s], sibling)
    tok_pair.start()
    tok_out[s] = tok_part[s]

    if cube:
        for fold in early_folds:
            fold.step(1)
        for group in mlp_groups:
            group.step(0)
        small_step(1)

        bridge_all[s, z, m] = bridge_fold.end().astype(B16)
        spread = [
            wire.copy(bridge_all.at[s, z, m], bridge_all.at[s, z, m], partner) for partner in others
        ]
        for copy in spread:
            copy.start()

        out_group.step(0)
        for group in attn_groups:
            group.step(0)
        small_step(2)
        for group in mlp_groups:
            group.step(1)

        wholes = jnp.concatenate([fold.end() for fold in early_folds], 1)
        for half_at in range(2):
            piece = wholes[24 * half_at : 24 * half_at + 24]
            pos_sum[half_at] = piece[:, :cells]
            attn_sum[half_at] = piece[:, pos_lanes : pos_lanes + span]
            mlp_out[:, pl.ds(half_at * span, span)] = piece[:, pos_lanes + span :]
        attn_over = wire.copy(attn_sum.at[1], attn_got, facing)
        attn_over.start()
        route_near = wire.copy(pos_sum.at[1 - s], pos_got.at[m], sibling)
        route_over = wire.copy(pos_sum.at[s], pos_got.at[m], facing)
        route_far = wire.copy(pos_sum.at[1 - s], pos_got.at[m], (1 - s, d, 1 - m))

        @pl.when(stays)
        def _():
            route_near.start()
            pos_got[m] = pos_sum[s]

        @pl.when(jnp.logical_not(stays))
        def _():
            route_over.start()
            route_far.start()


        out_group.step(1)
        for copy in spread:
            copy.wait()
        bridge_over = wire.copy(bridge_all.at[s, :, m], bridge_all.at[s, :, m], facing)
        bridge_over.start()
        for group in attn_groups:
            group.step(1)
        small_step(3)
        for group in mlp_groups:
            group.end()
        attn_over.wait()
        attn_out[...] = attn_sum[0] + attn_got[...]

        @pl.when(stays)
        def _():
            route_near.wait_send()
            route_over.wait_recv()

        @pl.when(jnp.logical_not(stays))
        def _():
            route_over.wait_send()
            route_far.wait_send()
            route_near.wait_recv()
            route_far.wait_recv()

        pos_out[...] = pos_got[0] + pos_got[1]
        out_group.end()
        bridge_over.wait()
        bridge_pair_all = wire.copy(bridge_all.at[s], bridge_all.at[s], sibling)
        bridge_pair_all.start()
        small_step(4)
        for group in attn_groups:
            group.end()
        bridge_pair_all.wait()

    tok_pair.wait()


def back(cube, dvis, bridge, gains, saved, small_dec, weights, dec_grads, cells, half, ident):
    unit1, unit2, stats, a, triple, probs, o, b, slope, h, enc_half = saved
    qkv, out, up, down = weights
    used, wide = unit1.shape
    feats, hidden = o.shape[1], h.shape[1]
    cols = 4 * feats + 2 * hidden
    narrow = bridge.shape[1]
    whole = pl.BlockSpec(memory_space=VMEM)
    there = pl.BlockSpec(memory_space=pl.ANY)
    shape = jax.ShapeDtypeStruct
    args = [dvis, bridge, gains[0], gains[1], *saved, small_dec, qkv, out, up, down]
    in_specs = [whole] * 16 + [there] * 4
    outs = [shape((2, half, wide // 2), F32), shape((24, 128), F32)]
    assert 2 * wide + 3 * narrow <= 24 * 128
    grads, bridge_grad = (wide, cols), (wide // 2, narrow)
    scratch = []
    if cube:
        pos, attn, mlp = dec_grads
        span = attn.shape[1]
        args += [
            pos.reshape(2, 2, 2, 48, -1), attn.reshape(2, 2, 2, 48, -1), mlp.reshape(2, 2, 2, 48, -1)
        ]
        in_specs += [there] * 3
        outs += [
            shape((48, cols), F32),
            shape((24, 2 * span), F32),
            shape((24, span), F32),
            shape((24, cells), F32),
            shape((2, 4, 2, 48, narrow), B16),
        ]

        def folded(axes, size):
            return [VMEM((2,) * (axes - k) + (48, size), B16) for k in range(axes + 1)]

        scratch = [
            VMEM((wide // 2, cols), B16),
            *folded(3, cols),
            *folded(3, pos.shape[1] + 2 * span),
            *folded(2, narrow),
            VMEM((48, narrow), B16),
            VMEM((2, 24, cells), F32),
            VMEM((2, 24, cells), F32),
            VMEM((2, 24, span), F32),
            VMEM((24, span), F32),
            VMEM((narrow // 2, narrow), B16),
            VMEM((5, 24, 128), F32),
            VMEM(grads, B16),
            VMEM(bridge_grad, B16),
        ]
    else:
        outs += [shape(grads, B16), shape(bridge_grad, B16)]
    scratch += [
        VMEM(qkv.shape, B16),
        VMEM(out.shape, B16),
        VMEM(up.shape, B16),
        VMEM(down.shape, B16),
        VMEM((used, hidden), B16),
        VMEM((used, wide), F32),
        VMEM((used, wide), B16),
        VMEM((2, used, wide), B16),
        VMEM((used, wide), F32),
        VMEM((used, wide), B16),
        VMEM((used, feats), B16),
        VMEM((3, used, feats), B16),
        VMEM((2, wide, used), B16),
        VMEM((2, half, wide // 2), F32),
        pltpu.SemaphoreType.DMA((14,)),
        pltpu.SemaphoreType.DMA((96,)),
        pltpu.SemaphoreType.DMA((96,)),
    ]
    return pl.pallas_call(
        functools.partial(back_kernel, cube),
        out_shape=outs,
        in_specs=in_specs,
        out_specs=[whole] * len(outs),
        scratch_shapes=scratch,
        compiler_params=remote_params(ident),
        name="encoder_back",
    )(*args)


def finish_kernel(step, *refs):
    decoded, tokens, small, enc, mlp, attn, pos, bridge = refs[:8]
    (
        decoded_out, tokens_out, e_qkv, e_out, e_up, e_down, one_e, two_e, bridge_out, mask_out,
        pos_out, d_qkv, d_out, d_up, d_down, one_d, two_d,
    ) = refs[8:]
    for i in range(2):
        decoded_out[i] = jnp.transpose(decoded[i].astype(F32))
    tokens_out[...] = tokens[...]
    for source, qkv, out in ((enc, e_qkv, e_out), (attn, d_qkv, d_out)):
        cols = qkv.shape[2]
        for slot in range(3):
            qkv[slot] = source[:, pl.ds(slot * cols, cols)]
        out[...] = source[:, pl.ds(3 * cols, cols)]
    first = 4 * e_qkv.shape[2]
    for i in range(e_up.shape[1] // step):
        at = pl.ds(i * step, step)
        e_down[:, at] = enc[:, pl.ds(first + 2 * i * step, step)]
        e_up[:, at] = enc[:, pl.ds(first + (2 * i + 1) * step, step)]
    hidden = d_up.shape[1]
    d_up[...] = mlp[:, :hidden]
    d_down[...] = mlp[:, hidden:]
    pos_out[...] = pos[...]
    own = bridge.shape[3]
    for side in range(2):
        for piece in range(8):
            rows = pl.ds((side * 8 + piece) * own, own)
            bridge_out[rows] = bridge[piece // 4, piece % 4, side].astype(F32)
    row = 0
    for out in (one_e, two_e, one_d, two_d, mask_out):
        for i in range(out.shape[0] // 128):
            out[pl.ds(i * 128, 128)] = small[row]
            row += 1


def finish(shapes, parts, step):
    whole = pl.BlockSpec(memory_space=VMEM)
    return pl.pallas_call(
        functools.partial(finish_kernel, step),
        out_shape=[jax.ShapeDtypeStruct(shape, F32) for shape in shapes],
        in_specs=[whole] * len(parts),
        out_specs=[whole] * len(shapes),
        compiler_params=pltpu.CompilerParams(vmem_limit_bytes=LIMIT),
        name="finish",
    )(*parts)


def per_device(
    tokens,
    clip_lengths,
    clip_cells,
    enc_qkv,
    enc_attn_out,
    enc_up,
    enc_down,
    enc_gain_one,
    enc_gain_two,
    bridge_weight,
    mask_token,
    position_embed,
    dec_qkv,
    dec_attn_out,
    dec_up,
    dec_down,
    dec_gain_one,
    dec_gain_two,
    cotangent,
):
    s, d, m = place_of()
    n = lax.axis_size("dp")
    owners = 2 * n
    cube = n == 8
    dec_wide = position_embed.shape[1]
    half_slots, enc_wide = tokens.shape[2:]
    used = -(-LONGEST // 32) * 32

    e_weights = (jnp.swapaxes(enc_qkv, 0, 1), enc_attn_out, enc_up, enc_down)
    d_qkv = jnp.transpose(dec_qkv, (1, 2, 0))
    vis, d_qkv_far, pos_far, enc, *saved = encoder(
        clip_lengths[:, 0],
        tokens[:, 0],
        e_weights,
        bridge_weight,
        (enc_gain_one, enc_gain_two),
        position_embed,
        d_qkv,
        used,
        1,
    )
    decoded, dvis, dec_small, enc_half, *dec_grads = decoder(
        cube,
        vis,
        clip_lengths[:, 0],
        clip_cells[:, 0],
        position_embed,
        pos_far,
        mask_token,
        (dec_gain_one, dec_gain_two),
        (d_qkv, d_qkv_far, dec_attn_out, dec_up, dec_down),
        cotangent[:, 0],
        enc,
        2,
    )
    tokens_grad, small, *rest = back(
        cube,
        dvis,
        bridge_weight,
        (enc_gain_one, enc_gain_two),
        (*saved, enc_half),
        dec_small,
        e_weights,
        dec_grads,
        position_embed.shape[0],
        half_slots,
        3,
    )
    if cube:
        e_own, d_own = enc_wide // owners, dec_wide // owners
        shapes = [
            (2, decoded.shape[2], decoded.shape[1]),
            tokens_grad.shape,
            (3, e_own, enc_qkv.shape[2]),
            (e_own, enc_attn_out.shape[0]),
            (e_own, enc_up.shape[1]),
            (e_own, enc_down.shape[0]),
            (enc_wide,),
            (enc_wide,),
            (enc_wide, dec_wide),
            (dec_wide,),
            (d_own, position_embed.shape[0]),
            (3, d_own, dec_qkv.shape[2]),
            (d_own, dec_attn_out.shape[0]),
            (d_own, dec_up.shape[1]),
            (d_own, dec_down.shape[0]),
            (dec_wide,),
            (dec_wide,),
        ]
        outs = list(finish(shapes, (decoded, tokens_grad, small, *rest), 512))
        outs[0] = jnp.swapaxes(outs[0], 1, 2)[:, None]
        outs[1] = outs[1][:, None]
        for i in (2, 11):
            outs[i] = jnp.swapaxes(outs[i], 0, 1)
        for i in (3, 5, 10, 12, 14):
            outs[i] = outs[i].T
        return tuple(outs)
    else:
        grads, bridge = rest
        pos_parts, dec_grads = dec_grads
        enc_final = unpack(scatter(pack(grads, owners)[None], 11), enc_wide // owners)
        packed = [
            pack(jnp.concatenate([dec_grads[side, t] for t in range(3)], 1), owners)
            for side in range(2)
        ]
        dec_final = unpack(scatter(jnp.stack(packed), 12), dec_wide // owners)
        parts = route(pos_parts, 13).astype(F32)
        packed = pack(jnp.transpose(parts[0] + parts[1]), n)
        zero = jnp.zeros_like(packed)
        packed = jnp.concatenate(
            [jnp.where(s == 0, packed, zero), jnp.where(s == 1, packed, zero)], 0
        )
        pos_final = unpack(scatter(packed[None], 14), dec_wide // owners)
        bridge_own = enc_wide // 2 // owners
        per = -(-small.size // owners)
        small = jnp.pad(small.reshape(-1), (0, per * owners - small.size)).reshape(owners, 1, per)
        rows = -(-(bridge_own + 1) // 16) * 16
        rep = jnp.concatenate(
            [
                bridge.astype(F32).reshape(owners, bridge_own, dec_wide),
                jnp.pad(small, ((0, 0), (0, 0), (0, dec_wide - per))),
                jnp.zeros((owners, rows - bridge_own - 1, dec_wide), F32),
            ],
            1,
        ).astype(B16)
        rep = scatter(rep[None], 15).astype(B16)
        everyone = gather(rep, n, 16).reshape(owners, 2, rows, dec_wide)
        bridge_grad = jnp.swapaxes(everyone[:, :, :bridge_own], 0, 1).reshape(enc_wide, dec_wide)
        small = everyone[:, 0, bridge_own, :per].astype(F32) + everyone[
            :, 1, bridge_own, :per
        ].astype(F32)
    cuts = [enc_wide, 2 * enc_wide, 2 * enc_wide + dec_wide, 2 * enc_wide + 2 * dec_wide]
    small = small.reshape(-1)[: 2 * enc_wide + 3 * dec_wide]
    one_e, two_e, one_d, two_d, mask_grad = jnp.split(small, cuts)

    def split(final, qkv, out, up, step):
        cols = qkv.shape[2]
        first = 3 * cols + out.shape[0]
        second = first + up.shape[1]
        if step:
            mlp = final[:, first:].reshape(final.shape[0], -1, 2, step)
            downs, ups = (mlp[:, :, i].reshape(final.shape[0], -1) for i in range(2))
        else:
            downs, ups = final[:, second:], final[:, first:second]
        return (
            final[:, : 3 * cols].reshape(-1, 3, cols), final[:, 3 * cols : first].T, ups, downs.T
        )

    return (
        decoded.astype(F32)[:, None],
        tokens_grad[:, None],
        *split(enc_final, enc_qkv, enc_attn_out, enc_up, 512),
        one_e,
        two_e,
        bridge_grad.astype(F32),
        mask_grad,
        pos_final.T,
        *split(dec_final, dec_qkv, dec_attn_out, dec_up, 0),
        one_d,
        two_d,
    )


def solution(mesh):
    return jax.shard_map(
        per_device,
        mesh=mesh,
        in_specs=(
            P(None, "dp", "mp", None),
            P(None, "dp"),
            P(None, "dp", None),
            P(None, None, "mp"),
            P("mp", None),
            P(None, "mp"),
            P("mp", None),
            P(),
            P(),
            P(),
            P(),
            P("mp", None),
            P(None, None, "mp"),
            P("mp", None),
            P(None, "mp"),
            P("mp", None),
            P(),
            P(),
            P(None, "dp", "mp", None),
        ),
        out_specs=(
            P(None, "dp", "mp", "section"),
            P(None, "dp", "mp", "section"),
            P(("section", "dp"), None, "mp"),
            P("mp", ("section", "dp")),
            P(("section", "dp"), "mp"),
            P("mp", ("section", "dp")),
            P(),
            P(),
            P(),
            P(),
            P("mp", ("section", "dp")),
            P(("section", "dp"), None, "mp"),
            P("mp", ("section", "dp")),
            P(("section", "dp"), "mp"),
            P("mp", ("section", "dp")),
            P(),
            P(),
        ),
        check_vma=False,
    )
```

```python
import functools
import itertools

import jax
import jax.numpy as jnp
from jax import lax
from jax.experimental import pallas as pl
from jax.experimental.pallas import tpu as pltpu
from jax.sharding import PartitionSpec as P

HEAD = 64
LONGEST = 157
EPS = 1e-06
NEG = -1e30
F32 = jnp.float32
B16 = jnp.bfloat16
MESH = pl.DeviceIdType.MESH
VMEM = pltpu.VMEM
LIMIT = 56 * 1024 * 1024


def place_of():
    return lax.axis_index("section"), lax.axis_index("dp"), lax.axis_index("mp")


def greet(partners):
    barrier = pltpu.get_barrier_semaphore()
    for partner in partners:
        pl.semaphore_signal(barrier, inc=1, device_id=partner, device_id_type=MESH)
    pl.semaphore_wait(barrier, len(partners))


def send(src, dst, send_sem, recv_sem, partner):
    return pltpu.make_async_remote_copy(
        src_ref=src,
        dst_ref=dst,
        send_sem=send_sem,
        recv_sem=recv_sem,
        device_id=partner,
        device_id_type=MESH,
    )


def remote_params(ident):
    return pltpu.CompilerParams(
        collective_id=ident, has_side_effects=True, vmem_limit_bytes=LIMIT
    )


def route_kernel(x_ref, out_ref, send_sem, recv_sem, local_sem):
    s, d, m = place_of()
    greet([(1 - s, d, m), (s, d, 1 - m), (1 - s, d, 1 - m)])
    stays = s == m

    @pl.when(stays)
    def _():
        mine = pltpu.make_async_copy(x_ref.at[s], out_ref.at[m], local_sem)
        mine.start()
        out = send(x_ref.at[1 - s], out_ref.at[m], send_sem.at[0], recv_sem.at[m], (1 - s, d, m))
        out.start()
        mine.wait()
        out.wait_send()

    @pl.when(jnp.logical_not(stays))
    def _():
        near = send(x_ref.at[s], out_ref.at[m], send_sem.at[0], recv_sem.at[m], (s, d, 1 - m))
        far = send(
            x_ref.at[1 - s], out_ref.at[m], send_sem.at[1], recv_sem.at[m], (1 - s, d, 1 - m)
        )
        near.start()
        far.start()
        near.wait_send()
        far.wait_send()

    pltpu.make_async_copy(out_ref.at[1 - m], out_ref.at[1 - m], recv_sem.at[1 - m]).wait()

    @pl.when(jnp.logical_not(stays))
    def _():
        pltpu.make_async_copy(out_ref.at[m], out_ref.at[m], recv_sem.at[m]).wait()


def route(x, ident):
    return pl.pallas_call(
        route_kernel,
        out_shape=jax.ShapeDtypeStruct(x.shape, x.dtype),
        in_specs=[pl.BlockSpec(memory_space=pl.ANY)],
        out_specs=pl.BlockSpec(memory_space=pl.ANY),
        scratch_shapes=[
            pltpu.SemaphoreType.DMA((2,)),
            pltpu.SemaphoreType.DMA((2,)),
            pltpu.SemaphoreType.DMA,
        ],
        compiler_params=remote_params(ident),
        name=f"route_{ident}",
    )(x)


def scatter_kernel(n, across, g_ref, out_ref, near, work, far, over, sems):
    near_send, near_recv, far_send, far_recv, over_send, over_recv = sems
    s, d, m = place_of()
    sibling, facing = (1 - s, d, m), (s, d, 1 - m)
    greet([sibling] + [facing] * across + [(s, lax.rem(d + k, n), m) for k in range(1, n)])
    order = [*range(1, n), 0]
    sides = 1 + across
    first = {}
    for side in reversed(range(sides)):
        for k in order:
            to = lax.rem(d + k, n)
            first[side, k] = send(
                g_ref.at[side, (1 - s) * n + to],
                near.at[side, to],
                near_send.at[side, k],
                near_recv.at[side, k],
                sibling,
            )
            first[side, k].start()

    def summed(side, k):
        to = lax.rem(d + k, n)
        first[side, k].wait()
        return to, g_ref[side, s * n + to].astype(F32) + near[side, to].astype(F32)

    second = {}
    if across:
        for k in order:
            to, part = summed(1, k)
            work[1, to] = part.astype(B16)
            second[k] = send(work.at[1, to], over.at[to], over_send.at[k], over_recv.at[k], facing)
            second[k].start()
    third = []
    for k in order:
        to, part = summed(0, k)
        if across:
            second[k].wait()
            part = part + over[to].astype(F32)
        if k:
            work[0, to] = part.astype(B16)
            copy = send(work.at[0, to], far.at[d], far_send.at[k], far_recv.at[k], (s, to, m))
            copy.start()
            third.append((k, copy))
    for k, copy in third:
        copy.wait()
        part = part + far[lax.rem(d + n - k, n)].astype(F32)
    out_ref[...] = part


def scatter(g, ident):
    sides, owners, rows, cols = g.shape
    n = owners // 2
    across = sides - 1
    kernel = functools.partial(scatter_kernel, n, across)

    def body(g_ref, out_ref, near, work, far, over, *sems):
        kernel(g_ref, out_ref, near, work, far, over, sems)

    pieces = (n, rows, cols)
    return pl.pallas_call(
        body,
        out_shape=jax.ShapeDtypeStruct((rows, cols), F32),
        in_specs=[pl.BlockSpec(memory_space=VMEM)],
        out_specs=pl.BlockSpec(memory_space=VMEM),
        scratch_shapes=[
            VMEM((sides,) + pieces, B16),
            VMEM((sides,) + pieces, B16),
            VMEM(pieces, B16),
            VMEM(pieces if across else (8, 128), B16),
            pltpu.SemaphoreType.DMA((sides, n)),
            pltpu.SemaphoreType.DMA((sides, n)),
            pltpu.SemaphoreType.DMA((n,)),
            pltpu.SemaphoreType.DMA((n,)),
            pltpu.SemaphoreType.DMA((n,)),
            pltpu.SemaphoreType.DMA((n,)),
        ],
        compiler_params=remote_params(ident),
        name=f"scatter_{ident}",
    )(g)


def gather_kernel(n, x_ref, out_ref, local_sem, send_sem, recv_sem):
    s, d, m = place_of()
    steps = [(a, k, b) for k in range(n) for a in range(2) for b in range(2) if a or k or b]

    def partner(step):
        a, k, b = step
        return (lax.rem(s + a, 2), lax.rem(d + k, n), lax.rem(m + b, 2))

    greet([partner(step) for step in steps])
    slot = (s * n + d) * 2 + m
    mine = pltpu.make_async_copy(x_ref, out_ref.at[slot], local_sem)
    mine.start()
    copies = [
        send(x_ref, out_ref.at[slot], send_sem.at[i], recv_sem.at[i], partner(step))
        for i, step in enumerate(steps)
    ]
    for copy in copies:
        copy.start()
    mine.wait()
    for copy in copies:
        copy.wait()


def gather(x, n, ident):
    count = 4 * n
    return pl.pallas_call(
        functools.partial(gather_kernel, n),
        out_shape=jax.ShapeDtypeStruct((count,) + x.shape, x.dtype),
        in_specs=[pl.BlockSpec(memory_space=VMEM)],
        out_specs=pl.BlockSpec(memory_space=VMEM),
        scratch_shapes=[
            pltpu.SemaphoreType.DMA,
            pltpu.SemaphoreType.DMA((count - 1,)),
            pltpu.SemaphoreType.DMA((count - 1,)),
        ],
        compiler_params=remote_params(ident),
        name=f"gather_{ident}",
    )(x)


def dot_nt(a, b):
    return lax.dot_general(a, b, (((1,), (1,)), ((), ())), preferred_element_type=F32)


def dot_nn(a, b):
    return lax.dot_general(a, b, (((1,), (0,)), ((), ())), preferred_element_type=F32)


def dot_tn(a, b):
    return lax.dot_general(a, b, (((0,), (0,)), ((), ())), preferred_element_type=F32)


def chunks_of(length, most=256):
    units = length // 16
    count = -(-length // most)
    cuts = [16 * (units * i // count) for i in range(count)] + [length]
    return [(a, b - a) for a, b in zip(cuts, cuts[1:])]


def head_masks():
    lanes = lax.broadcasted_iota(jnp.int32, (1, 2 * HEAD), 1)
    return (lanes < HEAD, lanes >= HEAD)


def fetch(src, dst, sem):
    copy = pltpu.make_async_copy(src, dst, sem)
    copy.start()
    return copy


class Wire:
    def __init__(self, send_sem, recv_sem):
        self.send_sem, self.recv_sem, self.used = send_sem, recv_sem, 0

    def copy(self, src, dst, partner):
        index = self.used
        self.used += 1
        assert index < self.send_sem.shape[0]
        return send(src, dst, self.send_sem.at[index], self.recv_sem.at[index], partner)


class Chip:
    def __init__(self, s, d, m):
        self.s, self.m = s, m
        z = d // 2
        self.z = z
        self.me = {"y": lax.rem(d, 2), "a": lax.rem(z + z // 2, 2), "b": z // 2}
        self.near = [self.beside(axis) for axis in "yab"]

    @staticmethod
    def z_of(a, b):
        return lax.rem(a + b, 2) + 2 * b

    @staticmethod
    def place(z):
        return (z + z // 2) % 2, z // 2

    def beside(self, axis):
        at = dict(self.me, **{axis: 1 - self.me[axis]})
        return (self.s, 2 * self.z_of(at["a"], at["b"]) + at["y"], self.m)

    def own_rows(self, value, out):
        for y in range(2):

            @pl.when(self.me["y"] == y)
            def _(y=y):
                out[...] = value[24 * y : 24 * y + 24]


class Fold:
    def __init__(self, wire, chip, held, boxes, lanes, axes, order, last):
        self.rounds = []
        kept = {}
        for k, axis in enumerate(order):

            def part(value):
                chosen = dict(kept, **{axis: value})
                index = tuple(chosen.get(name, slice(None)) for name in axes)
                return held.at[index + (slice(None), lanes)]

            box = boxes[k].at[(slice(None),) * (len(axes) - k) + (lanes,)]
            copy = wire.copy(part(1 - chip.me[axis]), box, chip.beside(axis))
            self.rounds.append((copy, part(chip.me[axis]), box))
            kept[axis] = chip.me[axis]
        if last:
            mine = held.at[tuple(kept[name] for name in axes) + (slice(None), lanes)]
            box = boxes[-1].at[:, lanes]
            self.rounds.append((wire.copy(mine, box, chip.beside("y")), mine, box))

    def start(self):
        self.rounds[0][0].start()

    def step(self, k):
        copy, mine, box = self.rounds[k]
        copy.wait()
        mine[...] = mine[...] + box[...]
        self.rounds[k + 1][0].start()

    def end(self):
        copy, mine, box = self.rounds[-1]
        copy.wait()
        return mine[...].astype(F32) + box[...].astype(F32)


def norm_of(z):
    centre = z - jnp.mean(z, -1, keepdims=True)
    inverse = lax.rsqrt(jnp.mean(centre * centre, -1, keepdims=True) + EPS)
    return centre * inverse, inverse


def each(count, body):
    def step(i, carry):
        body(i)
        return carry

    lax.fori_loop(0, count, step, 0)


def softmax_fwd(q, k, v):
    scores = dot_nt(q, k)
    raised = jnp.exp(scores - jnp.max(scores, -1, keepdims=True))
    scale = 1.0 / jnp.sum(raised, -1, keepdims=True)
    raised = raised.astype(B16)
    return raised, scale, dot_nn(raised, v) * scale


def dec_kernel(early, *refs):
    (
        vis_ref, lengths, cells_ref, pos_own, pos_far, mask_ref, gain1_ref, gain2_ref,
        qkv_own, qkv_far, out_own, up_hbm, down_hbm, cot_hbm, enc_hbm,
        routed, dvis_out, small_out, enc_half, *refs,
    ) = refs
    if early:
        pos_out, attn_out, mlp_out, grad_out, *refs = refs
    else:
        pos_out, grad_out, *refs = refs
    (
        dec_out, out_far, w_up, w_down, cot, z1, unit1, a_ref, q_ref, keys, values, probs, stats,
        o_ref, unit2, b_ref, h_ref, slope, z2, do_ref, flip, dkt, dvt, got_kv,
        dvis_mine, dvis_near, dvis_far, free_sem, local_sem, send_sem, recv_sem,
    ) = refs
    s, d, m = place_of()
    sibling, facing = (1 - s, d, m), (s, d, 1 - m)
    stays = s == m
    length, wide = z1.shape
    third = wide // 2
    heads = third // HEAD
    wire = Wire(send_sem, recv_sem)
    scale = HEAD**-0.5

    beyond = (1 - s, d, 1 - m)
    greet([sibling, facing, beyond])

    loads = [
        pltpu.make_async_copy(up_hbm, w_up.at[0], local_sem.at[0]),
        pltpu.make_async_copy(down_hbm, w_down.at[0], local_sem.at[1]),
    ]
    pos_loads = [fetch(pos_own, z1, local_sem.at[3]), fetch(pos_far, b_ref, local_sem.at[5])]
    cot_load = pltpu.make_async_copy(cot_hbm.at[m], cot, local_sem.at[2])
    for load in loads:
        load.start()
    over, share = [], []
    for own, held in ((out_own, out_far), (up_hbm, w_up.at[1]), (down_hbm, w_down.at[1])):
        half = own.shape[0] // 2
        mine = pl.ds(s * half, half)
        over.append(wire.copy(own.at[mine], held.at[mine], facing))
        share.append(wire.copy(held.at[mine], held.at[mine], sibling))
        over[-1].start()
    cot_over = wire.copy(cot_hbm.at[1 - m], cot, facing)
    mid = enc_hbm.shape[1] // 2
    enc_parts = [enc_hbm.at[:, pl.ds(pl.multiple_of(k * mid, 128), mid)] for k in (m, 1 - m)]
    enc_load = pltpu.make_async_copy(enc_parts[0], enc_half, local_sem.at[6])
    enc_over = wire.copy(enc_parts[1], enc_half, facing)

    @pl.when(stays)
    def _():
        cot_load.start()
        cot_over.start()
        enc_load.start()
        enc_over.start()

    lane = lax.broadcasted_iota(jnp.int32, (1, 128), 1)

    def keep(plane, rows, column, value):
        stats[plane, rows] = jnp.where(lane == column, value, stats[plane, rows])

    def kept(plane, rows, column):
        return stats[plane, rows][:, column : column + 1]

    for copy in pos_loads:
        copy.wait()
    rows_at = 112
    base = s * length

    used = vis_ref.shape[0]
    slots = lax.broadcasted_iota(jnp.int32, (1, used), 1)
    cells_row = jnp.where(m == 0, cells_ref[0:1, :used], cells_ref[1:2, :used])
    cells_row = jnp.where(slots < lengths[m], cells_row, -1)

    def fill(i):
        rows = pl.ds(pl.multiple_of(i * rows_at, 16), rows_at)
        ids = lax.broadcasted_iota(jnp.int32, (rows_at, 1), 0) + (base + i * rows_at)
        place = jnp.where(cells_row == ids, 1.0, 0.0)
        unseen = 1.0 - jnp.sum(place, -1, keepdims=True)
        pos = jnp.where(stays, z1[rows], b_ref[rows].astype(F32))
        z = dot_nn(place.astype(B16), vis_ref[...]) + unseen * mask_ref[...][None, :] + pos
        unit, inverse = norm_of(z)
        z1[rows] = z
        unit1[rows] = unit.astype(B16)
        keep(0, rows, heads, inverse)
        a_ref[rows] = (unit * gain1_ref[...][None, :]).astype(B16)

    each(length // rows_at, fill)

    a = a_ref[...]
    mine_rows = pl.ds(0, length)
    kv_copies = []
    for side, weight in enumerate((qkv_own, qkv_far)):
        keys[side, mine_rows] = dot_nt(a, weight[1]).astype(B16)
        values[side, mine_rows] = dot_nt(a, weight[2]).astype(B16)
        for held in (keys, values):
            copy = wire.copy(
                held.at[side, mine_rows], held.at[side, pl.ds(length, length)], sibling
            )
            copy.start()
            kv_copies.append(copy)
    for side, weight in enumerate((qkv_own, qkv_far)):
        q_ref[side] = (dot_nt(a, weight[0]).astype(B16).astype(F32) * scale).astype(B16)
    for copy in kv_copies:
        copy.wait()

    masks = head_masks()
    pair = pl.ds(0, 2 * HEAD)
    lone = pl.ds(2 * HEAD, HEAD)

    def attend_side(side):
        for start, size in chunks_of(length, 400):
            rows = pl.ds(start, size)
            halves = []
            for head in range(2):
                q = jnp.where(masks[head], q_ref[side, rows, pair], 0)
                raised, over_sum, o = softmax_fwd(q, keys[side, :, pair], values[side, :, pair])
                probs[side, head, rows] = raised
                keep(side, rows, head, over_sum)
                halves.append(o)
            o_ref[side, rows, pair] = jnp.where(masks[0], halves[0], halves[1]).astype(B16)
            raised, over_sum, o = softmax_fwd(
                q_ref[side, rows, lone], keys[side, :, lone], values[side, :, lone]
            )
            probs[side, 2, rows] = raised
            keep(side, rows, 2, over_sum)
            o_ref[side, rows, lone] = o.astype(B16)

    each(2, attend_side)

    for copy, other in zip(over, share):
        copy.wait()
        other.start()
    share[0].wait()

    z2[...] = z1[...] + dot_nn(o_ref[0], out_own[...]) + dot_nn(o_ref[1], out_far[...])

    def second(i):
        rows = pl.ds(pl.multiple_of(i * rows_at, 16), rows_at)
        unit, inverse = norm_of(z2[rows])
        unit2[rows] = unit.astype(B16)
        keep(1, rows, heads, inverse)
        b_ref[rows] = (unit * gain2_ref[...][None, :]).astype(B16)

    each(length // rows_at, second)
    for load in loads:
        load.wait()
    for copy in share[1:]:
        copy.wait()

    step = 256
    steps = w_up.shape[2] // step

    def hidden_at(i):
        return i // steps, pl.ds(pl.multiple_of((i % steps) * step, step), step)

    def up(i):
        side, cols = hidden_at(i)
        u = dot_nn(b_ref[...], w_up[side, :, cols])
        phi = 0.5 + 0.5 * lax.erf(u * 0.5**0.5)
        h_ref[side, :, cols] = (u * phi).astype(B16)
        bell = jnp.exp(u * u * -0.5) * (0.5 / jnp.pi) ** 0.5
        slope[side, :, cols] = (phi + u * bell).astype(B16)

    each(2 * steps, up)

    def cut(value, out):
        out[0] = value[:, :third].astype(B16)
        out[1] = value[:, third:].astype(B16)

    cut(z2[...] + dot_nn(h_ref[0], w_down[0]) + dot_nn(h_ref[1], w_down[1]), dec_out)

    route_local = pltpu.make_async_copy(dec_out.at[s], routed.at[m], local_sem.at[4])
    route_near = wire.copy(dec_out.at[1 - s], routed.at[m], sibling)
    route_over = wire.copy(dec_out.at[s], routed.at[m], facing)
    route_far = wire.copy(dec_out.at[1 - s], routed.at[m], beyond)

    @pl.when(stays)
    def _():
        route_local.start()
        route_near.start()

    @pl.when(jnp.logical_not(stays))
    def _():
        route_over.start()
        route_far.start()

    @pl.when(stays)
    def _():
        cot_load.wait()
        cot_over.wait_send()
        enc_load.wait()
        enc_over.wait_send()

    @pl.when(jnp.logical_not(stays))
    def _():
        cot_over.wait_recv()
        enc_over.wait_recv()

    def transposed(value):
        return jnp.transpose(value.astype(F32)).astype(B16)

    cot_flip = flip.at[0]
    b_flip = flip.at[1]
    cot_flip[...] = transposed(cot[...])
    b_flip[...] = transposed(b_ref[...])

    def down(i):
        side, cols = hidden_at(i)
        grad_out[side, 2, :, cols] = dot_nn(cot_flip[...], h_ref[side, :, cols]).astype(B16)
        grad_u = dot_nt(cot[...], w_down[side, cols, :]) * slope[side, :, cols].astype(F32)
        grad_u = grad_u.astype(B16)
        slope[side, :, cols] = grad_u
        grad_out[side, 1, :, cols] = dot_nn(b_flip[...], grad_u).astype(B16)

    each(2 * steps, down)
    if early:
        rows = wide // 2
        mine_grads = pl.ds(pl.multiple_of(s * rows, 16), rows)
        away_grads = pl.ds(pl.multiple_of((1 - s) * rows, 16), rows)
        for partner in (sibling, facing):
            pl.semaphore_signal(free_sem, inc=1, device_id=partner, device_id_type=MESH)
        pl.semaphore_wait(free_sem, 2)
        near = {}
        for side, t in ((1, 1), (1, 2), (0, 1), (0, 2)):
            held = h_ref.at[0, pl.ds((side * 2 + t - 1) * rows, rows)]
            near[side, t] = (held, wire.copy(grad_out.at[side, t, away_grads], held, sibling))
            near[side, t][1].start()
    z1[...] = dot_nt(slope[0], w_up[0]) + dot_nt(slope[1], w_up[1])

    def back_norm(grad, unit, inverse, gain):
        scaled = grad * gain
        mean = jnp.mean(scaled, -1, keepdims=True)
        tilt = jnp.mean(scaled * unit, -1, keepdims=True)
        return inverse * (scaled - mean - unit * tilt)

    def add_rows(total, value):
        return total + jnp.sum(value, 0, keepdims=True)

    def second_back(i, total):
        rows = pl.ds(pl.multiple_of(i * rows_at, 16), rows_at)
        grad = z1[rows]
        unit = unit2[rows].astype(F32)
        z = cot[rows].astype(F32) + back_norm(grad, unit, kept(1, rows, heads), gain2_ref[...][None, :])
        z2[rows] = z
        b_ref[rows] = z.astype(B16)
        return add_rows(total, grad * unit)

    zero = jnp.zeros((1, wide), F32)
    gain2_grad = lax.fori_loop(0, length // rows_at, second_back, zero)

    grad_a = b_ref[...]
    flip[0] = transposed(grad_a)
    for side, weight in enumerate((out_own, out_far)):
        grad_out[side, 0, :, pl.ds(3 * third, third)] = dot_nn(flip[0], o_ref[side]).astype(B16)
        do_ref[side] = dot_nt(grad_a, weight[...]).astype(B16)

    if early:
        across = {}
        for t in (1, 2):
            held, copy = near[1, t]
            copy.wait()
            held[...] = (held[...].astype(F32) + grad_out[1, t, mine_grads].astype(F32)).astype(B16)
            got = h_ref.at[1, pl.ds((t - 1) * rows, rows)]
            across[t] = (got, wire.copy(held, got, facing))
            across[t][1].start()

    def attend_back_side(side):
        for index, (start, size) in enumerate(chunks_of(length, 256)):
            rows = pl.ds(start, size)
            for feats, heads in ((pair, (0, 1)), (lone, (2,))):
                q = q_ref[side, rows, feats]
                do = do_ref[side, rows, feats].astype(F32)
                both = do * o_ref[side, rows, feats].astype(F32)
                k = keys[side, :, feats]
                v = values[side, :, feats]
                dq = []
                for head in heads:
                    over_sum = kept(side, rows, head)
                    if len(heads) == 2:
                        lanes = slice(head * HEAD, (head + 1) * HEAD)
                        mine = jnp.where(masks[head], both, 0.0)
                        do_head = jnp.where(masks[head], do, 0.0)
                    else:
                        lanes = slice(0, HEAD)
                        mine, do_head = both, do
                    delta = jnp.sum(mine, -1, keepdims=True) * over_sum
                    do_head = (do_head * over_sum).astype(B16)
                    raised = probs[side, head, rows]
                    ds = (raised.astype(F32) * (dot_nt(do_head, v) - delta)).astype(B16)
                    dq.append(dot_nn(ds, k))
                    dv_part = dot_tn(do_head[:, lanes], raised)
                    dk_part = dot_tn(q[:, lanes], ds)
                    at = pl.ds(head * HEAD, HEAD)
                    if index:
                        dv_part = dv_part + dvt[at]
                        dk_part = dk_part + dkt[at]
                    dvt[at] = dv_part
                    dkt[at] = dk_part
                dq = jnp.where(masks[0], dq[0], dq[1]) if len(heads) == 2 else dq[0]
                q_ref[side, rows, feats] = (dq * scale).astype(B16)
        for held, out in ((dkt, keys), (dvt, values)):
            for feats, at in ((pair, pl.ds(0, 2 * HEAD)), (lone, pl.ds(2 * HEAD, HEAD))):
                out[side, :, feats] = jnp.transpose(held[at]).astype(B16)

    each(2, attend_back_side)
    far_rows = pl.ds(length, length)
    kv_back = [
        [
            wire.copy(held.at[side, far_rows], got_kv.at[slot, side], sibling)
            for side in range(2)
        ]
        for slot, held in enumerate((keys, values))
    ]
    for copies in kv_back:
        for copy in copies:
            copy.start()
    if early:
        def stage(slot, halves, out, sem):
            lanes = pl.ds(0, out.shape[1])
            for owner in range(8):
                a, b = Chip.place(owner // 2)
                rows = pl.ds(48 * (4 * (owner % 2) + 2 * a + b), 48)
                piece = jnp.concatenate([half[24 * owner : 24 * owner + 24] for half in halves], 0)
                piece = jnp.pad(piece, ((0, 0), (0, out.shape[1] - piece.shape[1])))
                probs[0, slot, rows, lanes] = piece.astype(B16)
            return fetch(probs.at[0, slot, pl.ds(0, wide), lanes], out, sem)

        totals = []
        for t in (1, 2):
            held, copy = near[0, t]
            copy.wait()
            across[t][1].wait()
            totals.append(
                held[...].astype(F32)
                + grad_out[0, t, mine_grads].astype(F32)
                + across[t][0][...].astype(F32)
            )
        stores = [stage(2, totals, mlp_out, local_sem.at[1])]

    a_flip = flip.at[0]
    a_flip[...] = transposed(a_ref[...])
    total = None
    for slot in range(3):
        for side, weight in enumerate((qkv_own, qkv_far)):
            if slot:
                kv_back[slot - 1][side].wait()
                own = (keys, values)[slot - 1][side, mine_rows].astype(F32)
                grad = (own + got_kv[slot - 1, side].astype(F32)).astype(B16)
            else:
                grad = q_ref[side]
            grad_out[side, 0, :, pl.ds(slot * third, third)] = dot_nn(a_flip[...], grad).astype(B16)
            part = dot_nn(grad, weight[slot])
            total = part if total is None else total + part
    z1[...] = total
    if early:
        attn_pairs = []
        for side in (1, 0):
            held = h_ref.at[1, pl.ds((2 + side) * rows, rows)]
            copy = wire.copy(grad_out.at[side, 0, away_grads], held, sibling)
            copy.start()
            attn_pairs.append((held, copy))
    @pl.when(stays)
    def _():
        route_local.wait()
        route_near.wait_send()
        route_over.wait_recv()

    @pl.when(jnp.logical_not(stays))
    def _():
        route_over.wait_send()
        route_far.wait_send()
        route_near.wait_recv()
        route_far.wait_recv()

    def first_back(i, totals):
        rows = pl.ds(pl.multiple_of(i * rows_at, 16), rows_at)
        grad = z1[rows]
        unit = unit1[rows].astype(F32)
        z = z2[rows] + back_norm(grad, unit, kept(0, rows, heads), gain1_ref[...][None, :])
        b_ref[rows] = z.astype(B16)
        dec_out[0, rows] = z[:, :third].astype(B16)
        dec_out[1, rows] = z[:, third:].astype(B16)
        ids = lax.broadcasted_iota(jnp.int32, (rows_at, 1), 0) + (base + i * rows_at)
        seen = jnp.sum(jnp.where(cells_row == ids, 1.0, 0.0), -1, keepdims=True)
        return add_rows(totals[0], grad * unit), add_rows(totals[1], (1.0 - seen) * z)

    gain1_grad, mask_grad = lax.fori_loop(0, length // rows_at, first_back, (zero, zero))
    if not early:
        stores = [fetch(dec_out, pos_out, local_sem.at[0])]
    small_out[0:1] = gain1_grad
    small_out[1:2] = gain2_grad
    small_out[2:3] = mask_grad

    ids = (lax.broadcasted_iota(jnp.int32, (used, length), 1) + base).astype(F32)
    cells_col = jnp.transpose(jnp.broadcast_to(cells_row.astype(F32), (8, used)))[:, 0:1]
    place = jnp.where(cells_col == ids, 1.0, 0.0).astype(B16)
    dvis_mine[...] = dot_nn(place, b_ref[...]).astype(B16)
    dvis_pair = wire.copy(dvis_mine, dvis_near, sibling)
    dvis_over = wire.copy(dvis_mine, dvis_far, facing)
    dvis_cross = wire.copy(dvis_mine, dvis_near, beyond)

    @pl.when(stays)
    def _():
        dvis_over.start()

    @pl.when(jnp.logical_not(stays))
    def _():
        dvis_pair.start()
        dvis_cross.start()

    if early:
        halves = [jnp.transpose(dec_out[half].astype(F32)) for half in range(2)]
        stores.append(stage(0, halves, pos_out, local_sem.at[0]))
        halves = []
        for side, (held, copy) in zip((1, 0), attn_pairs):
            copy.wait()
            halves.insert(0, held[...].astype(F32) + grad_out[side, 0, mine_grads].astype(F32))
        stores.append(stage(1, halves, attn_out, local_sem.at[2]))

    def dvis_sum(first, second):
        dvis_out[...] = (first[...].astype(F32) + second[...].astype(F32)).astype(B16)

    @pl.when(stays)
    def _():
        dvis_pair.wait_recv()
        dvis_sum(dvis_mine, dvis_near)
        dvis_over.wait_send()

    @pl.when(jnp.logical_not(stays))
    def _():
        dvis_over.wait_recv()
        dvis_cross.wait_recv()
        dvis_sum(dvis_far, dvis_near)
        dvis_pair.wait_send()
        dvis_cross.wait_send()

    for copy in stores:
        copy.wait()


def decoder(early, vis, lengths, cells, pos_own, pos_far, mask, gains, weights, cot, enc, ident):
    qkv_own, qkv_far, out_own, up, down = weights
    length, wide = pos_own.shape
    used = vis.shape[0]
    third = wide // 2
    hidden = up.shape[1]
    keys = 2 * length
    heads = third // HEAD
    assert heads == 3 and length % 112 == 0
    whole = pl.BlockSpec(memory_space=VMEM)
    there = pl.BlockSpec(memory_space=pl.ANY)
    grads = (2, 3, wide, hidden)
    outs = [
        (jax.ShapeDtypeStruct((2, length, third), B16), there),
        (jax.ShapeDtypeStruct((used, wide), B16), whole),
        (jax.ShapeDtypeStruct((8, wide), F32), whole),
        (jax.ShapeDtypeStruct((used, enc.shape[1] // 2), B16), there),
    ]
    if early:
        lanes = -(-length // 128) * 128
        outs += [
            (jax.ShapeDtypeStruct((wide, lanes), B16), there),
            (jax.ShapeDtypeStruct((wide, hidden), B16), there),
            (jax.ShapeDtypeStruct((wide, hidden), B16), there),
        ]
    else:
        outs += [
            (jax.ShapeDtypeStruct((2, length, third), B16), there),
            (jax.ShapeDtypeStruct(grads, B16), whole),
        ]
    return pl.pallas_call(
        functools.partial(dec_kernel, early),
        out_shape=[item for item, _ in outs],
        in_specs=[whole, pl.BlockSpec(memory_space=pltpu.SMEM), whole]
        + [there] * 2
        + [whole] * 6
        + [there] * 4,
        out_specs=[spec for _, spec in outs],
        scratch_shapes=[VMEM(grads, B16)] * early
        + [
            VMEM((2, length, third), B16),
            VMEM(out_own.shape, B16),
            VMEM((2, wide, hidden), B16),
            VMEM((2, hidden, wide), B16),
            VMEM((length, wide), B16),
            VMEM((length, wide), F32),
            VMEM((length, wide), B16),
            VMEM((length, wide), B16),
            VMEM((2, length, third), B16),
            VMEM((2, keys, third), B16),
            VMEM((2, keys, third), B16),
            VMEM((2, heads, length, keys), B16),
            VMEM((2, length, 128), F32),
            VMEM((2, length, third), B16),
            VMEM((length, wide), B16),
            VMEM((length, wide), B16),
            VMEM((2, length, hidden), B16),
            VMEM((2, length, hidden), B16),
            VMEM((length, wide), F32),
            VMEM((2, length, third), B16),
            VMEM((2, wide, length), B16),
            VMEM((third, keys), F32),
            VMEM((third, keys), F32),
            VMEM((2, 2, length, third), B16),
            VMEM((used, wide), B16),
            VMEM((used, wide), B16),
            VMEM((used, wide), B16),
            pltpu.SemaphoreType.REGULAR,
            pltpu.SemaphoreType.DMA((7,)),
            pltpu.SemaphoreType.DMA((40,)),
            pltpu.SemaphoreType.DMA((40,)),
        ],
        compiler_params=pltpu.CompilerParams(
            collective_id=ident, has_side_effects=True, vmem_limit_bytes=int(63.9 * 1024) * 1024
        ),
        name="decoder",
    )(
        vis,
        lengths,
        cells,
        pos_own,
        pos_far,
        mask,
        gains[0],
        gains[1],
        qkv_own,
        qkv_far,
        out_own,
        up,
        down,
        cot,
        enc,
    )


def pack(grad, owners):
    rows, cols = grad.shape
    own = rows // owners
    fold = 1
    while own * fold % 16:
        fold *= 2
    grad = grad.astype(B16).reshape(owners, own, fold, cols // fold)
    return jnp.swapaxes(grad, 1, 2).reshape(owners, fold * own, cols // fold)


def unpack(piece, own):
    fold = piece.shape[0] // own
    return jnp.swapaxes(piece.reshape(fold, own, -1), 0, 1).reshape(own, -1)


def pick(pair, index):
    return lax.dynamic_index_in_dim(pair, index, 0, keepdims=False)


def enc_kernel(*refs):
    (
        length_ref, tok_hbm, qkv_hbm, out_hbm, up_hbm, down_hbm, bridge_ref, gain1_ref, gain2_ref,
        pos_hbm, dqkv_hbm,
        vis_out, dqkv_far, pos_far, enc_ref, unit1, unit2, stats, a_ref, triple, probs, o_ref, b_ref,
        slope, h_ref,
        x_ref, qkv, w_out, w_up, w_down, z2, part_ref, part_far, pos_full, pos_half,
        local_sem, send_sem, recv_sem,
    ) = refs
    s, d, m = place_of()
    sibling, facing = (1 - s, d, m), (s, d, 1 - m)
    stays = s == m
    used, wide = x_ref.shape
    half = tok_hbm.shape[1]
    rest = used - half
    wire = Wire(send_sem, recv_sem)

    y = lax.rem(d, 2)
    beside = (s, d + 1 - 2 * y, m)

    greet([sibling, facing, beside])
    first, last = pl.ds(0, half), pl.ds(half, rest)
    tok_first = wire.copy(tok_hbm.at[s], x_ref.at[first], facing)
    tok_last = wire.copy(tok_hbm.at[s, pl.ds(0, rest)], x_ref.at[last], facing)
    own_first = pltpu.make_async_copy(tok_hbm.at[s], x_ref.at[first], local_sem.at[0])
    own_last = pltpu.make_async_copy(
        tok_hbm.at[s, pl.ds(0, rest)], x_ref.at[last], local_sem.at[0]
    )

    @pl.when(m == 0)
    def _():
        tok_first.start()
        own_first.start()

    @pl.when(m == 1)
    def _():
        tok_last.start()
        own_last.start()

    pos_load = fetch(pos_hbm, pos_full, local_sem.at[5])
    loads = [
        fetch(hbm, held, local_sem.at[i + 1])
        for i, (hbm, held) in enumerate(
            ((qkv_hbm, qkv), (out_hbm, w_out), (up_hbm, w_up), (down_hbm, w_down))
        )
    ]
    size = dqkv_hbm.shape[1] // 2
    mine = (slice(None), pl.ds(s * size, size))
    over = wire.copy(dqkv_hbm.at[mine], dqkv_far.at[mine], facing)
    share = wire.copy(dqkv_far.at[mine], dqkv_far.at[mine], sibling)

    low = pos_hbm.shape[0] // 32 * 16
    pos_parts = [pl.ds(0, low), pl.ds(low, pos_hbm.shape[0] - low)]
    pos_over = [wire.copy(pos_half.at[part], pos_far.at[part], facing) for part in pos_parts]
    pos_trade = [wire.copy(pos_far.at[part], pos_far.at[part], beside) for part in pos_parts]

    def by_place(on_stays, act):
        for part in range(2):

            @pl.when(jnp.logical_and(stays if on_stays else jnp.logical_not(stays), y == part))
            def _(part=part):
                act(part)

    @pl.when(m == 0)
    def _():
        own_first.wait()
        tok_first.wait_send()
        tok_last.wait_recv()

    @pl.when(m == 1)
    def _():
        own_last.wait()
        tok_last.wait_send()
        tok_first.wait_recv()

    over.start()
    pos_load.wait()

    def send_positions(part):
        pos_half[pos_parts[part]] = pos_full[pos_parts[part]].astype(B16)
        pos_over[part].start()

    by_place(True, send_positions)

    lane = lax.broadcasted_iota(jnp.int32, (1, 128), 1)

    unit, inverse = norm_of(x_ref[...].astype(F32))
    unit1[...] = unit
    stats[...] = jnp.where(lane == 0, inverse, 0.0)
    a = (unit * gain1_ref[...][None, :]).astype(B16)
    a_ref[...] = a
    loads[0].wait()
    for slot in range(3):
        triple[slot] = dot_nn(a, qkv[slot]).astype(B16)

    valid = lax.broadcasted_iota(jnp.int32, (1, used), 1) < length_ref[s]
    masks = head_masks()
    for pair in range(triple.shape[2] // (2 * HEAD)):
        feats = pl.ds(pair * 2 * HEAD, 2 * HEAD)
        q, k, v = (triple[slot, :, feats] for slot in range(3))
        halves = []
        for head in range(2):
            scores = dot_nt(jnp.where(masks[head], q, 0), k) * HEAD**-0.5
            scores = jnp.where(valid, scores, NEG)
            raised = jnp.exp(scores - jnp.max(scores, -1, keepdims=True))
            p = (raised / jnp.sum(raised, -1, keepdims=True)).astype(B16)
            probs[2 * pair + head] = p
            halves.append(dot_nn(p, v))
        o_ref[:, feats] = jnp.where(masks[0], halves[0], halves[1]).astype(B16)

    loads[1].wait()
    part = dot_nn(o_ref[...], w_out[...])
    part_ref[0] = part.astype(B16)
    attn = wire.copy(part_ref.at[0], part_far.at[0], facing)
    attn.start()
    z2[...] = x_ref[...].astype(F32) + part

    attn.wait()
    z = z2[...] + part_far[0].astype(F32)
    z2[...] = z
    unit, inverse = norm_of(z)
    unit2[...] = unit
    stats[...] = jnp.where(lane == 1, inverse, stats[...])
    b = (unit * gain2_ref[...][None, :]).astype(B16)
    b_ref[...] = b
    loads[2].wait()
    step = 512

    def up(i):
        cols = pl.ds(pl.multiple_of(i * step, step), step)
        u = dot_nn(b_ref[...], w_up[:, cols])
        phi = 0.5 + 0.5 * lax.erf(u * 0.5**0.5)
        h_ref[:, cols] = (u * phi).astype(B16)
        bell = jnp.exp(u * u * -0.5) * (0.5 / jnp.pi) ** 0.5
        slope[:, cols] = (phi + u * bell).astype(B16)

    each(w_up.shape[1] // step, up)

    over.wait()
    share.start()

    def trade_positions(part):
        pos_over[part].wait_recv()
        pos_trade[part].start()

    by_place(False, trade_positions)
    loads[3].wait()
    part = dot_nn(h_ref[...], w_down[...])
    z2[...] = z2[...] + part
    part_ref[1] = part.astype(B16)
    mlp = wire.copy(part_ref.at[1], part_far.at[1], facing)
    vis_near = wire.copy(vis_out, vis_out, sibling)

    @pl.when(stays)
    def _():
        mlp.wait_recv()
        enc = (z2[...] + part_far[1].astype(F32)).astype(B16)
        enc_ref[...] = enc
        vis_out[...] = dot_nn(enc, bridge_ref[...]).astype(B16)
        vis_near.start()

    @pl.when(jnp.logical_not(stays))
    def _():
        mlp.start()
        enc_ref[...] = jnp.zeros(enc_ref.shape, B16)

    @pl.when(stays)
    def _():
        vis_near.wait_send()

    @pl.when(jnp.logical_not(stays))
    def _():
        mlp.wait_send()
        vis_near.wait_recv()

    def finish_positions(part):
        pos_trade[part].wait_send()
        pos_trade[1 - part].wait_recv()

    by_place(True, lambda part: pos_over[part].wait_send())
    by_place(False, finish_positions)
    share.wait()


def encoder(lengths, tokens, weights, bridge, gains, pos, dqkv, used, ident):
    qkv, out, up, down = weights
    wide = tokens.shape[2]
    feats = qkv.shape[2]
    hidden = up.shape[1]
    whole = pl.BlockSpec(memory_space=VMEM)
    there = pl.BlockSpec(memory_space=pl.ANY)
    shape = jax.ShapeDtypeStruct
    outs = [
        (shape((used, pos.shape[1]), B16), whole),
        (shape(dqkv.shape, B16), there),
        (shape(pos.shape, B16), there),
        (shape((used, wide), B16), whole),
        (shape((used, wide), F32), whole),
        (shape((used, wide), F32), whole),
        (shape((used, 128), F32), whole),
        (shape((used, wide), B16), whole),
        (shape((3, used, feats), B16), whole),
        (shape((feats // HEAD, used, used), B16), whole),
        (shape((used, feats), B16), whole),
        (shape((used, wide), B16), whole),
        (shape((used, hidden), B16), whole),
        (shape((used, hidden), B16), whole),
    ]
    return pl.pallas_call(
        enc_kernel,
        out_shape=[item for item, _ in outs],
        in_specs=[pl.BlockSpec(memory_space=pltpu.SMEM)]
        + [there] * 5
        + [whole] * 3
        + [there] * 2,
        out_specs=[spec for _, spec in outs],
        scratch_shapes=[
            VMEM((used, wide), B16),
            VMEM(qkv.shape, B16),
            VMEM(out.shape, B16),
            VMEM(up.shape, B16),
            VMEM(down.shape, B16),
            VMEM((used, wide), F32),
            VMEM((2, used, wide), B16),
            VMEM((2, used, wide), B16),
            VMEM(pos.shape, F32),
            VMEM(pos.shape, B16),
            pltpu.SemaphoreType.DMA((6,)),
            pltpu.SemaphoreType.DMA((16,)),
            pltpu.SemaphoreType.DMA((16,)),
        ],
        compiler_params=remote_params(ident),
        name="encoder",
    )(
        lengths, tokens, qkv, out, up, down, bridge, gains[0], gains[1],
        pos, dqkv,
    )


def back_kernel(cube, *refs):
    (
        dvis_ref, bridge_ref, gain1_ref, gain2_ref, unit1, unit2, stats, a_ref, triple, probs, o_ref,
        b_ref, slope, h_ref, enc_half, small_dec, qkv_hbm, out_hbm, up_hbm, down_hbm, *refs,
    ) = refs
    if cube:
        (
            pos_hbm, attn_hbm, mlp_hbm,
            tok_out, small_out, enc_out, mlp_out, attn_out, pos_out, bridge_all,
            near, held, box0, box1, box2,
            dec_held, dec_box0, dec_box1, dec_box2, side_held, side_box0, side_box1, side_box2,
            pos_sum, pos_got, attn_sum, attn_got, bridge_near, small_box, grads, bridge_grad, *refs,
        ) = refs
    else:
        tok_out, small_out, grads, bridge_grad, *refs = refs
    (
        qkv, w_out, w_up, w_down, gu, dy, part, part_far, dz, da_ref, do_ref, dqkv, flip, tok_part,
        local_sem, send_sem, recv_sem,
    ) = refs
    s, d, m = place_of()
    sibling, facing = (1 - s, d, m), (s, d, 1 - m)
    stays = s == m
    used, wide = unit1.shape
    feats = o_ref.shape[1]
    hidden = h_ref.shape[1]
    half = tok_part.shape[1]
    rest = used - half
    wire = Wire(send_sem, recv_sem)
    section = wide // 2

    if cube:
        chip = Chip(s, d, m)
        z, y = chip.z, chip.me["y"]
        others = [(s, 2 * lax.rem(z + k, 4) + y, m) for k in (1, 2, 3)]
        greet([sibling, facing, (1 - s, d, 1 - m), chip.near[0]] + others)
    else:
        greet([sibling, facing])

    if cube:
        cells = pos_sum.shape[2]
        pos_lanes = pos_hbm.shape[-1]
        span = attn_hbm.shape[-1]
        blank = (slice(None),) * 4
        early_loads = [
            fetch(hbm, dec_held.at[blank + (pl.ds(first, hbm.shape[-1]),)], local_sem.at[4 + i])
            for i, (hbm, first) in enumerate(
                ((pos_hbm, 0), (attn_hbm, pos_lanes), (mlp_hbm, pos_lanes + span))
            )
        ]
        for copy in early_loads:
            copy.wait()
        orders = ("yab", "ayb", "yab", "yab")
        mlp_orders = (("yab", "ayb"), ("yab", "ayb"), ("ayb", "yab"))
        attn_orders = ("yab", "yab", "ayb", "ayb")
        tiles = (pos_lanes + 2 * span) // 128
        cuts = [128 * (tiles * i // 4) for i in range(5)]
        early_folds = [
            Fold(
                wire, chip, dec_held, (dec_box0, dec_box1, dec_box2), pl.ds(low, high - low), "yab",
                order, False,
            )
            for low, high, order in zip(cuts, cuts[1:], orders)
        ]
        for fold in early_folds:
            fold.start()

    loads = [
        fetch(hbm, held, local_sem.at[i])
        for i, (hbm, held) in enumerate(
            ((down_hbm, w_down), (up_hbm, w_up), (out_hbm, w_out), (qkv_hbm, qkv))
        )
    ]

    def transposed(value):
        return jnp.transpose(value.astype(F32)).astype(B16)

    dvis = dvis_ref[...]
    grad = dot_nt(dvis, bridge_ref[...])
    dy[...] = grad
    dm = grad.astype(B16)
    da_ref[...] = dm
    flip[0] = transposed(dm)
    flip[1] = transposed(b_ref[...])
    bridge_grad[...] = dot_tn(enc_half[...], dvis).astype(B16)
    if cube:
        bridge_rows = bridge_near.shape[0]
        bridge_pair = wire.copy(
            bridge_grad.at[pl.ds(pl.multiple_of((1 - s) * bridge_rows, 16), bridge_rows)],
            bridge_near,
            sibling,
        )
        bridge_pair.start()

    loads[0].wait()
    step = 512
    first_mlp = 4 * feats
    steps = hidden // step
    if cube:
        away_rows = pl.ds(pl.multiple_of((1 - s) * section, 16), section)

        class Group:
            def __init__(self, first, size, orders):
                self.lanes, self.orders = pl.ds(first, size), orders
                self.pair = wire.copy(
                    grads.at[away_rows, self.lanes], near.at[:, self.lanes], sibling
                )
                self.pair.start()

            def start(self):
                self.pair.wait()
                for owner in range(8):
                    rows = pl.ds(48 * owner, 48)
                    from_rows = pl.ds(pl.multiple_of(s * section + 48 * owner, 16), 48)
                    index = (owner % 2,) + Chip.place(owner // 2) + (slice(None), self.lanes)
                    held[index] = near[rows, self.lanes] + grads[from_rows, self.lanes]
                part = self.lanes.size // len(self.orders)
                self.folds = [
                    Fold(
                        wire, chip, held, (box0, box1, box2), pl.ds(self.lanes.start + i * part, part),
                        "yab", order, False,
                    )
                    for i, order in enumerate(self.orders)
                ]
                for fold in self.folds:
                    fold.start()

            def step(self, k):
                for fold in self.folds:
                    fold.step(k)

            def end(self):
                part = self.lanes.size // len(self.folds)
                for i, fold in enumerate(self.folds):
                    enc_out[:, pl.ds(self.lanes.start + i * part, part)] = fold.end()

        mlp_groups = []

    for i in range(steps):
        cols = pl.ds(i * step, step)
        grads[:, pl.ds(first_mlp + 2 * i * step, step)] = dot_nn(flip[0], h_ref[:, cols]).astype(B16)
        grad_u = dot_nt(da_ref[...], w_down[cols, :]) * slope[:, cols].astype(F32)
        grad_u = grad_u.astype(B16)
        gu[:, cols] = grad_u
        grads[:, pl.ds(first_mlp + (2 * i + 1) * step, step)] = dot_nn(flip[1], grad_u).astype(B16)
        if cube:
            mlp_groups.append(Group(first_mlp + 2 * i * step, 2 * step, mlp_orders[i % 3]))
            if i:
                mlp_groups[i - 1].start()

    loads[1].wait()
    grad = dot_nt(gu[...], w_up[...])
    part[...] = grad.astype(B16)
    over = wire.copy(part, part_far.at[0], facing)
    over.start()
    dz[...] = grad
    gain2_grad = jnp.sum(grad * unit2[...], 0, keepdims=True)

    if cube:
        mlp_groups[-1].start()

    def back_norm(grad, unit, inverse, gain):
        scaled = grad * gain
        mean = jnp.mean(scaled, -1, keepdims=True)
        tilt = jnp.mean(scaled * unit, -1, keepdims=True)
        return inverse * (scaled - mean - unit * tilt)

    over.wait()
    whole = dz[...] + part_far[0].astype(F32)
    dz2 = dy[...] + back_norm(whole, unit2[...], stats[:, 1:2], gain2_ref[...][None, :])
    dy[...] = dz2
    grad_a = dz2.astype(B16)
    da_ref[...] = grad_a
    flip[0] = transposed(grad_a)
    loads[2].wait()
    grads[:, pl.ds(3 * feats, feats)] = dot_nn(flip[0], o_ref[...]).astype(B16)
    do_ref[...] = dot_nt(grad_a, w_out[...]).astype(B16)

    if cube:
        out_group = Group(3 * feats, feats, attn_orders[3:])
        bridge_pair.wait()
        narrow = bridge_near.shape[1]
        for at in range(4):
            side_held[Chip.place(at)] = (
                bridge_near[pl.ds(48 * at, 48)]
                + bridge_grad[pl.ds(pl.multiple_of(s * bridge_rows + 48 * at, 16), 48)]
            )
        bridge_fold = Fold(
            wire, chip, side_held, (side_box0, side_box1, side_box2), pl.ds(0, narrow), "ab", "ab", True
        )
        bridge_fold.start()

    masks = head_masks()
    scale = HEAD**-0.5
    for pair in range(feats // (2 * HEAD)):
        at = pl.ds(pair * 2 * HEAD, 2 * HEAD)
        q, k, v = (triple[slot, :, at] for slot in range(3))
        do = do_ref[:, at]
        both = do.astype(F32) * o_ref[:, at].astype(F32)
        parts = []
        for head in range(2):
            delta = jnp.sum(jnp.where(masks[head], both, 0.0), -1, keepdims=True)
            do_head = jnp.where(masks[head], do, 0)
            p = probs[2 * pair + head]
            ds = (p.astype(F32) * (dot_nt(do_head, v) - delta)).astype(B16)
            parts.append((dot_nn(ds, k) * scale, dot_tn(ds, q) * scale, dot_tn(p, do)))
        for slot in range(3):
            dqkv[slot, :, at] = jnp.where(masks[0], parts[0][slot], parts[1][slot]).astype(B16)

    if cube:
        out_group.start()
        for fold in early_folds:
            fold.step(0)
        bridge_fold.step(0)

    flip[1] = transposed(a_ref[...])
    loads[3].wait()
    total = None
    for slot in range(3):
        grads[:, pl.ds(slot * feats, feats)] = dot_nn(flip[1], dqkv[slot]).astype(B16)
        term = dot_nt(dqkv[slot], qkv[slot])
        total = term if total is None else total + term
    part[...] = total.astype(B16)
    dz[...] = total
    gain1_grad = jnp.sum(total * unit1[...], 0, keepdims=True)
    first, last = pl.ds(0, half), pl.ds(half, rest)
    over_first = wire.copy(part.at[first], part_far.at[1, first], facing)
    over_last = wire.copy(part.at[last], part_far.at[1, last], facing)

    @pl.when(m == 0)
    def _():
        over_last.start()

    @pl.when(m == 1)
    def _():
        over_first.start()

    small_out[...] = jnp.zeros(small_out.shape, F32)
    row = 0
    for value in (
        gain1_grad, gain2_grad, small_dec[0:1], small_dec[1:2], small_dec[2:3],
    ):
        for i in range(value.shape[1] // 128):
            small_out[row : row + 1] = value[:, i * 128 : (i + 1) * 128]
            row += 1

    if cube:
        attn_groups = [
            Group(i * feats, feats, (order,)) for i, order in enumerate(attn_orders[:3])
        ]
        small_copies = [
            wire.copy(small_out, small_box.at[i], partner)
            for i, partner in enumerate([sibling, facing] + chip.near)
        ]

        def small_step(i):
            small_copies[i].wait()
            small_out[...] = small_out[...] + small_box[i]
            if i + 1 < len(small_copies):
                small_copies[i + 1].start()

        small_copies[0].start()
        for group in attn_groups:
            group.start()
        bridge_fold.step(1)
        small_step(0)

    def finish(rows, size):
        whole = dz[rows] + part_far[1, rows].astype(F32)
        unit = unit1[rows]
        grad = dy[rows] + back_norm(whole, unit, stats[rows][:, 0:1], gain1_ref[...][None, :])
        for side in range(2):
            tok_part[side, pl.ds(0, size)] = grad[:, side * section : (side + 1) * section]

    @pl.when(m == 0)
    def _():
        over_last.wait_send()
        over_first.wait_recv()
        finish(first, half)

    @pl.when(m == 1)
    def _():
        over_first.wait_send()
        over_last.wait_recv()
        tok_part[...] = jnp.zeros(tok_part.shape, F32)
        finish(last, rest)

    tok_pair = wire.copy(tok_part.at[1 - s], tok_out.at[s], sibling)
    tok_pair.start()
    tok_out[s] = tok_part[s]

    if cube:
        for fold in early_folds:
            fold.step(1)
        for group in mlp_groups:
            group.step(0)
        small_step(1)

        bridge_all[s, z, m] = bridge_fold.end().astype(B16)
        spread = [
            wire.copy(bridge_all.at[s, z, m], bridge_all.at[s, z, m], partner) for partner in others
        ]
        for copy in spread:
            copy.start()

        out_group.step(0)
        for group in attn_groups:
            group.step(0)
        small_step(2)
        for group in mlp_groups:
            group.step(1)

        wholes = jnp.concatenate([fold.end() for fold in early_folds], 1)
        for half_at in range(2):
            piece = wholes[24 * half_at : 24 * half_at + 24]
            pos_sum[half_at] = piece[:, :cells]
            attn_sum[half_at] = piece[:, pos_lanes : pos_lanes + span]
            mlp_out[:, pl.ds(half_at * span, span)] = piece[:, pos_lanes + span :]
        attn_over = wire.copy(attn_sum.at[1], attn_got, facing)
        attn_over.start()
        route_near = wire.copy(pos_sum.at[1 - s], pos_got.at[m], sibling)
        route_over = wire.copy(pos_sum.at[s], pos_got.at[m], facing)
        route_far = wire.copy(pos_sum.at[1 - s], pos_got.at[m], (1 - s, d, 1 - m))

        @pl.when(stays)
        def _():
            route_near.start()
            pos_got[m] = pos_sum[s]

        @pl.when(jnp.logical_not(stays))
        def _():
            route_over.start()
            route_far.start()


        out_group.step(1)
        for copy in spread:
            copy.wait()
        bridge_over = wire.copy(bridge_all.at[s, :, m], bridge_all.at[s, :, m], facing)
        bridge_over.start()
        for group in attn_groups:
            group.step(1)
        small_step(3)
        for group in mlp_groups:
            group.end()
        attn_over.wait()
        attn_out[...] = attn_sum[0] + attn_got[...]

        @pl.when(stays)
        def _():
            route_near.wait_send()
            route_over.wait_recv()

        @pl.when(jnp.logical_not(stays))
        def _():
            route_over.wait_send()
            route_far.wait_send()
            route_near.wait_recv()
            route_far.wait_recv()

        pos_out[...] = pos_got[0] + pos_got[1]
        out_group.end()
        bridge_over.wait()
        bridge_pair_all = wire.copy(bridge_all.at[s], bridge_all.at[s], sibling)
        bridge_pair_all.start()
        small_step(4)
        for group in attn_groups:
            group.end()
        bridge_pair_all.wait()

    tok_pair.wait()


def back(cube, dvis, bridge, gains, saved, small_dec, weights, dec_grads, cells, half, ident):
    unit1, unit2, stats, a, triple, probs, o, b, slope, h, enc_half = saved
    qkv, out, up, down = weights
    used, wide = unit1.shape
    feats, hidden = o.shape[1], h.shape[1]
    cols = 4 * feats + 2 * hidden
    narrow = bridge.shape[1]
    whole = pl.BlockSpec(memory_space=VMEM)
    there = pl.BlockSpec(memory_space=pl.ANY)
    shape = jax.ShapeDtypeStruct
    args = [dvis, bridge, gains[0], gains[1], *saved, small_dec, qkv, out, up, down]
    in_specs = [whole] * 16 + [there] * 4
    outs = [shape((2, half, wide // 2), F32), shape((24, 128), F32)]
    assert 2 * wide + 3 * narrow <= 24 * 128
    grads, bridge_grad = (wide, cols), (wide // 2, narrow)
    scratch = []
    if cube:
        pos, attn, mlp = dec_grads
        span = attn.shape[1]
        args += [
            pos.reshape(2, 2, 2, 48, -1), attn.reshape(2, 2, 2, 48, -1), mlp.reshape(2, 2, 2, 48, -1)
        ]
        in_specs += [there] * 3
        outs += [
            shape((48, cols), F32),
            shape((24, 2 * span), F32),
            shape((24, span), F32),
            shape((24, cells), F32),
            shape((2, 4, 2, 48, narrow), B16),
        ]

        def folded(axes, size):
            return [VMEM((2,) * (axes - k) + (48, size), B16) for k in range(axes + 1)]

        scratch = [
            VMEM((wide // 2, cols), B16),
            *folded(3, cols),
            *folded(3, pos.shape[1] + 2 * span),
            *folded(2, narrow),
            VMEM((48, narrow), B16),
            VMEM((2, 24, cells), F32),
            VMEM((2, 24, cells), F32),
            VMEM((2, 24, span), F32),
            VMEM((24, span), F32),
            VMEM((narrow // 2, narrow), B16),
            VMEM((5, 24, 128), F32),
            VMEM(grads, B16),
            VMEM(bridge_grad, B16),
        ]
    else:
        outs += [shape(grads, B16), shape(bridge_grad, B16)]
    scratch += [
        VMEM(qkv.shape, B16),
        VMEM(out.shape, B16),
        VMEM(up.shape, B16),
        VMEM(down.shape, B16),
        VMEM((used, hidden), B16),
        VMEM((used, wide), F32),
        VMEM((used, wide), B16),
        VMEM((2, used, wide), B16),
        VMEM((used, wide), F32),
        VMEM((used, wide), B16),
        VMEM((used, feats), B16),
        VMEM((3, used, feats), B16),
        VMEM((2, wide, used), B16),
        VMEM((2, half, wide // 2), F32),
        pltpu.SemaphoreType.DMA((14,)),
        pltpu.SemaphoreType.DMA((96,)),
        pltpu.SemaphoreType.DMA((96,)),
    ]
    return pl.pallas_call(
        functools.partial(back_kernel, cube),
        out_shape=outs,
        in_specs=in_specs,
        out_specs=[whole] * len(outs),
        scratch_shapes=scratch,
        compiler_params=remote_params(ident),
        name="encoder_back",
    )(*args)


def finish_kernel(step, *refs):
    decoded, tokens, small, enc, mlp, attn, pos, bridge = refs[:8]
    (
        decoded_out, tokens_out, e_qkv, e_out, e_up, e_down, one_e, two_e, bridge_out, mask_out,
        pos_out, d_qkv, d_out, d_up, d_down, one_d, two_d,
    ) = refs[8:]
    for i in range(2):
        decoded_out[i] = jnp.transpose(decoded[i].astype(F32))
    tokens_out[...] = tokens[...]
    for source, qkv, out in ((enc, e_qkv, e_out), (attn, d_qkv, d_out)):
        cols = qkv.shape[2]
        for slot in range(3):
            qkv[slot] = source[:, pl.ds(slot * cols, cols)]
        out[...] = source[:, pl.ds(3 * cols, cols)]
    first = 4 * e_qkv.shape[2]
    for i in range(e_up.shape[1] // step):
        at = pl.ds(i * step, step)
        e_down[:, at] = enc[:, pl.ds(first + 2 * i * step, step)]
        e_up[:, at] = enc[:, pl.ds(first + (2 * i + 1) * step, step)]
    hidden = d_up.shape[1]
    d_up[...] = mlp[:, :hidden]
    d_down[...] = mlp[:, hidden:]
    pos_out[...] = pos[...]
    own = bridge.shape[3]
    for side in range(2):
        for piece in range(8):
            rows = pl.ds((side * 8 + piece) * own, own)
            bridge_out[rows] = bridge[piece // 4, piece % 4, side].astype(F32)
    row = 0
    for out in (one_e, two_e, one_d, two_d, mask_out):
        for i in range(out.shape[0] // 128):
            out[pl.ds(i * 128, 128)] = small[row]
            row += 1


def finish(shapes, parts, step):
    whole = pl.BlockSpec(memory_space=VMEM)
    return pl.pallas_call(
        functools.partial(finish_kernel, step),
        out_shape=[jax.ShapeDtypeStruct(shape, F32) for shape in shapes],
        in_specs=[whole] * len(parts),
        out_specs=[whole] * len(shapes),
        compiler_params=pltpu.CompilerParams(vmem_limit_bytes=LIMIT),
        name="finish",
    )(*parts)


def per_device(
    tokens,
    clip_lengths,
    clip_cells,
    enc_qkv,
    enc_attn_out,
    enc_up,
    enc_down,
    enc_gain_one,
    enc_gain_two,
    bridge_weight,
    mask_token,
    position_embed,
    dec_qkv,
    dec_attn_out,
    dec_up,
    dec_down,
    dec_gain_one,
    dec_gain_two,
    cotangent,
):
    s, d, m = place_of()
    n = lax.axis_size("dp")
    owners = 2 * n
    cube = n == 8
    dec_wide = position_embed.shape[1]
    half_slots, enc_wide = tokens.shape[2:]
    used = -(-LONGEST // 32) * 32

    e_weights = (jnp.swapaxes(enc_qkv, 0, 1), enc_attn_out, enc_up, enc_down)
    d_qkv = jnp.transpose(dec_qkv, (1, 2, 0))
    vis, d_qkv_far, pos_far, enc, *saved = encoder(
        clip_lengths[:, 0],
        tokens[:, 0],
        e_weights,
        bridge_weight,
        (enc_gain_one, enc_gain_two),
        position_embed,
        d_qkv,
        used,
        1,
    )
    decoded, dvis, dec_small, enc_half, *dec_grads = decoder(
        cube,
        vis,
        clip_lengths[:, 0],
        clip_cells[:, 0],
        position_embed,
        pos_far,
        mask_token,
        (dec_gain_one, dec_gain_two),
        (d_qkv, d_qkv_far, dec_attn_out, dec_up, dec_down),
        cotangent[:, 0],
        enc,
        2,
    )
    tokens_grad, small, *rest = back(
        cube,
        dvis,
        bridge_weight,
        (enc_gain_one, enc_gain_two),
        (*saved, enc_half),
        dec_small,
        e_weights,
        dec_grads,
        position_embed.shape[0],
        half_slots,
        3,
    )
    if cube:
        e_own, d_own = enc_wide // owners, dec_wide // owners
        shapes = [
            (2, decoded.shape[2], decoded.shape[1]),
            tokens_grad.shape,
            (3, e_own, enc_qkv.shape[2]),
            (e_own, enc_attn_out.shape[0]),
            (e_own, enc_up.shape[1]),
            (e_own, enc_down.shape[0]),
            (enc_wide,),
            (enc_wide,),
            (enc_wide, dec_wide),
            (dec_wide,),
            (d_own, position_embed.shape[0]),
            (3, d_own, dec_qkv.shape[2]),
            (d_own, dec_attn_out.shape[0]),
            (d_own, dec_up.shape[1]),
            (d_own, dec_down.shape[0]),
            (dec_wide,),
            (dec_wide,),
        ]
        outs = list(finish(shapes, (decoded, tokens_grad, small, *rest), 512))
        outs[0] = jnp.swapaxes(outs[0], 1, 2)[:, None]
        outs[1] = outs[1][:, None]
        for i in (2, 11):
            outs[i] = jnp.swapaxes(outs[i], 0, 1)
        for i in (3, 5, 10, 12, 14):
            outs[i] = outs[i].T
        return tuple(outs)
    else:
        grads, bridge = rest
        pos_parts, dec_grads = dec_grads
        enc_final = unpack(scatter(pack(grads, owners)[None], 11), enc_wide // owners)
        packed = [
            pack(jnp.concatenate([dec_grads[side, t] for t in range(3)], 1), owners)
            for side in range(2)
        ]
        dec_final = unpack(scatter(jnp.stack(packed), 12), dec_wide // owners)
        parts = route(pos_parts, 13).astype(F32)
        packed = pack(jnp.transpose(parts[0] + parts[1]), n)
        zero = jnp.zeros_like(packed)
        packed = jnp.concatenate(
            [jnp.where(s == 0, packed, zero), jnp.where(s == 1, packed, zero)], 0
        )
        pos_final = unpack(scatter(packed[None], 14), dec_wide // owners)
        bridge_own = enc_wide // 2 // owners
        per = -(-small.size // owners)
        small = jnp.pad(small.reshape(-1), (0, per * owners - small.size)).reshape(owners, 1, per)
        rows = -(-(bridge_own + 1) // 16) * 16
        rep = jnp.concatenate(
            [
                bridge.astype(F32).reshape(owners, bridge_own, dec_wide),
                jnp.pad(small, ((0, 0), (0, 0), (0, dec_wide - per))),
                jnp.zeros((owners, rows - bridge_own - 1, dec_wide), F32),
            ],
            1,
        ).astype(B16)
        rep = scatter(rep[None], 15).astype(B16)
        everyone = gather(rep, n, 16).reshape(owners, 2, rows, dec_wide)
        bridge_grad = jnp.swapaxes(everyone[:, :, :bridge_own], 0, 1).reshape(enc_wide, dec_wide)
        small = everyone[:, 0, bridge_own, :per].astype(F32) + everyone[
            :, 1, bridge_own, :per
        ].astype(F32)
    cuts = [enc_wide, 2 * enc_wide, 2 * enc_wide + dec_wide, 2 * enc_wide + 2 * dec_wide]
    small = small.reshape(-1)[: 2 * enc_wide + 3 * dec_wide]
    one_e, two_e, one_d, two_d, mask_grad = jnp.split(small, cuts)

    def split(final, qkv, out, up, step):
        cols = qkv.shape[2]
        first = 3 * cols + out.shape[0]
        second = first + up.shape[1]
        if step:
            mlp = final[:, first:].reshape(final.shape[0], -1, 2, step)
            downs, ups = (mlp[:, :, i].reshape(final.shape[0], -1) for i in range(2))
        else:
            downs, ups = final[:, second:], final[:, first:second]
        return (
            final[:, : 3 * cols].reshape(-1, 3, cols), final[:, 3 * cols : first].T, ups, downs.T
        )

    return (
        decoded.astype(F32)[:, None],
        tokens_grad[:, None],
        *split(enc_final, enc_qkv, enc_attn_out, enc_up, 512),
        one_e,
        two_e,
        bridge_grad.astype(F32),
        mask_grad,
        pos_final.T,
        *split(dec_final, dec_qkv, dec_attn_out, dec_up, 0),
        one_d,
        two_d,
    )


def solution(mesh):
    return jax.shard_map(
        per_device,
        mesh=mesh,
        in_specs=(
            P(None, "dp", "mp", None),
            P(None, "dp"),
            P(None, "dp", None),
            P(None, None, "mp"),
            P("mp", None),
            P(None, "mp"),
            P("mp", None),
            P(),
            P(),
            P(),
            P(),
            P("mp", None),
            P(None, None, "mp"),
            P("mp", None),
            P(None, "mp"),
            P("mp", None),
            P(),
            P(),
            P(None, "dp", "mp", None),
        ),
        out_specs=(
            P(None, "dp", "mp", "section"),
            P(None, "dp", "mp", "section"),
            P(("section", "dp"), None, "mp"),
            P("mp", ("section", "dp")),
            P(("section", "dp"), "mp"),
            P("mp", ("section", "dp")),
            P(),
            P(),
            P(),
            P(),
            P("mp", ("section", "dp")),
            P(("section", "dp"), None, "mp"),
            P("mp", ("section", "dp")),
            P(("section", "dp"), "mp"),
            P("mp", ("section", "dp")),
            P(),
            P(),
        ),
        check_vma=False,
    )
```
